32 devices in a mesh: tile: 8 (over z, y), cond: 4 (over x, core).
Axes of the slice: x: 2, y: 2, z: 4, core: 2. Of those that a mesh axis runs over, the one named last changes fastest.
Arguments:
- theta: float32 [4096, 512], P(('tile', 'cond')), may hold values from -6 to 6
- target: int32 [4096, 512], P('tile'), may hold values 0 or 1
- kernel_real: float32 [8, 2, 65, 65], P('cond'), may hold values from -24 to 24
- kernel_imag: float32 [8, 2, 65, 65], P('cond'), may hold values from -24 to 24
- weights: int32 [8], replicated, may hold values from 1 to 4
- thresholds: float32 [8], P('cond'), may hold values from 0.5 to 1.5
Outputs:
- gradient: float32 [4096, 512], P(('tile', 'cond'))
The draws below stay inside these ranges and needn't reach their ends.
Inputs may be any that keep to these rules, and one draw needn't show every extreme that they name: Each pixel of the target is 0 or 1. Condition weights are small positive integers.
All inputs are finite; a program needn't handle non-finite values. No bound on the sum of `target` on one device may be relied on, other than what follows from the above.
Results may differ from the reference program's by a relative error of at most 0.00021.
Values sent between devices are 32-bit elements; how exact they have to be, the bound alone decides.
No kernel may reach another device: no remote copies, remote signals or barrier semaphores. Data moves between devices by JAX's collectives and lax.ppermute only.
A program may use at most 64 MiB of HBM per device.

```python
import jax
import jax.numpy as jnp
from jax import lax

TP = 512
HALO = 32
KSUP = 65
KERNELS = 2
CONDS = 8
NX = 4096


def touch_ends(result, key, least, high):
    spot = [jax.random.randint(jax.random.fold_in(key, axis), (), 0, length) for axis, length in enumerate(result.shape)]
    main_axis = result.shape.index(max(result.shape))
    neighbour = spot[:main_axis] + [(spot[main_axis] + 1) % result.shape[main_axis]] + spot[main_axis + 1:]
    return result.at[tuple(spot)].set(least).at[tuple(neighbour)].set(high)


def level_of(stream_key, dims, pieces, low, high):
    loudness = 1.0
    for axis_at, parts in pieces:
        steps = jax.random.uniform(jax.random.fold_in(jax.random.fold_in(stream_key, 6), axis_at), (parts,), jnp.float32, low / len(pieces), high / len(pieces))
        loudness = loudness * jnp.repeat(jnp.exp(steps), dims[axis_at] // parts).reshape((-1,) + (1,) * (len(dims) - 1 - axis_at))
    return loudness


def gaussian(key, shape, deviation, most, pieces=(), kind=jnp.bfloat16):
    drawn = jax.random.normal(key, shape, jnp.float32) * deviation
    if len(pieces) > 0:
        drawn = level_of(key, shape, pieces, -0.22, 0.18) * drawn
    return jnp.clip(drawn, min=-most, max=most).astype(kind)


def setup_inputs(seed: int = 0) -> dict:
    splits = jax.random.split(jax.random.key(seed), 7)
    theta = gaussian(splits[0], (NX, TP), 1.0, 6.0, ((0, 32),), jnp.float32)
    target = touch_ends((jax.random.randint(splits[1], (NX, TP), 0, 2) < 1).astype(jnp.int32), jax.random.fold_in(splits[1], 1), 0, 1)
    kernel_real = gaussian(splits[2], (CONDS, KERNELS, KSUP, KSUP), 4.0, 24.0, ((0, 4),), jnp.float32)
    kernel_imag = gaussian(splits[3], (CONDS, KERNELS, KSUP, KSUP), 4.0, 24.0, ((0, 4),), jnp.float32)
    weights = touch_ends(jax.random.randint(splits[4], (CONDS,), 1, 5), jax.random.fold_in(splits[4], 1), 1, 4).astype(jnp.int32)
    thresholds = jnp.clip(0.5 + 1.0 * jax.random.uniform(splits[5], (CONDS,), jnp.float32) ** level_of(splits[5], (CONDS,), ((0, 4),), -0.2, 0.2), 0.5, 1.5)
    return dict(theta=theta, target=target, kernel_real=kernel_real, kernel_imag=kernel_imag, weights=weights, thresholds=thresholds)


mask_steep = 2.0
resist_steep = 4.0
band_weight = 1.0


def tile_gradient(extended, target_map, kern_real, kern_imag, cond_weights, cond_thresholds):
    size_full = TP + 2 * HALO
    freq_index = (jnp.arange(KSUP, dtype=jnp.int32) - KSUP // 2) % size_full
    padded = jnp.zeros((size_full, size_full), extended.dtype).at[:, HALO:HALO + TP].set(extended)
    spectrum = jnp.fft.fft2(padded)[freq_index][:, freq_index]
    kernels = lax.complex(kern_real, kern_imag)

    def place(values):
        empty = jnp.zeros((size_full, size_full), spectrum.dtype)
        return empty.at[freq_index[:, None], freq_index[None, :]].set(values)

    def amplitudes(cond_kernels):
        grids = jax.vmap(place)(cond_kernels * spectrum)
        return jnp.fft.ifft2(grids)[:, HALO:HALO + TP, HALO:HALO + TP]

    def intensity(cond_kernels):
        amp_field = amplitudes(cond_kernels)
        return jnp.sum(jnp.real(amp_field) ** 2 + jnp.imag(amp_field) ** 2, axis=0)

    intensities = lax.map(intensity, kernels)
    resist_maps = jax.nn.sigmoid(resist_steep * (intensities - cond_thresholds[:, None, None]))
    band_mean = jnp.sum(resist_maps, axis=0) / CONDS
    slopes = 2.0 * cond_weights[:, None, None] * (resist_maps - target_map) + (2.0 * band_weight / CONDS) * (resist_maps - band_mean)
    fields = 2.0 * slopes * resist_steep * resist_maps * (1.0 - resist_maps)

    def backward(item):
        cond_kernels, weight_field = item
        amp_field = amplitudes(cond_kernels)
        drive = weight_field * amp_field
        grids = jnp.zeros((KERNELS, size_full, size_full), amp_field.dtype).at[:, HALO:HALO + TP, HALO:HALO + TP].set(drive)
        back_spec = jnp.fft.fft2(grids)[:, freq_index][:, :, freq_index]
        return jnp.sum(jnp.conj(cond_kernels) * back_spec, axis=0)

    adjoint = jnp.sum(lax.map(backward, (kernels, fields)), axis=0)
    return jnp.real(jnp.fft.ifft2(place(adjoint)))[:, HALO:HALO + TP]


def reference(theta, target, kernel_real, kernel_imag, weights, thresholds):
    tile_count = NX // TP
    mask_flat = jnp.tanh(mask_steep * theta)
    mask_tiles = mask_flat.reshape(tile_count, TP, TP)
    zero_tile = jnp.zeros((1, TP, TP), mask_tiles.dtype)
    before = jnp.concatenate([zero_tile, mask_tiles[:-1]], axis=0)[:, TP - HALO:]
    after = jnp.concatenate([mask_tiles[1:], zero_tile], axis=0)[:, :HALO]
    extended = jnp.concatenate([before, mask_tiles, after], axis=1)
    target_tiles = target.astype(jnp.float32).reshape(tile_count, TP, TP)
    cond_weights = weights.astype(jnp.float32) / jnp.sum(weights).astype(jnp.float32)

    def one_tile(item):
        return tile_gradient(item[0], item[1], kernel_real, kernel_imag, cond_weights, thresholds)

    sensitivity = lax.map(one_tile, (extended, target_tiles))
    zero_rim = jnp.zeros((1, HALO, TP), sensitivity.dtype)
    from_left = jnp.concatenate([zero_rim, sensitivity[:-1, HALO + TP:]], axis=0)
    from_right = jnp.concatenate([sensitivity[1:, :HALO], zero_rim], axis=0)
    mask_gradient = sensitivity[:, HALO:HALO + TP]
    mask_gradient = mask_gradient + jnp.pad(from_left, ((0, 0), (0, TP - HALO), (0, 0)))
    mask_gradient = mask_gradient + jnp.pad(from_right, ((0, 0), (TP - HALO, 0), (0, 0)))
    return mask_gradient.reshape(NX, TP) * (mask_steep * (1.0 - mask_flat * mask_flat))
```

```python
import functools

import jax
import jax.numpy as jnp
import ml_dtypes
import numpy as np
from jax import lax
from jax.experimental import pallas as pl
from jax.experimental.pallas import tpu as pltpu
from jax.sharding import PartitionSpec as P

TP = 512
HALO = 32
KSUP = 65
HALF = KSUP // 2
KERNELS = 2
CONDS = 8
FULL = TP + 2 * HALO
PARTS = 4
ROWS = TP // PARTS
FA = 40
FB = 64
BF = jnp.bfloat16
F32 = jnp.float32

mask_steep = 2.0
resist_steep = 4.0
band_weight = 1.0


def waves(positions):
    angles = (np.outer(np.asarray(positions, np.int64), np.arange(HALF + 1)) % FULL) * (2.0 * np.pi / FULL)
    return np.cos(angles), np.sin(angles)


def halves(table):
    high = table.astype(np.float32).astype(ml_dtypes.bfloat16)
    low = (table - high.astype(np.float64)).astype(np.float32).astype(ml_dtypes.bfloat16)
    return high, low


def row_table(positions):
    cosine, sine = waves(positions)
    table = np.zeros((len(positions), 2 * FA))
    table[:, : HALF + 1] = cosine
    table[:, FA : FA + HALF + 1] = sine
    return table


def column_table(positions):
    cosine, sine = waves(positions)
    table = np.zeros((len(positions), 4 * FB))
    for block, values in enumerate((cosine, cosine, sine, -sine)):
        table[:, block * FB : block * FB + HALF + 1] = values
    return table


@functools.cache
def tables():
    pixels = np.arange(TP) + HALO
    column = column_table(pixels)
    column_high, column_low = halves(column)
    turned = np.concatenate([column[:, : 2 * FB].T, column[:, 2 * FB :].T], axis=1)
    turned_high, turned_low = halves(turned)
    row = row_table(pixels)
    row_high, row_low = halves(row)
    out = {}
    out["column"] = np.stack([column_high, column_low])
    spectrum_rows = []
    halo_rows = []
    forward = []
    backward = []
    for part in range(PARTS):
        own = np.arange(ROWS) + part * ROWS + HALO
        into = row_table(np.arange(HALO) + (FULL - HALO if part == PARTS - 1 else 0))
        high, low = halves(np.concatenate([row_table(own), into]).T)
        spectrum_rows.append(np.concatenate([high, low, high], axis=1))
        high, low = halves(row_table(np.arange(HALO) + (0 if part == PARTS - 1 else FULL - HALO)))
        halo_rows.append(np.concatenate([high, low, high], axis=1))
        cols = slice(part * ROWS, (part + 1) * ROWS)
        high = np.concatenate([turned_high[:, :TP][:, cols], turned_high[:, TP:][:, cols]], axis=1)
        low = np.concatenate([turned_low[:, :TP][:, cols], turned_low[:, TP:][:, cols]], axis=1)
        forward.append(np.concatenate([high, high, low]))
        backward.append(np.concatenate([column_high[cols], column_high[cols], column_low[cols]]))
    out["spectrum_rows"] = np.stack(spectrum_rows)
    out["halo_rows"] = np.stack(halo_rows)
    out["forward"] = np.stack(forward)
    out["backward"] = np.stack(backward)
    out["turned"] = np.concatenate([turned_high, turned_high, turned_low])
    out["row"] = np.concatenate([row_high, row_low, row_high], axis=1)
    out["row_turned"] = np.concatenate([row_high.T, row_low.T])
    pick = np.zeros((KSUP, 4 * FB))
    for b in range(HALF + 1):
        pick[HALF + b, b] = pick[HALF - b, FB + b] = pick[HALF - b, 2 * FB + b] = pick[HALF + b, 3 * FB + b] = 1
    turn = np.zeros((FA, KSUP))
    for a in range(HALF + 1):
        turn[a, HALF - a] = 1
    keep = np.zeros((2, FA, 2 * FB))
    keep[:, : HALF + 1, : HALF + 1] = 1
    keep[1, 0, 0] = 0
    keep[:, 1 : HALF + 1, FB + 1 : FB + HALF + 1] = 1
    out["pick"] = pick.astype(ml_dtypes.bfloat16)
    out["turn"] = turn.astype(ml_dtypes.bfloat16)
    out["keep"] = (keep / (FULL * FULL)).astype(np.float32)
    return out


def dot(left, right):
    return jnp.dot(left, right, preferred_element_type=F32)


def split(value):
    high = value.astype(BF)
    return high, (value - high.astype(F32)).astype(BF)


def prepare_kernel(real_ref, imag_ref, thresholds_ref, pick_ref, turn_ref, keep_ref, out_ref):
    local_conds = real_ref.shape[0]
    for cond in range(local_conds):
        level = thresholds_ref[cond]
        for kern in range(KERNELS):
            for part, ref in enumerate((real_ref, imag_ref)):
                value = ref[cond, kern]
                high = value.astype(BF)
                rest = value - high.astype(F32)
                middle = rest.astype(BF)
                low = (rest - middle.astype(F32)).astype(BF)
                picked = [dot(piece, pick_ref[...]) for piece in (high, middle, low)]
                turned = [dot(turn_ref[...], piece[:, 2 * FB :].astype(BF)) for piece in picked]
                whole = picked[0] + picked[1] + picked[2]
                top = jnp.concatenate([whole[HALF:, : 2 * FB], jnp.zeros((FA - HALF - 1, 2 * FB), F32)], axis=0)
                top = top * keep_ref[0]
                bottom = (turned[0] + turned[1] + turned[2]) * keep_ref[1]
                mark = lax.broadcasted_iota(jnp.int32, (FA, 2 * FB), 0) == FA - 1
                out_ref[cond * KERNELS + kern, part] = jnp.where(mark, level, top + bottom)
                out_ref[cond * KERNELS + kern, 2 + part] = top - bottom


def spectrum_kernel(part_ref, theta_ref, halo_ref, column_ref, rows_ref, out_ref):
    mask = jnp.tanh(mask_steep * jnp.concatenate([theta_ref[...], halo_ref[...]], axis=0))
    high, low = split(mask)
    across = dot(high, column_ref[0]) + dot(low, column_ref[0]) + dot(high, column_ref[1])
    high, low = split(across)
    both = dot(rows_ref[0], jnp.concatenate([high, high, low], axis=0))
    even = both[:FA, : 2 * FB] - both[FA:, 2 * FB :]
    odd = both[FA:, : 2 * FB] + both[:FA, 2 * FB :]
    value = jnp.concatenate([even, odd], axis=0)
    for copy in range(out_ref.shape[0]):
        out_ref[copy] = value


def fields_kernel(
    part_ref, weights_ref, spectra_ref, kernels_ref, target_ref, forward_ref, backward_ref, row_ref, row_turned_ref,
    out_ref, lines, folded, amps, resists, total, turned,
):
    count = kernels_ref.shape[0]
    spectrum = spectra_ref[0] + spectra_ref[1] + spectra_ref[2] + spectra_ref[3]
    even, odd = spectrum[:FA], spectrum[FA:]

    def grids(kern, carry):
        he_real, he_imag, ho_real, ho_imag = (kernels_ref[kern, i] for i in range(4))
        stack = jnp.concatenate(
            [
                even * he_real + odd * ho_imag,
                odd * he_real - even * ho_imag,
                even * he_imag - odd * ho_real,
                odd * he_imag + even * ho_real,
            ],
            axis=0,
        )
        high, low = split(stack)
        lines[kern] = jnp.concatenate([high, low, high], axis=1)
        return carry

    lax.fori_loop(0, count, grids, 0)

    def fold(kern, carry):
        result = dot(lines[kern], forward_ref[0])
        parts = []
        for i in range(2):
            x_part = result[2 * FA * i : 2 * FA * i + FA]
            y_part = result[2 * FA * i + FA : 2 * FA * (i + 1)]
            parts.append(
                jnp.concatenate(
                    [x_part[:, :ROWS] + y_part[:, ROWS:], y_part[:, :ROWS] - x_part[:, ROWS:]], axis=0
                )
            )
        high, low = split(jnp.concatenate(parts, axis=1))
        folded[kern] = jnp.concatenate([high, high, low], axis=0)
        return carry

    lax.fori_loop(0, count, fold, 0)
    total[...] = jnp.zeros_like(total)

    def expose(cond, carry):
        intensity = jnp.zeros((TP, ROWS), F32)
        for kern in range(KERNELS):
            index = cond * KERNELS + kern
            amp = dot(row_ref[...], folded[index])
            amps[index] = amp
            intensity = intensity + amp[:, :ROWS] * amp[:, :ROWS] + amp[:, ROWS:] * amp[:, ROWS:]
        level = kernels_ref[cond * KERNELS, 0, FA - 1 :, :]
        resist = 1.0 / (1.0 + jnp.exp(resist_steep * (level - intensity)))
        resists[cond] = resist
        total[...] += resist
        return carry

    lax.fori_loop(0, CONDS, expose, 0)
    weight_sum = weights_ref[0]
    for i in range(1, CONDS):
        weight_sum = weight_sum + weights_ref[i]
    weight_sum = weight_sum.astype(F32)

    def drive(cond, carry):
        weight = weights_ref[cond].astype(F32) / weight_sum
        resist = resists[cond]
        slope = 2.0 * weight * (resist - target_ref[...].astype(F32)) + (2.0 * band_weight / CONDS) * (
            resist - total[...] * (1.0 / CONDS)
        )
        field = 2.0 * resist_steep * slope * resist * (1.0 - resist)
        field = jnp.concatenate([field, field], axis=1)
        for kern in range(KERNELS):
            index = cond * KERNELS + kern
            high, low = split(field * amps[index])
            long = dot(row_turned_ref[...], high)
            back = long[: 2 * FA] + long[2 * FA :] + dot(row_turned_ref[: 2 * FA], low)
            high, low = split(jnp.concatenate([back[:, :ROWS], back[:, ROWS:]], axis=0))
            turned[index] = jnp.concatenate([high, low, high], axis=1)
        return carry

    lax.fori_loop(0, CONDS, drive, 0)

    def gather(kern, carry):
        sum_even, sum_odd = carry
        result = dot(turned[kern], backward_ref[0])
        grads = []
        for i in range(2):
            c_part = result[2 * FA * i : 2 * FA * i + FA]
            s_part = result[2 * FA * i + FA : 2 * FA * (i + 1)]
            grads.append(
                (
                    c_part[:, : 2 * FB] - s_part[:, 2 * FB :],
                    s_part[:, : 2 * FB] + c_part[:, 2 * FB :],
                )
            )
        (x_real, y_real), (x_imag, y_imag) = grads
        he_real, he_imag, ho_real, ho_imag = (kernels_ref[kern, i] for i in range(4))
        sum_even = sum_even + x_real * he_real + x_imag * he_imag - y_real * ho_imag + y_imag * ho_real
        sum_odd = sum_odd + x_real * ho_imag - x_imag * ho_real + y_real * he_real + y_imag * he_imag
        return sum_even, sum_odd

    zero = jnp.zeros((FA, 2 * FB), F32)
    sum_even, sum_odd = lax.fori_loop(0, count, gather, (zero, zero))
    value = jnp.concatenate([sum_even, sum_odd], axis=0)
    for copy in range(out_ref.shape[0]):
        out_ref[copy] = value


def gradient_kernel(part_ref, theta_ref, own_ref, other_ref, turned_ref, rows_ref, halo_rows_ref, out_ref):
    def fold(value):
        high, low = split(value)
        result = dot(jnp.concatenate([high, low, high], axis=1), turned_ref[...])
        x_part, y_part = result[:FA], result[FA:]
        both = jnp.concatenate(
            [x_part[:, :TP] + y_part[:, TP:], y_part[:, :TP] - x_part[:, TP:]], axis=0
        )
        high, low = split(both)
        return jnp.concatenate([high, high, low], axis=0)

    mask = jnp.tanh(mask_steep * theta_ref[...])
    scale = mask_steep * (1.0 - mask * mask)
    out_ref[...] = dot(rows_ref[...], fold(own_ref[...])) * scale
    start = pl.multiple_of(jnp.where(part_ref[0] == PARTS - 1, ROWS - HALO, 0), HALO)
    rim = dot(halo_rows_ref[0], fold(other_ref[...]))
    mask = jnp.tanh(mask_steep * theta_ref[pl.ds(start, HALO), :])
    out_ref[pl.ds(start, HALO), :] += rim * (mask_steep * (1.0 - mask * mask))


def whole_spec(array):
    rank = len(array.shape)
    return pl.BlockSpec(array.shape, lambda i, *refs: (0,) * rank)


def part_spec(array):
    rank = len(array.shape)
    return pl.BlockSpec((1,) + array.shape[1:], lambda i, part, *refs: (part[0],) + (0,) * (rank - 1))


def call(kernel, scalars, operands, specs, out_shape, scratch=(), name=None):
    out_rank = len(out_shape.shape)
    return pl.pallas_call(
        kernel,
        grid_spec=pltpu.PrefetchScalarGridSpec(
            num_scalar_prefetch=len(scalars),
            grid=(1,),
            in_specs=specs,
            out_specs=pl.BlockSpec(out_shape.shape, lambda i, *refs: (0,) * out_rank),
            scratch_shapes=list(scratch),
        ),
        out_shape=out_shape,
        compiler_params=pltpu.CompilerParams(vmem_limit_bytes=48 * 1024 * 1024),
        name=name,
    )(*scalars, *operands)


def shards(theta, target, kernel_real, kernel_imag, weights, thresholds):
    table = {name: jnp.asarray(value) for name, value in tables().items()}
    tiles = lax.axis_size("tile")
    part = lax.axis_index("cond")
    parts = part.reshape(1).astype(jnp.int32)
    local = kernel_real.shape[0] * KERNELS
    rim_pairs = [(PARTS * i + PARTS - 1, PARTS * (i + 1)) for i in range(tiles - 1)]
    rim_pairs += [(b, a) for a, b in rim_pairs]

    prepared = call(
        prepare_kernel,
        (),
        (kernel_real, kernel_imag, thresholds, table["pick"], table["turn"], table["keep"]),
        [
            whole_spec(kernel_real),
            whole_spec(kernel_imag),
            pl.BlockSpec(memory_space=pltpu.SMEM),
            whole_spec(table["pick"]),
            whole_spec(table["turn"]),
            whole_spec(table["keep"]),
        ],
        jax.ShapeDtypeStruct((local, 4, FA, 2 * FB), F32),
        name="prepare_kernels",
    )
    kernels = lax.all_gather(prepared, "cond", axis=0, tiled=True)

    rim = lax.dynamic_slice_in_dim(theta, jnp.where(part == 0, 0, ROWS - HALO), HALO, axis=0)
    rim = lax.ppermute(rim, ("tile", "cond"), rim_pairs)
    spectra = call(
        spectrum_kernel,
        (parts,),
        (theta, rim, table["column"], table["spectrum_rows"]),
        [whole_spec(theta), whole_spec(rim), whole_spec(table["column"]), part_spec(table["spectrum_rows"])],
        jax.ShapeDtypeStruct((PARTS, 2 * FA, 2 * FB), F32),
        name="mask_spectrum",
    )
    spectra = lax.all_to_all(spectra, "cond", 0, 0, tiled=True)
    count = CONDS * KERNELS
    adjoints = call(
        fields_kernel,
        (parts, weights),
        (
            spectra, kernels, target, table["forward"], table["backward"], table["row"], table["row_turned"],
        ),
        [
            whole_spec(spectra),
            whole_spec(kernels),
            pl.BlockSpec((TP, ROWS), lambda i, part, *refs: (0, part[0])),
            part_spec(table["forward"]),
            part_spec(table["backward"]),
            whole_spec(table["row"]),
            whole_spec(table["row_turned"]),
        ],
        jax.ShapeDtypeStruct((PARTS, 2 * FA, 2 * FB), F32),
        scratch=(
            pltpu.VMEM((count, 4 * FA, 6 * FB), BF),
            pltpu.VMEM((count, 6 * FA, 2 * ROWS), BF),
            pltpu.VMEM((count, TP, 2 * ROWS), F32),
            pltpu.VMEM((CONDS, TP, ROWS), F32),
            pltpu.VMEM((TP, ROWS), F32),
            pltpu.VMEM((count, 4 * FA, 3 * ROWS), BF),
        ),
        name="coherent_fields",
    )
    adjoints = lax.all_to_all(adjoints, "cond", 0, 0, tiled=True)
    own = jnp.sum(adjoints, axis=0)
    other = lax.ppermute(own, ("tile", "cond"), rim_pairs)
    return call(
        gradient_kernel,
        (parts,),
        (theta, own, other, table["turned"], table["row"], table["halo_rows"]),
        [
            whole_spec(theta),
            whole_spec(own),
            whole_spec(other),
            whole_spec(table["turned"]),
            pl.BlockSpec((ROWS, 6 * FA), lambda i, part, *refs: (part[0], 0)),
            part_spec(table["halo_rows"]),
        ],
        jax.ShapeDtypeStruct((ROWS, TP), F32),
        name="mask_gradient",
    )


def solution(mesh):
    in_specs = (
        P(("tile", "cond"), None),
        P("tile", None),
        P("cond", None, None, None),
        P("cond", None, None, None),
        P(),
        P("cond"),
    )
    out_specs = P(("tile", "cond"), None)
    return jax.shard_map(shards, mesh=mesh, in_specs=in_specs, out_specs=out_specs, check_vma=False)
```

```python
import functools

import jax
import jax.numpy as jnp
import ml_dtypes
import numpy as np
from jax import lax
from jax.experimental import pallas as pl
from jax.experimental.pallas import tpu as pltpu
from jax.sharding import PartitionSpec as P

TP = 512
HALO = 32
KSUP = 65
HALF = KSUP // 2
KERNELS = 2
CONDS = 8
FULL = TP + 2 * HALO
PARTS = 4
ROWS = TP // PARTS
FA = 40
FB = 64
BF = jnp.bfloat16
F32 = jnp.float32

mask_steep = 2.0
resist_steep = 4.0
band_weight = 1.0


def waves(positions):
    angles = (np.outer(np.asarray(positions, np.int64), np.arange(HALF + 1)) % FULL) * (2.0 * np.pi / FULL)
    return np.cos(angles), np.sin(angles)


def halves(table):
    high = table.astype(np.float32).astype(ml_dtypes.bfloat16)
    low = (table - high.astype(np.float64)).astype(np.float32).astype(ml_dtypes.bfloat16)
    return high, low


def row_table(positions):
    cosine, sine = waves(positions)
    table = np.zeros((len(positions), 2 * FA))
    table[:, : HALF + 1] = cosine
    table[:, FA : FA + HALF + 1] = sine
    return table


def column_table(positions):
    cosine, sine = waves(positions)
    table = np.zeros((len(positions), 4 * FB))
    for block, values in enumerate((cosine, cosine, sine, -sine)):
        table[:, block * FB : block * FB + HALF] = values[:, 1:]
    table[:, HALF] = 1.0
    return table


@functools.cache
def tables():
    pixels = np.arange(TP) + HALO
    column = column_table(pixels)
    column_high, column_low = halves(column)
    turned = np.concatenate([column[:, : 2 * FB].T, column[:, 2 * FB :].T], axis=1)
    turned_high, turned_low = halves(turned)
    row = row_table(pixels)
    row_high, row_low = halves(row)
    out = {}
    out["column"] = np.stack([column_high, column_low])
    spectrum_rows = []
    halo_rows = []
    forward = []
    backward = []
    for part in range(PARTS):
        own = np.arange(ROWS) + part * ROWS + HALO
        into = row_table(np.arange(HALO) + (FULL - HALO if part == PARTS - 1 else 0))
        high, low = halves(np.concatenate([row_table(own), into]).T)
        spectrum_rows.append(np.concatenate([high, low, high], axis=1))
        high, low = halves(row_table(np.arange(HALO) + (0 if part == PARTS - 1 else FULL - HALO)))
        halo_rows.append(np.concatenate([high, low, high], axis=1))
        cols = slice(part * ROWS, (part + 1) * ROWS)
        high = np.concatenate([turned_high[:, :TP][:, cols], turned_high[:, TP:][:, cols]], axis=1)
        low = np.concatenate([turned_low[:, :TP][:, cols], turned_low[:, TP:][:, cols]], axis=1)
        forward.append(np.concatenate([high, high, low]))
        backward.append(np.concatenate([column_high[cols], column_high[cols], column_low[cols]]))
    out["spectrum_rows"] = np.stack(spectrum_rows)
    out["halo_rows"] = np.stack(halo_rows)
    out["forward"] = np.stack(forward)
    out["backward"] = np.stack(backward)
    out["turned"] = np.concatenate([turned_high, turned_high, turned_low])
    out["row"] = np.concatenate([row_high, row_low, row_high], axis=1)
    out["row_turned"] = np.concatenate([row_high.T, row_low.T])
    return out


def dot(left, right):
    return jnp.dot(left, right, preferred_element_type=F32)


def split(value):
    high = value.astype(BF)
    return high, (value - high.astype(F32)).astype(BF)


def prepare_kernel(real_ref, imag_ref, thresholds_ref, out_ref, stage):
    local_conds = real_ref.shape[0]
    mats = local_conds * KERNELS * 2
    stage[...] = jnp.zeros_like(stage)
    for cond in range(local_conds):
        for kern in range(KERNELS):
            for part, ref in enumerate((real_ref, imag_ref)):
                stage[(cond * KERNELS + kern) * 2 + part, :KSUP, :KSUP] = ref[cond, kern]
    rows = stage.shape[1]
    source = lax.broadcasted_iota(jnp.int32, (2 * FB, 4 * FB), 0)
    target = lax.broadcasted_iota(jnp.int32, (2 * FB, 4 * FB), 1)
    lane = target % FB
    block = target // FB
    plus = (block == 0) | (block == 3)
    freq = jnp.where(lane < HALF, lane + 1, 0)
    used = (lane < HALF) | ((lane == HALF) & (block % 2 == 0))
    pick = (used & (source == jnp.where(plus, HALF + freq, HALF - freq))).astype(F32).astype(BF)
    high, low = split(stage[...].reshape(mats * rows, 2 * FB))
    picked = [dot(piece, pick) for piece in (high, low)]
    source = lax.broadcasted_iota(jnp.int32, (FA, 2 * rows), 1) % rows
    target = lax.broadcasted_iota(jnp.int32, (FA, 2 * rows), 0)
    turn = ((source == HALF - target) & (target <= HALF)).astype(F32).astype(BF)
    lane = lax.broadcasted_iota(jnp.int32, (FA, 2 * FB), 1)
    row = lax.broadcasted_iota(jnp.int32, (FA, 2 * FB), 0)
    valid = (row <= HALF) & ((lane <= HALF) | ((row > 0) & (lane >= FB) & (lane < FB + HALF)))
    scale = 1.0 / (FULL * FULL)
    keep_top = jnp.where(valid, scale, 0.0)
    keep_bottom = jnp.where((row == 0) & (lane == HALF), 0.0, keep_top)
    first = lane % FB < HALF
    extra = jnp.zeros((FA, 2 * FB), F32)
    for kern in range(local_conds * KERNELS):
        arrays = [[], []]
        for part in range(2):
            start = (kern * 2 + part) * rows
            top = picked[0][start + HALF : start + HALF + FA, : 2 * FB] + picked[1][start + HALF : start + HALF + FA, : 2 * FB]
            pieces = jnp.concatenate([piece[start : start + rows, 2 * FB :] for piece in picked], axis=0)
            bottom = dot(turn, pieces.astype(BF)) * keep_bottom
            top = top * keep_top
            arrays[0].append(top + bottom)
            arrays[1].append(top - bottom)
        for which, (real, imag) in enumerate(arrays):
            packed = jnp.where(first, real, pltpu.roll(imag, HALF, 1))
            if which == 0:
                packed = jnp.where(row == FA - 1, thresholds_ref[kern // KERNELS], packed)
            out_ref[kern * 2 + which] = packed
            for part, value in enumerate((real, imag)):
                place = kern * 4 + which * 2 + part
                extra = jnp.where(lane == place, pltpu.roll(value, (place - HALF) % (2 * FB), 1), extra)
    out_ref[local_conds * KERNELS * 2] = extra


def spectrum_kernel(part_ref, theta_ref, halo_ref, column_ref, rows_ref, out_ref):
    mask = jnp.tanh(mask_steep * jnp.concatenate([theta_ref[...], halo_ref[...]], axis=0))
    high, low = split(mask)
    across = dot(high, column_ref[0]) + dot(low, column_ref[0]) + dot(high, column_ref[1])
    high, low = split(across)
    both = dot(rows_ref[0], jnp.concatenate([high, high, low], axis=0))
    even = both[:FA, : 2 * FB] - both[FA:, 2 * FB :]
    odd = both[FA:, : 2 * FB] + both[:FA, 2 * FB :]
    out_ref[...] = jnp.concatenate([even, odd], axis=0)


def fields_kernel(
    part_ref, weights_ref, spectrum_ref, own_ref, side_ref, core_ref, cross_ref, target_ref, forward_ref, backward_ref,
    row_ref, row_turned_ref, out_ref, kernels_ref, lines, folded, amps, resists, total, turned,
):
    count = kernels_ref.shape[0]
    local = count // PARTS
    spectrum = spectrum_ref[...]
    even, odd = spectrum[:FA], spectrum[FA:]
    lane = lax.broadcasted_iota(jnp.int32, (FA, 2 * FB), 1)
    row = lax.broadcasted_iota(jnp.int32, (FA, 2 * FB), 0)
    zero_lane = (lane == HALF) & (row <= HALF)
    for group, ref in enumerate((own_ref, side_ref, core_ref, cross_ref)):
        extra = ref[2 * local]
        for kern in range(local):
            for which in range(2):
                packed = ref[2 * kern + which]
                for part, value in enumerate((packed, pltpu.roll(packed, 2 * FB - HALF, 1))):
                    place = kern * 4 + which * 2 + part
                    zeroth = pltpu.roll(extra, (HALF - place) % (2 * FB), 1)
                    kernels_ref[group * local + kern, which * 2 + part] = jnp.where(zero_lane, zeroth, value)

    def grids(kern, carry):
        he_real, he_imag, ho_real, ho_imag = (kernels_ref[kern, i] for i in range(4))
        stack = jnp.concatenate(
            [
                even * he_real + odd * ho_imag,
                odd * he_real - even * ho_imag,
                even * he_imag - odd * ho_real,
                odd * he_imag + even * ho_real,
            ],
            axis=0,
        )
        high, low = split(stack)
        lines[kern] = jnp.concatenate([high, low, high], axis=1)
        return carry

    lax.fori_loop(0, count, grids, 0)

    def fold(kern, carry):
        result = dot(lines[kern], forward_ref[0])
        parts = []
        for i in range(2):
            x_part = result[2 * FA * i : 2 * FA * i + FA]
            y_part = result[2 * FA * i + FA : 2 * FA * (i + 1)]
            parts.append(
                jnp.concatenate(
                    [x_part[:, :ROWS] + y_part[:, ROWS:], y_part[:, :ROWS] - x_part[:, ROWS:]], axis=0
                )
            )
        high, low = split(jnp.concatenate(parts, axis=1))
        folded[kern] = jnp.concatenate([high, high, low], axis=0)
        return carry

    lax.fori_loop(0, count, fold, 0)
    total[...] = jnp.zeros_like(total)

    def expose(cond, carry):
        intensity = jnp.zeros((TP, ROWS), F32)
        for kern in range(KERNELS):
            index = cond * KERNELS + kern
            amp = dot(row_ref[...], folded[index])
            amps[index] = amp
            intensity = intensity + amp[:, :ROWS] * amp[:, :ROWS] + amp[:, ROWS:] * amp[:, ROWS:]
        level = kernels_ref[cond * KERNELS, 0, FA - 1 :, :]
        resist = 1.0 / (1.0 + jnp.exp(resist_steep * (level - intensity)))
        resists[cond] = resist
        total[...] += resist
        return carry

    lax.fori_loop(0, CONDS, expose, 0)
    weight_sum = weights_ref[0]
    for i in range(1, CONDS):
        weight_sum = weight_sum + weights_ref[i]
    weight_sum = weight_sum.astype(F32)

    def drive(cond, carry):
        group = cond // (CONDS // PARTS)
        own = lax.bitwise_xor(part_ref[0], jnp.where(group == 0, 0, jnp.where(group == 1, 2, jnp.where(group == 2, 1, 3))))
        weight = weights_ref[own * (CONDS // PARTS) + cond % (CONDS // PARTS)].astype(F32) / weight_sum
        resist = resists[cond]
        slope = 2.0 * weight * (resist - target_ref[...].astype(F32)) + (2.0 * band_weight / CONDS) * (
            resist - total[...] * (1.0 / CONDS)
        )
        field = 2.0 * resist_steep * slope * resist * (1.0 - resist)
        field = jnp.concatenate([field, field], axis=1)
        for kern in range(KERNELS):
            index = cond * KERNELS + kern
            high, low = split(field * amps[index])
            long = dot(row_turned_ref[...], high)
            back = long[: 2 * FA] + long[2 * FA :] + dot(row_turned_ref[: 2 * FA], low)
            high, low = split(jnp.concatenate([back[:, :ROWS], back[:, ROWS:]], axis=0))
            turned[index] = jnp.concatenate([high, low, high], axis=1)
        return carry

    lax.fori_loop(0, CONDS, drive, 0)

    def gather(kern, carry):
        sum_even, sum_odd = carry
        result = dot(turned[kern], backward_ref[0])
        grads = []
        for i in range(2):
            c_part = result[2 * FA * i : 2 * FA * i + FA]
            s_part = result[2 * FA * i + FA : 2 * FA * (i + 1)]
            grads.append(
                (
                    c_part[:, : 2 * FB] - s_part[:, 2 * FB :],
                    s_part[:, : 2 * FB] + c_part[:, 2 * FB :],
                )
            )
        (x_real, y_real), (x_imag, y_imag) = grads
        he_real, he_imag, ho_real, ho_imag = (kernels_ref[kern, i] for i in range(4))
        sum_even = sum_even + x_real * he_real + x_imag * he_imag - y_real * ho_imag + y_imag * ho_real
        sum_odd = sum_odd + x_real * ho_imag - x_imag * ho_real + y_real * he_real + y_imag * he_imag
        return sum_even, sum_odd

    zero = jnp.zeros((FA, 2 * FB), F32)
    sum_even, sum_odd = lax.fori_loop(0, count, gather, (zero, zero))
    out_ref[...] = jnp.concatenate([sum_even, sum_odd], axis=0)


def gradient_kernel(part_ref, theta_ref, own_ref, other_ref, turned_ref, rows_ref, halo_rows_ref, out_ref):
    def fold(value):
        high, low = split(value)
        result = dot(jnp.concatenate([high, low, high], axis=1), turned_ref[...])
        x_part, y_part = result[:FA], result[FA:]
        both = jnp.concatenate(
            [x_part[:, :TP] + y_part[:, TP:], y_part[:, :TP] - x_part[:, TP:]], axis=0
        )
        high, low = split(both)
        return jnp.concatenate([high, high, low], axis=0)

    mask = jnp.tanh(mask_steep * theta_ref[...])
    scale = mask_steep * (1.0 - mask * mask)
    out_ref[...] = dot(rows_ref[...], fold(own_ref[...])) * scale
    start = pl.multiple_of(jnp.where(part_ref[0] == PARTS - 1, ROWS - HALO, 0), HALO)
    rim = dot(halo_rows_ref[0], fold(other_ref[...]))
    mask = jnp.tanh(mask_steep * theta_ref[pl.ds(start, HALO), :])
    out_ref[pl.ds(start, HALO), :] += rim * (mask_steep * (1.0 - mask * mask))


def whole_spec(array):
    rank = len(array.shape)
    return pl.BlockSpec(array.shape, lambda i, *refs: (0,) * rank)


def part_spec(array):
    rank = len(array.shape)
    return pl.BlockSpec((1,) + array.shape[1:], lambda i, part, *refs: (part[0],) + (0,) * (rank - 1))


def call(kernel, scalars, operands, specs, out_shape, scratch=(), name=None, flops=1 << 28):
    out_rank = len(out_shape.shape)
    return pl.pallas_call(
        kernel,
        grid_spec=pltpu.PrefetchScalarGridSpec(
            num_scalar_prefetch=len(scalars),
            grid=(1,),
            in_specs=specs,
            out_specs=pl.BlockSpec(out_shape.shape, lambda i, *refs: (0,) * out_rank),
            scratch_shapes=list(scratch),
        ),
        out_shape=out_shape,
        compiler_params=pltpu.CompilerParams(vmem_limit_bytes=40 * 1024 * 1024),
        cost_estimate=pl.CostEstimate(flops=flops, bytes_accessed=1 << 20, transcendentals=0),
        name=name,
    )(*scalars, *operands)


def shards(theta, target, kernel_real, kernel_imag, weights, thresholds):
    table = {name: jnp.asarray(value) for name, value in tables().items()}
    tiles = lax.axis_size("tile")
    part = lax.axis_index("cond")
    parts = part.reshape(1).astype(jnp.int32)
    local = kernel_real.shape[0] * KERNELS
    rim_pairs = [(PARTS * i + PARTS - 1, PARTS * (i + 1)) for i in range(tiles - 1)]
    rim_pairs += [(b, a) for a, b in rim_pairs]

    def partner(value, step):
        return lax.ppermute(value, "cond", [(i, i ^ step) for i in range(PARTS)])

    def total(value):
        value = value + partner(value, 1)
        return value + partner(value, 2)

    rim = lax.dynamic_slice_in_dim(theta, jnp.where(part == 0, 0, ROWS - HALO), HALO, axis=0)
    rim = lax.ppermute(rim, ("tile", "cond"), rim_pairs)
    own = call(
        prepare_kernel,
        (),
        (kernel_real, kernel_imag, thresholds),
        [whole_spec(kernel_real), whole_spec(kernel_imag), pl.BlockSpec(memory_space=pltpu.SMEM)],
        jax.ShapeDtypeStruct((2 * local + 1, FA, 2 * FB), F32),
        scratch=(pltpu.VMEM((2 * local, 72, 2 * FB), F32),),
        name="prepare_kernels",
    )
    side = partner(own, 2)
    core = partner(own, 1)
    cross = partner(side, 1)

    spectrum = total(
        call(
            spectrum_kernel,
            (parts,),
            (theta, rim, table["column"], table["spectrum_rows"]),
            [whole_spec(theta), whole_spec(rim), whole_spec(table["column"]), part_spec(table["spectrum_rows"])],
            jax.ShapeDtypeStruct((2 * FA, 2 * FB), F32),
            name="mask_spectrum",
        )
    )
    count = CONDS * KERNELS
    adjoint = total(
        call(
            fields_kernel,
            (parts, weights),
            (
                spectrum, own, side, core, cross, target, table["forward"], table["backward"], table["row"],
                table["row_turned"],
            ),
            [
                whole_spec(spectrum),
                whole_spec(own),
                whole_spec(side),
                whole_spec(core),
                whole_spec(cross),
                pl.BlockSpec((TP, ROWS), lambda i, part, *refs: (0, part[0])),
                part_spec(table["forward"]),
                part_spec(table["backward"]),
                whole_spec(table["row"]),
                whole_spec(table["row_turned"]),
            ],
            jax.ShapeDtypeStruct((2 * FA, 2 * FB), F32),
            scratch=(
                pltpu.VMEM((count, 4, FA, 2 * FB), F32),
                pltpu.VMEM((count, 4 * FA, 6 * FB), BF),
                pltpu.VMEM((count, 6 * FA, 2 * ROWS), BF),
                pltpu.VMEM((count, TP, 2 * ROWS), F32),
                pltpu.VMEM((CONDS, TP, ROWS), F32),
                pltpu.VMEM((TP, ROWS), F32),
                pltpu.VMEM((count, 4 * FA, 3 * ROWS), BF),
            ),
            name="coherent_fields",
            flops=1 << 33,
        )
    )
    other = lax.ppermute(adjoint, ("tile", "cond"), rim_pairs)
    return call(
        gradient_kernel,
        (parts,),
        (theta, adjoint, other, table["turned"], table["row"], table["halo_rows"]),
        [
            whole_spec(theta),
            whole_spec(adjoint),
            whole_spec(other),
            whole_spec(table["turned"]),
            pl.BlockSpec((ROWS, 6 * FA), lambda i, part, *refs: (part[0], 0)),
            part_spec(table["halo_rows"]),
        ],
        jax.ShapeDtypeStruct((ROWS, TP), F32),
        name="mask_gradient",
    )


def solution(mesh):
    in_specs = (
        P(("tile", "cond"), None),
        P("tile", None),
        P("cond", None, None, None),
        P("cond", None, None, None),
        P(),
        P("cond"),
    )
    out_specs = P(("tile", "cond"), None)
    return jax.shard_map(shards, mesh=mesh, in_specs=in_specs, out_specs=out_specs, check_vma=False)
```

```python
import functools

import jax
import jax.numpy as jnp
import ml_dtypes
import numpy as np
from jax import lax
from jax.experimental import pallas as pl
from jax.experimental.pallas import tpu as pltpu
from jax.sharding import PartitionSpec as P

TP = 512
HALO = 32
KSUP = 65
HALF = KSUP // 2
KERNELS = 2
CONDS = 8
FULL = TP + 2 * HALO
PARTS = 4
ROWS = TP // PARTS
FA = 40
FB = 64
BF = jnp.bfloat16
F32 = jnp.float32

mask_steep = 2.0
resist_steep = 4.0
band_weight = 1.0


def waves(positions):
    angles = (np.outer(np.asarray(positions, np.int64), np.arange(HALF + 1)) % FULL) * (2.0 * np.pi / FULL)
    return np.cos(angles), np.sin(angles)


def halves(table):
    high = table.astype(np.float32).astype(ml_dtypes.bfloat16)
    low = (table - high.astype(np.float64)).astype(np.float32).astype(ml_dtypes.bfloat16)
    return high, low


def row_table(positions):
    cosine, sine = waves(positions)
    table = np.zeros((len(positions), 2 * FA))
    table[:, : HALF + 1] = cosine
    table[:, FA : FA + HALF + 1] = sine
    return table


def column_table(positions):
    cosine, sine = waves(positions)
    table = np.zeros((len(positions), 4 * FB))
    for block, values in enumerate((cosine, cosine, sine, -sine)):
        table[:, block * FB : block * FB + HALF] = values[:, 1:]
    table[:, HALF] = 1.0
    return table


@functools.cache
def tables():
    pixels = np.arange(TP) + HALO
    column = column_table(pixels)
    column_high, column_low = halves(column)
    turned = np.concatenate([column[:, : 2 * FB].T, column[:, 2 * FB :].T], axis=1)
    turned_high, turned_low = halves(turned)
    row = row_table(pixels)
    row_high, row_low = halves(row)
    out = {}
    out["column"] = np.stack([column_high, column_low])
    spectrum_rows = []
    rim_rows = []
    halo_rows = []
    forward = []
    backward = []
    for part in range(PARTS):
        own = np.arange(ROWS) + part * ROWS + HALO
        high, low = halves(row_table(own).T)
        spectrum_rows.append(np.concatenate([high, low, high], axis=1))
        high, low = halves(row_table(np.arange(HALO) + (part % 2) * (FULL - HALO)).T)
        rim_rows.append(np.concatenate([high, low, high], axis=1))
        high, low = halves(row_table(np.arange(HALO) + (0 if part == PARTS - 1 else FULL - HALO)))
        halo_rows.append(np.concatenate([high, low, high], axis=1))
        cols = slice(part * ROWS, (part + 1) * ROWS)
        high = np.concatenate([turned_high[:, :TP][:, cols], turned_high[:, TP:][:, cols]], axis=1)
        low = np.concatenate([turned_low[:, :TP][:, cols], turned_low[:, TP:][:, cols]], axis=1)
        forward.append(np.concatenate([high, high, low]))
        backward.append(np.concatenate([column_high[cols], column_high[cols], column_low[cols]]))
    out["spectrum_rows"] = np.stack(spectrum_rows)
    out["rim_rows"] = np.stack(rim_rows)
    out["halo_rows"] = np.stack(halo_rows)
    out["forward"] = np.stack(forward)
    out["backward"] = np.stack(backward)
    out["turned"] = np.concatenate([turned_high, turned_high, turned_low])
    out["row"] = np.concatenate([row_high, row_low, row_high], axis=1)
    out["row_turned"] = np.concatenate([row_high.T, row_low.T])
    return out


def dot(left, right):
    return jnp.dot(left, right, preferred_element_type=F32)


def split(value):
    high = value.astype(BF)
    return high, (value - high.astype(F32)).astype(BF)


def spectrum_of(mask, column_ref, rows):
    high, low = split(mask)
    across = dot(high, column_ref[0]) + dot(low, column_ref[0]) + dot(high, column_ref[1])
    high, low = split(across)
    both = dot(rows, jnp.concatenate([high, high, low], axis=0))
    even = both[:FA, : 2 * FB] - both[FA:, 2 * FB :]
    odd = both[FA:, : 2 * FB] + both[:FA, 2 * FB :]
    return even, odd


def open_kernel(
    part_ref, theta_hbm, real_hbm, imag_hbm, thresholds_hbm, column_hbm, rows_hbm, forward_hbm, backward_hbm,
    out_ref, rim_ref, forward_ref, backward_ref, real_ref, imag_ref, theta_ref, column_ref, rows_ref, thresholds_ref, stage, sems,
):
    part = part_ref[0]
    moves = [
        (real_hbm, real_ref),
        (imag_hbm, imag_ref),
        (thresholds_hbm, thresholds_ref),
        (theta_hbm, theta_ref),
        (column_hbm, column_ref),
        (rows_hbm.at[part], rows_ref),
        (forward_hbm.at[part], forward_ref),
        (backward_hbm.at[part], backward_ref),
    ]
    copies = [pltpu.make_async_copy(source, target, sems.at[i]) for i, (source, target) in enumerate(moves)]
    for copy in copies:
        copy.start()
    local_conds = real_ref.shape[0]
    mats = local_conds * KERNELS * 2
    stage[...] = jnp.zeros_like(stage)
    for copy in copies[:3]:
        copy.wait()
    for cond in range(local_conds):
        for kern in range(KERNELS):
            for piece, ref in enumerate((real_ref, imag_ref)):
                stage[(cond * KERNELS + kern) * 2 + piece, :KSUP, :KSUP] = ref[cond, :, kern, :]
    rows = stage.shape[1]
    source = lax.broadcasted_iota(jnp.int32, (2 * FB, 4 * FB), 0)
    target = lax.broadcasted_iota(jnp.int32, (2 * FB, 4 * FB), 1)
    lane = target % FB
    block = target // FB
    plus = (block == 0) | (block == 3)
    freq = jnp.where(lane < HALF, lane + 1, 0)
    used = (lane < HALF) | ((lane == HALF) & (block % 2 == 0))
    pick = (used & (source == jnp.where(plus, HALF + freq, HALF - freq))).astype(F32).astype(BF)
    high, low = split(stage[...].reshape(mats * rows, 2 * FB))
    picked = [dot(piece, pick) for piece in (high, low)]
    source = lax.broadcasted_iota(jnp.int32, (FA, 2 * rows), 1) % rows
    target = lax.broadcasted_iota(jnp.int32, (FA, 2 * rows), 0)
    turn = ((source == HALF - target) & (target <= HALF)).astype(F32).astype(BF)
    lane = lax.broadcasted_iota(jnp.int32, (FA, 2 * FB), 1)
    row = lax.broadcasted_iota(jnp.int32, (FA, 2 * FB), 0)
    valid = (row <= HALF) & ((lane <= HALF) | ((row > 0) & (lane >= FB) & (lane < FB + HALF)))
    scale = 1.0 / (FULL * FULL)
    keep_top = jnp.where(valid, scale, 0.0)
    keep_bottom = jnp.where((row == 0) & (lane == HALF), 0.0, keep_top)
    first = lane % FB < HALF
    extra = jnp.zeros((FA, 2 * FB), F32)
    for kern in range(local_conds * KERNELS):
        arrays = [[], []]
        for piece in range(2):
            start = (kern * 2 + piece) * rows
            top = picked[0][start + HALF : start + HALF + FA, : 2 * FB] + picked[1][start + HALF : start + HALF + FA, : 2 * FB]
            pieces = jnp.concatenate([half[start : start + rows, 2 * FB :] for half in picked], axis=0)
            bottom = dot(turn, pieces.astype(BF)) * keep_bottom
            top = top * keep_top
            arrays[0].append(top + bottom)
            arrays[1].append(top - bottom)
        for which, (real, imag) in enumerate(arrays):
            packed = jnp.where(first, real, pltpu.roll(imag, HALF, 1))
            if which == 0:
                packed = jnp.where(row == FA - 1, thresholds_ref[kern // KERNELS], packed)
            out_ref[kern * 2 + which] = packed
            for piece, value in enumerate((real, imag)):
                place = kern * 4 + which * 2 + piece
                extra = jnp.where(lane == place, pltpu.roll(value, (place - HALF) % (2 * FB), 1), extra)
    out_ref[local_conds * KERNELS * 2] = extra
    for copy in copies[3:]:
        copy.wait()
    rim_ref[...] = jnp.where(part == 0, theta_ref[:HALO], theta_ref[ROWS - HALO :])
    even, odd = spectrum_of(jnp.tanh(mask_steep * theta_ref[...]), column_ref, rows_ref[...])
    out_ref[local_conds * KERNELS * 2 + 1] = even
    out_ref[local_conds * KERNELS * 2 + 2] = odd


def rim_kernel(part_ref, own_ref, side_ref, near_ref, far_ref, column_ref, rows_ref, out_ref):
    count = own_ref.shape[0]
    even, odd = spectrum_of(jnp.tanh(mask_steep * (near_ref[...] + far_ref[...])), column_ref, rows_ref[0])
    out_ref[:FA] = even + own_ref[count - 2] + side_ref[count - 2]
    out_ref[FA:] = odd + own_ref[count - 1] + side_ref[count - 1]


def fields_kernel(
    part_ref, weights_ref, spectrum_ref, partner_ref, own_ref, side_ref, core_ref, cross_ref, target_ref, forward_ref,
    backward_ref, row_ref, row_turned_ref, out_ref, kernels_ref, lines, folded, amps, tanhs, total, signs, turned, backs,
):
    count = kernels_ref.shape[0]
    local = count // PARTS
    tall = 4 * FA
    even = spectrum_ref[:FA] + partner_ref[:FA]
    odd = spectrum_ref[FA:] + partner_ref[FA:]
    lane = lax.broadcasted_iota(jnp.int32, (FA, 2 * FB), 1)
    row = lax.broadcasted_iota(jnp.int32, (FA, 2 * FB), 0)
    zero_lane = (lane == HALF) & (row <= HALF)
    for group, ref in enumerate((own_ref, side_ref, core_ref, cross_ref)):
        extra = ref[2 * local]
        for kern in range(local):
            values = []
            for which in range(2):
                packed = ref[2 * kern + which]
                for part, value in enumerate((packed, pltpu.roll(packed, 2 * FB - HALF, 1))):
                    place = kern * 4 + which * 2 + part
                    zeroth = pltpu.roll(extra, (HALF - place) % (2 * FB), 1)
                    value = jnp.where(zero_lane, zeroth, value)
                    kernels_ref[group * local + kern, which * 2 + part] = value
                    values.append(value)
            he_real, he_imag, ho_real, ho_imag = values
            start = (group * local + kern) * tall
            for i, value in enumerate(
                (
                    even * he_real + odd * ho_imag,
                    odd * he_real - even * ho_imag,
                    even * he_imag - odd * ho_real,
                    odd * he_imag + even * ho_real,
                )
            ):
                lines[start + i * FA : start + (i + 1) * FA] = value

    high, low = split(lines[...])
    lines_folded = dot(high, forward_ref[: 2 * FB]) + dot(low, forward_ref[: 2 * FB]) + dot(high, forward_ref[4 * FB :])
    for kern in range(count):
        parts = []
        for i in range(2):
            x_part = lines_folded[tall * kern + 2 * FA * i : tall * kern + 2 * FA * i + FA]
            y_part = lines_folded[tall * kern + 2 * FA * i + FA : tall * kern + 2 * FA * (i + 1)]
            parts.append(
                jnp.concatenate(
                    [x_part[:, :ROWS] + y_part[:, ROWS:], y_part[:, :ROWS] - x_part[:, ROWS:]], axis=0
                )
            )
        high, low = split(jnp.concatenate(parts, axis=1))
        folded[kern] = jnp.concatenate([high, high, low], axis=0)
    total[...] = jnp.zeros_like(total)
    signs[...] = 1.0 - 2.0 * target_ref[...].astype(F32)

    def expose(cond, carry):
        intensity = None
        for kern in range(KERNELS):
            index = cond * KERNELS + kern
            amp = dot(row_ref[...], folded[index])
            amps[index] = amp
            power = amp[:, :ROWS] * amp[:, :ROWS] + amp[:, ROWS:] * amp[:, ROWS:]
            intensity = power if intensity is None else intensity + power
        level = kernels_ref[cond * KERNELS, 0, FA - 1 :, :]
        value = jnp.tanh((0.5 * resist_steep) * (intensity - level))
        tanhs[cond] = value
        total[...] += value
        return carry

    lax.fori_loop(0, CONDS, expose, 0, unroll=2)
    weight_sum = weights_ref[0]
    for i in range(1, CONDS):
        weight_sum = weight_sum + weights_ref[i]
    weight_sum = weight_sum.astype(F32)
    total[...] = total[...] * (band_weight / (CONDS * CONDS))

    def drive(cond, carry):
        group = cond // (CONDS // PARTS)
        own = lax.bitwise_xor(part_ref[0], jnp.where(group == 0, 0, jnp.where(group == 1, 2, jnp.where(group == 2, 1, 3))))
        weight = weights_ref[own * (CONDS // PARTS) + cond % (CONDS // PARTS)].astype(F32) / weight_sum
        value = tanhs[cond]
        slope = (weight + band_weight / CONDS) * value + weight * signs[...] - total[...]
        field = (0.5 * resist_steep) * (1.0 - value * value) * slope
        field = jnp.concatenate([field, field], axis=1)
        for kern in range(KERNELS):
            index = cond * KERNELS + kern
            high, low = split(field * amps[index])
            long = dot(row_turned_ref[...], high)
            back = long[: 2 * FA] + long[2 * FA :] + dot(row_turned_ref[: 2 * FA], low)
            turned[pl.ds(index * 2, 2)] = jnp.stack([back[:, :ROWS], back[:, ROWS:]])
        return carry

    lax.fori_loop(0, CONDS, drive, 0, unroll=2)
    high, low = split(turned[...].reshape(count * tall, ROWS))
    backs[...] = dot(high, backward_ref[:ROWS]) + dot(low, backward_ref[:ROWS]) + dot(high, backward_ref[2 * ROWS :])

    sum_even = jnp.zeros((FA, 2 * FB), F32)
    sum_odd = jnp.zeros((FA, 2 * FB), F32)
    for kern in range(count):
        grads = []
        for i in range(2):
            c_part = backs[tall * kern + 2 * FA * i : tall * kern + 2 * FA * i + FA]
            s_part = backs[tall * kern + 2 * FA * i + FA : tall * kern + 2 * FA * (i + 1)]
            grads.append(
                (
                    c_part[:, : 2 * FB] - s_part[:, 2 * FB :],
                    s_part[:, : 2 * FB] + c_part[:, 2 * FB :],
                )
            )
        (x_real, y_real), (x_imag, y_imag) = grads
        he_real, he_imag, ho_real, ho_imag = (kernels_ref[kern, i] for i in range(4))
        sum_even = sum_even + x_real * he_real + x_imag * he_imag - y_real * ho_imag + y_imag * ho_real
        sum_odd = sum_odd + x_real * ho_imag - x_imag * ho_real + y_real * he_real + y_imag * he_imag
    out_ref[:FA] = sum_even
    out_ref[FA:] = sum_odd


def fold_rows(value, turned_ref):
    high, low = split(value)
    result = dot(jnp.concatenate([high, low, high], axis=1), turned_ref[...])
    x_part, y_part = result[:FA], result[FA:]
    both = jnp.concatenate([x_part[:, :TP] + y_part[:, TP:], y_part[:, :TP] - x_part[:, TP:]], axis=0)
    high, low = split(both)
    return jnp.concatenate([high, high, low], axis=0)


def gradient_kernel(part_ref, theta_ref, mine_ref, side_ref, turned_ref, rows_ref, out_ref):
    mask = jnp.tanh(mask_steep * theta_ref[...])
    scale = mask_steep * (1.0 - mask * mask)
    out_ref[...] = dot(rows_ref[...], fold_rows(mine_ref[...] + side_ref[...], turned_ref)) * scale


def edge_kernel(part_ref, theta_ref, gradient_ref, near_ref, far_ref, turned_ref, halo_rows_ref, out_ref):
    out_ref[...] = gradient_ref[...]
    start = pl.multiple_of(jnp.where(part_ref[0] == PARTS - 1, ROWS - HALO, 0), HALO)
    rim = dot(halo_rows_ref[0], fold_rows(near_ref[...] + far_ref[...], turned_ref))
    mask = jnp.tanh(mask_steep * theta_ref[pl.ds(start, HALO), :])
    out_ref[pl.ds(start, HALO), :] += rim * (mask_steep * (1.0 - mask * mask))


def whole_spec(array):
    rank = len(array.shape)
    return pl.BlockSpec(array.shape, lambda i, *refs: (0,) * rank)


def part_spec(array):
    rank = len(array.shape)
    return pl.BlockSpec((1,) + array.shape[1:], lambda i, part, *refs: (part[0],) + (0,) * (rank - 1))


def call(kernel, scalars, operands, specs, out_shapes, scratch=(), name=None, flops=1 << 28):
    many = isinstance(out_shapes, list)
    out_specs = [whole_spec(shape) for shape in (out_shapes if many else [out_shapes])]
    return pl.pallas_call(
        kernel,
        grid_spec=pltpu.PrefetchScalarGridSpec(
            num_scalar_prefetch=len(scalars),
            grid=(1,),
            in_specs=specs,
            out_specs=out_specs if many else out_specs[0],
            scratch_shapes=list(scratch),
        ),
        out_shape=out_shapes,
        compiler_params=pltpu.CompilerParams(vmem_limit_bytes=48 * 1024 * 1024),
        cost_estimate=pl.CostEstimate(flops=flops, bytes_accessed=1 << 20, transcendentals=0),
        name=name,
    )(*scalars, *operands)


def floats(*shape):
    return jax.ShapeDtypeStruct(shape, F32)


def shards(theta, target, kernel_real, kernel_imag, weights, thresholds):
    table = {name: jnp.asarray(value) for name, value in tables().items()}
    tiles = lax.axis_size("tile")
    part = lax.axis_index("cond")
    parts = part.reshape(1).astype(jnp.int32)
    local_conds = kernel_real.shape[0]
    local = local_conds * KERNELS
    count = CONDS * KERNELS
    last = PARTS - 1
    hbm = pl.BlockSpec(memory_space=pltpu.HBM)

    def pairs(down, up):
        return [(PARTS * (i + 1) + down[0], PARTS * i + down[1]) for i in range(tiles - 1)] + [
            (PARTS * i + up[0], PARTS * (i + 1) + up[1]) for i in range(tiles - 1)
        ]

    def across(value, down, up):
        return lax.ppermute(value, ("tile", "cond"), pairs(down, up))

    def partner(value, step):
        return lax.ppermute(value, "cond", [(i, i ^ step) for i in range(PARTS)])

    kernel_shape = (local_conds, KSUP, KERNELS, KSUP)
    own, rim, forward, backward = call(
        open_kernel,
        (parts,),
        (
            theta, kernel_real.transpose(0, 2, 1, 3), kernel_imag.transpose(0, 2, 1, 3), thresholds, table["column"],
            table["spectrum_rows"], table["forward"], table["backward"],
        ),
        [hbm] * 8,
        [
            floats(2 * local + 3, FA, 2 * FB),
            floats(HALO, TP),
            jax.ShapeDtypeStruct(table["forward"].shape[1:], BF),
            jax.ShapeDtypeStruct(table["backward"].shape[1:], BF),
        ],
        scratch=(
            pltpu.VMEM(kernel_shape, F32),
            pltpu.VMEM(kernel_shape, F32),
            pltpu.VMEM(theta.shape, F32),
            pltpu.VMEM(table["column"].shape, BF),
            pltpu.VMEM(table["spectrum_rows"].shape[1:], BF),
            pltpu.SMEM(thresholds.shape, F32),
            pltpu.VMEM((2 * local, 72, 2 * FB), F32),
            pltpu.SemaphoreType.DMA((8,)),
        ),
        name="open_parts",
    )
    side = partner(own, 2)
    core = partner(own, 1)
    cross = partner(side, 1)
    near = across(rim, (0, 1), (last, 2))
    far = across(rim, (0, last), (last, 0))
    spectrum = call(
        rim_kernel,
        (parts,),
        (own, side, near, far, table["column"], table["rim_rows"]),
        [
            whole_spec(own), whole_spec(side), whole_spec(near), whole_spec(far), whole_spec(table["column"]),
            part_spec(table["rim_rows"]),
        ],
        floats(2 * FA, 2 * FB),
        name="add_rims",
    )
    adjoint = call(
        fields_kernel,
        (parts, weights),
        (
            spectrum, partner(spectrum, 1), own, side, core, cross, target, forward, backward, table["row"],
            table["row_turned"],
        ),
        [
            whole_spec(spectrum),
            whole_spec(spectrum),
            whole_spec(own),
            whole_spec(own),
            whole_spec(own),
            whole_spec(own),
            pl.BlockSpec((TP, ROWS), lambda i, part, *refs: (0, part[0])),
            whole_spec(forward),
            whole_spec(backward),
            whole_spec(table["row"]),
            whole_spec(table["row_turned"]),
        ],
        floats(2 * FA, 2 * FB),
        scratch=(
            pltpu.VMEM((count, 4, FA, 2 * FB), F32),
            pltpu.VMEM((count * 4 * FA, 2 * FB), F32),
            pltpu.VMEM((count, 6 * FA, 2 * ROWS), BF),
            pltpu.VMEM((count, TP, 2 * ROWS), F32),
            pltpu.VMEM((CONDS, TP, ROWS), F32),
            pltpu.VMEM((TP, ROWS), F32),
            pltpu.VMEM((TP, ROWS), F32),
            pltpu.VMEM((count * 2, 2 * FA, ROWS), F32),
            pltpu.VMEM((count * 4 * FA, 4 * FB), F32),
        ),
        name="coherent_fields",
        flops=1 << 33,
    )
    adjoint = adjoint + partner(adjoint, 1)
    near = across(adjoint, (last, last), (0, 0))
    far = across(adjoint, (1, last), (2, 0))
    gradient = call(
        gradient_kernel,
        (parts,),
        (theta, adjoint, partner(adjoint, 2), table["turned"], table["row"]),
        [
            whole_spec(theta),
            whole_spec(adjoint),
            whole_spec(adjoint),
            whole_spec(table["turned"]),
            pl.BlockSpec((ROWS, 6 * FA), lambda i, part, *refs: (part[0], 0)),
        ],
        floats(ROWS, TP),
        name="own_gradient",
        flops=1 << 31,
    )
    return call(
        edge_kernel,
        (parts,),
        (theta, gradient, near, far, table["turned"], table["halo_rows"]),
        [
            whole_spec(theta),
            whole_spec(gradient),
            whole_spec(near),
            whole_spec(far),
            whole_spec(table["turned"]),
            part_spec(table["halo_rows"]),
        ],
        floats(ROWS, TP),
        name="edge_gradient",
    )


def solution(mesh):
    in_specs = (
        P(("tile", "cond"), None),
        P("tile", None),
        P("cond", None, None, None),
        P("cond", None, None, None),
        P(),
        P("cond"),
    )
    out_specs = P(("tile", "cond"), None)
    return jax.shard_map(shards, mesh=mesh, in_specs=in_specs, out_specs=out_specs, check_vma=False)
```

```python
import functools

import jax
import jax.numpy as jnp
import ml_dtypes
import numpy as np
from jax import lax
from jax.experimental import pallas as pl
from jax.experimental.pallas import tpu as pltpu
from jax.sharding import PartitionSpec as P

TP = 512
HALO = 32
KSUP = 65
HALF = KSUP // 2
KERNELS = 2
CONDS = 8
FULL = TP + 2 * HALO
PARTS = 4
ROWS = TP // PARTS
FA = 40
FB = 64
BF = jnp.bfloat16
F32 = jnp.float32

mask_steep = 2.0
resist_steep = 4.0
band_weight = 1.0


def waves(positions):
    angles = (np.outer(np.asarray(positions, np.int64), np.arange(HALF + 1)) % FULL) * (2.0 * np.pi / FULL)
    return np.cos(angles), np.sin(angles)


def halves(table):
    high = table.astype(np.float32).astype(ml_dtypes.bfloat16)
    low = (table - high.astype(np.float64)).astype(np.float32).astype(ml_dtypes.bfloat16)
    return high, low


def row_table(positions):
    cosine, sine = waves(positions)
    table = np.zeros((len(positions), 2 * FA))
    table[:, : HALF + 1] = cosine
    table[:, FA : FA + HALF + 1] = sine
    return table


def column_table(positions):
    cosine, sine = waves(positions)
    table = np.zeros((len(positions), 4 * FB))
    for block, values in enumerate((cosine, cosine, sine, -sine)):
        table[:, block * FB : block * FB + HALF] = values[:, 1:]
    table[:, HALF] = 1.0
    return table


@functools.cache
def tables():
    pixels = np.arange(TP) + HALO
    column = column_table(pixels)
    column_high, column_low = halves(column)
    turned = np.concatenate([column[:, : 2 * FB].T, column[:, 2 * FB :].T], axis=1)
    turned_high, turned_low = halves(turned)
    row = row_table(pixels)
    row_high, row_low = halves(row)
    out = {}
    out["column"] = np.stack([column_high, column_low])
    spectrum_rows = []
    rim_rows = []
    halo_rows = []
    forward = []
    backward = []
    for part in range(PARTS):
        own = np.arange(ROWS) + part * ROWS + HALO
        high, low = halves(row_table(own).T)
        spectrum_rows.append(np.concatenate([high, low, high], axis=1))
        high, low = halves(row_table(np.arange(HALO) + (part % 2) * (FULL - HALO)).T)
        rim_rows.append(np.concatenate([high, low, high], axis=1))
        high, low = halves(row_table(np.arange(HALO) + (0 if part == PARTS - 1 else FULL - HALO)))
        halo_rows.append(np.concatenate([high, low, high], axis=1))
        cols = slice(part * ROWS, (part + 1) * ROWS)
        high = np.concatenate([turned_high[:, :TP][:, cols], turned_high[:, TP:][:, cols]], axis=1)
        low = np.concatenate([turned_low[:, :TP][:, cols], turned_low[:, TP:][:, cols]], axis=1)
        forward.append(np.concatenate([high, high, low]))
        backward.append(np.concatenate([column_high[cols], column_high[cols], column_low[cols]]))
    out["spectrum_rows"] = np.stack(spectrum_rows)
    out["rim_rows"] = np.stack(rim_rows)
    out["halo_rows"] = np.stack(halo_rows)
    out["forward"] = np.stack(forward)
    out["backward"] = np.stack(backward)
    out["turned"] = np.concatenate([turned_high, turned_high, turned_low])
    out["row"] = np.concatenate([row_high, row_low, row_high], axis=1)
    out["row_turned"] = np.concatenate([row_high.T, row_low.T])
    return out


def dot(left, right):
    return jnp.dot(left, right, preferred_element_type=F32)


def split(value):
    high = value.astype(BF)
    return high, (value - high.astype(F32)).astype(BF)


def spectrum_of(mask, column_ref, rows):
    high, low = split(mask)
    across = dot(high, column_ref[0]) + dot(low, column_ref[0]) + dot(high, column_ref[1])
    high, low = split(across)
    both = dot(rows, jnp.concatenate([high, high, low], axis=0))
    even = both[:FA, : 2 * FB] - both[FA:, 2 * FB :]
    odd = both[FA:, : 2 * FB] + both[:FA, 2 * FB :]
    return even, odd


def open_kernel(
    part_ref, theta_hbm, real_hbm, imag_hbm, thresholds_hbm, weights_hbm, column_hbm, rows_hbm, forward_hbm, backward_hbm,
    out_ref, rim_ref, shares_ref, forward_ref, backward_ref, real_ref, imag_ref, theta_ref, column_ref, rows_ref,
    thresholds_ref, weights_ref, stage, sems,
):
    part = part_ref[0]
    moves = [
        (real_hbm, real_ref),
        (imag_hbm, imag_ref),
        (thresholds_hbm, thresholds_ref),
        (weights_hbm, weights_ref),
        (theta_hbm, theta_ref),
        (column_hbm, column_ref),
        (rows_hbm.at[part], rows_ref),
        (forward_hbm.at[part], forward_ref),
        (backward_hbm.at[part], backward_ref),
    ]
    copies = [pltpu.make_async_copy(source, target, sems.at[i]) for i, (source, target) in enumerate(moves)]
    for copy in copies:
        copy.start()
    local_conds = real_ref.shape[0]
    mats = local_conds * KERNELS * 2
    stage[...] = jnp.zeros_like(stage)
    for copy in copies[:4]:
        copy.wait()
    for cond in range(local_conds):
        for kern in range(KERNELS):
            for piece, ref in enumerate((real_ref, imag_ref)):
                stage[(cond * KERNELS + kern) * 2 + piece, :KSUP, :KSUP] = ref[cond, :, kern, :]
    rows = stage.shape[1]
    source = lax.broadcasted_iota(jnp.int32, (2 * FB, 4 * FB), 0)
    target = lax.broadcasted_iota(jnp.int32, (2 * FB, 4 * FB), 1)
    lane = target % FB
    block = target // FB
    plus = (block == 0) | (block == 3)
    freq = jnp.where(lane < HALF, lane + 1, 0)
    used = (lane < HALF) | ((lane == HALF) & (block % 2 == 0))
    pick = (used & (source == jnp.where(plus, HALF + freq, HALF - freq))).astype(F32).astype(BF)
    high, low = split(stage[...].reshape(mats * rows, 2 * FB))
    picked = [dot(piece, pick) for piece in (high, low)]
    source = lax.broadcasted_iota(jnp.int32, (FA, 2 * rows), 1) % rows
    target = lax.broadcasted_iota(jnp.int32, (FA, 2 * rows), 0)
    turn = ((source == HALF - target) & (target <= HALF)).astype(F32).astype(BF)
    lane = lax.broadcasted_iota(jnp.int32, (FA, 2 * FB), 1)
    row = lax.broadcasted_iota(jnp.int32, (FA, 2 * FB), 0)
    valid = (row <= HALF) & ((lane <= HALF) | ((row > 0) & (lane >= FB) & (lane < FB + HALF)))
    scale = 1.0 / (FULL * FULL)
    keep_top = jnp.where(valid, scale, 0.0)
    keep_bottom = jnp.where((row == 0) & (lane == HALF), 0.0, keep_top)
    first = lane % FB < HALF
    extra = jnp.zeros((FA, 2 * FB), F32)
    for kern in range(local_conds * KERNELS):
        arrays = [[], []]
        for piece in range(2):
            start = (kern * 2 + piece) * rows
            top = picked[0][start + HALF : start + HALF + FA, : 2 * FB] + picked[1][start + HALF : start + HALF + FA, : 2 * FB]
            pieces = jnp.concatenate([half[start : start + rows, 2 * FB :] for half in picked], axis=0)
            bottom = dot(turn, pieces.astype(BF)) * keep_bottom
            top = top * keep_top
            arrays[0].append(top + bottom)
            arrays[1].append(top - bottom)
        for which, (real, imag) in enumerate(arrays):
            packed = jnp.where(first, real, pltpu.roll(imag, HALF, 1))
            if which == 0:
                packed = jnp.where(row == FA - 1, thresholds_ref[kern // KERNELS], packed)
            out_ref[kern * 2 + which] = packed
            for piece, value in enumerate((real, imag)):
                place = kern * 4 + which * 2 + piece
                extra = jnp.where(lane == place, pltpu.roll(value, (place - HALF) % (2 * FB), 1), extra)
    out_ref[local_conds * KERNELS * 2] = extra
    for copy in copies[4:]:
        copy.wait()
    weight_sum = weights_ref[0]
    for i in range(1, CONDS):
        weight_sum = weight_sum + weights_ref[i]
    row = lax.broadcasted_iota(jnp.int32, shares_ref.shape, 0)
    shares = jnp.zeros(shares_ref.shape, F32)
    for group, step in enumerate((0, 2, 1, 3)):
        for i in range(local_conds):
            weight = weights_ref[lax.bitwise_xor(part, step) * local_conds + i]
            shares = jnp.where(row == group * local_conds + i, weight.astype(F32), shares)
    shares_ref[...] = shares / weight_sum.astype(F32)
    rim_ref[...] = jnp.where(part == 0, theta_ref[:HALO], theta_ref[ROWS - HALO :])
    even, odd = spectrum_of(jnp.tanh(mask_steep * theta_ref[...]), column_ref, rows_ref[...])
    out_ref[local_conds * KERNELS * 2 + 1] = even
    out_ref[local_conds * KERNELS * 2 + 2] = odd


def rim_kernel(part_ref, own_ref, side_ref, near_ref, far_ref, column_ref, rows_ref, out_ref):
    count = own_ref.shape[0]
    even, odd = spectrum_of(jnp.tanh(mask_steep * (near_ref[...] + far_ref[...])), column_ref, rows_ref[0])
    out_ref[: count - 2] = side_ref[: count - 2]
    out_ref[count - 2] = even + own_ref[count - 2] + side_ref[count - 2]
    out_ref[count - 1] = odd + own_ref[count - 1] + side_ref[count - 1]


def fields_kernel(
    part_ref, own_ref, side_ref, core_ref, cross_ref, shares_ref, target_ref, forward_ref, backward_ref, row_ref,
    row_turned_ref, out_ref, kernels_ref, lines, folded, amps, tanhs, total, signs, turned, backs,
):
    count = kernels_ref.shape[0]
    local = count // PARTS
    tall = 4 * FA
    even = side_ref[2 * local + 1] + cross_ref[2 * local + 1]
    odd = side_ref[2 * local + 2] + cross_ref[2 * local + 2]
    lane = lax.broadcasted_iota(jnp.int32, (FA, 2 * FB), 1)
    row = lax.broadcasted_iota(jnp.int32, (FA, 2 * FB), 0)
    zero_lane = (lane == HALF) & (row <= HALF)
    for group, ref in enumerate((own_ref, side_ref, core_ref, cross_ref)):
        extra = ref[2 * local]
        for kern in range(local):
            values = []
            for which in range(2):
                packed = ref[2 * kern + which]
                for part, value in enumerate((packed, pltpu.roll(packed, 2 * FB - HALF, 1))):
                    place = kern * 4 + which * 2 + part
                    zeroth = pltpu.roll(extra, (HALF - place) % (2 * FB), 1)
                    value = jnp.where(zero_lane, zeroth, value)
                    kernels_ref[group * local + kern, which * 2 + part] = value
                    values.append(value)
            he_real, he_imag, ho_real, ho_imag = values
            start = (group * local + kern) * tall
            for i, value in enumerate(
                (
                    even * he_real + odd * ho_imag,
                    odd * he_real - even * ho_imag,
                    even * he_imag - odd * ho_real,
                    odd * he_imag + even * ho_real,
                )
            ):
                lines[start + i * FA : start + (i + 1) * FA] = value

    high, low = split(lines[...])
    lines_folded = dot(high, forward_ref[: 2 * FB]) + dot(low, forward_ref[: 2 * FB]) + dot(high, forward_ref[4 * FB :])
    for kern in range(count):
        parts = []
        for i in range(2):
            x_part = lines_folded[tall * kern + 2 * FA * i : tall * kern + 2 * FA * i + FA]
            y_part = lines_folded[tall * kern + 2 * FA * i + FA : tall * kern + 2 * FA * (i + 1)]
            parts.append(
                jnp.concatenate(
                    [x_part[:, :ROWS] + y_part[:, ROWS:], y_part[:, :ROWS] - x_part[:, ROWS:]], axis=0
                )
            )
        high, low = split(jnp.concatenate(parts, axis=1))
        folded[kern] = jnp.concatenate([high, high, low], axis=0)
    total[...] = jnp.zeros_like(total)
    signs[...] = 1.0 - 2.0 * target_ref[...].astype(F32)

    def expose(cond, carry):
        intensity = None
        for kern in range(KERNELS):
            index = cond * KERNELS + kern
            amp = dot(row_ref[...], folded[index])
            amps[index] = amp
            power = amp[:, :ROWS] * amp[:, :ROWS] + amp[:, ROWS:] * amp[:, ROWS:]
            intensity = power if intensity is None else intensity + power
        level = kernels_ref[cond * KERNELS, 0, FA - 1 :, :]
        value = jnp.tanh((0.5 * resist_steep) * (intensity - level))
        tanhs[cond] = value
        total[...] += value
        return carry

    lax.fori_loop(0, CONDS, expose, 0, unroll=2)
    total[...] = total[...] * (band_weight / (CONDS * CONDS))

    def drive(cond, carry):
        weight = shares_ref[pl.ds(cond, 1), :]
        value = tanhs[cond]
        slope = (weight + band_weight / CONDS) * value + weight * signs[...] - total[...]
        field = (0.5 * resist_steep) * (1.0 - value * value) * slope
        field = jnp.concatenate([field, field], axis=1)
        for kern in range(KERNELS):
            index = cond * KERNELS + kern
            high, low = split(field * amps[index])
            long = dot(row_turned_ref[...], high)
            back = long[: 2 * FA] + long[2 * FA :] + dot(row_turned_ref[: 2 * FA], low)
            turned[pl.ds(index * 2, 2)] = jnp.stack([back[:, :ROWS], back[:, ROWS:]])
        return carry

    lax.fori_loop(0, CONDS, drive, 0, unroll=2)
    high, low = split(turned[...].reshape(count * tall, ROWS))
    backs[...] = dot(high, backward_ref[:ROWS]) + dot(low, backward_ref[:ROWS]) + dot(high, backward_ref[2 * ROWS :])

    sum_even = jnp.zeros((FA, 2 * FB), F32)
    sum_odd = jnp.zeros((FA, 2 * FB), F32)
    for kern in range(count):
        grads = []
        for i in range(2):
            c_part = backs[tall * kern + 2 * FA * i : tall * kern + 2 * FA * i + FA]
            s_part = backs[tall * kern + 2 * FA * i + FA : tall * kern + 2 * FA * (i + 1)]
            grads.append(
                (
                    c_part[:, : 2 * FB] - s_part[:, 2 * FB :],
                    s_part[:, : 2 * FB] + c_part[:, 2 * FB :],
                )
            )
        (x_real, y_real), (x_imag, y_imag) = grads
        he_real, he_imag, ho_real, ho_imag = (kernels_ref[kern, i] for i in range(4))
        sum_even = sum_even + x_real * he_real + x_imag * he_imag - y_real * ho_imag + y_imag * ho_real
        sum_odd = sum_odd + x_real * ho_imag - x_imag * ho_real + y_real * he_real + y_imag * he_imag
    out_ref[:FA] = sum_even
    out_ref[FA:] = sum_odd


def fold_rows(value, turned_ref):
    high, low = split(value)
    result = dot(jnp.concatenate([high, low, high], axis=1), turned_ref[...])
    x_part, y_part = result[:FA], result[FA:]
    both = jnp.concatenate([x_part[:, :TP] + y_part[:, TP:], y_part[:, :TP] - x_part[:, TP:]], axis=0)
    high, low = split(both)
    return jnp.concatenate([high, high, low], axis=0)


def gradient_kernel(part_ref, theta_ref, mine_ref, side_ref, turned_ref, rows_ref, out_ref):
    mask = jnp.tanh(mask_steep * theta_ref[...])
    scale = mask_steep * (1.0 - mask * mask)
    out_ref[...] = dot(rows_ref[...], fold_rows(mine_ref[...] + side_ref[...], turned_ref)) * scale


def edge_kernel(part_ref, theta_ref, gradient_ref, near_ref, far_ref, turned_ref, halo_rows_ref, out_ref):
    out_ref[...] = gradient_ref[...]
    start = pl.multiple_of(jnp.where(part_ref[0] == PARTS - 1, ROWS - HALO, 0), HALO)
    rim = dot(halo_rows_ref[0], fold_rows(near_ref[...] + far_ref[...], turned_ref))
    mask = jnp.tanh(mask_steep * theta_ref[pl.ds(start, HALO), :])
    out_ref[pl.ds(start, HALO), :] += rim * (mask_steep * (1.0 - mask * mask))


def whole_spec(array):
    rank = len(array.shape)
    return pl.BlockSpec(array.shape, lambda i, *refs: (0,) * rank)


def part_spec(array):
    rank = len(array.shape)
    return pl.BlockSpec((1,) + array.shape[1:], lambda i, part, *refs: (part[0],) + (0,) * (rank - 1))


def call(kernel, scalars, operands, specs, out_shapes, scratch=(), name=None, flops=1 << 28):
    many = isinstance(out_shapes, list)
    out_specs = [whole_spec(shape) for shape in (out_shapes if many else [out_shapes])]
    return pl.pallas_call(
        kernel,
        grid_spec=pltpu.PrefetchScalarGridSpec(
            num_scalar_prefetch=len(scalars),
            grid=(1,),
            in_specs=specs,
            out_specs=out_specs if many else out_specs[0],
            scratch_shapes=list(scratch),
        ),
        out_shape=out_shapes,
        compiler_params=pltpu.CompilerParams(vmem_limit_bytes=48 * 1024 * 1024),
        cost_estimate=pl.CostEstimate(flops=flops, bytes_accessed=1 << 20, transcendentals=0),
        name=name,
    )(*scalars, *operands)


def floats(*shape):
    return jax.ShapeDtypeStruct(shape, F32)


def shards(theta, target, kernel_real, kernel_imag, weights, thresholds):
    table = {name: jnp.asarray(value) for name, value in tables().items()}
    tiles = lax.axis_size("tile")
    part = lax.axis_index("cond")
    parts = part.reshape(1).astype(jnp.int32)
    local_conds = kernel_real.shape[0]
    local = local_conds * KERNELS
    count = CONDS * KERNELS
    last = PARTS - 1
    hbm = pl.BlockSpec(memory_space=pltpu.HBM)

    def pairs(down, up):
        return [(PARTS * (i + 1) + down[0], PARTS * i + down[1]) for i in range(tiles - 1)] + [
            (PARTS * i + up[0], PARTS * (i + 1) + up[1]) for i in range(tiles - 1)
        ]

    def across(value, down, up):
        return lax.ppermute(value, ("tile", "cond"), pairs(down, up))

    def partner(value, step):
        return lax.ppermute(value, "cond", [(i, i ^ step) for i in range(PARTS)])

    kernel_shape = (local_conds, KSUP, KERNELS, KSUP)
    own, rim, shares, forward, backward = call(
        open_kernel,
        (parts,),
        tuple(
            pltpu.with_memory_space_constraint(value, pltpu.HBM)
            for value in (
                theta, kernel_real.transpose(0, 2, 1, 3), kernel_imag.transpose(0, 2, 1, 3), thresholds, weights,
                table["column"], table["spectrum_rows"], table["forward"], table["backward"],
            )
        ),
        [hbm] * 9,
        [
            floats(2 * local + 3, FA, 2 * FB),
            floats(HALO, TP),
            floats(CONDS, ROWS),
            jax.ShapeDtypeStruct(table["forward"].shape[1:], BF),
            jax.ShapeDtypeStruct(table["backward"].shape[1:], BF),
        ],
        scratch=(
            pltpu.VMEM(kernel_shape, F32),
            pltpu.VMEM(kernel_shape, F32),
            pltpu.VMEM(theta.shape, F32),
            pltpu.VMEM(table["column"].shape, BF),
            pltpu.VMEM(table["spectrum_rows"].shape[1:], BF),
            pltpu.SMEM(thresholds.shape, F32),
            pltpu.SMEM(weights.shape, jnp.int32),
            pltpu.VMEM((2 * local, 72, 2 * FB), F32),
            pltpu.SemaphoreType.DMA((9,)),
        ),
        name="open_parts",
    )
    side = partner(own, 2)
    core = partner(own, 1)
    near = across(rim, (0, 1), (last, 2))
    far = across(rim, (0, last), (last, 0))
    mixed = call(
        rim_kernel,
        (parts,),
        (own, side, near, far, table["column"], table["rim_rows"]),
        [
            whole_spec(own), whole_spec(side), whole_spec(near), whole_spec(far), whole_spec(table["column"]),
            part_spec(table["rim_rows"]),
        ],
        floats(*own.shape),
        name="add_rims",
    )
    adjoint = call(
        fields_kernel,
        (parts,),
        (own, mixed, core, partner(mixed, 1), shares, target, forward, backward, table["row"], table["row_turned"]),
        [
            whole_spec(own),
            whole_spec(own),
            whole_spec(own),
            whole_spec(own),
            whole_spec(shares),
            pl.BlockSpec((TP, ROWS), lambda i, part, *refs: (0, part[0])),
            whole_spec(forward),
            whole_spec(backward),
            whole_spec(table["row"]),
            whole_spec(table["row_turned"]),
        ],
        floats(2 * FA, 2 * FB),
        scratch=(
            pltpu.VMEM((count, 4, FA, 2 * FB), F32),
            pltpu.VMEM((count * 4 * FA, 2 * FB), F32),
            pltpu.VMEM((count, 6 * FA, 2 * ROWS), BF),
            pltpu.VMEM((count, TP, 2 * ROWS), F32),
            pltpu.VMEM((CONDS, TP, ROWS), F32),
            pltpu.VMEM((TP, ROWS), F32),
            pltpu.VMEM((TP, ROWS), F32),
            pltpu.VMEM((count * 2, 2 * FA, ROWS), F32),
            pltpu.VMEM((count * 4 * FA, 4 * FB), F32),
        ),
        name="coherent_fields",
        flops=1 << 33,
    )
    adjoint = adjoint + partner(adjoint, 1)
    near = across(adjoint, (last, last), (0, 0))
    far = across(adjoint, (1, last), (2, 0))
    gradient = call(
        gradient_kernel,
        (parts,),
        (theta, adjoint, partner(adjoint, 2), table["turned"], table["row"]),
        [
            whole_spec(theta),
            whole_spec(adjoint),
            whole_spec(adjoint),
            whole_spec(table["turned"]),
            pl.BlockSpec((ROWS, 6 * FA), lambda i, part, *refs: (part[0], 0)),
        ],
        floats(ROWS, TP),
        name="own_gradient",
        flops=1 << 31,
    )
    return call(
        edge_kernel,
        (parts,),
        (theta, gradient, near, far, table["turned"], table["halo_rows"]),
        [
            whole_spec(theta),
            whole_spec(gradient),
            whole_spec(near),
            whole_spec(far),
            whole_spec(table["turned"]),
            part_spec(table["halo_rows"]),
        ],
        floats(ROWS, TP),
        name="edge_gradient",
    )


def solution(mesh):
    in_specs = (
        P(("tile", "cond"), None),
        P("tile", None),
        P("cond", None, None, None),
        P("cond", None, None, None),
        P(),
        P("cond"),
    )
    out_specs = P(("tile", "cond"), None)
    return jax.shard_map(shards, mesh=mesh, in_specs=in_specs, out_specs=out_specs, check_vma=False)
```

```python
import functools

import jax
import jax.numpy as jnp
import ml_dtypes
import numpy as np
from jax import lax
from jax.experimental import pallas as pl
from jax.experimental.pallas import tpu as pltpu
from jax.sharding import PartitionSpec as P

TP = 512
HALO = 32
KSUP = 65
HALF = KSUP // 2
KERNELS = 2
CONDS = 8
FULL = TP + 2 * HALO
PARTS = 4
ROWS = TP // PARTS
FA = 40
FB = 64
BF = jnp.bfloat16
F32 = jnp.float32

mask_steep = 2.0
resist_steep = 4.0
band_weight = 1.0


def waves(positions):
    angles = (np.outer(np.asarray(positions, np.int64), np.arange(HALF + 1)) % FULL) * (2.0 * np.pi / FULL)
    return np.cos(angles), np.sin(angles)


def halves(table):
    high = table.astype(np.float32).astype(ml_dtypes.bfloat16)
    low = (table - high.astype(np.float64)).astype(np.float32).astype(ml_dtypes.bfloat16)
    return high, low


def row_table(positions):
    cosine, sine = waves(positions)
    table = np.zeros((len(positions), 2 * FA))
    table[:, : HALF + 1] = cosine
    table[:, FA : FA + HALF + 1] = sine
    return table


def column_table(positions):
    cosine, sine = waves(positions)
    table = np.zeros((len(positions), 4 * FB))
    for block, values in enumerate((cosine, cosine, sine, -sine)):
        table[:, block * FB : block * FB + HALF] = values[:, 1:]
    table[:, HALF] = 1.0
    return table


@functools.cache
def tables():
    pixels = np.arange(TP) + HALO
    column = column_table(pixels)
    column_high, column_low = halves(column)
    turned = np.concatenate([column[:, : 2 * FB].T, column[:, 2 * FB :].T], axis=1)
    turned_high, turned_low = halves(turned)
    row = row_table(pixels)
    row_high, row_low = halves(row)
    out = {}
    out["column"] = np.stack([column_high, column_low])
    spectrum_rows = []
    halo_rows = []
    forward = []
    backward = []
    for part in range(PARTS):
        own = np.arange(ROWS) + part * ROWS + HALO
        rim = np.arange(HALO) + (0 if part == PARTS - 1 else FULL - HALO)
        high, low = halves(row_table(np.concatenate([own, rim])).T)
        spectrum_rows.append(np.concatenate([high, low, high], axis=1))
        high, low = halves(row_table(np.arange(HALO) + (0 if part == PARTS - 1 else FULL - HALO)))
        halo_rows.append(np.concatenate([high, low, high], axis=1))
        cols = slice(part * ROWS, (part + 1) * ROWS)
        high = np.concatenate([turned_high[:, :TP][:, cols], turned_high[:, TP:][:, cols]], axis=1)
        low = np.concatenate([turned_low[:, :TP][:, cols], turned_low[:, TP:][:, cols]], axis=1)
        forward.append(np.concatenate([high, high, low]))
        backward.append(np.concatenate([column_high[cols], column_high[cols], column_low[cols]]))
    out["spectrum_rows"] = np.stack(spectrum_rows)
    out["halo_rows"] = np.stack(halo_rows)
    out["forward"] = np.stack(forward)
    out["backward"] = np.stack(backward)
    out["turned"] = np.concatenate([turned_high, turned_high, turned_low])
    out["row"] = np.concatenate([row_high, row_low, row_high], axis=1)
    out["row_turned"] = np.concatenate([row_high.T, row_low.T])
    return out


def dot(left, right):
    return jnp.dot(left, right, preferred_element_type=F32)


def split(value):
    high = value.astype(BF)
    return high, (value - high.astype(F32)).astype(BF)


def spectrum_of(mask, column_ref, rows):
    high, low = split(mask)
    across = dot(high, column_ref[0]) + dot(low, column_ref[0]) + dot(high, column_ref[1])
    high, low = split(across)
    both = dot(rows, jnp.concatenate([high, high, low], axis=0))
    even = both[:FA, : 2 * FB] - both[FA:, 2 * FB :]
    odd = both[FA:, : 2 * FB] + both[:FA, 2 * FB :]
    return even, odd


def open_kernel(
    part_ref, theta_hbm, real_hbm, imag_hbm, thresholds_hbm, weights_hbm, forward_hbm, backward_hbm,
    out_ref, rim_ref, shares_ref, forward_ref, backward_ref, real_ref, imag_ref, thresholds_ref, weights_ref, stage, sems,
):
    part = part_ref[0]
    moves = [
        (real_hbm, real_ref),
        (imag_hbm, imag_ref),
        (thresholds_hbm, thresholds_ref),
        (weights_hbm, weights_ref),
        (theta_hbm.at[pl.ds(pl.multiple_of(jnp.where(part == 0, 0, ROWS - HALO), HALO), HALO)], rim_ref),
        (forward_hbm.at[part], forward_ref),
        (backward_hbm.at[part], backward_ref),
    ]
    copies = [pltpu.make_async_copy(source, target, sems.at[i]) for i, (source, target) in enumerate(moves)]
    for copy in copies:
        copy.start()
    local_conds = real_ref.shape[0]
    mats = local_conds * KERNELS * 2
    stage[...] = jnp.zeros_like(stage)
    for copy in copies[:4]:
        copy.wait()
    for cond in range(local_conds):
        for kern in range(KERNELS):
            for piece, ref in enumerate((real_ref, imag_ref)):
                stage[(cond * KERNELS + kern) * 2 + piece, :KSUP, :KSUP] = ref[cond, :, kern, :]
    rows = stage.shape[1]
    source = lax.broadcasted_iota(jnp.int32, (2 * FB, 4 * FB), 0)
    target = lax.broadcasted_iota(jnp.int32, (2 * FB, 4 * FB), 1)
    lane = target % FB
    block = target // FB
    plus = (block == 0) | (block == 3)
    freq = jnp.where(lane < HALF, lane + 1, 0)
    used = (lane < HALF) | ((lane == HALF) & (block % 2 == 0))
    pick = (used & (source == jnp.where(plus, HALF + freq, HALF - freq))).astype(F32).astype(BF)
    high, low = split(stage[...].reshape(mats * rows, 2 * FB))
    picked = [dot(piece, pick) for piece in (high, low)]
    source = lax.broadcasted_iota(jnp.int32, (FA, 2 * rows), 1) % rows
    target = lax.broadcasted_iota(jnp.int32, (FA, 2 * rows), 0)
    turn = ((source == HALF - target) & (target <= HALF)).astype(F32).astype(BF)
    lane = lax.broadcasted_iota(jnp.int32, (FA, 2 * FB), 1)
    row = lax.broadcasted_iota(jnp.int32, (FA, 2 * FB), 0)
    valid = (row <= HALF) & ((lane <= HALF) | ((row > 0) & (lane >= FB) & (lane < FB + HALF)))
    scale = 1.0 / (FULL * FULL)
    keep_top = jnp.where(valid, scale, 0.0)
    keep_bottom = jnp.where((row == 0) & (lane == HALF), 0.0, keep_top)
    first = lane % FB < HALF
    extra = jnp.zeros((FA, 2 * FB), F32)
    for kern in range(local_conds * KERNELS):
        arrays = [[], []]
        for piece in range(2):
            start = (kern * 2 + piece) * rows
            top = picked[0][start + HALF : start + HALF + FA, : 2 * FB] + picked[1][start + HALF : start + HALF + FA, : 2 * FB]
            pieces = jnp.concatenate([half[start : start + rows, 2 * FB :] for half in picked], axis=0)
            bottom = dot(turn, pieces.astype(BF)) * keep_bottom
            top = top * keep_top
            arrays[0].append(top + bottom)
            arrays[1].append(top - bottom)
        for which, (real, imag) in enumerate(arrays):
            packed = jnp.where(first, real, pltpu.roll(imag, HALF, 1))
            if which == 0:
                packed = jnp.where(row == FA - 1, thresholds_ref[kern // KERNELS], packed)
            out_ref[kern * 2 + which] = packed
            for piece, value in enumerate((real, imag)):
                place = kern * 4 + which * 2 + piece
                extra = jnp.where(lane == place, pltpu.roll(value, (place - HALF) % (2 * FB), 1), extra)
    out_ref[local_conds * KERNELS * 2] = extra
    weight_sum = weights_ref[0]
    for i in range(1, CONDS):
        weight_sum = weight_sum + weights_ref[i]
    row = lax.broadcasted_iota(jnp.int32, shares_ref.shape, 0)
    shares = jnp.zeros(shares_ref.shape, F32)
    for group, step in enumerate((0, 2, 1, 3)):
        for i in range(local_conds):
            weight = weights_ref[lax.bitwise_xor(part, step) * local_conds + i]
            shares = jnp.where(row == group * local_conds + i, weight.astype(F32), shares)
    shares_ref[...] = shares / weight_sum.astype(F32)
    for copy in copies[4:]:
        copy.wait()


def spectrum_kernel(part_ref, theta_ref, rim_ref, column_ref, rows_ref, out_ref):
    mask = jnp.tanh(mask_steep * jnp.concatenate([theta_ref[...], rim_ref[...]], axis=0))
    even, odd = spectrum_of(mask, column_ref, rows_ref[0])
    out_ref[0] = even
    out_ref[1] = odd


def fields_kernel(
    part_ref, own_ref, side_ref, core_ref, cross_ref, shares_ref, target_ref, forward_ref, backward_ref, row_ref,
    row_turned_ref, out_ref, kernels_ref, lines, folded, amps, tanhs, total, signs, turned, backs,
):
    count = kernels_ref.shape[0]
    local = count // PARTS
    tall = 4 * FA
    even = side_ref[2 * local + 1] + cross_ref[2 * local + 1]
    odd = side_ref[2 * local + 2] + cross_ref[2 * local + 2]
    lane = lax.broadcasted_iota(jnp.int32, (FA, 2 * FB), 1)
    row = lax.broadcasted_iota(jnp.int32, (FA, 2 * FB), 0)
    zero_lane = (lane == HALF) & (row <= HALF)
    for group, ref in enumerate((own_ref, side_ref, core_ref, cross_ref)):
        extra = ref[2 * local]
        for kern in range(local):
            values = []
            for which in range(2):
                packed = ref[2 * kern + which]
                for part, value in enumerate((packed, pltpu.roll(packed, 2 * FB - HALF, 1))):
                    place = kern * 4 + which * 2 + part
                    zeroth = pltpu.roll(extra, (HALF - place) % (2 * FB), 1)
                    value = jnp.where(zero_lane, zeroth, value)
                    kernels_ref[group * local + kern, which * 2 + part] = value
                    values.append(value)
            he_real, he_imag, ho_real, ho_imag = values
            start = (group * local + kern) * tall
            for i, value in enumerate(
                (
                    even * he_real + odd * ho_imag,
                    odd * he_real - even * ho_imag,
                    even * he_imag - odd * ho_real,
                    odd * he_imag + even * ho_real,
                )
            ):
                lines[start + i * FA : start + (i + 1) * FA] = value

    high, low = split(lines[...])
    lines_folded = dot(high, forward_ref[: 2 * FB]) + dot(low, forward_ref[: 2 * FB]) + dot(high, forward_ref[4 * FB :])
    for kern in range(count):
        parts = []
        for i in range(2):
            x_part = lines_folded[tall * kern + 2 * FA * i : tall * kern + 2 * FA * i + FA]
            y_part = lines_folded[tall * kern + 2 * FA * i + FA : tall * kern + 2 * FA * (i + 1)]
            parts.append(
                jnp.concatenate(
                    [x_part[:, :ROWS] + y_part[:, ROWS:], y_part[:, :ROWS] - x_part[:, ROWS:]], axis=0
                )
            )
        high, low = split(jnp.concatenate(parts, axis=1))
        folded[kern] = jnp.concatenate([high, high, low], axis=0)
    total[...] = jnp.zeros_like(total)
    signs[...] = 1.0 - 2.0 * target_ref[...].astype(F32)

    def expose(cond, carry):
        intensity = None
        for kern in range(KERNELS):
            index = cond * KERNELS + kern
            amp = dot(row_ref[...], folded[index])
            amps[index] = amp
            power = amp[:, :ROWS] * amp[:, :ROWS] + amp[:, ROWS:] * amp[:, ROWS:]
            intensity = power if intensity is None else intensity + power
        level = kernels_ref[cond * KERNELS, 0, FA - 1 :, :]
        value = jnp.tanh((0.5 * resist_steep) * (intensity - level))
        tanhs[cond] = value
        total[...] += value
        return carry

    lax.fori_loop(0, CONDS, expose, 0, unroll=2)
    total[...] = total[...] * (band_weight / (CONDS * CONDS))

    def drive(cond, carry):
        weight = shares_ref[pl.ds(cond, 1), :]
        value = tanhs[cond]
        slope = (weight + band_weight / CONDS) * value + weight * signs[...] - total[...]
        field = (0.5 * resist_steep) * (1.0 - value * value) * slope
        field = jnp.concatenate([field, field], axis=1)
        for kern in range(KERNELS):
            index = cond * KERNELS + kern
            high, low = split(field * amps[index])
            long = dot(row_turned_ref[...], high)
            back = long[: 2 * FA] + long[2 * FA :] + dot(row_turned_ref[: 2 * FA], low)
            turned[pl.ds(index * 2, 2)] = jnp.stack([back[:, :ROWS], back[:, ROWS:]])
        return carry

    lax.fori_loop(0, CONDS, drive, 0, unroll=2)
    high, low = split(turned[...].reshape(count * tall, ROWS))
    backs[...] = dot(high, backward_ref[:ROWS]) + dot(low, backward_ref[:ROWS]) + dot(high, backward_ref[2 * ROWS :])

    sum_even = jnp.zeros((FA, 2 * FB), F32)
    sum_odd = jnp.zeros((FA, 2 * FB), F32)
    for kern in range(count):
        grads = []
        for i in range(2):
            c_part = backs[tall * kern + 2 * FA * i : tall * kern + 2 * FA * i + FA]
            s_part = backs[tall * kern + 2 * FA * i + FA : tall * kern + 2 * FA * (i + 1)]
            grads.append(
                (
                    c_part[:, : 2 * FB] - s_part[:, 2 * FB :],
                    s_part[:, : 2 * FB] + c_part[:, 2 * FB :],
                )
            )
        (x_real, y_real), (x_imag, y_imag) = grads
        he_real, he_imag, ho_real, ho_imag = (kernels_ref[kern, i] for i in range(4))
        sum_even = sum_even + x_real * he_real + x_imag * he_imag - y_real * ho_imag + y_imag * ho_real
        sum_odd = sum_odd + x_real * ho_imag - x_imag * ho_real + y_real * he_real + y_imag * he_imag
    out_ref[:FA] = sum_even
    out_ref[FA:] = sum_odd


def fold_rows(value, turned_ref):
    high, low = split(value)
    result = dot(jnp.concatenate([high, low, high], axis=1), turned_ref[...])
    x_part, y_part = result[:FA], result[FA:]
    both = jnp.concatenate([x_part[:, :TP] + y_part[:, TP:], y_part[:, :TP] - x_part[:, TP:]], axis=0)
    high, low = split(both)
    return jnp.concatenate([high, high, low], axis=0)


def gradient_kernel(part_ref, theta_ref, mine_ref, turned_ref, rows_ref, out_ref):
    mask = jnp.tanh(mask_steep * theta_ref[...])
    scale = mask_steep * (1.0 - mask * mask)
    out_ref[...] = dot(rows_ref[...], fold_rows(mine_ref[...], turned_ref)) * scale


def edge_kernel(part_ref, theta_ref, gradient_ref, near_ref, turned_ref, halo_rows_ref, out_ref):
    out_ref[...] = gradient_ref[...]
    start = pl.multiple_of(jnp.where(part_ref[0] == PARTS - 1, ROWS - HALO, 0), HALO)
    rim = dot(halo_rows_ref[0], fold_rows(near_ref[...], turned_ref))
    mask = jnp.tanh(mask_steep * theta_ref[pl.ds(start, HALO), :])
    out_ref[pl.ds(start, HALO), :] += rim * (mask_steep * (1.0 - mask * mask))


def whole_spec(array):
    rank = len(array.shape)
    return pl.BlockSpec(array.shape, lambda i, *refs: (0,) * rank)


def part_spec(array):
    rank = len(array.shape)
    return pl.BlockSpec((1,) + array.shape[1:], lambda i, part, *refs: (part[0],) + (0,) * (rank - 1))


def call(kernel, scalars, operands, specs, out_shapes, scratch=(), name=None, flops=1 << 28):
    many = isinstance(out_shapes, list)
    out_specs = [whole_spec(shape) for shape in (out_shapes if many else [out_shapes])]
    return pl.pallas_call(
        kernel,
        grid_spec=pltpu.PrefetchScalarGridSpec(
            num_scalar_prefetch=len(scalars),
            grid=(1,),
            in_specs=specs,
            out_specs=out_specs if many else out_specs[0],
            scratch_shapes=list(scratch),
        ),
        out_shape=out_shapes,
        compiler_params=pltpu.CompilerParams(vmem_limit_bytes=48 * 1024 * 1024),
        cost_estimate=pl.CostEstimate(flops=flops, bytes_accessed=1 << 20, transcendentals=0),
        name=name,
    )(*scalars, *operands)


def floats(*shape):
    return jax.ShapeDtypeStruct(shape, F32)


def shards(theta, target, kernel_real, kernel_imag, weights, thresholds):
    table = {name: jnp.asarray(value) for name, value in tables().items()}
    tiles = lax.axis_size("tile")
    part = lax.axis_index("cond")
    parts = part.reshape(1).astype(jnp.int32)
    local_conds = kernel_real.shape[0]
    local = local_conds * KERNELS
    count = CONDS * KERNELS
    last = PARTS - 1
    hbm = pl.BlockSpec(memory_space=pltpu.HBM)

    def pairs(down, up):
        return [(PARTS * (i + 1) + down[0], PARTS * i + down[1]) for i in range(tiles - 1)] + [
            (PARTS * i + up[0], PARTS * (i + 1) + up[1]) for i in range(tiles - 1)
        ]

    def across(value, down, up):
        return lax.ppermute(value, ("tile", "cond"), pairs(down, up))

    def partner(value, step):
        return lax.ppermute(value, "cond", [(i, i ^ step) for i in range(PARTS)])

    kernel_shape = (local_conds, KSUP, KERNELS, KSUP)
    own, rim, shares, forward, backward = call(
        open_kernel,
        (parts,),
        tuple(
            pltpu.with_memory_space_constraint(value, pltpu.HBM)
            for value in (
                theta, kernel_real.transpose(0, 2, 1, 3), kernel_imag.transpose(0, 2, 1, 3), thresholds, weights,
                table["forward"], table["backward"],
            )
        ),
        [hbm] * 7,
        [
            floats(2 * local + 1, FA, 2 * FB),
            floats(HALO, TP),
            floats(CONDS, ROWS),
            jax.ShapeDtypeStruct(table["forward"].shape[1:], BF),
            jax.ShapeDtypeStruct(table["backward"].shape[1:], BF),
        ],
        scratch=(
            pltpu.VMEM(kernel_shape, F32),
            pltpu.VMEM(kernel_shape, F32),
            pltpu.SMEM(thresholds.shape, F32),
            pltpu.SMEM(weights.shape, jnp.int32),
            pltpu.VMEM((2 * local, 72, 2 * FB), F32),
            pltpu.SemaphoreType.DMA((7,)),
        ),
        name="open_parts",
    )
    near = across(rim, (0, 0), (last, last))
    side = partner(own, 2)
    core = partner(own, 1)
    spectrum = call(
        spectrum_kernel,
        (parts,),
        (theta, near, table["column"], table["spectrum_rows"]),
        [whole_spec(theta), whole_spec(near), whole_spec(table["column"]), part_spec(table["spectrum_rows"])],
        floats(2, FA, 2 * FB),
        name="mask_spectrum",
    )
    mixed = jnp.concatenate([side, spectrum + partner(spectrum, 2)], axis=0)
    adjoint = call(
        fields_kernel,
        (parts,),
        (own, mixed, core, partner(mixed, 1), shares, target, forward, backward, table["row"], table["row_turned"]),
        [
            whole_spec(own),
            whole_spec(mixed),
            whole_spec(core),
            whole_spec(mixed),
            whole_spec(shares),
            pl.BlockSpec((TP, ROWS), lambda i, part, *refs: (0, part[0])),
            whole_spec(forward),
            whole_spec(backward),
            whole_spec(table["row"]),
            whole_spec(table["row_turned"]),
        ],
        floats(2 * FA, 2 * FB),
        scratch=(
            pltpu.VMEM((count, 4, FA, 2 * FB), F32),
            pltpu.VMEM((count * 4 * FA, 2 * FB), F32),
            pltpu.VMEM((count, 6 * FA, 2 * ROWS), BF),
            pltpu.VMEM((count, TP, 2 * ROWS), F32),
            pltpu.VMEM((CONDS, TP, ROWS), F32),
            pltpu.VMEM((TP, ROWS), F32),
            pltpu.VMEM((TP, ROWS), F32),
            pltpu.VMEM((count * 2, 2 * FA, ROWS), F32),
            pltpu.VMEM((count * 4 * FA, 4 * FB), F32),
        ),
        name="coherent_fields",
        flops=1 << 33,
    )
    adjoint = adjoint + partner(adjoint, 1)
    adjoint = adjoint + partner(adjoint, 2)
    near = across(adjoint, (last, last), (0, 0))
    gradient = call(
        gradient_kernel,
        (parts,),
        (theta, adjoint, table["turned"], table["row"]),
        [
            whole_spec(theta),
            whole_spec(adjoint),
            whole_spec(table["turned"]),
            pl.BlockSpec((ROWS, 6 * FA), lambda i, part, *refs: (part[0], 0)),
        ],
        floats(ROWS, TP),
        name="own_gradient",
        flops=1 << 31,
    )
    return call(
        edge_kernel,
        (parts,),
        (theta, gradient, near, table["turned"], table["halo_rows"]),
        [
            whole_spec(theta),
            whole_spec(gradient),
            whole_spec(near),
            whole_spec(table["turned"]),
            part_spec(table["halo_rows"]),
        ],
        floats(ROWS, TP),
        name="edge_gradient",
    )


def solution(mesh):
    in_specs = (
        P(("tile", "cond"), None),
        P("tile", None),
        P("cond", None, None, None),
        P("cond", None, None, None),
        P(),
        P("cond"),
    )
    out_specs = P(("tile", "cond"), None)
    return jax.shard_map(shards, mesh=mesh, in_specs=in_specs, out_specs=out_specs, check_vma=False)
```

```python
import functools

import jax
import jax.numpy as jnp
import ml_dtypes
import numpy as np
from jax import lax
from jax.experimental import pallas as pl
from jax.experimental.pallas import tpu as pltpu
from jax.sharding import PartitionSpec as P

TP = 512
HALO = 32
KSUP = 65
HALF = KSUP // 2
KERNELS = 2
CONDS = 8
FULL = TP + 2 * HALO
PARTS = 4
ROWS = TP // PARTS
FA = 40
FB = 64
BF = jnp.bfloat16
F32 = jnp.float32

mask_steep = 2.0
resist_steep = 4.0
band_weight = 1.0


def waves(positions):
    angles = (np.outer(np.asarray(positions, np.int64), np.arange(HALF + 1)) % FULL) * (2.0 * np.pi / FULL)
    return np.cos(angles), np.sin(angles)


def halves(table):
    high = table.astype(np.float32).astype(ml_dtypes.bfloat16)
    low = (table - high.astype(np.float64)).astype(np.float32).astype(ml_dtypes.bfloat16)
    return high, low


def row_table(positions):
    cosine, sine = waves(positions)
    table = np.zeros((len(positions), 2 * FA))
    table[:, : HALF + 1] = cosine
    table[:, FA : FA + HALF + 1] = sine
    return table


def pair_table(positions):
    table = row_table(positions)
    return np.concatenate([table, np.concatenate([-table[:, FA:], table[:, :FA]], axis=1)])


def column_table(positions):
    cosine, sine = waves(positions)
    table = np.zeros((len(positions), 4 * FB))
    for block, values in enumerate((cosine, cosine, sine, -sine)):
        table[:, block * FB : block * FB + HALF] = values[:, 1:]
    table[:, HALF] = 1.0
    return table


@functools.cache
def tables():
    pixels = np.arange(TP) + HALO
    column = column_table(pixels)
    column_high, column_low = halves(column)
    turned = np.concatenate([column[:, : 2 * FB].T, column[:, 2 * FB :].T], axis=1)
    turned_high, turned_low = halves(turned)
    row = row_table(pixels)
    row_high, row_low = halves(row)
    out = {}
    out["column"] = np.stack([column_high, column_low])
    spectrum_rows = []
    halo_rows = []
    own_rows = []
    forward = []
    backward = []
    for part in range(PARTS):
        own = np.arange(ROWS) + part * ROWS + HALO
        rim = np.arange(HALO) + (0 if part == PARTS - 1 else FULL - HALO)
        high, low = halves(row_table(np.concatenate([own, rim])).T)
        spectrum_rows.append(np.concatenate([high, low, high], axis=1))
        high, low = halves(pair_table(rim))
        halo_rows.append(np.concatenate([high, low, high], axis=1))
        high, low = halves(pair_table(own))
        own_rows.append(np.concatenate([high, low, high], axis=1))
        cols = slice(part * ROWS, (part + 1) * ROWS)
        high = np.concatenate([turned_high[:, :TP][:, cols], turned_high[:, TP:][:, cols]], axis=1)
        low = np.concatenate([turned_low[:, :TP][:, cols], turned_low[:, TP:][:, cols]], axis=1)
        forward.append(np.concatenate([high, high, low]))
        backward.append(np.concatenate([column_high[cols], column_high[cols], column_low[cols]]))
    out["spectrum_rows"] = np.stack(spectrum_rows)
    out["own_rows"] = np.stack(own_rows)
    out["halo_rows"] = np.stack(halo_rows)
    out["forward"] = np.stack(forward)
    out["backward"] = np.stack(backward)
    out["turned"] = np.stack([column_high.T, column_low.T])
    out["row"] = np.concatenate([row_high, row_low, row_high], axis=1)
    out["row_turned"] = np.concatenate([row_high.T, row_low.T])
    return out


def dot(left, right):
    return jnp.dot(left, right, preferred_element_type=F32)


def split(value):
    high = value.astype(BF)
    return high, (value - high.astype(F32)).astype(BF)


def spectrum_of(mask, column_ref, rows):
    high, low = split(mask)
    across = dot(high, column_ref[0]) + dot(low, column_ref[0]) + dot(high, column_ref[1])
    high, low = split(across)
    both = dot(rows, jnp.concatenate([high, high, low], axis=0))
    even = both[:FA, : 2 * FB] - both[FA:, 2 * FB :]
    odd = both[FA:, : 2 * FB] + both[:FA, 2 * FB :]
    return even, odd


def open_kernel(
    part_ref, theta_hbm, real_hbm, imag_hbm, thresholds_hbm, weights_hbm, forward_hbm, backward_hbm,
    out_ref, rim_ref, shares_ref, forward_ref, backward_ref, real_ref, imag_ref, thresholds_ref, weights_ref, stage, sems,
):
    part = part_ref[0]
    moves = [
        (real_hbm, real_ref),
        (imag_hbm, imag_ref),
        (thresholds_hbm, thresholds_ref),
        (weights_hbm, weights_ref),
        (theta_hbm.at[pl.ds(pl.multiple_of(jnp.where(part == 0, 0, ROWS - HALO), HALO), HALO)], rim_ref),
        (forward_hbm.at[part], forward_ref),
        (backward_hbm.at[part], backward_ref),
    ]
    copies = [pltpu.make_async_copy(source, target, sems.at[i]) for i, (source, target) in enumerate(moves)]
    for copy in copies:
        copy.start()
    local_conds = real_ref.shape[0]
    mats = local_conds * KERNELS * 2
    stage[...] = jnp.zeros_like(stage)
    for copy in copies[:4]:
        copy.wait()
    for cond in range(local_conds):
        for kern in range(KERNELS):
            for piece, ref in enumerate((real_ref, imag_ref)):
                stage[(cond * KERNELS + kern) * 2 + piece, :KSUP, :KSUP] = ref[cond, :, kern, :]
    rows = stage.shape[1]
    source = lax.broadcasted_iota(jnp.int32, (2 * FB, 4 * FB), 0)
    target = lax.broadcasted_iota(jnp.int32, (2 * FB, 4 * FB), 1)
    lane = target % FB
    block = target // FB
    plus = (block == 0) | (block == 3)
    freq = jnp.where(lane < HALF, lane + 1, 0)
    used = (lane < HALF) | ((lane == HALF) & (block % 2 == 0))
    pick = (used & (source == jnp.where(plus, HALF + freq, HALF - freq))).astype(F32).astype(BF)
    high, low = split(stage[...].reshape(mats * rows, 2 * FB))
    picked = [dot(piece, pick) for piece in (high, low)]
    source = lax.broadcasted_iota(jnp.int32, (FA, 2 * rows), 1) % rows
    target = lax.broadcasted_iota(jnp.int32, (FA, 2 * rows), 0)
    turn = ((source == HALF - target) & (target <= HALF)).astype(F32).astype(BF)
    lane = lax.broadcasted_iota(jnp.int32, (FA, 2 * FB), 1)
    row = lax.broadcasted_iota(jnp.int32, (FA, 2 * FB), 0)
    valid = (row <= HALF) & ((lane <= HALF) | ((row > 0) & (lane >= FB) & (lane < FB + HALF)))
    scale = 1.0 / (FULL * FULL)
    keep_top = jnp.where(valid, scale, 0.0)
    keep_bottom = jnp.where((row == 0) & (lane == HALF), 0.0, keep_top)
    first = lane % FB < HALF
    extra = jnp.zeros((FA, 2 * FB), F32)
    for kern in range(local_conds * KERNELS):
        arrays = [[], []]
        for piece in range(2):
            start = (kern * 2 + piece) * rows
            top = picked[0][start + HALF : start + HALF + FA, : 2 * FB] + picked[1][start + HALF : start + HALF + FA, : 2 * FB]
            pieces = jnp.concatenate([half[start : start + rows, 2 * FB :] for half in picked], axis=0)
            bottom = dot(turn, pieces.astype(BF)) * keep_bottom
            top = top * keep_top
            arrays[0].append(top + bottom)
            arrays[1].append(top - bottom)
        for which, (real, imag) in enumerate(arrays):
            packed = jnp.where(first, real, pltpu.roll(imag, HALF, 1))
            if which == 0:
                packed = jnp.where(row == FA - 1, thresholds_ref[kern // KERNELS], packed)
            out_ref[kern * 2 + which] = packed
            for piece, value in enumerate((real, imag)):
                place = kern * 4 + which * 2 + piece
                extra = jnp.where(lane == place, pltpu.roll(value, (place - HALF) % (2 * FB), 1), extra)
    out_ref[local_conds * KERNELS * 2] = extra
    weight_sum = weights_ref[0]
    for i in range(1, CONDS):
        weight_sum = weight_sum + weights_ref[i]
    row = lax.broadcasted_iota(jnp.int32, shares_ref.shape, 0)
    shares = jnp.zeros(shares_ref.shape, F32)
    for group, step in enumerate((0, 2, 1, 3)):
        for i in range(local_conds):
            weight = weights_ref[lax.bitwise_xor(part, step) * local_conds + i]
            shares = jnp.where(row == group * local_conds + i, weight.astype(F32), shares)
    shares_ref[...] = shares / weight_sum.astype(F32)
    for copy in copies[4:]:
        copy.wait()


def spectrum_kernel(part_ref, theta_ref, rim_ref, column_ref, rows_ref, out_ref):
    mask = jnp.tanh(mask_steep * jnp.concatenate([theta_ref[...], rim_ref[...]], axis=0))
    even, odd = spectrum_of(mask, column_ref, rows_ref[0])
    out_ref[0] = even
    out_ref[1] = odd


def fields_kernel(
    part_ref, own_ref, side_ref, core_ref, cross_ref, shares_ref, target_ref, forward_ref, backward_ref, row_ref,
    row_turned_ref, out_ref, kernels_ref, lines, folded, amps, tanhs, total, signs, turned, backs,
):
    count = kernels_ref.shape[0]
    local = count // PARTS
    tall = 4 * FA
    even = side_ref[2 * local + 1] + cross_ref[2 * local + 1]
    odd = side_ref[2 * local + 2] + cross_ref[2 * local + 2]
    lane = lax.broadcasted_iota(jnp.int32, (FA, 2 * FB), 1)
    row = lax.broadcasted_iota(jnp.int32, (FA, 2 * FB), 0)
    zero_lane = (lane == HALF) & (row <= HALF)
    for group, ref in enumerate((own_ref, side_ref, core_ref, cross_ref)):
        extra = ref[2 * local]
        for kern in range(local):
            values = []
            for which in range(2):
                packed = ref[2 * kern + which]
                for part, value in enumerate((packed, pltpu.roll(packed, 2 * FB - HALF, 1))):
                    place = kern * 4 + which * 2 + part
                    zeroth = pltpu.roll(extra, (HALF - place) % (2 * FB), 1)
                    value = jnp.where(zero_lane, zeroth, value)
                    kernels_ref[group * local + kern, which * 2 + part] = value
                    values.append(value)
            he_real, he_imag, ho_real, ho_imag = values
            start = (group * local + kern) * tall
            for i, value in enumerate(
                (
                    even * he_real + odd * ho_imag,
                    odd * he_real - even * ho_imag,
                    even * he_imag - odd * ho_real,
                    odd * he_imag + even * ho_real,
                )
            ):
                lines[start + i * FA : start + (i + 1) * FA] = value

    high, low = split(lines[...])
    lines_folded = dot(jnp.concatenate([high, low], axis=1), forward_ref[: 4 * FB]) + dot(high, forward_ref[4 * FB :])
    for kern in range(count):
        parts = []
        for i in range(2):
            x_part = lines_folded[tall * kern + 2 * FA * i : tall * kern + 2 * FA * i + FA]
            y_part = lines_folded[tall * kern + 2 * FA * i + FA : tall * kern + 2 * FA * (i + 1)]
            parts.append(
                jnp.concatenate(
                    [x_part[:, :ROWS] + y_part[:, ROWS:], y_part[:, :ROWS] - x_part[:, ROWS:]], axis=0
                )
            )
        high, low = split(jnp.concatenate(parts, axis=1))
        folded[kern] = jnp.concatenate([high, high, low], axis=0)
    total[...] = jnp.zeros_like(total)
    signs[...] = 1.0 - 2.0 * target_ref[...].astype(F32)

    def expose(cond, carry):
        intensity = None
        for kern in range(KERNELS):
            index = cond * KERNELS + kern
            amp = dot(row_ref[...], folded[index])
            amps[index] = amp
            power = amp[:, :ROWS] * amp[:, :ROWS] + amp[:, ROWS:] * amp[:, ROWS:]
            intensity = power if intensity is None else intensity + power
        level = kernels_ref[cond * KERNELS, 0, FA - 1 :, :]
        value = jnp.tanh((0.5 * resist_steep) * (intensity - level))
        tanhs[cond] = value
        total[...] += value
        return carry

    lax.fori_loop(0, CONDS, expose, 0, unroll=4)
    total[...] = total[...] * (band_weight / (CONDS * CONDS))

    def drive(cond, carry):
        weight = shares_ref[pl.ds(cond, 1), :]
        value = tanhs[cond]
        slope = (weight + band_weight / CONDS) * value + weight * signs[...] - total[...]
        field = (0.5 * resist_steep) * (1.0 - value * value) * slope
        field = jnp.concatenate([field, field], axis=1)
        for kern in range(KERNELS):
            index = cond * KERNELS + kern
            high, low = split(field * amps[index])
            long = dot(row_turned_ref[...], high)
            back = long[: 2 * FA] + long[2 * FA :] + dot(row_turned_ref[: 2 * FA], low)
            turned[pl.ds(index * 2, 2)] = jnp.stack([back[:, :ROWS], back[:, ROWS:]])
        return carry

    lax.fori_loop(0, CONDS, drive, 0, unroll=4)
    high, low = split(turned[...].reshape(count * tall, ROWS))
    backs[...] = dot(jnp.concatenate([high, low], axis=1), backward_ref[: 2 * ROWS]) + dot(high, backward_ref[2 * ROWS :])

    sum_even = jnp.zeros((FA, 2 * FB), F32)
    sum_odd = jnp.zeros((FA, 2 * FB), F32)
    for kern in range(count):
        grads = []
        for i in range(2):
            c_part = backs[tall * kern + 2 * FA * i : tall * kern + 2 * FA * i + FA]
            s_part = backs[tall * kern + 2 * FA * i + FA : tall * kern + 2 * FA * (i + 1)]
            grads.append(
                (
                    c_part[:, : 2 * FB] - s_part[:, 2 * FB :],
                    s_part[:, : 2 * FB] + c_part[:, 2 * FB :],
                )
            )
        (x_real, y_real), (x_imag, y_imag) = grads
        he_real, he_imag, ho_real, ho_imag = (kernels_ref[kern, i] for i in range(4))
        sum_even = sum_even + x_real * he_real + x_imag * he_imag - y_real * ho_imag + y_imag * ho_real
        sum_odd = sum_odd + x_real * ho_imag - x_imag * ho_real + y_real * he_real + y_imag * he_imag
    out_ref[:FA] = sum_even
    out_ref[FA:] = sum_odd


def image_rows(value, rows, turned_ref):
    high, low = split(value)
    pair = dot(rows, jnp.concatenate([high, high, low], axis=0))
    count = pair.shape[0] // 2
    high, low = split(jnp.concatenate([pair[:count], pair[count:]], axis=1))
    return dot(high, turned_ref[0]) + dot(low, turned_ref[0]) + dot(high, turned_ref[1])


def edge_start(part_ref):
    return pl.multiple_of(jnp.where(part_ref[0] == PARTS - 1, ROWS - HALO, 0), HALO)


def gradient_kernel(part_ref, theta_ref, sum_ref, back_ref, turned_ref, rows_ref, out_ref, edge_ref, scale_ref):
    middle = (part_ref[0] == 1) | (part_ref[0] == 2)
    mask = jnp.tanh(mask_steep * theta_ref[...])
    scale = mask_steep * (1.0 - mask * mask)
    mine = jnp.where(middle, sum_ref[...], back_ref[...])
    gradient = image_rows(mine, rows_ref[0], turned_ref) * scale
    out_ref[...] = gradient
    last = part_ref[0] == PARTS - 1
    edge_ref[...] = jnp.where(last, gradient[ROWS - HALO :], gradient[:HALO])
    scale_ref[...] = jnp.where(last, scale[ROWS - HALO :], scale[:HALO])


def edge_kernel(part_ref, gradient_hbm, edge_ref, scale_ref, near_ref, turned_ref, rows_ref, out_hbm, stage, sem):
    stage[...] = edge_ref[...] + image_rows(near_ref[...], rows_ref[0], turned_ref) * scale_ref[...]
    copy = pltpu.make_async_copy(stage, out_hbm.at[pl.ds(edge_start(part_ref), HALO)], sem)
    copy.start()
    copy.wait()


def whole_spec(array):
    rank = len(array.shape)
    return pl.BlockSpec(array.shape, lambda i, *refs: (0,) * rank)


def part_spec(array):
    rank = len(array.shape)
    return pl.BlockSpec((1,) + array.shape[1:], lambda i, part, *refs: (part[0],) + (0,) * (rank - 1))


def call(kernel, scalars, operands, specs, out_shapes, scratch=(), name=None, flops=1 << 28, out_specs=None, aliases=None):
    many = isinstance(out_shapes, list)
    if out_specs is None:
        out_specs = [whole_spec(shape) for shape in out_shapes] if many else whole_spec(out_shapes)
    return pl.pallas_call(
        kernel,
        grid_spec=pltpu.PrefetchScalarGridSpec(
            num_scalar_prefetch=len(scalars),
            grid=(1,),
            in_specs=specs,
            out_specs=out_specs,
            scratch_shapes=list(scratch),
        ),
        out_shape=out_shapes,
        input_output_aliases=aliases or {},
        compiler_params=pltpu.CompilerParams(vmem_limit_bytes=48 * 1024 * 1024),
        cost_estimate=pl.CostEstimate(flops=flops, bytes_accessed=1 << 20, transcendentals=0),
        name=name,
    )(*scalars, *operands)


def floats(*shape):
    return jax.ShapeDtypeStruct(shape, F32)


def shards(theta, target, kernel_real, kernel_imag, weights, thresholds):
    table = {name: jnp.asarray(value) for name, value in tables().items()}
    tiles = lax.axis_size("tile")
    part = lax.axis_index("cond")
    parts = part.reshape(1).astype(jnp.int32)
    local_conds = kernel_real.shape[0]
    local = local_conds * KERNELS
    count = CONDS * KERNELS
    last = PARTS - 1
    hbm = pl.BlockSpec(memory_space=pltpu.HBM)

    def pairs(down, up):
        return [(PARTS * (i + 1) + down[0], PARTS * i + down[1]) for i in range(tiles - 1)] + [
            (PARTS * i + up[0], PARTS * (i + 1) + up[1]) for i in range(tiles - 1)
        ]

    def across(value, down, up):
        return lax.ppermute(value, ("tile", "cond"), pairs(down, up))

    def partner(value, step):
        return lax.ppermute(value, "cond", [(i, i ^ step) for i in range(PARTS)])

    kernel_shape = (local_conds, KSUP, KERNELS, KSUP)
    own, rim, shares, forward, backward = call(
        open_kernel,
        (parts,),
        tuple(
            pltpu.with_memory_space_constraint(value, pltpu.HBM)
            for value in (
                theta, kernel_real.transpose(0, 2, 1, 3), kernel_imag.transpose(0, 2, 1, 3), thresholds, weights,
                table["forward"], table["backward"],
            )
        ),
        [hbm] * 7,
        [
            floats(2 * local + 1, FA, 2 * FB),
            floats(HALO, TP),
            floats(CONDS, ROWS),
            jax.ShapeDtypeStruct(table["forward"].shape[1:], BF),
            jax.ShapeDtypeStruct(table["backward"].shape[1:], BF),
        ],
        scratch=(
            pltpu.VMEM(kernel_shape, F32),
            pltpu.VMEM(kernel_shape, F32),
            pltpu.SMEM(thresholds.shape, F32),
            pltpu.SMEM(weights.shape, jnp.int32),
            pltpu.VMEM((2 * local, 72, 2 * FB), F32),
            pltpu.SemaphoreType.DMA((7,)),
        ),
        name="open_parts",
    )
    near = across(rim, (0, 0), (last, last))
    side = partner(own, 2)
    core = partner(own, 1)
    spectrum = call(
        spectrum_kernel,
        (parts,),
        (theta, near, table["column"], table["spectrum_rows"]),
        [whole_spec(theta), whole_spec(near), whole_spec(table["column"]), part_spec(table["spectrum_rows"])],
        floats(2, FA, 2 * FB),
        name="mask_spectrum",
    )
    mixed = jnp.concatenate([side, spectrum + partner(spectrum, 2)], axis=0)
    adjoint = call(
        fields_kernel,
        (parts,),
        (own, mixed, core, partner(mixed, 1), shares, target, forward, backward, table["row"], table["row_turned"]),
        [
            whole_spec(own),
            whole_spec(mixed),
            whole_spec(core),
            whole_spec(mixed),
            whole_spec(shares),
            pl.BlockSpec((TP, ROWS), lambda i, part, *refs: (0, part[0])),
            whole_spec(forward),
            whole_spec(backward),
            whole_spec(table["row"]),
            whole_spec(table["row_turned"]),
        ],
        floats(2 * FA, 2 * FB),
        scratch=(
            pltpu.VMEM((count, 4, FA, 2 * FB), F32),
            pltpu.VMEM((count * 4 * FA, 2 * FB), F32),
            pltpu.VMEM((count, 6 * FA, 2 * ROWS), BF),
            pltpu.VMEM((count, TP, 2 * ROWS), F32),
            pltpu.VMEM((CONDS, TP, ROWS), F32),
            pltpu.VMEM((TP, ROWS), F32),
            pltpu.VMEM((TP, ROWS), F32),
            pltpu.VMEM((count * 2, 2 * FA, ROWS), F32),
            pltpu.VMEM((count * 4 * FA, 4 * FB), F32),
        ),
        name="coherent_fields",
        flops=1 << 33,
    )
    adjoint = adjoint + lax.ppermute(adjoint, "cond", [(0, 1), (last, 2)])
    adjoint = adjoint + lax.ppermute(adjoint, "cond", [(1, 2), (2, 1)])
    near = across(adjoint, (2, last), (1, 0))
    back = lax.ppermute(adjoint, "cond", [(1, 0), (2, last)])
    gradient, edge, scale = call(
        gradient_kernel,
        (parts,),
        (theta, adjoint, back, table["turned"], table["own_rows"]),
        [
            whole_spec(theta),
            whole_spec(adjoint),
            whole_spec(back),
            whole_spec(table["turned"]),
            part_spec(table["own_rows"]),
        ],
        [floats(ROWS, TP), floats(HALO, TP), floats(HALO, TP)],
        name="own_gradient",
        flops=1 << 31,
    )
    return call(
        edge_kernel,
        (parts,),
        (gradient, edge, scale, near, table["turned"], table["halo_rows"]),
        [
            hbm,
            whole_spec(edge),
            whole_spec(scale),
            whole_spec(near),
            whole_spec(table["turned"]),
            part_spec(table["halo_rows"]),
        ],
        floats(ROWS, TP),
        scratch=(pltpu.VMEM((HALO, TP), F32), pltpu.SemaphoreType.DMA),
        name="edge_gradient",
        out_specs=hbm,
        aliases={1: 0},
    )


def solution(mesh):
    in_specs = (
        P(("tile", "cond"), None),
        P("tile", None),
        P("cond", None, None, None),
        P("cond", None, None, None),
        P(),
        P("cond"),
    )
    out_specs = P(("tile", "cond"), None)
    return jax.shard_map(shards, mesh=mesh, in_specs=in_specs, out_specs=out_specs, check_vma=False)
```

```python
import functools

import jax
import jax.numpy as jnp
import ml_dtypes
import numpy as np
from jax import lax
from jax.experimental import pallas as pl
from jax.experimental.pallas import tpu as pltpu
from jax.sharding import PartitionSpec as P

TP = 512
HALO = 32
KSUP = 65
HALF = KSUP // 2
KERNELS = 2
CONDS = 8
FULL = TP + 2 * HALO
PARTS = 4
ROWS = TP // PARTS
FA = 40
FB = 64
BF = jnp.bfloat16
F32 = jnp.float32

mask_steep = 2.0
resist_steep = 4.0
band_weight = 1.0


def waves(positions):
    angles = (np.outer(np.asarray(positions, np.int64), np.arange(HALF + 1)) % FULL) * (2.0 * np.pi / FULL)
    return np.cos(angles), np.sin(angles)


def halves(table):
    high = table.astype(np.float32).astype(ml_dtypes.bfloat16)
    low = (table - high.astype(np.float64)).astype(np.float32).astype(ml_dtypes.bfloat16)
    return high, low


def row_table(positions):
    cosine, sine = waves(positions)
    table = np.zeros((len(positions), 2 * FA))
    table[:, : HALF + 1] = cosine
    table[:, FA : FA + HALF + 1] = sine
    return table


def pair_table(positions):
    table = row_table(positions)
    return np.concatenate([table, np.concatenate([-table[:, FA:], table[:, :FA]], axis=1)])


def column_table(positions):
    cosine, sine = waves(positions)
    table = np.zeros((len(positions), 4 * FB))
    for block, values in enumerate((cosine, cosine, sine, -sine)):
        table[:, block * FB : block * FB + HALF] = values[:, 1:]
    table[:, HALF] = 1.0
    return table


@functools.cache
def tables():
    pixels = np.arange(TP) + HALO
    column = column_table(pixels)
    column_high, column_low = halves(column)
    turned = np.concatenate([column[:, : 2 * FB].T, column[:, 2 * FB :].T], axis=1)
    turned_high, turned_low = halves(turned)
    row = row_table(pixels)
    row_high, row_low = halves(row)
    out = {}
    out["column"] = np.stack([column_high, column_low])
    spectrum_rows = []
    rim_rows = []
    halo_rows = []
    own_rows = []
    forward = []
    backward = []
    for part in range(PARTS):
        own = np.arange(ROWS) + part * ROWS + HALO
        rim = np.arange(HALO) + (0 if part == PARTS - 1 else FULL - HALO)
        for rows, positions in ((spectrum_rows, own), (rim_rows, rim)):
            high, low = halves(row_table(positions).T)
            rows.append(np.concatenate([high, low, high], axis=1))
        high, low = halves(pair_table(rim))
        halo_rows.append(np.concatenate([high, low, high], axis=1))
        high, low = halves(pair_table(own))
        own_rows.append(np.concatenate([high, low, high], axis=1))
        cols = slice(part * ROWS, (part + 1) * ROWS)
        high = np.concatenate([turned_high[:, :TP][:, cols], turned_high[:, TP:][:, cols]], axis=1)
        low = np.concatenate([turned_low[:, :TP][:, cols], turned_low[:, TP:][:, cols]], axis=1)
        forward.append(np.concatenate([high, high, low]))
        backward.append(np.concatenate([column_high[cols], column_high[cols], column_low[cols]]))
    out["spectrum_rows"] = np.stack(spectrum_rows)
    out["own_rows"] = np.stack(own_rows)
    out["rim_rows"] = np.stack(rim_rows)
    out["halo_rows"] = np.stack(halo_rows)
    out["forward"] = np.stack(forward)
    out["backward"] = np.stack(backward)
    out["turned"] = np.stack([column_high.T, column_low.T])
    out["row"] = np.concatenate([row_high, row_low, row_high], axis=1)
    out["row_turned"] = np.concatenate([row_high.T, row_low.T])
    return out


def dot(left, right):
    return jnp.dot(left, right, preferred_element_type=F32)


def split(value):
    high = value.astype(BF)
    return high, (value - high.astype(F32)).astype(BF)


def spectrum_of(mask, column_ref, rows):
    high, low = split(mask)
    across = dot(high, column_ref[0]) + dot(low, column_ref[0]) + dot(high, column_ref[1])
    high, low = split(across)
    both = dot(rows, jnp.concatenate([high, high, low], axis=0))
    even = both[:FA, : 2 * FB] - both[FA:, 2 * FB :]
    odd = both[FA:, : 2 * FB] + both[:FA, 2 * FB :]
    return even, odd


def open_kernel(
    part_ref, theta_hbm, real_hbm, imag_hbm, thresholds_hbm, weights_hbm, forward_hbm, backward_hbm,
    out_ref, rim_ref, shares_ref, forward_ref, backward_ref, real_ref, imag_ref, thresholds_ref, weights_ref, stage, sems,
):
    part = part_ref[0]
    moves = [
        (real_hbm, real_ref),
        (imag_hbm, imag_ref),
        (thresholds_hbm, thresholds_ref),
        (weights_hbm, weights_ref),
        (theta_hbm.at[pl.ds(pl.multiple_of(jnp.where(part == 0, 0, ROWS - HALO), HALO), HALO)], rim_ref),
        (forward_hbm.at[part], forward_ref),
        (backward_hbm.at[part], backward_ref),
    ]
    copies = [pltpu.make_async_copy(source, target, sems.at[i]) for i, (source, target) in enumerate(moves)]
    for copy in copies:
        copy.start()
    local_conds = real_ref.shape[0]
    mats = local_conds * KERNELS * 2
    stage[...] = jnp.zeros_like(stage)
    for copy in copies[:4]:
        copy.wait()
    for cond in range(local_conds):
        for kern in range(KERNELS):
            for piece, ref in enumerate((real_ref, imag_ref)):
                stage[(cond * KERNELS + kern) * 2 + piece, :KSUP, :KSUP] = ref[cond, :, kern, :]
    rows = stage.shape[1]
    source = lax.broadcasted_iota(jnp.int32, (2 * FB, 4 * FB), 0)
    target = lax.broadcasted_iota(jnp.int32, (2 * FB, 4 * FB), 1)
    lane = target % FB
    block = target // FB
    plus = (block == 0) | (block == 3)
    freq = jnp.where(lane < HALF, lane + 1, 0)
    used = (lane < HALF) | ((lane == HALF) & (block % 2 == 0))
    pick = (used & (source == jnp.where(plus, HALF + freq, HALF - freq))).astype(F32).astype(BF)
    high, low = split(stage[...].reshape(mats * rows, 2 * FB))
    picked = [dot(piece, pick) for piece in (high, low)]
    source = lax.broadcasted_iota(jnp.int32, (FA, 2 * rows), 1) % rows
    target = lax.broadcasted_iota(jnp.int32, (FA, 2 * rows), 0)
    turn = ((source == HALF - target) & (target <= HALF)).astype(F32).astype(BF)
    lane = lax.broadcasted_iota(jnp.int32, (FA, 2 * FB), 1)
    row = lax.broadcasted_iota(jnp.int32, (FA, 2 * FB), 0)
    valid = (row <= HALF) & ((lane <= HALF) | ((row > 0) & (lane >= FB) & (lane < FB + HALF)))
    scale = 1.0 / (FULL * FULL)
    keep_top = jnp.where(valid, scale, 0.0)
    keep_bottom = jnp.where((row == 0) & (lane == HALF), 0.0, keep_top)
    first = lane % FB < HALF
    extra = jnp.zeros((FA, 2 * FB), F32)
    for kern in range(local_conds * KERNELS):
        arrays = [[], []]
        for piece in range(2):
            start = (kern * 2 + piece) * rows
            top = picked[0][start + HALF : start + HALF + FA, : 2 * FB] + picked[1][start + HALF : start + HALF + FA, : 2 * FB]
            pieces = jnp.concatenate([half[start : start + rows, 2 * FB :] for half in picked], axis=0)
            bottom = dot(turn, pieces.astype(BF)) * keep_bottom
            top = top * keep_top
            arrays[0].append(top + bottom)
            arrays[1].append(top - bottom)
        for which, (real, imag) in enumerate(arrays):
            packed = jnp.where(first, real, pltpu.roll(imag, HALF, 1))
            if which == 0:
                packed = jnp.where(row == FA - 1, thresholds_ref[kern // KERNELS], packed)
            out_ref[kern * 2 + which] = packed
            for piece, value in enumerate((real, imag)):
                place = kern * 4 + which * 2 + piece
                extra = jnp.where(lane == place, pltpu.roll(value, (place - HALF) % (2 * FB), 1), extra)
    out_ref[local_conds * KERNELS * 2] = extra
    weight_sum = weights_ref[0]
    for i in range(1, CONDS):
        weight_sum = weight_sum + weights_ref[i]
    row = lax.broadcasted_iota(jnp.int32, shares_ref.shape, 0)
    shares = jnp.zeros(shares_ref.shape, F32)
    for group, step in enumerate((0, 3, 1, 2)):
        for i in range(local_conds):
            weight = weights_ref[lax.bitwise_xor(part, step) * local_conds + i]
            shares = jnp.where(row == group * local_conds + i, weight.astype(F32), shares)
    shares_ref[...] = shares / weight_sum.astype(F32)
    for copy in copies[4:]:
        copy.wait()


def spectrum_kernel(part_ref, theta_ref, column_ref, rows_ref, out_ref):
    even, odd = spectrum_of(jnp.tanh(mask_steep * theta_ref[...]), column_ref, rows_ref[0])
    out_ref[0] = even
    out_ref[1] = odd


def rim_kernel(part_ref, spectrum_ref, rim_ref, column_ref, rows_ref, out_ref):
    mask = jnp.where(part_ref[1] > 0, jnp.tanh(mask_steep * rim_ref[...]), 0.0)
    even, odd = spectrum_of(mask, column_ref, rows_ref[0])
    out_ref[0] = even + spectrum_ref[0]
    out_ref[1] = odd + spectrum_ref[1]


def fields_kernel(
    part_ref, own_ref, side_ref, core_ref, cross_ref, shares_ref, target_ref, forward_ref, backward_ref, row_ref,
    row_turned_ref, out_ref, kernels_ref, lines, folded, amps, tanhs, total, signs, turned, backs,
):
    count = kernels_ref.shape[0]
    local = count // PARTS
    tall = 4 * FA
    even = side_ref[2 * local + 1] + cross_ref[2 * local + 1]
    odd = side_ref[2 * local + 2] + cross_ref[2 * local + 2]
    lane = lax.broadcasted_iota(jnp.int32, (FA, 2 * FB), 1)
    row = lax.broadcasted_iota(jnp.int32, (FA, 2 * FB), 0)
    zero_lane = (lane == HALF) & (row <= HALF)
    for group, ref in enumerate((own_ref, side_ref, core_ref, cross_ref)):
        extra = ref[2 * local]
        for kern in range(local):
            values = []
            for which in range(2):
                packed = ref[2 * kern + which]
                for part, value in enumerate((packed, pltpu.roll(packed, 2 * FB - HALF, 1))):
                    place = kern * 4 + which * 2 + part
                    zeroth = pltpu.roll(extra, (HALF - place) % (2 * FB), 1)
                    value = jnp.where(zero_lane, zeroth, value)
                    kernels_ref[group * local + kern, which * 2 + part] = value
                    values.append(value)
            he_real, he_imag, ho_real, ho_imag = values
            start = (group * local + kern) * tall
            for i, value in enumerate(
                (
                    even * he_real + odd * ho_imag,
                    odd * he_real - even * ho_imag,
                    even * he_imag - odd * ho_real,
                    odd * he_imag + even * ho_real,
                )
            ):
                lines[start + i * FA : start + (i + 1) * FA] = value

    high, low = split(lines[...])
    lines_folded = dot(jnp.concatenate([high, low], axis=1), forward_ref[: 4 * FB]) + dot(high, forward_ref[4 * FB :])
    for kern in range(count):
        parts = []
        for i in range(2):
            x_part = lines_folded[tall * kern + 2 * FA * i : tall * kern + 2 * FA * i + FA]
            y_part = lines_folded[tall * kern + 2 * FA * i + FA : tall * kern + 2 * FA * (i + 1)]
            parts.append(
                jnp.concatenate(
                    [x_part[:, :ROWS] + y_part[:, ROWS:], y_part[:, :ROWS] - x_part[:, ROWS:]], axis=0
                )
            )
        high, low = split(jnp.concatenate(parts, axis=1))
        folded[kern] = jnp.concatenate([high, high, low], axis=0)
    total[...] = jnp.zeros_like(total)
    signs[...] = 1.0 - 2.0 * target_ref[...].astype(F32)

    def expose(cond, carry):
        intensity = None
        for kern in range(KERNELS):
            index = cond * KERNELS + kern
            amp = dot(row_ref[...], folded[index])
            amps[index] = amp
            power = amp[:, :ROWS] * amp[:, :ROWS] + amp[:, ROWS:] * amp[:, ROWS:]
            intensity = power if intensity is None else intensity + power
        level = kernels_ref[cond * KERNELS, 0, FA - 1 :, :]
        value = jnp.tanh((0.5 * resist_steep) * (intensity - level))
        tanhs[cond] = value
        total[...] += value
        return carry

    lax.fori_loop(0, CONDS, expose, 0, unroll=4)
    total[...] = total[...] * (band_weight / (CONDS * CONDS))

    def drive(cond, carry):
        weight = shares_ref[pl.ds(cond, 1), :]
        value = tanhs[cond]
        slope = (weight + band_weight / CONDS) * value + weight * signs[...] - total[...]
        field = (0.5 * resist_steep) * (1.0 - value * value) * slope
        field = jnp.concatenate([field, field], axis=1)
        for kern in range(KERNELS):
            index = cond * KERNELS + kern
            high, low = split(field * amps[index])
            long = dot(row_turned_ref[...], high)
            back = long[: 2 * FA] + long[2 * FA :] + dot(row_turned_ref[: 2 * FA], low)
            turned[pl.ds(index * 2, 2)] = jnp.stack([back[:, :ROWS], back[:, ROWS:]])
        return carry

    lax.fori_loop(0, CONDS, drive, 0, unroll=4)
    high, low = split(turned[...].reshape(count * tall, ROWS))
    backs[...] = dot(jnp.concatenate([high, low], axis=1), backward_ref[: 2 * ROWS]) + dot(high, backward_ref[2 * ROWS :])

    sum_even = jnp.zeros((FA, 2 * FB), F32)
    sum_odd = jnp.zeros((FA, 2 * FB), F32)
    for kern in range(count):
        grads = []
        for i in range(2):
            c_part = backs[tall * kern + 2 * FA * i : tall * kern + 2 * FA * i + FA]
            s_part = backs[tall * kern + 2 * FA * i + FA : tall * kern + 2 * FA * (i + 1)]
            grads.append(
                (
                    c_part[:, : 2 * FB] - s_part[:, 2 * FB :],
                    s_part[:, : 2 * FB] + c_part[:, 2 * FB :],
                )
            )
        (x_real, y_real), (x_imag, y_imag) = grads
        he_real, he_imag, ho_real, ho_imag = (kernels_ref[kern, i] for i in range(4))
        sum_even = sum_even + x_real * he_real + x_imag * he_imag - y_real * ho_imag + y_imag * ho_real
        sum_odd = sum_odd + x_real * ho_imag - x_imag * ho_real + y_real * he_real + y_imag * he_imag
    out_ref[:FA] = sum_even
    out_ref[FA:] = sum_odd


def image_rows(value, rows, turned_ref):
    high, low = split(value)
    pair = dot(rows, jnp.concatenate([high, high, low], axis=0))
    count = pair.shape[0] // 2
    high, low = split(jnp.concatenate([pair[:count], pair[count:]], axis=1))
    return dot(high, turned_ref[0]) + dot(low, turned_ref[0]) + dot(high, turned_ref[1])


def edge_start(part_ref):
    return pl.multiple_of(jnp.where(part_ref[0] == PARTS - 1, ROWS - HALO, 0), HALO)


def gradient_kernel(part_ref, theta_ref, sum_ref, back_ref, turned_ref, rows_ref, out_ref, edge_ref, scale_ref):
    middle = (part_ref[0] == 1) | (part_ref[0] == 2)
    mask = jnp.tanh(mask_steep * theta_ref[...])
    scale = mask_steep * (1.0 - mask * mask)
    mine = jnp.where(middle, sum_ref[...], back_ref[...])
    gradient = image_rows(mine, rows_ref[0], turned_ref) * scale
    out_ref[...] = gradient
    last = part_ref[0] == PARTS - 1
    edge_ref[...] = jnp.where(last, gradient[ROWS - HALO :], gradient[:HALO])
    scale_ref[...] = jnp.where(last, scale[ROWS - HALO :], scale[:HALO])


def edge_kernel(part_ref, gradient_hbm, edge_ref, scale_ref, near_ref, turned_ref, rows_ref, out_hbm, stage, sem):
    rim = image_rows(near_ref[...], rows_ref[0], turned_ref) * scale_ref[...]
    stage[...] = edge_ref[...] + jnp.where(part_ref[2] > 0, rim, 0.0)
    copy = pltpu.make_async_copy(stage, out_hbm.at[pl.ds(edge_start(part_ref), HALO)], sem)
    copy.start()
    copy.wait()


def whole_spec(array):
    rank = len(array.shape)
    return pl.BlockSpec(array.shape, lambda i, *refs: (0,) * rank)


def part_spec(array):
    rank = len(array.shape)
    return pl.BlockSpec((1,) + array.shape[1:], lambda i, part, *refs: (part[0],) + (0,) * (rank - 1))


def call(kernel, scalars, operands, specs, out_shapes, scratch=(), name=None, flops=1 << 28, out_specs=None, aliases=None):
    many = isinstance(out_shapes, list)
    if out_specs is None:
        out_specs = [whole_spec(shape) for shape in out_shapes] if many else whole_spec(out_shapes)
    return pl.pallas_call(
        kernel,
        grid_spec=pltpu.PrefetchScalarGridSpec(
            num_scalar_prefetch=len(scalars),
            grid=(1,),
            in_specs=specs,
            out_specs=out_specs,
            scratch_shapes=list(scratch),
        ),
        out_shape=out_shapes,
        input_output_aliases=aliases or {},
        compiler_params=pltpu.CompilerParams(vmem_limit_bytes=48 * 1024 * 1024),
        cost_estimate=pl.CostEstimate(flops=flops, bytes_accessed=1 << 20, transcendentals=0),
        name=name,
    )(*scalars, *operands)


def floats(*shape):
    return jax.ShapeDtypeStruct(shape, F32)


def shards(theta, target, kernel_real, kernel_imag, weights, thresholds):
    table = {name: jnp.asarray(value) for name, value in tables().items()}
    tiles = lax.axis_size("tile")
    part = lax.axis_index("cond")
    tile = lax.axis_index("tile")
    last = PARTS - 1
    above = ((part == 0) & (tile > 0)) | ((part == last) & (tile < tiles - 1))
    below = ((part == 0) & (tile < tiles - 1)) | ((part == last) & (tile > 0))
    parts = jnp.stack([part, below, above]).astype(jnp.int32)
    local_conds = kernel_real.shape[0]
    local = local_conds * KERNELS
    count = CONDS * KERNELS
    hbm = pl.BlockSpec(memory_space=pltpu.HBM)

    def across(value, within, down, up):
        pairs = [(PARTS * i + a, PARTS * i + b) for i in range(tiles) for a, b in within]
        pairs += [(PARTS * (i + 1) + down[0], PARTS * i + down[1]) for i in range(tiles - 1)]
        pairs += [(PARTS * i + up[0], PARTS * (i + 1) + up[1]) for i in range(tiles - 1)]
        pairs += [(down[0], up[1]), (PARTS * (tiles - 1) + up[0], PARTS * (tiles - 1) + down[1])]
        return lax.ppermute(value, ("tile", "cond"), pairs)

    def partner(value, step):
        return lax.ppermute(value, "cond", [(i, i ^ step) for i in range(PARTS)])

    kernel_shape = (local_conds, KSUP, KERNELS, KSUP)
    own, rim, shares, forward, backward = call(
        open_kernel,
        (parts,),
        tuple(
            pltpu.with_memory_space_constraint(value, pltpu.HBM)
            for value in (
                theta, kernel_real.transpose(0, 2, 1, 3), kernel_imag.transpose(0, 2, 1, 3), thresholds, weights,
                table["forward"], table["backward"],
            )
        ),
        [hbm] * 7,
        [
            floats(2 * local + 1, FA, 2 * FB),
            floats(HALO, TP),
            floats(CONDS, ROWS),
            jax.ShapeDtypeStruct(table["forward"].shape[1:], BF),
            jax.ShapeDtypeStruct(table["backward"].shape[1:], BF),
        ],
        scratch=(
            pltpu.VMEM(kernel_shape, F32),
            pltpu.VMEM(kernel_shape, F32),
            pltpu.SMEM(thresholds.shape, F32),
            pltpu.SMEM(weights.shape, jnp.int32),
            pltpu.VMEM((2 * local, 72, 2 * FB), F32),
            pltpu.SemaphoreType.DMA((7,)),
        ),
        name="open_parts",
    )
    rim = across(rim, [(1, 1), (2, 2)], (0, 0), (last, last))
    spectrum = call(
        spectrum_kernel,
        (parts,),
        (theta, table["column"], table["spectrum_rows"]),
        [whole_spec(theta), whole_spec(table["column"]), part_spec(table["spectrum_rows"])],
        floats(2, FA, 2 * FB),
        name="own_spectrum",
        flops=1 << 31,
    )
    side = partner(own, 3)
    core = partner(own, 1)
    spectrum = call(
        rim_kernel,
        (parts,),
        (spectrum, rim, table["column"], table["rim_rows"]),
        [whole_spec(spectrum), whole_spec(rim), whole_spec(table["column"]), part_spec(table["rim_rows"])],
        floats(2, FA, 2 * FB),
        name="add_rim",
    )
    mixed = jnp.concatenate([side, spectrum + partner(spectrum, 3)], axis=0)
    adjoint = call(
        fields_kernel,
        (parts,),
        (own, mixed, core, partner(mixed, 1), shares, target, forward, backward, table["row"], table["row_turned"]),
        [
            whole_spec(own),
            whole_spec(mixed),
            whole_spec(core),
            whole_spec(mixed),
            whole_spec(shares),
            pl.BlockSpec((TP, ROWS), lambda i, part, *refs: (0, part[0])),
            whole_spec(forward),
            whole_spec(backward),
            whole_spec(table["row"]),
            whole_spec(table["row_turned"]),
        ],
        floats(2 * FA, 2 * FB),
        scratch=(
            pltpu.VMEM((count, 4, FA, 2 * FB), F32),
            pltpu.VMEM((count * 4 * FA, 2 * FB), F32),
            pltpu.VMEM((count, 6 * FA, 2 * ROWS), BF),
            pltpu.VMEM((count, TP, 2 * ROWS), F32),
            pltpu.VMEM((CONDS, TP, ROWS), F32),
            pltpu.VMEM((TP, ROWS), F32),
            pltpu.VMEM((TP, ROWS), F32),
            pltpu.VMEM((count * 2, 2 * FA, ROWS), F32),
            pltpu.VMEM((count * 4 * FA, 4 * FB), F32),
        ),
        name="coherent_fields",
        flops=1 << 33,
    )
    adjoint = adjoint + partner(adjoint, 1)
    adjoint = adjoint + lax.ppermute(adjoint, "cond", [(0, 0), (1, 2), (2, 1), (last, last)])
    near = across(adjoint, [(0, 1), (last, 2)], (2, last), (1, 0))
    back = partner(adjoint, 1)
    gradient, edge, scale = call(
        gradient_kernel,
        (parts,),
        (theta, adjoint, back, table["turned"], table["own_rows"]),
        [
            whole_spec(theta),
            whole_spec(adjoint),
            whole_spec(back),
            whole_spec(table["turned"]),
            part_spec(table["own_rows"]),
        ],
        [floats(ROWS, TP), floats(HALO, TP), floats(HALO, TP)],
        name="own_gradient",
        flops=1 << 31,
    )
    return call(
        edge_kernel,
        (parts,),
        (gradient, edge, scale, near, table["turned"], table["halo_rows"]),
        [
            hbm,
            whole_spec(edge),
            whole_spec(scale),
            whole_spec(near),
            whole_spec(table["turned"]),
            part_spec(table["halo_rows"]),
        ],
        floats(ROWS, TP),
        scratch=(pltpu.VMEM((HALO, TP), F32), pltpu.SemaphoreType.DMA),
        name="edge_gradient",
        out_specs=hbm,
        aliases={1: 0},
    )


def solution(mesh):
    in_specs = (
        P(("tile", "cond"), None),
        P("tile", None),
        P("cond", None, None, None),
        P("cond", None, None, None),
        P(),
        P("cond"),
    )
    out_specs = P(("tile", "cond"), None)
    return jax.shard_map(shards, mesh=mesh, in_specs=in_specs, out_specs=out_specs, check_vma=False)
```

```python
import functools

import jax
import jax.numpy as jnp
import ml_dtypes
import numpy as np
from jax import lax
from jax.experimental import pallas as pl
from jax.experimental.pallas import tpu as pltpu
from jax.sharding import PartitionSpec as P

TP = 512
HALO = 32
KSUP = 65
HALF = KSUP // 2
KERNELS = 2
CONDS = 8
FULL = TP + 2 * HALO
PARTS = 4
ROWS = TP // PARTS
FA = 40
FB = 64
BF = jnp.bfloat16
F32 = jnp.float32

mask_steep = 2.0
resist_steep = 4.0
band_weight = 1.0


def waves(positions):
    angles = (np.outer(np.asarray(positions, np.int64), np.arange(HALF + 1)) % FULL) * (2.0 * np.pi / FULL)
    return np.cos(angles), np.sin(angles)


def halves(table):
    high = table.astype(np.float32).astype(ml_dtypes.bfloat16)
    low = (table - high.astype(np.float64)).astype(np.float32).astype(ml_dtypes.bfloat16)
    return high, low


def row_table(positions):
    cosine, sine = waves(positions)
    table = np.zeros((len(positions), 2 * FA))
    table[:, : HALF + 1] = cosine
    table[:, FA : FA + HALF + 1] = sine
    return table


def pair_table(positions):
    table = row_table(positions)
    return np.concatenate([table, np.concatenate([-table[:, FA:], table[:, :FA]], axis=1)])


def column_table(positions):
    cosine, sine = waves(positions)
    table = np.zeros((len(positions), 4 * FB))
    for block, values in enumerate((cosine, cosine, sine, -sine)):
        table[:, block * FB : block * FB + HALF] = values[:, 1:]
    table[:, HALF] = 1.0
    return table


@functools.cache
def tables():
    pixels = np.arange(TP) + HALO
    column = column_table(pixels)
    column_high, column_low = halves(column)
    turned = np.concatenate([column[:, : 2 * FB].T, column[:, 2 * FB :].T], axis=1)
    turned_high, turned_low = halves(turned)
    row = row_table(pixels)
    row_high, row_low = halves(row)
    out = {}
    out["column"] = np.stack([column_high, column_low])
    spectrum_rows = []
    rim_rows = []
    halo_rows = []
    own_rows = []
    forward = []
    backward = []
    for part in range(PARTS):
        own = np.arange(ROWS) + part * ROWS + HALO
        rim = np.arange(HALO) + (0 if part == PARTS - 1 else FULL - HALO)
        for rows, positions in ((spectrum_rows, own), (rim_rows, rim)):
            high, low = halves(row_table(positions).T)
            rows.append(np.concatenate([high, low, high], axis=1))
        high, low = halves(pair_table(rim))
        halo_rows.append(np.concatenate([high, low, high], axis=1))
        high, low = halves(pair_table(own))
        own_rows.append(np.concatenate([high, low, high], axis=1))
        cols = slice(part * ROWS, (part + 1) * ROWS)
        high = np.concatenate([turned_high[:, :TP][:, cols], turned_high[:, TP:][:, cols]], axis=1)
        low = np.concatenate([turned_low[:, :TP][:, cols], turned_low[:, TP:][:, cols]], axis=1)
        forward.append(np.concatenate([high, high, low]))
        backward.append(np.concatenate([column_high[cols], column_high[cols], column_low[cols]]))
    out["spectrum_rows"] = np.stack(spectrum_rows)
    out["own_rows"] = np.stack(own_rows)
    out["rim_rows"] = np.stack(rim_rows)
    out["halo_rows"] = np.stack(halo_rows)
    out["forward"] = np.stack(forward)
    out["backward"] = np.stack(backward)
    out["turned"] = np.stack([column_high.T, column_low.T])
    out["row"] = np.concatenate([row_high, row_low, row_high], axis=1)
    out["row_turned"] = np.concatenate([row_high.T, row_low.T])
    return out


def part_of(ref):
    return ref[0] % PARTS


def has_mask_halo(ref):
    return ref[0] // PARTS % 2 > 0


def has_adjoint_halo(ref):
    return ref[0] // (2 * PARTS) > 0


def dot(left, right):
    return jnp.dot(left, right, preferred_element_type=F32)


def split(value):
    high = value.astype(BF)
    return high, (value - high.astype(F32)).astype(BF)


def spectrum_of(mask, column_ref, rows):
    high, low = split(mask)
    across = dot(high, column_ref[0]) + dot(low, column_ref[0]) + dot(high, column_ref[1])
    high, low = split(across)
    both = dot(rows, jnp.concatenate([high, high, low], axis=0))
    even = both[:FA, : 2 * FB] - both[FA:, 2 * FB :]
    odd = both[FA:, : 2 * FB] + both[:FA, 2 * FB :]
    return even, odd


def open_kernel(
    part_ref, theta_hbm, real_hbm, imag_hbm, thresholds_hbm, weights_hbm, forward_hbm, backward_hbm,
    out_ref, rim_ref, shares_ref, forward_ref, backward_ref, real_ref, imag_ref, thresholds_ref, weights_ref, stage, sems,
):
    part = part_of(part_ref)
    moves = [
        (real_hbm, real_ref),
        (imag_hbm, imag_ref),
        (thresholds_hbm, thresholds_ref),
        (weights_hbm, weights_ref),
        (theta_hbm.at[pl.ds(pl.multiple_of(jnp.where(part == 0, 0, ROWS - HALO), HALO), HALO)], rim_ref),
        (forward_hbm.at[part], forward_ref),
        (backward_hbm.at[part], backward_ref),
    ]
    copies = [pltpu.make_async_copy(source, target, sems.at[i]) for i, (source, target) in enumerate(moves)]
    for copy in copies:
        copy.start()
    local_conds = real_ref.shape[0]
    mats = local_conds * KERNELS * 2
    stage[...] = jnp.zeros_like(stage)
    for copy in copies[:4]:
        copy.wait()
    for cond in range(local_conds):
        for kern in range(KERNELS):
            for piece, ref in enumerate((real_ref, imag_ref)):
                stage[(cond * KERNELS + kern) * 2 + piece, :KSUP, :KSUP] = ref[cond, :, kern, :]
    rows = stage.shape[1]
    source = lax.broadcasted_iota(jnp.int32, (2 * FB, 4 * FB), 0)
    target = lax.broadcasted_iota(jnp.int32, (2 * FB, 4 * FB), 1)
    lane = target % FB
    block = target // FB
    plus = (block == 0) | (block == 3)
    freq = jnp.where(lane < HALF, lane + 1, 0)
    used = (lane < HALF) | ((lane == HALF) & (block % 2 == 0))
    pick = (used & (source == jnp.where(plus, HALF + freq, HALF - freq))).astype(F32).astype(BF)
    high, low = split(stage[...].reshape(mats * rows, 2 * FB))
    picked = [dot(piece, pick) for piece in (high, low)]
    source = lax.broadcasted_iota(jnp.int32, (FA, 2 * rows), 1) % rows
    target = lax.broadcasted_iota(jnp.int32, (FA, 2 * rows), 0)
    turn = ((source == HALF - target) & (target <= HALF)).astype(F32).astype(BF)
    lane = lax.broadcasted_iota(jnp.int32, (FA, 2 * FB), 1)
    row = lax.broadcasted_iota(jnp.int32, (FA, 2 * FB), 0)
    valid = (row <= HALF) & ((lane <= HALF) | ((row > 0) & (lane >= FB) & (lane < FB + HALF)))
    scale = 1.0 / (FULL * FULL)
    keep_top = jnp.where(valid, scale, 0.0)
    keep_bottom = jnp.where((row == 0) & (lane == HALF), 0.0, keep_top)
    first = lane % FB < HALF
    extra = jnp.zeros((FA, 2 * FB), F32)
    for kern in range(local_conds * KERNELS):
        arrays = [[], []]
        for piece in range(2):
            start = (kern * 2 + piece) * rows
            top = picked[0][start + HALF : start + HALF + FA, : 2 * FB] + picked[1][start + HALF : start + HALF + FA, : 2 * FB]
            pieces = jnp.concatenate([half[start : start + rows, 2 * FB :] for half in picked], axis=0)
            bottom = dot(turn, pieces.astype(BF)) * keep_bottom
            top = top * keep_top
            arrays[0].append(top + bottom)
            arrays[1].append(top - bottom)
        for which, (real, imag) in enumerate(arrays):
            packed = jnp.where(first, real, pltpu.roll(imag, HALF, 1))
            if which == 0:
                packed = jnp.where(row == FA - 1, thresholds_ref[kern // KERNELS], packed)
            out_ref[kern * 2 + which] = packed
            for piece, value in enumerate((real, imag)):
                place = kern * 4 + which * 2 + piece
                extra = jnp.where(lane == place, pltpu.roll(value, (place - HALF) % (2 * FB), 1), extra)
    out_ref[local_conds * KERNELS * 2] = extra
    weight_sum = weights_ref[0]
    for i in range(1, CONDS):
        weight_sum = weight_sum + weights_ref[i]
    row = lax.broadcasted_iota(jnp.int32, shares_ref.shape, 0)
    shares = jnp.zeros(shares_ref.shape, F32)
    for group, step in enumerate((0, 3, 1, 2)):
        for i in range(local_conds):
            weight = weights_ref[lax.bitwise_xor(part, step) * local_conds + i]
            shares = jnp.where(row == group * local_conds + i, weight.astype(F32), shares)
    shares_ref[...] = shares / weight_sum.astype(F32)
    for copy in copies[4:]:
        copy.wait()


def spectrum_kernel(part_ref, theta_ref, column_ref, rows_ref, out_ref):
    even, odd = spectrum_of(jnp.tanh(mask_steep * theta_ref[...]), column_ref, rows_ref[0])
    out_ref[0] = even
    out_ref[1] = odd


def rim_kernel(part_ref, spectrum_ref, rim_ref, column_ref, rows_ref, out_ref):
    mask = jnp.where(has_mask_halo(part_ref), jnp.tanh(mask_steep * rim_ref[...]), 0.0)
    even, odd = spectrum_of(mask, column_ref, rows_ref[0])
    out_ref[0] = even + spectrum_ref[0]
    out_ref[1] = odd + spectrum_ref[1]


def fields_kernel(
    part_ref, own_ref, side_ref, core_ref, cross_ref, shares_ref, target_ref, forward_ref, backward_ref, row_ref,
    row_turned_ref, out_ref, kernels_ref, lines, folded, amps, tanhs, total, signs, turned, backs,
):
    count = kernels_ref.shape[0]
    local = count // PARTS
    tall = 4 * FA
    even = side_ref[2 * local + 1] + cross_ref[2 * local + 1]
    odd = side_ref[2 * local + 2] + cross_ref[2 * local + 2]
    lane = lax.broadcasted_iota(jnp.int32, (FA, 2 * FB), 1)
    row = lax.broadcasted_iota(jnp.int32, (FA, 2 * FB), 0)
    zero_lane = (lane == HALF) & (row <= HALF)
    for group, ref in enumerate((own_ref, side_ref, core_ref, cross_ref)):
        extra = ref[2 * local]
        for kern in range(local):
            values = []
            for which in range(2):
                packed = ref[2 * kern + which]
                for part, value in enumerate((packed, pltpu.roll(packed, 2 * FB - HALF, 1))):
                    place = kern * 4 + which * 2 + part
                    zeroth = pltpu.roll(extra, (HALF - place) % (2 * FB), 1)
                    value = jnp.where(zero_lane, zeroth, value)
                    kernels_ref[group * local + kern, which * 2 + part] = value
                    values.append(value)
            he_real, he_imag, ho_real, ho_imag = values
            start = (group * local + kern) * tall
            for i, value in enumerate(
                (
                    even * he_real + odd * ho_imag,
                    odd * he_real - even * ho_imag,
                    even * he_imag - odd * ho_real,
                    odd * he_imag + even * ho_real,
                )
            ):
                lines[start + i * FA : start + (i + 1) * FA] = value

    high, low = split(lines[...])
    lines_folded = dot(jnp.concatenate([high, low], axis=1), forward_ref[: 4 * FB]) + dot(high, forward_ref[4 * FB :])
    for kern in range(count):
        parts = []
        for i in range(2):
            x_part = lines_folded[tall * kern + 2 * FA * i : tall * kern + 2 * FA * i + FA]
            y_part = lines_folded[tall * kern + 2 * FA * i + FA : tall * kern + 2 * FA * (i + 1)]
            parts.append(
                jnp.concatenate(
                    [x_part[:, :ROWS] + y_part[:, ROWS:], y_part[:, :ROWS] - x_part[:, ROWS:]], axis=0
                )
            )
        high, low = split(jnp.concatenate(parts, axis=1))
        folded[kern] = jnp.concatenate([high, high, low], axis=0)
    total[...] = jnp.zeros_like(total)
    signs[...] = 1.0 - 2.0 * target_ref[...].astype(F32)

    def expose(cond, carry):
        intensity = None
        for kern in range(KERNELS):
            index = cond * KERNELS + kern
            amp = dot(row_ref[...], folded[index])
            amps[index] = amp
            power = amp[:, :ROWS] * amp[:, :ROWS] + amp[:, ROWS:] * amp[:, ROWS:]
            intensity = power if intensity is None else intensity + power
        level = kernels_ref[cond * KERNELS, 0, FA - 1 :, :]
        value = jnp.tanh((0.5 * resist_steep) * (intensity - level))
        tanhs[cond] = value
        total[...] += value
        return carry

    lax.fori_loop(0, CONDS, expose, 0, unroll=4)
    total[...] = total[...] * (band_weight / (CONDS * CONDS))

    def drive(cond, carry):
        weight = shares_ref[pl.ds(cond, 1), :]
        value = tanhs[cond]
        slope = (weight + band_weight / CONDS) * value + weight * signs[...] - total[...]
        field = (0.5 * resist_steep) * (1.0 - value * value) * slope
        field = jnp.concatenate([field, field], axis=1)
        for kern in range(KERNELS):
            index = cond * KERNELS + kern
            high, low = split(field * amps[index])
            long = dot(row_turned_ref[...], high)
            back = long[: 2 * FA] + long[2 * FA :] + dot(row_turned_ref[: 2 * FA], low)
            turned[pl.ds(index * 2, 2)] = jnp.stack([back[:, :ROWS], back[:, ROWS:]])
        return carry

    lax.fori_loop(0, CONDS, drive, 0, unroll=4)
    high, low = split(turned[...].reshape(count * tall, ROWS))
    backs[...] = dot(jnp.concatenate([high, low], axis=1), backward_ref[: 2 * ROWS]) + dot(high, backward_ref[2 * ROWS :])

    sum_even = jnp.zeros((FA, 2 * FB), F32)
    sum_odd = jnp.zeros((FA, 2 * FB), F32)
    for kern in range(count):
        grads = []
        for i in range(2):
            c_part = backs[tall * kern + 2 * FA * i : tall * kern + 2 * FA * i + FA]
            s_part = backs[tall * kern + 2 * FA * i + FA : tall * kern + 2 * FA * (i + 1)]
            grads.append(
                (
                    c_part[:, : 2 * FB] - s_part[:, 2 * FB :],
                    s_part[:, : 2 * FB] + c_part[:, 2 * FB :],
                )
            )
        (x_real, y_real), (x_imag, y_imag) = grads
        he_real, he_imag, ho_real, ho_imag = (kernels_ref[kern, i] for i in range(4))
        sum_even = sum_even + x_real * he_real + x_imag * he_imag - y_real * ho_imag + y_imag * ho_real
        sum_odd = sum_odd + x_real * ho_imag - x_imag * ho_real + y_real * he_real + y_imag * he_imag
    out_ref[:FA] = sum_even
    out_ref[FA:] = sum_odd


def image_rows(value, rows, turned_ref):
    high, low = split(value)
    pair = dot(rows, jnp.concatenate([high, high, low], axis=0))
    count = pair.shape[0] // 2
    high, low = split(jnp.concatenate([pair[:count], pair[count:]], axis=1))
    return dot(high, turned_ref[0]) + dot(low, turned_ref[0]) + dot(high, turned_ref[1])


def edge_start(part_ref):
    return pl.multiple_of(jnp.where(part_of(part_ref) == PARTS - 1, ROWS - HALO, 0), HALO)


def gradient_kernel(part_ref, theta_ref, sum_ref, chip_ref, back_ref, turned_ref, rows_ref, out_ref, edge_ref, scale_ref):
    part = part_of(part_ref)
    middle = (part == 1) | (part == 2)
    mask = jnp.tanh(mask_steep * theta_ref[...])
    scale = mask_steep * (1.0 - mask * mask)
    mine = jnp.where(middle, sum_ref[...], chip_ref[...] + back_ref[...])
    gradient = image_rows(mine, rows_ref[0], turned_ref) * scale
    out_ref[...] = gradient
    last = part == PARTS - 1
    edge_ref[...] = jnp.where(last, gradient[ROWS - HALO :], gradient[:HALO])
    scale_ref[...] = jnp.where(last, scale[ROWS - HALO :], scale[:HALO])


def edge_kernel(part_ref, gradient_hbm, edge_ref, scale_ref, near_ref, turned_ref, rows_ref, out_hbm, stage, sem):
    rim = image_rows(near_ref[...], rows_ref[0], turned_ref) * scale_ref[...]
    stage[...] = edge_ref[...] + jnp.where(has_adjoint_halo(part_ref), rim, 0.0)
    copy = pltpu.make_async_copy(stage, out_hbm.at[pl.ds(edge_start(part_ref), HALO)], sem)
    copy.start()
    copy.wait()


def whole_spec(array):
    rank = len(array.shape)
    return pl.BlockSpec(array.shape, lambda i, *refs: (0,) * rank)


def part_spec(array):
    rank = len(array.shape)
    return pl.BlockSpec((1,) + array.shape[1:], lambda i, part, *refs: (part_of(part),) + (0,) * (rank - 1))


def call(kernel, scalars, operands, specs, out_shapes, scratch=(), name=None, flops=1 << 28, out_specs=None, aliases=None):
    many = isinstance(out_shapes, list)
    if out_specs is None:
        out_specs = [whole_spec(shape) for shape in out_shapes] if many else whole_spec(out_shapes)
    return pl.pallas_call(
        kernel,
        grid_spec=pltpu.PrefetchScalarGridSpec(
            num_scalar_prefetch=len(scalars),
            grid=(1,),
            in_specs=specs,
            out_specs=out_specs,
            scratch_shapes=list(scratch),
        ),
        out_shape=out_shapes,
        input_output_aliases=aliases or {},
        compiler_params=pltpu.CompilerParams(vmem_limit_bytes=48 * 1024 * 1024),
        cost_estimate=pl.CostEstimate(flops=flops, bytes_accessed=1 << 20, transcendentals=0),
        name=name,
    )(*scalars, *operands)


def floats(*shape):
    return jax.ShapeDtypeStruct(shape, F32)


def shards(theta, target, kernel_real, kernel_imag, weights, thresholds):
    table = {name: jnp.asarray(value) for name, value in tables().items()}
    tiles = lax.axis_size("tile")
    part = lax.axis_index("cond")
    tile = lax.axis_index("tile")
    last = PARTS - 1
    above = ((part == 0) & (tile > 0)) | ((part == last) & (tile < tiles - 1))
    below = ((part == 0) & (tile < tiles - 1)) | ((part == last) & (tile > 0))
    parts = (part + PARTS * below.astype(jnp.int32) + 2 * PARTS * above.astype(jnp.int32)).reshape(1).astype(jnp.int32)
    local_conds = kernel_real.shape[0]
    local = local_conds * KERNELS
    count = CONDS * KERNELS
    hbm = pl.BlockSpec(memory_space=pltpu.HBM)

    def across(value, within, down, up):
        pairs = [(PARTS * i + a, PARTS * i + b) for i in range(tiles) for a, b in within]
        pairs += [(PARTS * (i + 1) + down[0], PARTS * i + down[1]) for i in range(tiles - 1)]
        pairs += [(PARTS * i + up[0], PARTS * (i + 1) + up[1]) for i in range(tiles - 1)]
        pairs += [(down[0], up[1]), (PARTS * (tiles - 1) + up[0], PARTS * (tiles - 1) + down[1])]
        return lax.ppermute(value, ("tile", "cond"), pairs)

    def partner(value, step):
        return lax.ppermute(value, "cond", [(i, i ^ step) for i in range(PARTS)])

    kernel_shape = (local_conds, KSUP, KERNELS, KSUP)
    own, rim, shares, forward, backward = call(
        open_kernel,
        (parts,),
        tuple(
            pltpu.with_memory_space_constraint(value, pltpu.HBM)
            for value in (
                theta, kernel_real.transpose(0, 2, 1, 3), kernel_imag.transpose(0, 2, 1, 3), thresholds, weights,
                table["forward"], table["backward"],
            )
        ),
        [hbm] * 7,
        [
            floats(2 * local + 1, FA, 2 * FB),
            floats(HALO, TP),
            floats(CONDS, ROWS),
            jax.ShapeDtypeStruct(table["forward"].shape[1:], BF),
            jax.ShapeDtypeStruct(table["backward"].shape[1:], BF),
        ],
        scratch=(
            pltpu.VMEM(kernel_shape, F32),
            pltpu.VMEM(kernel_shape, F32),
            pltpu.SMEM(thresholds.shape, F32),
            pltpu.SMEM(weights.shape, jnp.int32),
            pltpu.VMEM((2 * local, 72, 2 * FB), F32),
            pltpu.SemaphoreType.DMA((7,)),
        ),
        name="open_parts",
    )
    rim = across(rim, [(1, 1), (2, 2)], (0, 0), (last, last))
    spectrum = call(
        spectrum_kernel,
        (parts,),
        (theta, table["column"], table["spectrum_rows"]),
        [whole_spec(theta), whole_spec(table["column"]), part_spec(table["spectrum_rows"])],
        floats(2, FA, 2 * FB),
        name="own_spectrum",
        flops=1 << 31,
    )
    side = partner(own, 3)
    core = partner(own, 1)
    spectrum = call(
        rim_kernel,
        (parts,),
        (spectrum, rim, table["column"], table["rim_rows"]),
        [whole_spec(spectrum), whole_spec(rim), whole_spec(table["column"]), part_spec(table["rim_rows"])],
        floats(2, FA, 2 * FB),
        name="add_rim",
    )
    mixed = jnp.concatenate([side, spectrum + partner(spectrum, 3)], axis=0)
    adjoint = call(
        fields_kernel,
        (parts,),
        (own, mixed, core, partner(mixed, 1), shares, target, forward, backward, table["row"], table["row_turned"]),
        [
            whole_spec(own),
            whole_spec(mixed),
            whole_spec(core),
            whole_spec(mixed),
            whole_spec(shares),
            pl.BlockSpec((TP, ROWS), lambda i, part, *refs: (0, part_of(part))),
            whole_spec(forward),
            whole_spec(backward),
            whole_spec(table["row"]),
            whole_spec(table["row_turned"]),
        ],
        floats(2 * FA, 2 * FB),
        scratch=(
            pltpu.VMEM((count, 4, FA, 2 * FB), F32),
            pltpu.VMEM((count * 4 * FA, 2 * FB), F32),
            pltpu.VMEM((count, 6 * FA, 2 * ROWS), BF),
            pltpu.VMEM((count, TP, 2 * ROWS), F32),
            pltpu.VMEM((CONDS, TP, ROWS), F32),
            pltpu.VMEM((TP, ROWS), F32),
            pltpu.VMEM((TP, ROWS), F32),
            pltpu.VMEM((count * 2, 2 * FA, ROWS), F32),
            pltpu.VMEM((count * 4 * FA, 4 * FB), F32),
        ),
        name="coherent_fields",
        flops=1 << 33,
    )
    chip = adjoint + partner(adjoint, 1)
    adjoint = chip + lax.ppermute(chip, "cond", [(0, 0), (1, 2), (2, 1), (last, last)])
    back = lax.ppermute(chip, "cond", [(0, last), (1, 1), (2, 2), (last, 0)])
    near = across(adjoint, [(0, 1), (last, 2)], (2, last), (1, 0))
    gradient, edge, scale = call(
        gradient_kernel,
        (parts,),
        (theta, adjoint, chip, back, table["turned"], table["own_rows"]),
        [
            whole_spec(theta),
            whole_spec(adjoint),
            whole_spec(chip),
            whole_spec(back),
            whole_spec(table["turned"]),
            part_spec(table["own_rows"]),
        ],
        [floats(ROWS, TP), floats(HALO, TP), floats(HALO, TP)],
        name="own_gradient",
        flops=1 << 31,
    )
    return call(
        edge_kernel,
        (parts,),
        (gradient, edge, scale, near, table["turned"], table["halo_rows"]),
        [
            hbm,
            whole_spec(edge),
            whole_spec(scale),
            whole_spec(near),
            whole_spec(table["turned"]),
            part_spec(table["halo_rows"]),
        ],
        floats(ROWS, TP),
        scratch=(pltpu.VMEM((HALO, TP), F32), pltpu.SemaphoreType.DMA),
        name="edge_gradient",
        out_specs=hbm,
        aliases={1: 0},
    )


def solution(mesh):
    in_specs = (
        P(("tile", "cond"), None),
        P("tile", None),
        P("cond", None, None, None),
        P("cond", None, None, None),
        P(),
        P("cond"),
    )
    out_specs = P(("tile", "cond"), None)
    return jax.shard_map(shards, mesh=mesh, in_specs=in_specs, out_specs=out_specs, check_vma=False)
```

```python
import functools

import jax
import jax.numpy as jnp
import ml_dtypes
import numpy as np
from jax import lax
from jax.experimental import pallas as pl
from jax.experimental.pallas import tpu as pltpu
from jax.sharding import PartitionSpec as P

TP = 512
HALO = 32
KSUP = 65
HALF = KSUP // 2
KERNELS = 2
CONDS = 8
FULL = TP + 2 * HALO
PARTS = 4
ROWS = TP // PARTS
FA = 40
FB = 64
BF = jnp.bfloat16
F32 = jnp.float32

mask_steep = 2.0
resist_steep = 4.0
band_weight = 1.0


def waves(positions):
    angles = (np.outer(np.asarray(positions, np.int64), np.arange(HALF + 1)) % FULL) * (2.0 * np.pi / FULL)
    return np.cos(angles), np.sin(angles)


def halves(table):
    high = table.astype(np.float32).astype(ml_dtypes.bfloat16)
    low = (table - high.astype(np.float64)).astype(np.float32).astype(ml_dtypes.bfloat16)
    return high, low


def row_table(positions):
    cosine, sine = waves(positions)
    table = np.zeros((len(positions), 2 * FA))
    table[:, : HALF + 1] = cosine
    table[:, FA : FA + HALF + 1] = sine
    return table


def pair_table(positions):
    table = row_table(positions)
    return np.concatenate([table, np.concatenate([-table[:, FA:], table[:, :FA]], axis=1)])


def column_table(positions):
    cosine, sine = waves(positions)
    table = np.zeros((len(positions), 4 * FB))
    for block, values in enumerate((cosine, cosine, sine, -sine)):
        table[:, block * FB : block * FB + HALF] = values[:, 1:]
    table[:, HALF] = 1.0
    return table


@functools.cache
def tables():
    pixels = np.arange(TP) + HALO
    column = column_table(pixels)
    column_high, column_low = halves(column)
    turned = np.concatenate([column[:, : 2 * FB].T, column[:, 2 * FB :].T], axis=1)
    turned_high, turned_low = halves(turned)
    row = row_table(pixels)
    row_high, row_low = halves(row)
    out = {}
    out["column"] = np.stack([column_high, column_low])
    spectrum_rows = []
    rim_rows = []
    halo_rows = []
    own_rows = []
    forward = []
    backward = []
    for part in range(PARTS):
        own = np.arange(ROWS) + part * ROWS + HALO
        rim = np.arange(HALO) + (0 if part == PARTS - 1 else FULL - HALO)
        for rows, positions in ((spectrum_rows, own), (rim_rows, rim)):
            high, low = halves(row_table(positions).T)
            rows.append(np.concatenate([high, low, high], axis=1))
        high, low = halves(pair_table(rim))
        halo_rows.append(np.concatenate([high, low, high], axis=1))
        high, low = halves(pair_table(own))
        own_rows.append(np.concatenate([high, low, high], axis=1))
        cols = slice(part * ROWS, (part + 1) * ROWS)
        high = np.concatenate([turned_high[:, :TP][:, cols], turned_high[:, TP:][:, cols]], axis=1)
        low = np.concatenate([turned_low[:, :TP][:, cols], turned_low[:, TP:][:, cols]], axis=1)
        forward.append(np.concatenate([high, high, low]))
        backward.append(np.concatenate([column_high[cols], column_high[cols], column_low[cols]]))
    out["spectrum_rows"] = np.stack(spectrum_rows)
    out["own_rows"] = np.stack(own_rows)
    out["rim_rows"] = np.stack(rim_rows)
    out["halo_rows"] = np.stack(halo_rows)
    out["forward"] = np.stack(forward)
    out["backward"] = np.stack(backward)
    out["turned"] = np.stack([column_high.T, column_low.T])
    out["row"] = np.concatenate([row_high, row_low, row_high], axis=1)
    out["row_turned"] = np.concatenate([row_high.T, row_low.T])
    return out


def part_of(ref):
    return ref[0] % PARTS


def has_mask_halo(ref):
    return ref[0] // PARTS % 2 > 0


def has_adjoint_halo(ref):
    return ref[0] // (2 * PARTS) > 0


def dot(left, right):
    return jnp.dot(left, right, preferred_element_type=F32)


def split(value):
    high = value.astype(BF)
    return high, (value - high.astype(F32)).astype(BF)


def spectrum_of(mask, column_ref, rows):
    high, low = split(mask)
    across = dot(high, column_ref[0]) + dot(low, column_ref[0]) + dot(high, column_ref[1])
    high, low = split(across)
    both = dot(rows, jnp.concatenate([high, high, low], axis=0))
    even = both[:FA, : 2 * FB] - both[FA:, 2 * FB :]
    odd = both[FA:, : 2 * FB] + both[:FA, 2 * FB :]
    return even, odd


def open_kernel(
    part_ref, real_hbm, imag_hbm, thresholds_hbm, weights_hbm, forward_hbm, backward_hbm,
    out_ref, shares_ref, forward_ref, backward_ref, real_ref, imag_ref, thresholds_ref, weights_ref, stage, sems,
):
    part = part_of(part_ref)
    moves = [
        (real_hbm, real_ref),
        (imag_hbm, imag_ref),
        (thresholds_hbm, thresholds_ref),
        (weights_hbm, weights_ref),
        (forward_hbm.at[part], forward_ref),
        (backward_hbm.at[part], backward_ref),
    ]
    copies = [pltpu.make_async_copy(source, target, sems.at[i]) for i, (source, target) in enumerate(moves)]
    for copy in copies:
        copy.start()
    local_conds = real_ref.shape[0]
    mats = local_conds * KERNELS * 2
    stage[...] = jnp.zeros_like(stage)
    for copy in copies[:4]:
        copy.wait()
    for cond in range(local_conds):
        for kern in range(KERNELS):
            for piece, ref in enumerate((real_ref, imag_ref)):
                stage[(cond * KERNELS + kern) * 2 + piece, :KSUP, :KSUP] = ref[cond, :, kern, :]
    rows = stage.shape[1]
    source = lax.broadcasted_iota(jnp.int32, (2 * FB, 4 * FB), 0)
    target = lax.broadcasted_iota(jnp.int32, (2 * FB, 4 * FB), 1)
    lane = target % FB
    block = target // FB
    plus = (block == 0) | (block == 3)
    freq = jnp.where(lane < HALF, lane + 1, 0)
    used = (lane < HALF) | ((lane == HALF) & (block % 2 == 0))
    pick = (used & (source == jnp.where(plus, HALF + freq, HALF - freq))).astype(F32).astype(BF)
    high, low = split(stage[...].reshape(mats * rows, 2 * FB))
    picked = [dot(piece, pick) for piece in (high, low)]
    source = lax.broadcasted_iota(jnp.int32, (FA, 2 * rows), 1) % rows
    target = lax.broadcasted_iota(jnp.int32, (FA, 2 * rows), 0)
    turn = ((source == HALF - target) & (target <= HALF)).astype(F32).astype(BF)
    lane = lax.broadcasted_iota(jnp.int32, (FA, 2 * FB), 1)
    row = lax.broadcasted_iota(jnp.int32, (FA, 2 * FB), 0)
    valid = (row <= HALF) & ((lane <= HALF) | ((row > 0) & (lane >= FB) & (lane < FB + HALF)))
    scale = 1.0 / (FULL * FULL)
    keep_top = jnp.where(valid, scale, 0.0)
    keep_bottom = jnp.where((row == 0) & (lane == HALF), 0.0, keep_top)
    first = lane % FB < HALF
    extra = jnp.zeros((FA, 2 * FB), F32)
    for kern in range(local_conds * KERNELS):
        arrays = [[], []]
        for piece in range(2):
            start = (kern * 2 + piece) * rows
            top = picked[0][start + HALF : start + HALF + FA, : 2 * FB] + picked[1][start + HALF : start + HALF + FA, : 2 * FB]
            pieces = jnp.concatenate([half[start : start + rows, 2 * FB :] for half in picked], axis=0)
            bottom = dot(turn, pieces.astype(BF)) * keep_bottom
            top = top * keep_top
            arrays[0].append(top + bottom)
            arrays[1].append(top - bottom)
        for which, (real, imag) in enumerate(arrays):
            packed = jnp.where(first, real, pltpu.roll(imag, HALF, 1))
            if which == 0:
                packed = jnp.where(row == FA - 1, thresholds_ref[kern // KERNELS], packed)
            out_ref[kern * 2 + which] = packed
            for piece, value in enumerate((real, imag)):
                place = kern * 4 + which * 2 + piece
                extra = jnp.where(lane == place, pltpu.roll(value, (place - HALF) % (2 * FB), 1), extra)
    out_ref[local_conds * KERNELS * 2] = extra
    weight_sum = weights_ref[0]
    for i in range(1, CONDS):
        weight_sum = weight_sum + weights_ref[i]
    row = lax.broadcasted_iota(jnp.int32, shares_ref.shape, 0)
    shares = jnp.zeros(shares_ref.shape, F32)
    for group, step in enumerate((0, 3, 1, 2)):
        for i in range(local_conds):
            weight = weights_ref[lax.bitwise_xor(part, step) * local_conds + i]
            shares = jnp.where(row == group * local_conds + i, weight.astype(F32), shares)
    shares_ref[...] = shares / weight_sum.astype(F32)
    for copy in copies[4:]:
        copy.wait()


def spectrum_kernel(part_ref, theta_ref, column_ref, rows_ref, out_ref):
    even, odd = spectrum_of(jnp.tanh(mask_steep * theta_ref[...]), column_ref, rows_ref[0])
    out_ref[0] = even
    out_ref[1] = odd


def rim_kernel(part_ref, spectrum_ref, rim_ref, column_ref, rows_ref, out_ref):
    mask = jnp.where(has_mask_halo(part_ref), jnp.tanh(mask_steep * rim_ref[...]), 0.0)
    even, odd = spectrum_of(mask, column_ref, rows_ref[0])
    out_ref[0] = even + spectrum_ref[0]
    out_ref[1] = odd + spectrum_ref[1]


def fields_kernel(
    part_ref, own_ref, side_ref, core_ref, cross_ref, shares_ref, target_ref, forward_ref, backward_ref, row_ref,
    row_turned_ref, out_ref, kernels_ref, lines, folded, amps, tanhs, total, signs, turned, backs,
):
    count = kernels_ref.shape[0]
    local = count // PARTS
    tall = 4 * FA
    even = side_ref[2 * local + 1] + cross_ref[2 * local + 1]
    odd = side_ref[2 * local + 2] + cross_ref[2 * local + 2]
    lane = lax.broadcasted_iota(jnp.int32, (FA, 2 * FB), 1)
    row = lax.broadcasted_iota(jnp.int32, (FA, 2 * FB), 0)
    zero_lane = (lane == HALF) & (row <= HALF)
    for group, ref in enumerate((own_ref, side_ref, core_ref, cross_ref)):
        extra = ref[2 * local]
        for kern in range(local):
            values = []
            for which in range(2):
                packed = ref[2 * kern + which]
                for part, value in enumerate((packed, pltpu.roll(packed, 2 * FB - HALF, 1))):
                    place = kern * 4 + which * 2 + part
                    zeroth = pltpu.roll(extra, (HALF - place) % (2 * FB), 1)
                    value = jnp.where(zero_lane, zeroth, value)
                    kernels_ref[group * local + kern, which * 2 + part] = value
                    values.append(value)
            he_real, he_imag, ho_real, ho_imag = values
            start = (group * local + kern) * tall
            for i, value in enumerate(
                (
                    even * he_real + odd * ho_imag,
                    odd * he_real - even * ho_imag,
                    even * he_imag - odd * ho_real,
                    odd * he_imag + even * ho_real,
                )
            ):
                lines[start + i * FA : start + (i + 1) * FA] = value

    high, low = split(lines[...])
    lines_folded = dot(jnp.concatenate([high, low], axis=1), forward_ref[: 4 * FB]) + dot(high, forward_ref[4 * FB :])
    for kern in range(count):
        parts = []
        for i in range(2):
            x_part = lines_folded[tall * kern + 2 * FA * i : tall * kern + 2 * FA * i + FA]
            y_part = lines_folded[tall * kern + 2 * FA * i + FA : tall * kern + 2 * FA * (i + 1)]
            parts.append(
                jnp.concatenate(
                    [x_part[:, :ROWS] + y_part[:, ROWS:], y_part[:, :ROWS] - x_part[:, ROWS:]], axis=0
                )
            )
        high, low = split(jnp.concatenate(parts, axis=1))
        folded[kern] = jnp.concatenate([high, high, low], axis=0)
    total[...] = jnp.zeros_like(total)
    signs[...] = 1.0 - 2.0 * target_ref[...].astype(F32)

    def expose(cond, carry):
        intensity = None
        for kern in range(KERNELS):
            index = cond * KERNELS + kern
            amp = dot(row_ref[...], folded[index])
            amps[index] = amp
            power = amp[:, :ROWS] * amp[:, :ROWS] + amp[:, ROWS:] * amp[:, ROWS:]
            intensity = power if intensity is None else intensity + power
        level = kernels_ref[cond * KERNELS, 0, FA - 1 :, :]
        value = jnp.tanh((0.5 * resist_steep) * (intensity - level))
        tanhs[cond] = value
        total[...] += value
        return carry

    lax.fori_loop(0, CONDS, expose, 0, unroll=4)
    total[...] = total[...] * (band_weight / (CONDS * CONDS))

    def drive(cond, carry):
        weight = shares_ref[pl.ds(cond, 1), :]
        value = tanhs[cond]
        slope = (weight + band_weight / CONDS) * value + weight * signs[...] - total[...]
        field = (0.5 * resist_steep) * (1.0 - value * value) * slope
        field = jnp.concatenate([field, field], axis=1)
        for kern in range(KERNELS):
            index = cond * KERNELS + kern
            high, low = split(field * amps[index])
            long = dot(row_turned_ref[...], high)
            back = long[: 2 * FA] + long[2 * FA :] + dot(row_turned_ref[: 2 * FA], low)
            turned[pl.ds(index * 2, 2)] = jnp.stack([back[:, :ROWS], back[:, ROWS:]])
        return carry

    lax.fori_loop(0, CONDS, drive, 0, unroll=4)
    high, low = split(turned[...].reshape(count * tall, ROWS))
    backs[...] = dot(jnp.concatenate([high, low], axis=1), backward_ref[: 2 * ROWS]) + dot(high, backward_ref[2 * ROWS :])

    sum_even = jnp.zeros((FA, 2 * FB), F32)
    sum_odd = jnp.zeros((FA, 2 * FB), F32)
    for kern in range(count):
        grads = []
        for i in range(2):
            c_part = backs[tall * kern + 2 * FA * i : tall * kern + 2 * FA * i + FA]
            s_part = backs[tall * kern + 2 * FA * i + FA : tall * kern + 2 * FA * (i + 1)]
            grads.append(
                (
                    c_part[:, : 2 * FB] - s_part[:, 2 * FB :],
                    s_part[:, : 2 * FB] + c_part[:, 2 * FB :],
                )
            )
        (x_real, y_real), (x_imag, y_imag) = grads
        he_real, he_imag, ho_real, ho_imag = (kernels_ref[kern, i] for i in range(4))
        sum_even = sum_even + x_real * he_real + x_imag * he_imag - y_real * ho_imag + y_imag * ho_real
        sum_odd = sum_odd + x_real * ho_imag - x_imag * ho_real + y_real * he_real + y_imag * he_imag
    out_ref[:FA] = sum_even
    out_ref[FA:] = sum_odd


def image_rows(value, rows, turned_ref):
    high, low = split(value)
    pair = dot(rows, jnp.concatenate([high, high, low], axis=0))
    count = pair.shape[0] // 2
    high, low = split(jnp.concatenate([pair[:count], pair[count:]], axis=1))
    return dot(high, turned_ref[0]) + dot(low, turned_ref[0]) + dot(high, turned_ref[1])


def edge_start(part_ref):
    return pl.multiple_of(jnp.where(part_of(part_ref) == PARTS - 1, ROWS - HALO, 0), HALO)


def gradient_kernel(part_ref, theta_ref, sum_ref, chip_ref, back_ref, turned_ref, rows_ref, out_ref, edge_ref, scale_ref):
    part = part_of(part_ref)
    middle = (part == 1) | (part == 2)
    mask = jnp.tanh(mask_steep * theta_ref[...])
    scale = mask_steep * (1.0 - mask * mask)
    mine = jnp.where(middle, sum_ref[...], chip_ref[...] + back_ref[...])
    gradient = image_rows(mine, rows_ref[0], turned_ref) * scale
    out_ref[...] = gradient
    last = part == PARTS - 1
    edge_ref[...] = jnp.where(last, gradient[ROWS - HALO :], gradient[:HALO])
    scale_ref[...] = jnp.where(last, scale[ROWS - HALO :], scale[:HALO])


def edge_kernel(part_ref, gradient_hbm, edge_ref, scale_ref, near_ref, turned_ref, rows_ref, out_hbm, stage, sem):
    rim = image_rows(near_ref[...], rows_ref[0], turned_ref) * scale_ref[...]
    stage[...] = edge_ref[...] + jnp.where(has_adjoint_halo(part_ref), rim, 0.0)
    copy = pltpu.make_async_copy(stage, out_hbm.at[pl.ds(edge_start(part_ref), HALO)], sem)
    copy.start()
    copy.wait()


def whole_spec(array):
    rank = len(array.shape)
    return pl.BlockSpec(array.shape, lambda i, *refs: (0,) * rank)


def part_spec(array):
    rank = len(array.shape)
    return pl.BlockSpec((1,) + array.shape[1:], lambda i, part, *refs: (part_of(part),) + (0,) * (rank - 1))


def call(kernel, scalars, operands, specs, out_shapes, scratch=(), name=None, flops=1 << 28, out_specs=None, aliases=None):
    many = isinstance(out_shapes, list)
    if out_specs is None:
        out_specs = [whole_spec(shape) for shape in out_shapes] if many else whole_spec(out_shapes)
    return pl.pallas_call(
        kernel,
        grid_spec=pltpu.PrefetchScalarGridSpec(
            num_scalar_prefetch=len(scalars),
            grid=(1,),
            in_specs=specs,
            out_specs=out_specs,
            scratch_shapes=list(scratch),
        ),
        out_shape=out_shapes,
        input_output_aliases=aliases or {},
        compiler_params=pltpu.CompilerParams(vmem_limit_bytes=48 * 1024 * 1024),
        cost_estimate=pl.CostEstimate(flops=flops, bytes_accessed=1 << 20, transcendentals=0),
        name=name,
    )(*scalars, *operands)


def floats(*shape):
    return jax.ShapeDtypeStruct(shape, F32)


def shards(theta, target, kernel_real, kernel_imag, weights, thresholds):
    table = {name: jnp.asarray(value) for name, value in tables().items()}
    tiles = lax.axis_size("tile")
    part = lax.axis_index("cond")
    tile = lax.axis_index("tile")
    last = PARTS - 1
    above = ((part == 0) & (tile > 0)) | ((part == last) & (tile < tiles - 1))
    below = ((part == 0) & (tile < tiles - 1)) | ((part == last) & (tile > 0))
    parts = (part + PARTS * below.astype(jnp.int32) + 2 * PARTS * above.astype(jnp.int32)).reshape(1).astype(jnp.int32)
    local_conds = kernel_real.shape[0]
    local = local_conds * KERNELS
    count = CONDS * KERNELS
    hbm = pl.BlockSpec(memory_space=pltpu.HBM)

    def across(value, within, down, up):
        pairs = [(PARTS * i + a, PARTS * i + b) for i in range(tiles) for a, b in within]
        pairs += [(PARTS * (i + 1) + down[0], PARTS * i + down[1]) for i in range(tiles - 1)]
        pairs += [(PARTS * i + up[0], PARTS * (i + 1) + up[1]) for i in range(tiles - 1)]
        pairs += [(down[0], up[1]), (PARTS * (tiles - 1) + up[0], PARTS * (tiles - 1) + down[1])]
        return lax.ppermute(value, ("tile", "cond"), pairs)

    def partner(value, step):
        return lax.ppermute(value, "cond", [(i, i ^ step) for i in range(PARTS)])

    kernel_shape = (local_conds, KSUP, KERNELS, KSUP)
    own, shares, forward, backward = call(
        open_kernel,
        (parts,),
        tuple(
            pltpu.with_memory_space_constraint(value, pltpu.HBM)
            for value in (
                kernel_real.transpose(0, 2, 1, 3), kernel_imag.transpose(0, 2, 1, 3), thresholds, weights,
                table["forward"], table["backward"],
            )
        ),
        [hbm] * 6,
        [
            floats(2 * local + 1, FA, 2 * FB),
            floats(CONDS, ROWS),
            jax.ShapeDtypeStruct(table["forward"].shape[1:], BF),
            jax.ShapeDtypeStruct(table["backward"].shape[1:], BF),
        ],
        scratch=(
            pltpu.VMEM(kernel_shape, F32),
            pltpu.VMEM(kernel_shape, F32),
            pltpu.SMEM(thresholds.shape, F32),
            pltpu.SMEM(weights.shape, jnp.int32),
            pltpu.VMEM((2 * local, 72, 2 * FB), F32),
            pltpu.SemaphoreType.DMA((6,)),
        ),
        name="open_parts",
    )
    rim = lax.dynamic_slice_in_dim(theta, jnp.where(part == 0, 0, ROWS - HALO), HALO, axis=0)
    rim = across(rim, [(1, 1), (2, 2)], (0, 0), (last, last))
    spectrum = call(
        spectrum_kernel,
        (parts,),
        (theta, table["column"], table["spectrum_rows"]),
        [whole_spec(theta), whole_spec(table["column"]), part_spec(table["spectrum_rows"])],
        floats(2, FA, 2 * FB),
        name="own_spectrum",
        flops=1 << 31,
    )
    side = partner(own, 3)
    core = partner(own, 1)
    spectrum = call(
        rim_kernel,
        (parts,),
        (spectrum, rim, table["column"], table["rim_rows"]),
        [whole_spec(spectrum), whole_spec(rim), whole_spec(table["column"]), part_spec(table["rim_rows"])],
        floats(2, FA, 2 * FB),
        name="add_rim",
    )
    mixed = jnp.concatenate([side, spectrum + partner(spectrum, 3)], axis=0)
    adjoint = call(
        fields_kernel,
        (parts,),
        (own, mixed, core, partner(mixed, 1), shares, target, forward, backward, table["row"], table["row_turned"]),
        [
            whole_spec(own),
            whole_spec(mixed),
            whole_spec(core),
            whole_spec(mixed),
            whole_spec(shares),
            pl.BlockSpec((TP, ROWS), lambda i, part, *refs: (0, part_of(part))),
            whole_spec(forward),
            whole_spec(backward),
            whole_spec(table["row"]),
            whole_spec(table["row_turned"]),
        ],
        floats(2 * FA, 2 * FB),
        scratch=(
            pltpu.VMEM((count, 4, FA, 2 * FB), F32),
            pltpu.VMEM((count * 4 * FA, 2 * FB), F32),
            pltpu.VMEM((count, 6 * FA, 2 * ROWS), BF),
            pltpu.VMEM((count, TP, 2 * ROWS), F32),
            pltpu.VMEM((CONDS, TP, ROWS), F32),
            pltpu.VMEM((TP, ROWS), F32),
            pltpu.VMEM((TP, ROWS), F32),
            pltpu.VMEM((count * 2, 2 * FA, ROWS), F32),
            pltpu.VMEM((count * 4 * FA, 4 * FB), F32),
        ),
        name="coherent_fields",
        flops=1 << 33,
    )
    chip = adjoint + partner(adjoint, 1)
    adjoint = chip + lax.ppermute(chip, "cond", [(0, 0), (1, 2), (2, 1), (last, last)])
    back = lax.ppermute(chip, "cond", [(0, last), (1, 1), (2, 2), (last, 0)])
    near = across(adjoint, [(0, 1), (last, 2)], (2, last), (1, 0))
    gradient, edge, scale = call(
        gradient_kernel,
        (parts,),
        (theta, adjoint, chip, back, table["turned"], table["own_rows"]),
        [
            whole_spec(theta),
            whole_spec(adjoint),
            whole_spec(chip),
            whole_spec(back),
            whole_spec(table["turned"]),
            part_spec(table["own_rows"]),
        ],
        [floats(ROWS, TP), floats(HALO, TP), floats(HALO, TP)],
        name="own_gradient",
        flops=1 << 31,
    )
    return call(
        edge_kernel,
        (parts,),
        (gradient, edge, scale, near, table["turned"], table["halo_rows"]),
        [
            hbm,
            whole_spec(edge),
            whole_spec(scale),
            whole_spec(near),
            whole_spec(table["turned"]),
            part_spec(table["halo_rows"]),
        ],
        floats(ROWS, TP),
        scratch=(pltpu.VMEM((HALO, TP), F32), pltpu.SemaphoreType.DMA),
        name="edge_gradient",
        out_specs=hbm,
        aliases={1: 0},
    )


def solution(mesh):
    in_specs = (
        P(("tile", "cond"), None),
        P("tile", None),
        P("cond", None, None, None),
        P("cond", None, None, None),
        P(),
        P("cond"),
    )
    out_specs = P(("tile", "cond"), None)
    return jax.shard_map(shards, mesh=mesh, in_specs=in_specs, out_specs=out_specs, check_vma=False)
```

```python
import functools

import jax
import jax.numpy as jnp
import ml_dtypes
import numpy as np
from jax import lax
from jax.experimental import pallas as pl
from jax.experimental.pallas import tpu as pltpu
from jax.sharding import PartitionSpec as P

TP = 512
HALO = 32
KSUP = 65
HALF = KSUP // 2
KERNELS = 2
CONDS = 8
FULL = TP + 2 * HALO
PARTS = 4
ROWS = TP // PARTS
FA = 40
FB = 64
BF = jnp.bfloat16
F32 = jnp.float32

mask_steep = 2.0
resist_steep = 4.0
band_weight = 1.0


def waves(positions):
    angles = (np.outer(np.asarray(positions, np.int64), np.arange(HALF + 1)) % FULL) * (2.0 * np.pi / FULL)
    return np.cos(angles), np.sin(angles)


def halves(table):
    high = table.astype(np.float32).astype(ml_dtypes.bfloat16)
    low = (table - high.astype(np.float64)).astype(np.float32).astype(ml_dtypes.bfloat16)
    return high, low


def row_table(positions):
    cosine, sine = waves(positions)
    table = np.zeros((len(positions), 2 * FA))
    table[:, : HALF + 1] = cosine
    table[:, FA : FA + HALF + 1] = sine
    return table


def pair_table(positions):
    table = row_table(positions)
    return np.concatenate([table, np.concatenate([-table[:, FA:], table[:, :FA]], axis=1)])


def column_table(positions):
    cosine, sine = waves(positions)
    table = np.zeros((len(positions), 4 * FB))
    for block, values in enumerate((cosine, cosine, sine, -sine)):
        table[:, block * FB : block * FB + HALF] = values[:, 1:]
    table[:, HALF] = 1.0
    return table


@functools.cache
def tables():
    pixels = np.arange(TP) + HALO
    column = column_table(pixels)
    column_high, column_low = halves(column)
    turned = np.concatenate([column[:, : 2 * FB].T, column[:, 2 * FB :].T], axis=1)
    turned_high, turned_low = halves(turned)
    row = row_table(pixels)
    row_high, row_low = halves(row)
    out = {}
    out["column"] = np.stack([column_high, column_low])
    spectrum_rows = []
    rim_rows = []
    halo_rows = []
    own_rows = []
    forward = []
    backward = []
    for part in range(PARTS):
        own = np.arange(ROWS) + part * ROWS + HALO
        rim = np.arange(HALO) + (0 if part == PARTS - 1 else FULL - HALO)
        for rows, positions in ((spectrum_rows, own), (rim_rows, rim)):
            high, low = halves(row_table(positions).T)
            rows.append(np.concatenate([high, low, high], axis=1))
        high, low = halves(pair_table(rim))
        halo_rows.append(np.concatenate([high, low, high], axis=1))
        high, low = halves(pair_table(own))
        own_rows.append(np.concatenate([high, low, high], axis=1))
        cols = slice(part * ROWS, (part + 1) * ROWS)
        high = np.concatenate([turned_high[:, :TP][:, cols], turned_high[:, TP:][:, cols]], axis=1)
        low = np.concatenate([turned_low[:, :TP][:, cols], turned_low[:, TP:][:, cols]], axis=1)
        forward.append(np.concatenate([high, high, low]))
        backward.append(np.concatenate([column_high[cols], column_high[cols], column_low[cols]]))
    out["spectrum_rows"] = np.stack(spectrum_rows)
    out["own_rows"] = np.stack(own_rows)
    out["rim_rows"] = np.stack(rim_rows)
    out["halo_rows"] = np.stack(halo_rows)
    out["forward"] = np.stack(forward)
    out["backward"] = np.stack(backward)
    out["turned"] = np.stack([column_high.T, column_low.T])
    out["row"] = np.concatenate([row_high, row_low, row_high], axis=1)
    out["row_turned"] = np.concatenate([row_high.T, row_low.T])
    return out


def part_of(ref):
    return ref[0] % PARTS


def has_halo(ref):
    return ref[0] // PARTS > 0


def dot(left, right):
    return jnp.dot(left, right, preferred_element_type=F32)


def split(value):
    high = value.astype(BF)
    return high, (value - high.astype(F32)).astype(BF)


def spectrum_of(mask, column_ref, rows):
    high, low = split(mask)
    across = dot(high, column_ref[0]) + dot(low, column_ref[0]) + dot(high, column_ref[1])
    high, low = split(across)
    both = dot(rows, jnp.concatenate([high, high, low], axis=0))
    even = both[:FA, : 2 * FB] - both[FA:, 2 * FB :]
    odd = both[FA:, : 2 * FB] + both[:FA, 2 * FB :]
    return even, odd


def open_kernel(
    part_ref, real_hbm, imag_hbm, thresholds_hbm, weights_hbm, forward_hbm, backward_hbm,
    out_ref, shares_ref, forward_ref, backward_ref, real_ref, imag_ref, thresholds_ref, weights_ref, stage, sems,
):
    part = part_of(part_ref)
    moves = [
        (real_hbm, real_ref),
        (imag_hbm, imag_ref),
        (thresholds_hbm, thresholds_ref),
        (weights_hbm, weights_ref),
        (forward_hbm.at[part], forward_ref),
        (backward_hbm.at[part], backward_ref),
    ]
    copies = [pltpu.make_async_copy(source, target, sems.at[i]) for i, (source, target) in enumerate(moves)]
    for copy in copies:
        copy.start()
    local_conds = real_ref.shape[0]
    mats = local_conds * KERNELS * 2
    stage[...] = jnp.zeros_like(stage)
    for copy in copies[:4]:
        copy.wait()
    for cond in range(local_conds):
        for kern in range(KERNELS):
            for piece, ref in enumerate((real_ref, imag_ref)):
                stage[(cond * KERNELS + kern) * 2 + piece, :KSUP, :KSUP] = ref[cond, :, kern, :]
    rows = stage.shape[1]
    source = lax.broadcasted_iota(jnp.int32, (2 * FB, 4 * FB), 0)
    target = lax.broadcasted_iota(jnp.int32, (2 * FB, 4 * FB), 1)
    lane = target % FB
    block = target // FB
    plus = (block == 0) | (block == 3)
    freq = jnp.where(lane < HALF, lane + 1, 0)
    used = (lane < HALF) | ((lane == HALF) & (block % 2 == 0))
    pick = (used & (source == jnp.where(plus, HALF + freq, HALF - freq))).astype(F32).astype(BF)
    high, low = split(stage[...].reshape(mats * rows, 2 * FB))
    picked = [dot(piece, pick) for piece in (high, low)]
    source = lax.broadcasted_iota(jnp.int32, (FA, 2 * rows), 1) % rows
    target = lax.broadcasted_iota(jnp.int32, (FA, 2 * rows), 0)
    turn = ((source == HALF - target) & (target <= HALF)).astype(F32).astype(BF)
    lane = lax.broadcasted_iota(jnp.int32, (FA, 2 * FB), 1)
    row = lax.broadcasted_iota(jnp.int32, (FA, 2 * FB), 0)
    valid = (row <= HALF) & ((lane <= HALF) | ((row > 0) & (lane >= FB) & (lane < FB + HALF)))
    scale = 1.0 / (FULL * FULL)
    keep_top = jnp.where(valid, scale, 0.0)
    keep_bottom = jnp.where((row == 0) & (lane == HALF), 0.0, keep_top)
    first = lane % FB < HALF
    extra = jnp.zeros((FA, 2 * FB), F32)
    for kern in range(local_conds * KERNELS):
        arrays = [[], []]
        for piece in range(2):
            start = (kern * 2 + piece) * rows
            top = picked[0][start + HALF : start + HALF + FA, : 2 * FB] + picked[1][start + HALF : start + HALF + FA, : 2 * FB]
            pieces = jnp.concatenate([half[start : start + rows, 2 * FB :] for half in picked], axis=0)
            bottom = dot(turn, pieces.astype(BF)) * keep_bottom
            top = top * keep_top
            arrays[0].append(top + bottom)
            arrays[1].append(top - bottom)
        for which, (real, imag) in enumerate(arrays):
            packed = jnp.where(first, real, pltpu.roll(imag, HALF, 1))
            if which == 0:
                packed = jnp.where(row == FA - 1, thresholds_ref[kern // KERNELS], packed)
            out_ref[kern * 2 + which] = packed
            for piece, value in enumerate((real, imag)):
                place = kern * 4 + which * 2 + piece
                extra = jnp.where(lane == place, pltpu.roll(value, (place - HALF) % (2 * FB), 1), extra)
    out_ref[local_conds * KERNELS * 2] = extra
    weight_sum = weights_ref[0]
    for i in range(1, CONDS):
        weight_sum = weight_sum + weights_ref[i]
    row = lax.broadcasted_iota(jnp.int32, shares_ref.shape, 0)
    shares = jnp.zeros(shares_ref.shape, F32)
    for group, step in enumerate((0, 3, 1, 2)):
        for i in range(local_conds):
            weight = weights_ref[lax.bitwise_xor(part, step) * local_conds + i]
            shares = jnp.where(row == group * local_conds + i, weight.astype(F32), shares)
    shares_ref[...] = shares / weight_sum.astype(F32)
    for copy in copies[4:]:
        copy.wait()


def spectrum_kernel(part_ref, theta_ref, column_ref, rows_ref, out_ref):
    even, odd = spectrum_of(jnp.tanh(mask_steep * theta_ref[...]), column_ref, rows_ref[0])
    out_ref[0] = even
    out_ref[1] = odd


def rim_kernel(part_ref, spectrum_ref, rim_ref, column_ref, rows_ref, out_ref):
    even, odd = spectrum_of(jnp.tanh(mask_steep * rim_ref[...]), column_ref, rows_ref[0])
    out_ref[0] = even + spectrum_ref[0]
    out_ref[1] = odd + spectrum_ref[1]


def fields_kernel(
    part_ref, mixed_ref, other_ref, shares_ref, target_ref, forward_ref, backward_ref, row_ref,
    row_turned_ref, out_ref, kernels_ref, lines, folded, amps, tanhs, total, signs, turned, backs,
):
    count = kernels_ref.shape[0]
    local = count // PARTS
    tall = 4 * FA
    each = 2 * local + 1
    even = mixed_ref[2 * each] + other_ref[2 * each]
    odd = mixed_ref[2 * each + 1] + other_ref[2 * each + 1]
    lane = lax.broadcasted_iota(jnp.int32, (FA, 2 * FB), 1)
    row = lax.broadcasted_iota(jnp.int32, (FA, 2 * FB), 0)
    zero_lane = (lane == HALF) & (row <= HALF)
    for group in range(PARTS):
        ref = (mixed_ref, other_ref)[group // 2].at[pl.ds(group % 2 * each, each)]
        extra = ref[2 * local]
        for kern in range(local):
            values = []
            for which in range(2):
                packed = ref[2 * kern + which]
                for part, value in enumerate((packed, pltpu.roll(packed, 2 * FB - HALF, 1))):
                    place = kern * 4 + which * 2 + part
                    zeroth = pltpu.roll(extra, (HALF - place) % (2 * FB), 1)
                    value = jnp.where(zero_lane, zeroth, value)
                    kernels_ref[group * local + kern, which * 2 + part] = value
                    values.append(value)
            he_real, he_imag, ho_real, ho_imag = values
            start = (group * local + kern) * tall
            for i, value in enumerate(
                (
                    even * he_real + odd * ho_imag,
                    odd * he_real - even * ho_imag,
                    even * he_imag - odd * ho_real,
                    odd * he_imag + even * ho_real,
                )
            ):
                lines[start + i * FA : start + (i + 1) * FA] = value

    high, low = split(lines[...])
    lines_folded = dot(jnp.concatenate([high, low], axis=1), forward_ref[: 4 * FB]) + dot(high, forward_ref[4 * FB :])
    for kern in range(count):
        parts = []
        for i in range(2):
            x_part = lines_folded[tall * kern + 2 * FA * i : tall * kern + 2 * FA * i + FA]
            y_part = lines_folded[tall * kern + 2 * FA * i + FA : tall * kern + 2 * FA * (i + 1)]
            parts.append(
                jnp.concatenate(
                    [x_part[:, :ROWS] + y_part[:, ROWS:], y_part[:, :ROWS] - x_part[:, ROWS:]], axis=0
                )
            )
        high, low = split(jnp.concatenate(parts, axis=1))
        folded[kern] = jnp.concatenate([high, high, low], axis=0)
    total[...] = jnp.zeros_like(total)
    signs[...] = 1.0 - 2.0 * target_ref[...].astype(F32)

    def expose(cond, carry):
        intensity = None
        for kern in range(KERNELS):
            index = cond * KERNELS + kern
            amp = dot(row_ref[...], folded[index])
            amps[index] = amp
            power = amp[:, :ROWS] * amp[:, :ROWS] + amp[:, ROWS:] * amp[:, ROWS:]
            intensity = power if intensity is None else intensity + power
        level = kernels_ref[cond * KERNELS, 0, FA - 1 :, :]
        value = jnp.tanh((0.5 * resist_steep) * (intensity - level))
        tanhs[cond] = value
        total[...] += value
        return carry

    lax.fori_loop(0, CONDS, expose, 0, unroll=8)
    total[...] = total[...] * (band_weight / (CONDS * CONDS))

    def drive(cond, carry):
        weight = shares_ref[pl.ds(cond, 1), :]
        value = tanhs[cond]
        slope = (weight + band_weight / CONDS) * value + weight * signs[...] - total[...]
        field = (0.5 * resist_steep) * (1.0 - value * value) * slope
        field = jnp.concatenate([field, field], axis=1)
        for kern in range(KERNELS):
            index = cond * KERNELS + kern
            high, low = split(field * amps[index])
            long = dot(row_turned_ref[...], high)
            back = long[: 2 * FA] + long[2 * FA :] + dot(row_turned_ref[: 2 * FA], low)
            turned[pl.ds(index * 2, 2)] = jnp.stack([back[:, :ROWS], back[:, ROWS:]])
        return carry

    lax.fori_loop(0, CONDS, drive, 0, unroll=8)
    high, low = split(turned[...].reshape(count * tall, ROWS))
    backs[...] = dot(jnp.concatenate([high, low], axis=1), backward_ref[: 2 * ROWS]) + dot(high, backward_ref[2 * ROWS :])

    sum_even = jnp.zeros((FA, 2 * FB), F32)
    sum_odd = jnp.zeros((FA, 2 * FB), F32)
    for kern in range(count):
        grads = []
        for i in range(2):
            c_part = backs[tall * kern + 2 * FA * i : tall * kern + 2 * FA * i + FA]
            s_part = backs[tall * kern + 2 * FA * i + FA : tall * kern + 2 * FA * (i + 1)]
            grads.append(
                (
                    c_part[:, : 2 * FB] - s_part[:, 2 * FB :],
                    s_part[:, : 2 * FB] + c_part[:, 2 * FB :],
                )
            )
        (x_real, y_real), (x_imag, y_imag) = grads
        he_real, he_imag, ho_real, ho_imag = (kernels_ref[kern, i] for i in range(4))
        sum_even = sum_even + x_real * he_real + x_imag * he_imag - y_real * ho_imag + y_imag * ho_real
        sum_odd = sum_odd + x_real * ho_imag - x_imag * ho_real + y_real * he_real + y_imag * he_imag
    out_ref[:FA] = sum_even
    out_ref[FA:] = sum_odd


def image_rows(value, rows, turned_ref):
    high, low = split(value)
    pair = dot(rows, jnp.concatenate([high, high, low], axis=0))
    count = pair.shape[0] // 2
    high, low = split(jnp.concatenate([pair[:count], pair[count:]], axis=1))
    return dot(high, turned_ref[0]) + dot(low, turned_ref[0]) + dot(high, turned_ref[1])


def edge_start(part_ref):
    return pl.multiple_of(jnp.where(part_of(part_ref) == PARTS - 1, ROWS - HALO, 0), HALO)


def gradient_kernel(part_ref, theta_ref, sum_ref, chip_ref, back_ref, turned_ref, rows_ref, out_ref, edge_ref, scale_ref):
    part = part_of(part_ref)
    middle = (part == 1) | (part == 2)
    mask = jnp.tanh(mask_steep * theta_ref[...])
    scale = mask_steep * (1.0 - mask * mask)
    mine = jnp.where(middle, sum_ref[...], chip_ref[...] + back_ref[...])
    gradient = image_rows(mine, rows_ref[0], turned_ref) * scale
    out_ref[...] = gradient
    last = part == PARTS - 1
    edge_ref[...] = jnp.where(last, gradient[ROWS - HALO :], gradient[:HALO])
    scale_ref[...] = jnp.where(last, scale[ROWS - HALO :], scale[:HALO])


def edge_kernel(part_ref, gradient_hbm, edge_ref, scale_ref, near_ref, turned_ref, rows_ref, out_hbm, stage, sem):
    rim = image_rows(near_ref[...], rows_ref[0], turned_ref) * scale_ref[...]
    stage[...] = edge_ref[...] + jnp.where(has_halo(part_ref), rim, 0.0)
    copy = pltpu.make_async_copy(stage, out_hbm.at[pl.ds(edge_start(part_ref), HALO)], sem)
    copy.start()
    copy.wait()


def whole_spec(array):
    rank = len(array.shape)
    return pl.BlockSpec(array.shape, lambda i, *refs: (0,) * rank)


def part_spec(array):
    rank = len(array.shape)
    return pl.BlockSpec((1,) + array.shape[1:], lambda i, part, *refs: (part_of(part),) + (0,) * (rank - 1))


def call(kernel, scalars, operands, specs, out_shapes, scratch=(), name=None, flops=1 << 28, out_specs=None, aliases=None):
    many = isinstance(out_shapes, list)
    if out_specs is None:
        out_specs = [whole_spec(shape) for shape in out_shapes] if many else whole_spec(out_shapes)
    return pl.pallas_call(
        kernel,
        grid_spec=pltpu.PrefetchScalarGridSpec(
            num_scalar_prefetch=len(scalars),
            grid=(1,),
            in_specs=specs,
            out_specs=out_specs,
            scratch_shapes=list(scratch),
        ),
        out_shape=out_shapes,
        input_output_aliases=aliases or {},
        compiler_params=pltpu.CompilerParams(vmem_limit_bytes=48 * 1024 * 1024),
        cost_estimate=pl.CostEstimate(flops=flops, bytes_accessed=1 << 20, transcendentals=0),
        name=name,
    )(*scalars, *operands)


def floats(*shape):
    return jax.ShapeDtypeStruct(shape, F32)


def shards(theta, target, kernel_real, kernel_imag, weights, thresholds):
    table = {name: jnp.asarray(value) for name, value in tables().items()}
    tiles = lax.axis_size("tile")
    part = lax.axis_index("cond")
    tile = lax.axis_index("tile")
    last = PARTS - 1
    above = ((part == 0) & (tile > 0)) | ((part == last) & (tile < tiles - 1))
    parts = (part + PARTS * above.astype(jnp.int32)).reshape(1).astype(jnp.int32)
    local_conds = kernel_real.shape[0]
    local = local_conds * KERNELS
    count = CONDS * KERNELS
    hbm = pl.BlockSpec(memory_space=pltpu.HBM)

    def across(value, down, up, within=()):
        pairs = [(PARTS * i + a, PARTS * i + b) for i in range(tiles) for a, b in within]
        pairs += [(PARTS * (i + 1) + down[0], PARTS * i + down[1]) for i in range(tiles - 1)]
        pairs += [(PARTS * i + up[0], PARTS * (i + 1) + up[1]) for i in range(tiles - 1)]
        if within:
            pairs += [(down[0], up[1]), (PARTS * (tiles - 1) + up[0], PARTS * (tiles - 1) + down[1])]
        return lax.ppermute(value, ("tile", "cond"), pairs)

    def partner(value, step):
        return lax.ppermute(value, "cond", [(i, i ^ step) for i in range(PARTS)])

    kernel_shape = (local_conds, KSUP, KERNELS, KSUP)
    own, shares, forward, backward = call(
        open_kernel,
        (parts,),
        tuple(
            pltpu.with_memory_space_constraint(value, pltpu.HBM)
            for value in (
                kernel_real.transpose(0, 2, 1, 3), kernel_imag.transpose(0, 2, 1, 3), thresholds, weights,
                table["forward"], table["backward"],
            )
        ),
        [hbm] * 6,
        [
            floats(2 * local + 1, FA, 2 * FB),
            floats(CONDS, ROWS),
            jax.ShapeDtypeStruct(table["forward"].shape[1:], BF),
            jax.ShapeDtypeStruct(table["backward"].shape[1:], BF),
        ],
        scratch=(
            pltpu.VMEM(kernel_shape, F32),
            pltpu.VMEM(kernel_shape, F32),
            pltpu.SMEM(thresholds.shape, F32),
            pltpu.SMEM(weights.shape, jnp.int32),
            pltpu.VMEM((2 * local, 72, 2 * FB), F32),
            pltpu.SemaphoreType.DMA((6,)),
        ),
        name="open_parts",
    )
    rim = lax.dynamic_slice_in_dim(theta, jnp.where(part == 0, 0, ROWS - HALO), HALO, axis=0)
    rim = across(rim, (0, 0), (last, last))
    spectrum = call(
        spectrum_kernel,
        (parts,),
        (theta, table["column"], table["spectrum_rows"]),
        [whole_spec(theta), whole_spec(table["column"]), part_spec(table["spectrum_rows"])],
        floats(2, FA, 2 * FB),
        name="own_spectrum",
        flops=1 << 31,
    )
    side = partner(own, 3)
    spectrum = call(
        rim_kernel,
        (parts,),
        (spectrum, rim, table["column"], table["rim_rows"]),
        [whole_spec(spectrum), whole_spec(rim), whole_spec(table["column"]), part_spec(table["rim_rows"])],
        floats(2, FA, 2 * FB),
        name="add_rim",
    )
    mixed = jnp.concatenate([own, side, spectrum + partner(spectrum, 3)], axis=0)
    adjoint = call(
        fields_kernel,
        (parts,),
        (mixed, partner(mixed, 1), shares, target, forward, backward, table["row"], table["row_turned"]),
        [
            whole_spec(mixed),
            whole_spec(mixed),
            whole_spec(shares),
            pl.BlockSpec((TP, ROWS), lambda i, part, *refs: (0, part_of(part))),
            whole_spec(forward),
            whole_spec(backward),
            whole_spec(table["row"]),
            whole_spec(table["row_turned"]),
        ],
        floats(2 * FA, 2 * FB),
        scratch=(
            pltpu.VMEM((count, 4, FA, 2 * FB), F32),
            pltpu.VMEM((count * 4 * FA, 2 * FB), F32),
            pltpu.VMEM((count, 6 * FA, 2 * ROWS), BF),
            pltpu.VMEM((count, TP, 2 * ROWS), F32),
            pltpu.VMEM((CONDS, TP, ROWS), F32),
            pltpu.VMEM((TP, ROWS), F32),
            pltpu.VMEM((TP, ROWS), F32),
            pltpu.VMEM((count * 2, 2 * FA, ROWS), F32),
            pltpu.VMEM((count * 4 * FA, 4 * FB), F32),
        ),
        name="coherent_fields",
        flops=1 << 33,
    )
    chip = adjoint + partner(adjoint, 1)
    adjoint = chip + lax.ppermute(chip, "cond", [(0, 0), (1, 2), (2, 1), (last, last)])
    back = lax.ppermute(chip, "cond", [(0, last), (1, 1), (2, 2), (last, 0)])
    near = across(adjoint, (2, last), (1, 0), within=[(0, 1), (last, 2)])
    gradient, edge, scale = call(
        gradient_kernel,
        (parts,),
        (theta, adjoint, chip, back, table["turned"], table["own_rows"]),
        [
            whole_spec(theta),
            whole_spec(adjoint),
            whole_spec(chip),
            whole_spec(back),
            whole_spec(table["turned"]),
            part_spec(table["own_rows"]),
        ],
        [floats(ROWS, TP), floats(HALO, TP), floats(HALO, TP)],
        name="own_gradient",
        flops=1 << 31,
    )
    return call(
        edge_kernel,
        (parts,),
        (gradient, edge, scale, near, table["turned"], table["halo_rows"]),
        [
            hbm,
            whole_spec(edge),
            whole_spec(scale),
            whole_spec(near),
            whole_spec(table["turned"]),
            part_spec(table["halo_rows"]),
        ],
        floats(ROWS, TP),
        scratch=(pltpu.VMEM((HALO, TP), F32), pltpu.SemaphoreType.DMA),
        name="edge_gradient",
        out_specs=hbm,
        aliases={1: 0},
    )


def solution(mesh):
    in_specs = (
        P(("tile", "cond"), None),
        P("tile", None),
        P("cond", None, None, None),
        P("cond", None, None, None),
        P(),
        P("cond"),
    )
    out_specs = P(("tile", "cond"), None)
    return jax.shard_map(shards, mesh=mesh, in_specs=in_specs, out_specs=out_specs, check_vma=False)
```

```python
import functools

import jax
import jax.numpy as jnp
import ml_dtypes
import numpy as np
from jax import lax
from jax.experimental import pallas as pl
from jax.experimental.pallas import tpu as pltpu
from jax.sharding import PartitionSpec as P

TP = 512
HALO = 32
KSUP = 65
HALF = KSUP // 2
KERNELS = 2
CONDS = 8
FULL = TP + 2 * HALO
PARTS = 4
ROWS = TP // PARTS
FA = 40
FB = 64
BF = jnp.bfloat16
F32 = jnp.float32

mask_steep = 2.0
resist_steep = 4.0
band_weight = 1.0


def waves(positions):
    angles = (np.outer(np.asarray(positions, np.int64), np.arange(HALF + 1)) % FULL) * (2.0 * np.pi / FULL)
    return np.cos(angles), np.sin(angles)


def halves(table):
    high = table.astype(np.float32).astype(ml_dtypes.bfloat16)
    low = (table - high.astype(np.float64)).astype(np.float32).astype(ml_dtypes.bfloat16)
    return high, low


def row_table(positions):
    cosine, sine = waves(positions)
    table = np.zeros((len(positions), 2 * FA))
    table[:, : HALF + 1] = cosine
    table[:, FA : FA + HALF + 1] = sine
    return table


def pair_table(positions):
    table = row_table(positions)
    return np.concatenate([table, np.concatenate([-table[:, FA:], table[:, :FA]], axis=1)])


def column_table(positions):
    cosine, sine = waves(positions)
    table = np.zeros((len(positions), 4 * FB))
    for block, values in enumerate((cosine, cosine, sine, -sine)):
        table[:, block * FB : block * FB + HALF] = values[:, 1:]
    table[:, HALF] = 1.0
    return table


@functools.cache
def tables():
    pixels = np.arange(TP) + HALO
    column = column_table(pixels)
    column_high, column_low = halves(column)
    turned = np.concatenate([column[:, : 2 * FB].T, column[:, 2 * FB :].T], axis=1)
    turned_high, turned_low = halves(turned)
    row = row_table(pixels)
    row_high, row_low = halves(row)
    out = {}
    out["column"] = np.stack([column_high, column_low])
    waves_only = np.s_[:, np.r_[0:FB, 2 * FB : 3 * FB]]
    out["waves"] = np.stack([column_high[waves_only], column_low[waves_only]])
    spectrum_rows = []
    rim_rows = []
    halo_rows = []
    own_rows = []
    forward = []
    backward = []
    for part in range(PARTS):
        own = np.arange(ROWS) + part * ROWS + HALO
        rim = np.arange(HALO) + (0 if part == PARTS - 1 else FULL - HALO)
        for rows, positions in ((spectrum_rows, own), (rim_rows, rim)):
            high, low = halves(row_table(positions).T)
            rows.append(np.concatenate([high, low, high], axis=1))
        high, low = halves(pair_table(rim))
        halo_rows.append(np.concatenate([high, low, high], axis=1))
        high, low = halves(pair_table(own))
        own_rows.append(np.concatenate([high, low, high], axis=1))
        cols = slice(part * ROWS, (part + 1) * ROWS)
        high = np.concatenate([turned_high[:, :TP][:, cols], turned_high[:, TP:][:, cols]], axis=1)
        low = np.concatenate([turned_low[:, :TP][:, cols], turned_low[:, TP:][:, cols]], axis=1)
        forward.append(np.concatenate([high, high, low]))
        backward.append(np.concatenate([column_high[cols], column_high[cols], column_low[cols]]))
    out["spectrum_rows"] = np.stack(spectrum_rows)
    out["own_rows"] = np.stack(own_rows)
    out["rim_rows"] = np.stack(rim_rows)
    out["halo_rows"] = np.stack(halo_rows)
    out["forward"] = np.stack(forward)
    out["backward"] = np.stack(backward)
    out["turned"] = np.stack([column_high.T, column_low.T])
    out["row"] = np.concatenate([row_high, row_low, row_high], axis=1)
    out["row_turned"] = np.concatenate([row_high.T, row_low.T])
    return out


def part_of(ref):
    return ref[0] % PARTS


def has_halo(ref):
    return ref[0] // PARTS > 0


def dot(left, right):
    return jnp.dot(left, right, preferred_element_type=F32)


def split(value):
    high = value.astype(BF)
    return high, (value - high.astype(F32)).astype(BF)


def lanes_and_rows():
    shape = (FA, 2 * FB)
    return lax.broadcasted_iota(jnp.int32, shape, 1), lax.broadcasted_iota(jnp.int32, shape, 0)


def pack(even, odd):
    lane, row = lanes_and_rows()
    packed = jnp.where(lane % FB < HALF, even, pltpu.roll(odd, HALF, 1))
    for place, value in ((FA - 2, even), (FA - 3, odd)):
        line = jnp.sum(jnp.where(lane == row, value[:, HALF : HALF + 1], 0.0), axis=0, keepdims=True)
        packed = jnp.where(row == place, line, packed)
    return packed


def unpack(packed):
    lane, row = lanes_and_rows()
    values = []
    for place, value in ((FA - 2, packed), (FA - 3, pltpu.roll(packed, 2 * FB - HALF, 1))):
        column = jnp.sum(jnp.where((lane == row) & (row <= HALF), packed[place : place + 1], 0.0), axis=1, keepdims=True)
        value = jnp.where(lane == HALF, column, jnp.where(lane % FB < HALF, value, 0.0))
        values.append(jnp.where(row <= HALF, value, 0.0))
    return values


def columns_of(mask, column_ref):
    high, low = split(mask)
    return dot(high, column_ref[0]) + dot(low, column_ref[0]) + dot(high, column_ref[1])


def spectrum_of(across, rows):
    high, low = split(across)
    both = dot(rows, jnp.concatenate([high, high, low], axis=0))
    even = both[:FA, : 2 * FB] - both[FA:, 2 * FB :]
    odd = both[FA:, : 2 * FB] + both[:FA, 2 * FB :]
    return even, odd


def open_kernel(
    part_ref, real_hbm, imag_hbm, thresholds_hbm, weights_hbm, forward_hbm, backward_hbm,
    out_ref, shares_ref, forward_ref, backward_ref, real_ref, imag_ref, thresholds_ref, weights_ref, stage, sems,
):
    part = part_of(part_ref)
    moves = [
        (real_hbm, real_ref),
        (imag_hbm, imag_ref),
        (thresholds_hbm, thresholds_ref),
        (weights_hbm, weights_ref),
        (forward_hbm.at[part], forward_ref),
        (backward_hbm.at[part], backward_ref),
    ]
    copies = [pltpu.make_async_copy(source, target, sems.at[i]) for i, (source, target) in enumerate(moves)]
    for copy in copies:
        copy.start()
    local_conds = real_ref.shape[0]
    mats = local_conds * KERNELS * 2
    stage[...] = jnp.zeros_like(stage)
    for copy in copies[:4]:
        copy.wait()
    for cond in range(local_conds):
        for kern in range(KERNELS):
            for piece, ref in enumerate((real_ref, imag_ref)):
                stage[(cond * KERNELS + kern) * 2 + piece, :KSUP, :KSUP] = ref[cond, :, kern, :]
    rows = stage.shape[1]
    source = lax.broadcasted_iota(jnp.int32, (2 * FB, 4 * FB), 0)
    target = lax.broadcasted_iota(jnp.int32, (2 * FB, 4 * FB), 1)
    lane = target % FB
    block = target // FB
    plus = (block == 0) | (block == 3)
    freq = jnp.where(lane < HALF, lane + 1, 0)
    used = (lane < HALF) | ((lane == HALF) & (block % 2 == 0))
    pick = (used & (source == jnp.where(plus, HALF + freq, HALF - freq))).astype(F32).astype(BF)
    high, low = split(stage[...].reshape(mats * rows, 2 * FB))
    picked = [dot(piece, pick) for piece in (high, low)]
    source = lax.broadcasted_iota(jnp.int32, (FA, 2 * rows), 1) % rows
    target = lax.broadcasted_iota(jnp.int32, (FA, 2 * rows), 0)
    turn = ((source == HALF - target) & (target <= HALF)).astype(F32).astype(BF)
    lane = lax.broadcasted_iota(jnp.int32, (FA, 2 * FB), 1)
    row = lax.broadcasted_iota(jnp.int32, (FA, 2 * FB), 0)
    valid = (row <= HALF) & ((lane <= HALF) | ((row > 0) & (lane >= FB) & (lane < FB + HALF)))
    scale = 1.0 / (FULL * FULL)
    keep_top = jnp.where(valid, scale, 0.0)
    keep_bottom = jnp.where((row == 0) & (lane == HALF), 0.0, keep_top)
    first = lane % FB < HALF
    extra = jnp.zeros((FA, 2 * FB), F32)
    for kern in range(local_conds * KERNELS):
        arrays = [[], []]
        for piece in range(2):
            start = (kern * 2 + piece) * rows
            top = picked[0][start + HALF : start + HALF + FA, : 2 * FB] + picked[1][start + HALF : start + HALF + FA, : 2 * FB]
            pieces = jnp.concatenate([half[start : start + rows, 2 * FB :] for half in picked], axis=0)
            bottom = dot(turn, pieces.astype(BF)) * keep_bottom
            top = top * keep_top
            arrays[0].append(top + bottom)
            arrays[1].append(top - bottom)
        for which, (real, imag) in enumerate(arrays):
            packed = jnp.where(first, real, pltpu.roll(imag, HALF, 1))
            if which == 0:
                packed = jnp.where(row == FA - 1, thresholds_ref[kern // KERNELS], packed)
            out_ref[kern * 2 + which] = packed
            for piece, value in enumerate((real, imag)):
                place = kern * 4 + which * 2 + piece
                extra = jnp.where(lane == place, pltpu.roll(value, (place - HALF) % (2 * FB), 1), extra)
    out_ref[local_conds * KERNELS * 2] = extra
    weight_sum = weights_ref[0]
    for i in range(1, CONDS):
        weight_sum = weight_sum + weights_ref[i]
    row = lax.broadcasted_iota(jnp.int32, shares_ref.shape, 0)
    shares = jnp.zeros(shares_ref.shape, F32)
    for group, step in enumerate((0, 3, 1, 2)):
        for i in range(local_conds):
            weight = weights_ref[lax.bitwise_xor(part, step) * local_conds + i]
            shares = jnp.where(row == group * local_conds + i, weight.astype(F32), shares)
    shares_ref[...] = shares / weight_sum.astype(F32)
    for copy in copies[4:]:
        copy.wait()


def send_rim_kernel(part_ref, theta_hbm, waves_hbm, out_ref, theta_ref, waves_ref, sems):
    rows = pl.ds(pl.multiple_of(jnp.where(part_of(part_ref) == 0, 0, ROWS - HALO), HALO), HALO)
    copies = [
        pltpu.make_async_copy(theta_hbm.at[rows], theta_ref, sems.at[0]),
        pltpu.make_async_copy(waves_hbm, waves_ref, sems.at[1]),
    ]
    for copy in copies:
        copy.start()
    copies[0].wait()
    mask = jnp.tanh(mask_steep * theta_ref[...])
    copies[1].wait()
    out_ref[...] = columns_of(mask, waves_ref)


def spectrum_kernel(part_ref, theta_ref, column_ref, rows_ref, out_ref):
    across = columns_of(jnp.tanh(mask_steep * theta_ref[...]), column_ref)
    even, odd = spectrum_of(across, rows_ref[0])
    out_ref[0] = even
    out_ref[1] = odd


def rim_kernel(part_ref, spectrum_ref, rim_ref, rows_ref, out_ref):
    rim = rim_ref[...]
    turned = pltpu.roll(rim, FB, 1)
    first = lax.broadcasted_iota(jnp.int32, rim.shape, 1) < FB
    across = jnp.concatenate([jnp.where(first, rim, turned), jnp.where(first, turned, -rim)], axis=1)
    even, odd = spectrum_of(across, rows_ref[0])
    out_ref[0] = pack(even + spectrum_ref[0], odd + spectrum_ref[1])


def fields_kernel(
    part_ref, mixed_ref, other_ref, shares_ref, target_ref, forward_ref, backward_ref, row_ref,
    row_turned_ref, out_ref, kernels_ref, lines, folded, amps, tanhs, total, signs, turned, backs,
):
    count = kernels_ref.shape[0]
    local = count // PARTS
    tall = 4 * FA
    each = 2 * local + 1
    even, odd = unpack(mixed_ref[2 * each] + other_ref[2 * each])
    lane, row = lanes_and_rows()
    zero_lane = (lane == HALF) & (row <= HALF)
    for group in range(PARTS):
        ref = (mixed_ref, other_ref)[group // 2].at[pl.ds(group % 2 * each, each)]
        extra = ref[2 * local]
        for kern in range(local):
            values = []
            for which in range(2):
                packed = ref[2 * kern + which]
                for part, value in enumerate((packed, pltpu.roll(packed, 2 * FB - HALF, 1))):
                    place = kern * 4 + which * 2 + part
                    zeroth = pltpu.roll(extra, (HALF - place) % (2 * FB), 1)
                    value = jnp.where(zero_lane, zeroth, value)
                    kernels_ref[group * local + kern, which * 2 + part] = value
                    values.append(value)
            he_real, he_imag, ho_real, ho_imag = values
            start = (group * local + kern) * tall
            for i, value in enumerate(
                (
                    even * he_real + odd * ho_imag,
                    odd * he_real - even * ho_imag,
                    even * he_imag - odd * ho_real,
                    odd * he_imag + even * ho_real,
                )
            ):
                lines[start + i * FA : start + (i + 1) * FA] = value

    high, low = split(lines[...])
    lines_folded = dot(jnp.concatenate([high, low], axis=1), forward_ref[: 4 * FB]) + dot(high, forward_ref[4 * FB :])
    for kern in range(count):
        parts = []
        for i in range(2):
            x_part = lines_folded[tall * kern + 2 * FA * i : tall * kern + 2 * FA * i + FA]
            y_part = lines_folded[tall * kern + 2 * FA * i + FA : tall * kern + 2 * FA * (i + 1)]
            parts.append(
                jnp.concatenate(
                    [x_part[:, :ROWS] + y_part[:, ROWS:], y_part[:, :ROWS] - x_part[:, ROWS:]], axis=0
                )
            )
        high, low = split(jnp.concatenate(parts, axis=1))
        folded[kern] = jnp.concatenate([high, high, low], axis=0)
    total[...] = jnp.zeros_like(total)
    signs[...] = 1.0 - 2.0 * target_ref[...].astype(F32)

    def expose(cond, carry):
        intensity = None
        for kern in range(KERNELS):
            index = cond * KERNELS + kern
            amp = dot(row_ref[...], folded[index])
            amps[index] = amp
            power = amp[:, :ROWS] * amp[:, :ROWS] + amp[:, ROWS:] * amp[:, ROWS:]
            intensity = power if intensity is None else intensity + power
        level = kernels_ref[cond * KERNELS, 0, FA - 1 :, :]
        value = jnp.tanh((0.5 * resist_steep) * (intensity - level))
        tanhs[cond] = value
        total[...] += value
        return carry

    lax.fori_loop(0, CONDS, expose, 0, unroll=4)
    total[...] = total[...] * (band_weight / (CONDS * CONDS))

    def drive(cond, carry):
        weight = shares_ref[pl.ds(cond, 1), :]
        value = tanhs[cond]
        slope = (weight + band_weight / CONDS) * value + weight * signs[...] - total[...]
        field = (0.5 * resist_steep) * (1.0 - value * value) * slope
        field = jnp.concatenate([field, field], axis=1)
        for kern in range(KERNELS):
            index = cond * KERNELS + kern
            high, low = split(field * amps[index])
            long = dot(row_turned_ref[...], high)
            back = long[: 2 * FA] + long[2 * FA :] + dot(row_turned_ref[: 2 * FA], low)
            turned[pl.ds(index * 2, 2)] = jnp.stack([back[:, :ROWS], back[:, ROWS:]])
        return carry

    lax.fori_loop(0, CONDS, drive, 0, unroll=4)
    high, low = split(turned[...].reshape(count * tall, ROWS))
    backs[...] = dot(jnp.concatenate([high, low], axis=1), backward_ref[: 2 * ROWS]) + dot(high, backward_ref[2 * ROWS :])

    sum_even = jnp.zeros((FA, 2 * FB), F32)
    sum_odd = jnp.zeros((FA, 2 * FB), F32)
    for kern in range(count):
        grads = []
        for i in range(2):
            c_part = backs[tall * kern + 2 * FA * i : tall * kern + 2 * FA * i + FA]
            s_part = backs[tall * kern + 2 * FA * i + FA : tall * kern + 2 * FA * (i + 1)]
            grads.append(
                (
                    c_part[:, : 2 * FB] - s_part[:, 2 * FB :],
                    s_part[:, : 2 * FB] + c_part[:, 2 * FB :],
                )
            )
        (x_real, y_real), (x_imag, y_imag) = grads
        he_real, he_imag, ho_real, ho_imag = (kernels_ref[kern, i] for i in range(4))
        sum_even = sum_even + x_real * he_real + x_imag * he_imag - y_real * ho_imag + y_imag * ho_real
        sum_odd = sum_odd + x_real * ho_imag - x_imag * ho_real + y_real * he_real + y_imag * he_imag
    out_ref[...] = pack(sum_even, sum_odd)


def image_rows(packed, rows, turned_ref):
    high, low = split(jnp.concatenate(unpack(packed), axis=0))
    pair = dot(rows, jnp.concatenate([high, high, low], axis=0))
    count = pair.shape[0] // 2
    high, low = split(jnp.concatenate([pair[:count], pair[count:]], axis=1))
    return dot(high, turned_ref[0]) + dot(low, turned_ref[0]) + dot(high, turned_ref[1])


def edge_start(part_ref):
    return pl.multiple_of(jnp.where(part_of(part_ref) == PARTS - 1, ROWS - HALO, 0), HALO)


def gradient_kernel(part_ref, theta_ref, sum_ref, chip_ref, back_ref, turned_ref, rows_ref, out_ref, edge_ref, scale_ref):
    part = part_of(part_ref)
    middle = (part == 1) | (part == 2)
    mask = jnp.tanh(mask_steep * theta_ref[...])
    scale = mask_steep * (1.0 - mask * mask)
    mine = jnp.where(middle, sum_ref[...], chip_ref[...] + back_ref[...])
    gradient = image_rows(mine, rows_ref[0], turned_ref) * scale
    out_ref[...] = gradient
    last = part == PARTS - 1
    edge_ref[...] = jnp.where(last, gradient[ROWS - HALO :], gradient[:HALO])
    scale_ref[...] = jnp.where(last, scale[ROWS - HALO :], scale[:HALO])


def edge_kernel(part_ref, gradient_hbm, edge_ref, scale_ref, near_ref, turned_ref, rows_ref, out_hbm, stage, sem):
    rim = image_rows(near_ref[...], rows_ref[0], turned_ref) * scale_ref[...]
    stage[...] = edge_ref[...] + jnp.where(has_halo(part_ref), rim, 0.0)
    copy = pltpu.make_async_copy(stage, out_hbm.at[pl.ds(edge_start(part_ref), HALO)], sem)
    copy.start()
    copy.wait()


def whole_spec(array):
    rank = len(array.shape)
    return pl.BlockSpec(array.shape, lambda i, *refs: (0,) * rank)


def part_spec(array):
    rank = len(array.shape)
    return pl.BlockSpec((1,) + array.shape[1:], lambda i, part, *refs: (part_of(part),) + (0,) * (rank - 1))


def call(kernel, scalars, operands, specs, out_shapes, scratch=(), name=None, flops=1 << 28, out_specs=None, aliases=None):
    many = isinstance(out_shapes, list)
    if out_specs is None:
        out_specs = [whole_spec(shape) for shape in out_shapes] if many else whole_spec(out_shapes)
    return pl.pallas_call(
        kernel,
        grid_spec=pltpu.PrefetchScalarGridSpec(
            num_scalar_prefetch=len(scalars),
            grid=(1,),
            in_specs=specs,
            out_specs=out_specs,
            scratch_shapes=list(scratch),
        ),
        out_shape=out_shapes,
        input_output_aliases=aliases or {},
        compiler_params=pltpu.CompilerParams(vmem_limit_bytes=48 * 1024 * 1024),
        cost_estimate=pl.CostEstimate(flops=flops, bytes_accessed=1 << 20, transcendentals=0),
        name=name,
    )(*scalars, *operands)


def floats(*shape):
    return jax.ShapeDtypeStruct(shape, F32)


def shards(theta, target, kernel_real, kernel_imag, weights, thresholds):
    table = {name: jnp.asarray(value) for name, value in tables().items()}
    tiles = lax.axis_size("tile")
    part = lax.axis_index("cond")
    tile = lax.axis_index("tile")
    last = PARTS - 1
    above = ((part == 0) & (tile > 0)) | ((part == last) & (tile < tiles - 1))
    parts = (part + PARTS * above.astype(jnp.int32)).reshape(1).astype(jnp.int32)
    local_conds = kernel_real.shape[0]
    local = local_conds * KERNELS
    count = CONDS * KERNELS
    hbm = pl.BlockSpec(memory_space=pltpu.HBM)

    def across(value, down, up, within=()):
        pairs = [(PARTS * i + a, PARTS * i + b) for i in range(tiles) for a, b in within]
        pairs += [(PARTS * (i + 1) + down[0], PARTS * i + down[1]) for i in range(tiles - 1)]
        pairs += [(PARTS * i + up[0], PARTS * (i + 1) + up[1]) for i in range(tiles - 1)]
        if within:
            pairs += [(down[0], up[1]), (PARTS * (tiles - 1) + up[0], PARTS * (tiles - 1) + down[1])]
        return lax.ppermute(value, ("tile", "cond"), pairs)

    def partner(value, step):
        return lax.ppermute(value, "cond", [(i, i ^ step) for i in range(PARTS)])

    kernel_shape = (local_conds, KSUP, KERNELS, KSUP)
    own, shares, forward, backward = call(
        open_kernel,
        (parts,),
        tuple(
            pltpu.with_memory_space_constraint(value, pltpu.HBM)
            for value in (
                kernel_real.transpose(0, 2, 1, 3), kernel_imag.transpose(0, 2, 1, 3), thresholds, weights,
                table["forward"], table["backward"],
            )
        ),
        [hbm] * 6,
        [
            floats(2 * local + 1, FA, 2 * FB),
            floats(CONDS, ROWS),
            jax.ShapeDtypeStruct(table["forward"].shape[1:], BF),
            jax.ShapeDtypeStruct(table["backward"].shape[1:], BF),
        ],
        scratch=(
            pltpu.VMEM(kernel_shape, F32),
            pltpu.VMEM(kernel_shape, F32),
            pltpu.SMEM(thresholds.shape, F32),
            pltpu.SMEM(weights.shape, jnp.int32),
            pltpu.VMEM((2 * local, 72, 2 * FB), F32),
            pltpu.SemaphoreType.DMA((6,)),
        ),
        name="open_parts",
    )
    rim = call(
        send_rim_kernel,
        (parts,),
        tuple(pltpu.with_memory_space_constraint(value, pltpu.HBM) for value in (theta, table["waves"])),
        [hbm, hbm],
        floats(HALO, 2 * FB),
        scratch=(
            pltpu.VMEM((HALO, TP), F32),
            pltpu.VMEM(table["waves"].shape, BF),
            pltpu.SemaphoreType.DMA((2,)),
        ),
        name="edge_columns",
    )
    rim = across(rim, (0, 0), (last, last))
    spectrum = call(
        spectrum_kernel,
        (parts,),
        (theta, table["column"], table["spectrum_rows"]),
        [whole_spec(theta), whole_spec(table["column"]), part_spec(table["spectrum_rows"])],
        floats(2, FA, 2 * FB),
        name="own_spectrum",
        flops=1 << 31,
    )
    side = partner(own, 3)
    spectrum = call(
        rim_kernel,
        (parts,),
        (spectrum, rim, table["rim_rows"]),
        [whole_spec(spectrum), whole_spec(rim), part_spec(table["rim_rows"])],
        floats(1, FA, 2 * FB),
        name="add_rim",
    )
    mixed = jnp.concatenate([own, side, spectrum + partner(spectrum, 3)], axis=0)
    adjoint = call(
        fields_kernel,
        (parts,),
        (mixed, partner(mixed, 1), shares, target, forward, backward, table["row"], table["row_turned"]),
        [
            whole_spec(mixed),
            whole_spec(mixed),
            whole_spec(shares),
            pl.BlockSpec((TP, ROWS), lambda i, part, *refs: (0, part_of(part))),
            whole_spec(forward),
            whole_spec(backward),
            whole_spec(table["row"]),
            whole_spec(table["row_turned"]),
        ],
        floats(FA, 2 * FB),
        scratch=(
            pltpu.VMEM((count, 4, FA, 2 * FB), F32),
            pltpu.VMEM((count * 4 * FA, 2 * FB), F32),
            pltpu.VMEM((count, 6 * FA, 2 * ROWS), BF),
            pltpu.VMEM((count, TP, 2 * ROWS), F32),
            pltpu.VMEM((CONDS, TP, ROWS), F32),
            pltpu.VMEM((TP, ROWS), F32),
            pltpu.VMEM((TP, ROWS), F32),
            pltpu.VMEM((count * 2, 2 * FA, ROWS), F32),
            pltpu.VMEM((count * 4 * FA, 4 * FB), F32),
        ),
        name="coherent_fields",
        flops=1 << 33,
    )
    chip = adjoint + partner(adjoint, 1)
    adjoint = chip + lax.ppermute(chip, "cond", [(0, 0), (1, 2), (2, 1), (last, last)])
    back = lax.ppermute(chip, "cond", [(0, last), (1, 1), (2, 2), (last, 0)])
    near = across(adjoint, (2, last), (1, 0), within=[(0, 1), (last, 2)])
    gradient, edge, scale = call(
        gradient_kernel,
        (parts,),
        (theta, adjoint, chip, back, table["turned"], table["own_rows"]),
        [
            whole_spec(theta),
            whole_spec(adjoint),
            whole_spec(chip),
            whole_spec(back),
            whole_spec(table["turned"]),
            part_spec(table["own_rows"]),
        ],
        [floats(ROWS, TP), floats(HALO, TP), floats(HALO, TP)],
        name="own_gradient",
        flops=1 << 31,
    )
    return call(
        edge_kernel,
        (parts,),
        (gradient, edge, scale, near, table["turned"], table["halo_rows"]),
        [
            hbm,
            whole_spec(edge),
            whole_spec(scale),
            whole_spec(near),
            whole_spec(table["turned"]),
            part_spec(table["halo_rows"]),
        ],
        floats(ROWS, TP),
        scratch=(pltpu.VMEM((HALO, TP), F32), pltpu.SemaphoreType.DMA),
        name="edge_gradient",
        out_specs=hbm,
        aliases={1: 0},
    )


def solution(mesh):
    in_specs = (
        P(("tile", "cond"), None),
        P("tile", None),
        P("cond", None, None, None),
        P("cond", None, None, None),
        P(),
        P("cond"),
    )
    out_specs = P(("tile", "cond"), None)
    return jax.shard_map(shards, mesh=mesh, in_specs=in_specs, out_specs=out_specs, check_vma=False)
```

```python
import functools

import jax
import jax.numpy as jnp
import ml_dtypes
import numpy as np
from jax import lax
from jax.experimental import pallas as pl
from jax.experimental.pallas import tpu as pltpu
from jax.sharding import PartitionSpec as P

TP = 512
HALO = 32
KSUP = 65
HALF = KSUP // 2
KERNELS = 2
CONDS = 8
FULL = TP + 2 * HALO
PARTS = 4
ROWS = TP // PARTS
FA = 40
FB = 64
SPARE = FA - HALF - 1
SPARE_BLOCKS = -(-(HALF + 1) // SPARE)
BF = jnp.bfloat16
F32 = jnp.float32

mask_steep = 2.0
resist_steep = 4.0
band_weight = 1.0


def waves(positions):
    angles = (np.outer(np.asarray(positions, np.int64), np.arange(HALF + 1)) % FULL) * (2.0 * np.pi / FULL)
    return np.cos(angles), np.sin(angles)


def halves(table):
    high = table.astype(np.float32).astype(ml_dtypes.bfloat16)
    low = (table - high.astype(np.float64)).astype(np.float32).astype(ml_dtypes.bfloat16)
    return high, low


def row_table(positions):
    cosine, sine = waves(positions)
    table = np.zeros((len(positions), 2 * FA))
    table[:, : HALF + 1] = cosine
    table[:, FA : FA + HALF + 1] = sine
    return table


def pair_table(positions):
    table = row_table(positions)
    return np.concatenate([table, np.concatenate([-table[:, FA:], table[:, :FA]], axis=1)])


def column_table(positions):
    cosine, sine = waves(positions)
    table = np.zeros((len(positions), 4 * FB))
    for block, values in enumerate((cosine, cosine, sine, -sine)):
        table[:, block * FB : block * FB + HALF] = values[:, 1:]
    table[:, HALF] = 1.0
    return table


@functools.cache
def tables():
    pixels = np.arange(TP) + HALO
    column = column_table(pixels)
    column_high, column_low = halves(column)
    turned = np.concatenate([column[:, : 2 * FB].T, column[:, 2 * FB :].T], axis=1)
    turned_high, turned_low = halves(turned)
    row = row_table(pixels)
    row_high, row_low = halves(row)
    out = {}
    out["column"] = np.stack([column_high, column_low])
    waves_only = np.s_[:, np.r_[0:FB, 2 * FB : 3 * FB]]
    out["waves"] = np.stack([column_high[waves_only], column_low[waves_only]])
    spectrum_rows = []
    rim_rows = []
    halo_rows = []
    own_rows = []
    forward = []
    backward = []
    for part in range(PARTS):
        own = np.arange(ROWS) + part * ROWS + HALO
        rim = np.arange(HALO) + (0 if part == PARTS - 1 else FULL - HALO)
        for rows, positions in ((spectrum_rows, own), (rim_rows, rim)):
            high, low = halves(row_table(positions).T)
            rows.append(np.concatenate([high, low, high], axis=1))
        high, low = halves(pair_table(rim))
        halo_rows.append(np.concatenate([high, low, high], axis=1))
        high, low = halves(pair_table(own))
        own_rows.append(np.concatenate([high, low, high], axis=1))
        cols = slice(part * ROWS, (part + 1) * ROWS)
        high = np.concatenate([turned_high[:, :TP][:, cols], turned_high[:, TP:][:, cols]], axis=1)
        low = np.concatenate([turned_low[:, :TP][:, cols], turned_low[:, TP:][:, cols]], axis=1)
        forward.append(np.concatenate([high, high, low]))
        backward.append(np.concatenate([column_high[cols], column_high[cols], column_low[cols]]))
    out["spectrum_rows"] = np.stack(spectrum_rows)
    out["own_rows"] = np.stack(own_rows)
    out["rim_rows"] = np.stack(rim_rows)
    out["halo_rows"] = np.stack(halo_rows)
    out["forward"] = np.stack(forward)
    out["backward"] = np.stack(backward)
    out["turned"] = np.stack([column_high.T, column_low.T])
    out["row"] = np.concatenate([row_high, row_low, row_high], axis=1)
    out["row_turned"] = np.concatenate([row_high.T, row_low.T])
    return out


def part_of(ref):
    return ref[0] % PARTS


def has_halo(ref):
    return ref[0] // PARTS > 0


def dot(left, right):
    return jnp.dot(left, right, preferred_element_type=F32)


def split(value):
    high = value.astype(BF)
    return high, (value - high.astype(F32)).astype(BF)


def lanes_and_rows():
    shape = (FA, 2 * FB)
    return lax.broadcasted_iota(jnp.int32, shape, 1), lax.broadcasted_iota(jnp.int32, shape, 0)


def pack(even, odd):
    lane, row = lanes_and_rows()
    packed = jnp.where(lane % FB < HALF, even, pltpu.roll(odd, HALF, 1))
    for place, value in ((FA - 2, even), (FA - 3, odd)):
        line = jnp.sum(jnp.where(lane == row, value[:, HALF : HALF + 1], 0.0), axis=0, keepdims=True)
        packed = jnp.where(row == place, line, packed)
    return packed


def unpack(packed):
    lane, row = lanes_and_rows()
    values = []
    for place, value in ((FA - 2, packed), (FA - 3, pltpu.roll(packed, 2 * FB - HALF, 1))):
        column = jnp.sum(jnp.where((lane == row) & (row <= HALF), packed[place : place + 1], 0.0), axis=1, keepdims=True)
        value = jnp.where(lane == HALF, column, jnp.where(lane % FB < HALF, value, 0.0))
        values.append(jnp.where(row <= HALF, value, 0.0))
    return values


def columns_of(mask, column_ref):
    high, low = split(mask)
    return dot(high, column_ref[0]) + dot(low, column_ref[0]) + dot(high, column_ref[1])


def spectrum_of(across, rows):
    high, low = split(across)
    both = dot(rows, jnp.concatenate([high, high, low], axis=0))
    even = both[:FA, : 2 * FB] - both[FA:, 2 * FB :]
    odd = both[FA:, : 2 * FB] + both[:FA, 2 * FB :]
    return even, odd


def open_kernel(
    part_ref, real_hbm, imag_hbm, thresholds_hbm, weights_hbm, forward_hbm, backward_hbm,
    out_ref, shares_ref, forward_ref, backward_ref, real_ref, imag_ref, thresholds_ref, weights_ref, stage, sems,
):
    part = part_of(part_ref)
    moves = [
        (real_hbm, real_ref),
        (imag_hbm, imag_ref),
        (thresholds_hbm, thresholds_ref),
        (weights_hbm, weights_ref),
        (forward_hbm.at[part], forward_ref),
        (backward_hbm.at[part], backward_ref),
    ]
    copies = [pltpu.make_async_copy(source, target, sems.at[i]) for i, (source, target) in enumerate(moves)]
    for copy in copies:
        copy.start()
    local_conds = real_ref.shape[0]
    mats = local_conds * KERNELS * 2
    stage[...] = jnp.zeros_like(stage)
    for copy in copies[:4]:
        copy.wait()
    for cond in range(local_conds):
        for kern in range(KERNELS):
            for piece, ref in enumerate((real_ref, imag_ref)):
                stage[(cond * KERNELS + kern) * 2 + piece, :KSUP, :KSUP] = ref[cond, :, kern, :]
    rows = stage.shape[1]
    source = lax.broadcasted_iota(jnp.int32, (2 * FB, 4 * FB), 0)
    target = lax.broadcasted_iota(jnp.int32, (2 * FB, 4 * FB), 1)
    lane = target % FB
    block = target // FB
    plus = (block == 0) | (block == 3)
    freq = jnp.where(lane < HALF, lane + 1, 0)
    used = (lane < HALF) | ((lane == HALF) & (block % 2 == 0))
    pick = (used & (source == jnp.where(plus, HALF + freq, HALF - freq))).astype(F32).astype(BF)
    high, low = split(stage[...].reshape(mats * rows, 2 * FB))
    picked = [dot(piece, pick) for piece in (high, low)]
    source = lax.broadcasted_iota(jnp.int32, (FA, 2 * rows), 1) % rows
    target = lax.broadcasted_iota(jnp.int32, (FA, 2 * rows), 0)
    turn = ((source == HALF - target) & (target <= HALF)).astype(F32).astype(BF)
    lane = lax.broadcasted_iota(jnp.int32, (FA, 2 * FB), 1)
    row = lax.broadcasted_iota(jnp.int32, (FA, 2 * FB), 0)
    valid = (row <= HALF) & ((lane <= HALF) | ((row > 0) & (lane >= FB) & (lane < FB + HALF)))
    scale = 1.0 / (FULL * FULL)
    keep_top = jnp.where(valid, scale, 0.0)
    keep_bottom = jnp.where((row == 0) & (lane == HALF), 0.0, keep_top)
    first = lane % FB < HALF
    extra = jnp.zeros((FA, 2 * FB), F32)
    blocks = []
    for kern in range(local_conds * KERNELS):
        arrays = [[], []]
        for piece in range(2):
            start = (kern * 2 + piece) * rows
            top = picked[0][start + HALF : start + HALF + FA, : 2 * FB] + picked[1][start + HALF : start + HALF + FA, : 2 * FB]
            pieces = jnp.concatenate([half[start : start + rows, 2 * FB :] for half in picked], axis=0)
            bottom = dot(turn, pieces.astype(BF)) * keep_bottom
            top = top * keep_top
            arrays[0].append(top + bottom)
            arrays[1].append(top - bottom)
        for which, (real, imag) in enumerate(arrays):
            blocks.append(jnp.where(first, real, pltpu.roll(imag, HALF, 1)))
            for piece, value in enumerate((real, imag)):
                place = kern * 4 + which * 2 + piece
                extra = jnp.where(lane == place, pltpu.roll(value, (place - HALF) % (2 * FB), 1), extra)
    for i, block in enumerate(blocks):
        if i < SPARE_BLOCKS:
            block = jnp.concatenate([block[: HALF + 1], extra[SPARE * i : SPARE * (i + 1)]], axis=0)
        elif i < SPARE_BLOCKS + local_conds:
            block = jnp.where(row == FA - 1, thresholds_ref[i - SPARE_BLOCKS], block)
        out_ref[i] = block
    weight_sum = weights_ref[0]
    for i in range(1, CONDS):
        weight_sum = weight_sum + weights_ref[i]
    row = lax.broadcasted_iota(jnp.int32, shares_ref.shape, 0)
    shares = jnp.zeros(shares_ref.shape, F32)
    for group, step in enumerate((0, 3, 1, 2)):
        for i in range(local_conds):
            weight = weights_ref[lax.bitwise_xor(part, step) * local_conds + i]
            shares = jnp.where(row == group * local_conds + i, weight.astype(F32), shares)
    shares_ref[...] = shares / weight_sum.astype(F32)
    for copy in copies[4:]:
        copy.wait()


def send_rim_kernel(part_ref, theta_hbm, waves_hbm, out_ref, theta_ref, waves_ref, sems):
    rows = pl.ds(pl.multiple_of(jnp.where(part_of(part_ref) == 0, 0, ROWS - HALO), HALO), HALO)
    copies = [
        pltpu.make_async_copy(theta_hbm.at[rows], theta_ref, sems.at[0]),
        pltpu.make_async_copy(waves_hbm, waves_ref, sems.at[1]),
    ]
    for copy in copies:
        copy.start()
    copies[0].wait()
    mask = jnp.tanh(mask_steep * theta_ref[...])
    copies[1].wait()
    out_ref[...] = columns_of(mask, waves_ref)


def spectrum_kernel(part_ref, theta_ref, column_ref, rows_ref, out_ref):
    across = columns_of(jnp.tanh(mask_steep * theta_ref[...]), column_ref)
    even, odd = spectrum_of(across, rows_ref[0])
    out_ref[0] = even
    out_ref[1] = odd


def rim_kernel(part_ref, spectrum_ref, rim_ref, rows_ref, out_ref):
    rim = rim_ref[...]
    turned = pltpu.roll(rim, FB, 1)
    first = lax.broadcasted_iota(jnp.int32, rim.shape, 1) < FB
    across = jnp.concatenate([jnp.where(first, rim, turned), jnp.where(first, turned, -rim)], axis=1)
    even, odd = spectrum_of(across, rows_ref[0])
    out_ref[0] = pack(even + spectrum_ref[0], odd + spectrum_ref[1])


def fields_kernel(
    part_ref, mixed_ref, other_ref, shares_ref, target_ref, forward_ref, backward_ref, row_ref,
    row_turned_ref, out_ref, kernels_ref, levels_ref, lines, folded, amps, tanhs, total, signs, turned, backs,
):
    count = kernels_ref.shape[0]
    local = count // PARTS
    tall = 4 * FA
    each = 2 * local
    even, odd = unpack(mixed_ref[2 * each] + other_ref[2 * each])
    lane, row = lanes_and_rows()
    zero_lane = (lane == HALF) & (row <= HALF)
    for group in range(PARTS):
        ref = (mixed_ref, other_ref)[group // 2].at[pl.ds(group % 2 * each, each)]
        extra = [ref[i][HALF + 1 :] for i in range(SPARE_BLOCKS)]
        extra = jnp.concatenate(extra + [jnp.zeros((FA - SPARE * SPARE_BLOCKS, 2 * FB), F32)], axis=0)
        for i in range(CONDS // PARTS):
            place = group * (CONDS // PARTS) + i
            levels_ref[place : place + 1] = ref[SPARE_BLOCKS + i][FA - 1 :]
        for kern in range(local):
            values = []
            for which in range(2):
                packed = ref[2 * kern + which]
                for part, value in enumerate((packed, pltpu.roll(packed, 2 * FB - HALF, 1))):
                    place = kern * 4 + which * 2 + part
                    zeroth = pltpu.roll(extra, (HALF - place) % (2 * FB), 1)
                    value = jnp.where(zero_lane, zeroth, value)
                    kernels_ref[group * local + kern, which * 2 + part] = value
                    values.append(value)
            he_real, he_imag, ho_real, ho_imag = values
            start = (group * local + kern) * tall
            for i, value in enumerate(
                (
                    even * he_real + odd * ho_imag,
                    odd * he_real - even * ho_imag,
                    even * he_imag - odd * ho_real,
                    odd * he_imag + even * ho_real,
                )
            ):
                lines[start + i * FA : start + (i + 1) * FA] = value

    high, low = split(lines[...])
    lines_folded = dot(jnp.concatenate([high, low], axis=1), forward_ref[: 4 * FB]) + dot(high, forward_ref[4 * FB :])
    for kern in range(count):
        parts = []
        for i in range(2):
            x_part = lines_folded[tall * kern + 2 * FA * i : tall * kern + 2 * FA * i + FA]
            y_part = lines_folded[tall * kern + 2 * FA * i + FA : tall * kern + 2 * FA * (i + 1)]
            parts.append(
                jnp.concatenate(
                    [x_part[:, :ROWS] + y_part[:, ROWS:], y_part[:, :ROWS] - x_part[:, ROWS:]], axis=0
                )
            )
        high, low = split(jnp.concatenate(parts, axis=1))
        folded[kern] = jnp.concatenate([high, high, low], axis=0)
    total[...] = jnp.zeros_like(total)
    signs[...] = 1.0 - 2.0 * target_ref[...].astype(F32)

    def expose(cond, carry):
        intensity = None
        for kern in range(KERNELS):
            index = cond * KERNELS + kern
            amp = dot(row_ref[...], folded[index])
            amps[index] = amp
            power = amp[:, :ROWS] * amp[:, :ROWS] + amp[:, ROWS:] * amp[:, ROWS:]
            intensity = power if intensity is None else intensity + power
        level = levels_ref[pl.ds(cond, 1), :]
        value = jnp.tanh((0.5 * resist_steep) * (intensity - level))
        tanhs[cond] = value
        total[...] += value
        return carry

    lax.fori_loop(0, CONDS, expose, 0, unroll=4)
    total[...] = total[...] * (band_weight / (CONDS * CONDS))

    def drive(cond, carry):
        weight = shares_ref[pl.ds(cond, 1), :]
        value = tanhs[cond]
        slope = (weight + band_weight / CONDS) * value + weight * signs[...] - total[...]
        field = (0.5 * resist_steep) * (1.0 - value * value) * slope
        field = jnp.concatenate([field, field], axis=1)
        for kern in range(KERNELS):
            index = cond * KERNELS + kern
            high, low = split(field * amps[index])
            long = dot(row_turned_ref[...], high)
            back = long[: 2 * FA] + long[2 * FA :] + dot(row_turned_ref[: 2 * FA], low)
            turned[pl.ds(index * 2, 2)] = jnp.stack([back[:, :ROWS], back[:, ROWS:]])
        return carry

    lax.fori_loop(0, CONDS, drive, 0, unroll=4)
    high, low = split(turned[...].reshape(count * tall, ROWS))
    backs[...] = dot(jnp.concatenate([high, low], axis=1), backward_ref[: 2 * ROWS]) + dot(high, backward_ref[2 * ROWS :])

    sum_even = jnp.zeros((FA, 2 * FB), F32)
    sum_odd = jnp.zeros((FA, 2 * FB), F32)
    for kern in range(count):
        grads = []
        for i in range(2):
            c_part = backs[tall * kern + 2 * FA * i : tall * kern + 2 * FA * i + FA]
            s_part = backs[tall * kern + 2 * FA * i + FA : tall * kern + 2 * FA * (i + 1)]
            grads.append(
                (
                    c_part[:, : 2 * FB] - s_part[:, 2 * FB :],
                    s_part[:, : 2 * FB] + c_part[:, 2 * FB :],
                )
            )
        (x_real, y_real), (x_imag, y_imag) = grads
        he_real, he_imag, ho_real, ho_imag = (kernels_ref[kern, i] for i in range(4))
        sum_even = sum_even + x_real * he_real + x_imag * he_imag - y_real * ho_imag + y_imag * ho_real
        sum_odd = sum_odd + x_real * ho_imag - x_imag * ho_real + y_real * he_real + y_imag * he_imag
    out_ref[...] = pack(sum_even, sum_odd)


def image_rows(packed, rows, turned_ref):
    high, low = split(jnp.concatenate(unpack(packed), axis=0))
    pair = dot(rows, jnp.concatenate([high, high, low], axis=0))
    count = pair.shape[0] // 2
    high, low = split(jnp.concatenate([pair[:count], pair[count:]], axis=1))
    return dot(high, turned_ref[0]) + dot(low, turned_ref[0]) + dot(high, turned_ref[1])


def edge_start(part_ref):
    return pl.multiple_of(jnp.where(part_of(part_ref) == PARTS - 1, ROWS - HALO, 0), HALO)


def gradient_kernel(part_ref, theta_ref, sum_ref, turned_ref, rows_ref, out_ref, edge_ref, scale_ref):
    part = part_of(part_ref)
    mask = jnp.tanh(mask_steep * theta_ref[...])
    scale = mask_steep * (1.0 - mask * mask)
    gradient = image_rows(sum_ref[...], rows_ref[0], turned_ref) * scale
    out_ref[...] = gradient
    last = part == PARTS - 1
    edge_ref[...] = jnp.where(last, gradient[ROWS - HALO :], gradient[:HALO])
    scale_ref[...] = jnp.where(last, scale[ROWS - HALO :], scale[:HALO])


def edge_kernel(part_ref, gradient_hbm, edge_ref, scale_ref, near_ref, turned_ref, rows_ref, out_hbm, stage, sem):
    rim = image_rows(near_ref[...], rows_ref[0], turned_ref) * scale_ref[...]
    stage[...] = edge_ref[...] + jnp.where(has_halo(part_ref), rim, 0.0)
    copy = pltpu.make_async_copy(stage, out_hbm.at[pl.ds(edge_start(part_ref), HALO)], sem)
    copy.start()
    copy.wait()


def whole_spec(array):
    rank = len(array.shape)
    return pl.BlockSpec(array.shape, lambda i, *refs: (0,) * rank)


def part_spec(array):
    rank = len(array.shape)
    return pl.BlockSpec((1,) + array.shape[1:], lambda i, part, *refs: (part_of(part),) + (0,) * (rank - 1))


def call(kernel, scalars, operands, specs, out_shapes, scratch=(), name=None, flops=1 << 28, out_specs=None, aliases=None):
    many = isinstance(out_shapes, list)
    if out_specs is None:
        out_specs = [whole_spec(shape) for shape in out_shapes] if many else whole_spec(out_shapes)
    return pl.pallas_call(
        kernel,
        grid_spec=pltpu.PrefetchScalarGridSpec(
            num_scalar_prefetch=len(scalars),
            grid=(1,),
            in_specs=specs,
            out_specs=out_specs,
            scratch_shapes=list(scratch),
        ),
        out_shape=out_shapes,
        input_output_aliases=aliases or {},
        compiler_params=pltpu.CompilerParams(vmem_limit_bytes=48 * 1024 * 1024),
        cost_estimate=pl.CostEstimate(flops=flops, bytes_accessed=1 << 20, transcendentals=0),
        name=name,
    )(*scalars, *operands)


def floats(*shape):
    return jax.ShapeDtypeStruct(shape, F32)


def shards(theta, target, kernel_real, kernel_imag, weights, thresholds):
    table = {name: jnp.asarray(value) for name, value in tables().items()}
    tiles = lax.axis_size("tile")
    part = lax.axis_index("cond")
    tile = lax.axis_index("tile")
    last = PARTS - 1
    above = ((part == 0) & (tile > 0)) | ((part == last) & (tile < tiles - 1))
    parts = (part + PARTS * above.astype(jnp.int32)).reshape(1).astype(jnp.int32)
    local_conds = kernel_real.shape[0]
    local = local_conds * KERNELS
    count = CONDS * KERNELS
    hbm = pl.BlockSpec(memory_space=pltpu.HBM)

    def across(value, down, up, within=()):
        pairs = [(PARTS * i + a, PARTS * i + b) for i in range(tiles) for a, b in within]
        pairs += [(PARTS * (i + 1) + down[0], PARTS * i + down[1]) for i in range(tiles - 1)]
        pairs += [(PARTS * i + up[0], PARTS * (i + 1) + up[1]) for i in range(tiles - 1)]
        if within:
            pairs += [(down[0], up[1]), (PARTS * (tiles - 1) + up[0], PARTS * (tiles - 1) + down[1])]
        return lax.ppermute(value, ("tile", "cond"), pairs)

    def partner(value, step):
        return lax.ppermute(value, "cond", [(i, i ^ step) for i in range(PARTS)])

    kernel_shape = (local_conds, KSUP, KERNELS, KSUP)
    own, shares, forward, backward = call(
        open_kernel,
        (parts,),
        tuple(
            pltpu.with_memory_space_constraint(value, pltpu.HBM)
            for value in (
                kernel_real.transpose(0, 2, 1, 3), kernel_imag.transpose(0, 2, 1, 3), thresholds, weights,
                table["forward"], table["backward"],
            )
        ),
        [hbm] * 6,
        [
            floats(2 * local, FA, 2 * FB),
            floats(CONDS, ROWS),
            jax.ShapeDtypeStruct(table["forward"].shape[1:], BF),
            jax.ShapeDtypeStruct(table["backward"].shape[1:], BF),
        ],
        scratch=(
            pltpu.VMEM(kernel_shape, F32),
            pltpu.VMEM(kernel_shape, F32),
            pltpu.SMEM(thresholds.shape, F32),
            pltpu.SMEM(weights.shape, jnp.int32),
            pltpu.VMEM((2 * local, 72, 2 * FB), F32),
            pltpu.SemaphoreType.DMA((6,)),
        ),
        name="open_parts",
    )
    rim = call(
        send_rim_kernel,
        (parts,),
        tuple(pltpu.with_memory_space_constraint(value, pltpu.HBM) for value in (theta, table["waves"])),
        [hbm, hbm],
        floats(HALO, 2 * FB),
        scratch=(
            pltpu.VMEM((HALO, TP), F32),
            pltpu.VMEM(table["waves"].shape, BF),
            pltpu.SemaphoreType.DMA((2,)),
        ),
        name="edge_columns",
    )
    rim = across(rim, (0, 0), (last, last))
    spectrum = call(
        spectrum_kernel,
        (parts,),
        (theta, table["column"], table["spectrum_rows"]),
        [whole_spec(theta), whole_spec(table["column"]), part_spec(table["spectrum_rows"])],
        floats(2, FA, 2 * FB),
        name="own_spectrum",
        flops=1 << 31,
    )
    side = partner(own, 3)
    spectrum = call(
        rim_kernel,
        (parts,),
        (spectrum, rim, table["rim_rows"]),
        [whole_spec(spectrum), whole_spec(rim), part_spec(table["rim_rows"])],
        floats(1, FA, 2 * FB),
        name="add_rim",
    )
    mixed = jnp.concatenate([own, side, spectrum + partner(spectrum, 3)], axis=0)
    adjoint = call(
        fields_kernel,
        (parts,),
        (mixed, partner(mixed, 1), shares, target, forward, backward, table["row"], table["row_turned"]),
        [
            whole_spec(mixed),
            whole_spec(mixed),
            whole_spec(shares),
            pl.BlockSpec((TP, ROWS), lambda i, part, *refs: (0, part_of(part))),
            whole_spec(forward),
            whole_spec(backward),
            whole_spec(table["row"]),
            whole_spec(table["row_turned"]),
        ],
        floats(FA, 2 * FB),
        scratch=(
            pltpu.VMEM((count, 4, FA, 2 * FB), F32),
            pltpu.VMEM((CONDS, ROWS), F32),
            pltpu.VMEM((count * 4 * FA, 2 * FB), F32),
            pltpu.VMEM((count, 6 * FA, 2 * ROWS), BF),
            pltpu.VMEM((count, TP, 2 * ROWS), F32),
            pltpu.VMEM((CONDS, TP, ROWS), F32),
            pltpu.VMEM((TP, ROWS), F32),
            pltpu.VMEM((TP, ROWS), F32),
            pltpu.VMEM((count * 2, 2 * FA, ROWS), F32),
            pltpu.VMEM((count * 4 * FA, 4 * FB), F32),
        ),
        name="coherent_fields",
        flops=1 << 33,
    )
    adjoint = adjoint + partner(adjoint, 1)
    adjoint = adjoint + partner(adjoint, 3)
    near = across(adjoint, (2, last), (1, 0), within=[(0, 1), (last, 2)])
    gradient, edge, scale = call(
        gradient_kernel,
        (parts,),
        (theta, adjoint, table["turned"], table["own_rows"]),
        [
            whole_spec(theta),
            whole_spec(adjoint),
            whole_spec(table["turned"]),
            part_spec(table["own_rows"]),
        ],
        [floats(ROWS, TP), floats(HALO, TP), floats(HALO, TP)],
        name="own_gradient",
        flops=1 << 31,
    )
    return call(
        edge_kernel,
        (parts,),
        (gradient, edge, scale, near, table["turned"], table["halo_rows"]),
        [
            hbm,
            whole_spec(edge),
            whole_spec(scale),
            whole_spec(near),
            whole_spec(table["turned"]),
            part_spec(table["halo_rows"]),
        ],
        floats(ROWS, TP),
        scratch=(pltpu.VMEM((HALO, TP), F32), pltpu.SemaphoreType.DMA),
        name="edge_gradient",
        out_specs=hbm,
        aliases={1: 0},
    )


def solution(mesh):
    in_specs = (
        P(("tile", "cond"), None),
        P("tile", None),
        P("cond", None, None, None),
        P("cond", None, None, None),
        P(),
        P("cond"),
    )
    out_specs = P(("tile", "cond"), None)
    return jax.shard_map(shards, mesh=mesh, in_specs=in_specs, out_specs=out_specs, check_vma=False)
```

```python
import functools

import jax
import jax.numpy as jnp
import ml_dtypes
import numpy as np
from jax import lax
from jax.experimental import pallas as pl
from jax.experimental.pallas import tpu as pltpu
from jax.sharding import PartitionSpec as P

TP = 512
HALO = 32
KSUP = 65
HALF = KSUP // 2
KERNELS = 2
CONDS = 8
FULL = TP + 2 * HALO
PARTS = 4
ROWS = TP // PARTS
FA = 40
FB = 64
SPARE = FA - HALF - 1
SPARE_BLOCKS = -(-(HALF + 1) // SPARE)
BF = jnp.bfloat16
F32 = jnp.float32

mask_steep = 2.0
resist_steep = 4.0
band_weight = 1.0


def waves(positions):
    angles = (np.outer(np.asarray(positions, np.int64), np.arange(HALF + 1)) % FULL) * (2.0 * np.pi / FULL)
    return np.cos(angles), np.sin(angles)


def halves(table):
    high = table.astype(np.float32).astype(ml_dtypes.bfloat16)
    low = (table - high.astype(np.float64)).astype(np.float32).astype(ml_dtypes.bfloat16)
    return high, low


def row_table(positions):
    cosine, sine = waves(positions)
    table = np.zeros((len(positions), 2 * FA))
    table[:, : HALF + 1] = cosine
    table[:, FA : FA + HALF + 1] = sine
    return table


def pair_table(positions):
    table = row_table(positions)
    return np.concatenate([table, np.concatenate([-table[:, FA:], table[:, :FA]], axis=1)])


def column_table(positions):
    cosine, sine = waves(positions)
    table = np.zeros((len(positions), 4 * FB))
    for block, values in enumerate((cosine, cosine, sine, -sine)):
        table[:, block * FB : block * FB + HALF] = values[:, 1:]
    table[:, HALF] = 1.0
    return table


def folded_table(positions):
    cosine, sine = waves(positions)
    count = len(positions)
    table = np.zeros((2, count, 2, 2, 2, HALF))
    for part in range(2):
        for block, sign in enumerate((1.0, -1.0)):
            table[part, :, 0, block, part] = cosine[:, 1:]
            table[part, :, 1, block, part] = sign * sine[:, 1:]
    return table.reshape(2 * count, 4 * FB)


def forward_table(positions):
    count = len(positions)
    table = folded_table(positions).reshape(2, count, 2, 2 * FB).transpose(3, 2, 0, 1).reshape(2 * FB, 4 * count)
    high, low = halves(table)
    zeroth = np.zeros((2 * FB, 4, count), ml_dtypes.bfloat16)
    for lane in range(4):
        zeroth[lane, lane % 2] = 1
    return np.concatenate([high, high, low, zeroth.reshape(2 * FB, 4 * count)])


@functools.cache
def tables():
    pixels = np.arange(TP) + HALO
    column = column_table(pixels)
    column_high, column_low = halves(column)
    row = row_table(pixels)
    row_high, row_low = halves(row)
    out = {}
    out["column"] = np.stack([column_high, column_low])
    waves_only = np.s_[:, np.r_[0:FB, 2 * FB : 3 * FB]]
    out["waves"] = np.stack([column_high[waves_only], column_low[waves_only]])
    spectrum_rows = []
    rim_rows = []
    halo_rows = []
    own_rows = []
    forward = []
    backward = []
    for part in range(PARTS):
        own = np.arange(ROWS) + part * ROWS + HALO
        rim = np.arange(HALO) + (0 if part == PARTS - 1 else FULL - HALO)
        for rows, positions in ((spectrum_rows, own), (rim_rows, rim)):
            high, low = halves(row_table(positions).T)
            rows.append(np.concatenate([high, low, high], axis=1))
        high, low = halves(pair_table(rim))
        halo_rows.append(np.concatenate([high, low, high], axis=1))
        high, low = halves(pair_table(own))
        own_rows.append(np.concatenate([high, low, high], axis=1))
        forward.append(forward_table(own))
        backward.append(np.concatenate(halves(folded_table(own))))
    out["spectrum_rows"] = np.stack(spectrum_rows)
    out["own_rows"] = np.stack(own_rows)
    out["rim_rows"] = np.stack(rim_rows)
    out["halo_rows"] = np.stack(halo_rows)
    out["forward"] = np.stack(forward)
    out["backward"] = np.stack(backward)
    out["turned"] = np.stack([column_high.T, column_low.T])
    out["row"] = np.concatenate([row_high, row_low, row_high], axis=1)
    out["row_turned"] = np.concatenate([row_high.T, row_low.T])
    return out


def part_of(ref):
    return ref[0] % PARTS


def has_halo(ref):
    return ref[0] // PARTS > 0


def dot(left, right):
    return jnp.dot(left, right, preferred_element_type=F32)


def split(value):
    high = value.astype(BF)
    return high, (value - high.astype(F32)).astype(BF)


def lanes_and_rows():
    shape = (FA, 2 * FB)
    return lax.broadcasted_iota(jnp.int32, shape, 1), lax.broadcasted_iota(jnp.int32, shape, 0)


def pack(even, odd):
    lane, row = lanes_and_rows()
    packed = jnp.where(lane % FB < HALF, even, pltpu.roll(odd, HALF, 1))
    for place, value in ((FA - 2, even), (FA - 3, odd)):
        line = jnp.sum(jnp.where(lane == row, value[:, HALF : HALF + 1], 0.0), axis=0, keepdims=True)
        packed = jnp.where(row == place, line, packed)
    return packed


def unpack(packed):
    lane, row = lanes_and_rows()
    values = []
    for place, value in ((FA - 2, packed), (FA - 3, pltpu.roll(packed, 2 * FB - HALF, 1))):
        column = jnp.sum(jnp.where((lane == row) & (row <= HALF), packed[place : place + 1], 0.0), axis=1, keepdims=True)
        value = jnp.where(lane == HALF, column, jnp.where(lane % FB < HALF, value, 0.0))
        values.append(jnp.where(row <= HALF, value, 0.0))
    return values


def columns_of(mask, column_ref):
    high, low = split(mask)
    return dot(high, column_ref[0]) + dot(low, column_ref[0]) + dot(high, column_ref[1])


def spectrum_of(across, rows):
    high, low = split(across)
    both = dot(rows, jnp.concatenate([high, high, low], axis=0))
    even = both[:FA, : 2 * FB] - both[FA:, 2 * FB :]
    odd = both[FA:, : 2 * FB] + both[:FA, 2 * FB :]
    return even, odd


def open_kernel(
    part_ref, real_hbm, imag_hbm, thresholds_hbm, weights_hbm, forward_hbm, backward_hbm,
    out_ref, shares_ref, forward_ref, backward_ref, real_ref, imag_ref, thresholds_ref, weights_ref, stage, sems,
):
    part = part_of(part_ref)
    moves = [
        (real_hbm, real_ref),
        (imag_hbm, imag_ref),
        (thresholds_hbm, thresholds_ref),
        (weights_hbm, weights_ref),
        (forward_hbm.at[part], forward_ref),
        (backward_hbm.at[part], backward_ref),
    ]
    copies = [pltpu.make_async_copy(source, target, sems.at[i]) for i, (source, target) in enumerate(moves)]
    for copy in copies:
        copy.start()
    local_conds = real_ref.shape[0]
    mats = local_conds * KERNELS * 2
    stage[...] = jnp.zeros_like(stage)
    for copy in copies[:4]:
        copy.wait()
    for cond in range(local_conds):
        for kern in range(KERNELS):
            for piece, ref in enumerate((real_ref, imag_ref)):
                stage[(cond * KERNELS + kern) * 2 + piece, :KSUP, :KSUP] = ref[cond, :, kern, :]
    rows = stage.shape[1]
    source = lax.broadcasted_iota(jnp.int32, (2 * FB, 4 * FB), 0)
    target = lax.broadcasted_iota(jnp.int32, (2 * FB, 4 * FB), 1)
    lane = target % FB
    block = target // FB
    plus = (block == 0) | (block == 3)
    freq = jnp.where(lane < HALF, lane + 1, 0)
    used = (lane < HALF) | ((lane == HALF) & (block % 2 == 0))
    pick = (used & (source == jnp.where(plus, HALF + freq, HALF - freq))).astype(F32).astype(BF)
    high, low = split(stage[...].reshape(mats * rows, 2 * FB))
    picked = [dot(piece, pick) for piece in (high, low)]
    source = lax.broadcasted_iota(jnp.int32, (FA, 2 * rows), 1) % rows
    target = lax.broadcasted_iota(jnp.int32, (FA, 2 * rows), 0)
    turn = ((source == HALF - target) & (target <= HALF)).astype(F32).astype(BF)
    lane = lax.broadcasted_iota(jnp.int32, (FA, 2 * FB), 1)
    row = lax.broadcasted_iota(jnp.int32, (FA, 2 * FB), 0)
    valid = (row <= HALF) & ((lane <= HALF) | ((row > 0) & (lane >= FB) & (lane < FB + HALF)))
    scale = 1.0 / (FULL * FULL)
    keep_top = jnp.where(valid, scale, 0.0)
    keep_bottom = jnp.where((row == 0) & (lane == HALF), 0.0, keep_top)
    first = lane % FB < HALF
    extra = jnp.zeros((FA, 2 * FB), F32)
    blocks = []
    for kern in range(local_conds * KERNELS):
        arrays = [[], []]
        for piece in range(2):
            start = (kern * 2 + piece) * rows
            top = picked[0][start + HALF : start + HALF + FA, : 2 * FB] + picked[1][start + HALF : start + HALF + FA, : 2 * FB]
            pieces = jnp.concatenate([half[start : start + rows, 2 * FB :] for half in picked], axis=0)
            bottom = dot(turn, pieces.astype(BF)) * keep_bottom
            top = top * keep_top
            arrays[0].append(top + bottom)
            arrays[1].append(top - bottom)
        (he_real, he_imag), (ho_real, ho_imag) = arrays
        for which, pair in enumerate(((he_real, he_imag), (ho_imag, -ho_real))):
            blocks.append(jnp.where(first, pair[0], pltpu.roll(pair[1], HALF, 1)))
            for piece, value in enumerate(pair):
                place = which * FB + kern * 4 + piece
                extra = jnp.where(lane == place, pltpu.roll(value, (place - HALF) % (2 * FB), 1), extra)
    for i, block in enumerate(blocks):
        if i < SPARE_BLOCKS:
            block = jnp.concatenate([block[: HALF + 1], extra[SPARE * i : SPARE * (i + 1)]], axis=0)
        elif i < SPARE_BLOCKS + local_conds:
            block = jnp.where(row == FA - 1, thresholds_ref[i - SPARE_BLOCKS], block)
        out_ref[i] = block
    weight_sum = weights_ref[0]
    for i in range(1, CONDS):
        weight_sum = weight_sum + weights_ref[i]
    row = lax.broadcasted_iota(jnp.int32, shares_ref.shape, 0)
    shares = jnp.zeros(shares_ref.shape, F32)
    for group, step in enumerate((0, 3, 1, 2)):
        for i in range(local_conds):
            weight = weights_ref[lax.bitwise_xor(part, step) * local_conds + i]
            shares = jnp.where(row == group * local_conds + i, weight.astype(F32), shares)
    shares_ref[...] = shares / weight_sum.astype(F32)
    for copy in copies[4:]:
        copy.wait()


def send_rim_kernel(part_ref, theta_hbm, waves_hbm, out_ref, theta_ref, waves_ref, sems):
    rows = pl.ds(pl.multiple_of(jnp.where(part_of(part_ref) == 0, 0, ROWS - HALO), HALO), HALO)
    copies = [
        pltpu.make_async_copy(theta_hbm.at[rows], theta_ref, sems.at[0]),
        pltpu.make_async_copy(waves_hbm, waves_ref, sems.at[1]),
    ]
    for copy in copies:
        copy.start()
    copies[0].wait()
    mask = jnp.tanh(mask_steep * theta_ref[...])
    copies[1].wait()
    out_ref[...] = columns_of(mask, waves_ref)


def spectrum_kernel(part_ref, theta_ref, column_ref, rows_ref, out_ref):
    across = columns_of(jnp.tanh(mask_steep * theta_ref[...]), column_ref)
    even, odd = spectrum_of(across, rows_ref[0])
    out_ref[0] = even
    out_ref[1] = odd


def rim_kernel(part_ref, spectrum_ref, rim_ref, rows_ref, out_ref):
    rim = rim_ref[...]
    turned = pltpu.roll(rim, FB, 1)
    first = lax.broadcasted_iota(jnp.int32, rim.shape, 1) < FB
    across = jnp.concatenate([jnp.where(first, rim, turned), jnp.where(first, turned, -rim)], axis=1)
    even, odd = spectrum_of(across, rows_ref[0])
    out_ref[0] = pack(even + spectrum_ref[0], odd + spectrum_ref[1])


def fields_kernel(
    part_ref, mixed_ref, other_ref, shares_ref, target_ref, forward_ref, backward_ref, row_ref,
    row_turned_ref, out_ref, extras_ref, levels_ref, lines, zeroth, folded, amps, tanhs, total, signs, turned,
):
    count = folded.shape[0]
    local = count // PARTS
    tall = 2 * FA
    each = 2 * local
    lane, row = lanes_and_rows()
    first = lane % FB < HALF
    packed = mixed_ref[2 * each] + other_ref[2 * each]
    even_0, odd_0 = (
        jnp.sum(jnp.where((lane == row) & (row <= HALF), packed[place : place + 1], 0.0), axis=1, keepdims=True)
        for place in (FA - 2, FA - 3)
    )
    packed = jnp.where(row <= HALF, packed, 0.0)
    even = jnp.where(first, packed, pltpu.roll(packed, HALF, 1))
    odd = jnp.where(first, pltpu.roll(packed, 2 * FB - HALF, 1), packed)

    def blocks_of(group):
        return (mixed_ref, other_ref)[group // 2].at[pl.ds(group % 2 * each, each)]

    for group in range(PARTS):
        ref = blocks_of(group)
        extra = [ref[i][HALF + 1 :] for i in range(SPARE_BLOCKS)]
        extra = jnp.concatenate(extra + [jnp.zeros((FA - SPARE * SPARE_BLOCKS, 2 * FB), F32)], axis=0)
        extra_b = pltpu.roll(extra, FB, 1)
        extras_ref[group, 0] = extra
        extras_ref[group, 1] = extra_b
        for i in range(CONDS // PARTS):
            place = group * (CONDS // PARTS) + i
            levels_ref[place : place + 1] = ref[SPARE_BLOCKS + i][FA - 1 :]
        columns = []
        for value in (even_0 * extra + odd_0 * extra_b, odd_0 * extra - even_0 * extra_b):
            high = value.astype(BF).astype(F32)
            columns.append(jnp.where(lane % 4 < 2, high, pltpu.roll(value - high, 2, 1)))
        for kern in range(local):
            start = (group * local + kern) * tall
            a_block, b_block = ref[2 * kern], ref[2 * kern + 1]
            lines[start : start + FA] = even * a_block + odd * b_block
            lines[start + FA : start + tall] = odd * a_block - even * b_block
            for i, value in enumerate(columns):
                value = pltpu.roll(value, 2 * FB - 4 * kern, 1) if kern else value
                zeroth[start + FA * i : start + FA * (i + 1)] = value

    high, low = split(lines[...])
    lines_folded = dot(jnp.concatenate([high, low], axis=1), forward_ref[: 4 * FB])
    lines_folded += dot(jnp.concatenate([high, zeroth[...].astype(BF)], axis=1), forward_ref[4 * FB :])
    for kern in range(count):
        x_part = lines_folded[tall * kern : tall * kern + FA]
        y_part = lines_folded[tall * kern + FA : tall * (kern + 1)]
        both = jnp.concatenate(
            [
                x_part[:, : 2 * ROWS] + y_part[:, 2 * ROWS :],
                y_part[:, : 2 * ROWS] - x_part[:, 2 * ROWS :],
            ],
            axis=0,
        )
        high, low = split(both)
        folded[kern] = jnp.concatenate([high, high, low], axis=0)
    total[...] = jnp.zeros_like(total)
    signs[...] = 1.0 - 2.0 * target_ref[...].astype(F32)

    def expose(cond, carry):
        intensity = None
        for kern in range(KERNELS):
            index = cond * KERNELS + kern
            amp = dot(row_ref[...], folded[index])
            amps[index] = amp
            power = amp[:, :ROWS] * amp[:, :ROWS] + amp[:, ROWS:] * amp[:, ROWS:]
            intensity = power if intensity is None else intensity + power
        level = levels_ref[pl.ds(cond, 1), :]
        value = jnp.tanh((0.5 * resist_steep) * (intensity - level))
        tanhs[cond] = value
        total[...] += value
        return carry

    lax.fori_loop(0, CONDS, expose, 0, unroll=4)
    total[...] = total[...] * (band_weight / (CONDS * CONDS))

    def drive(cond, carry):
        weight = shares_ref[pl.ds(cond, 1), :]
        value = tanhs[cond]
        slope = (weight + band_weight / CONDS) * value + weight * signs[...] - total[...]
        field = (0.5 * resist_steep) * (1.0 - value * value) * slope
        field = jnp.concatenate([field, field], axis=1)
        for kern in range(KERNELS):
            index = cond * KERNELS + kern
            high, low = split(field * amps[index])
            long = dot(row_turned_ref[...], high)
            back = long[: 2 * FA] + long[2 * FA :] + dot(row_turned_ref[: 2 * FA], low)
            turned[index] = back
        return carry

    lax.fori_loop(0, CONDS, drive, 0, unroll=4)
    high, low = split(turned[...].reshape(count * tall, 2 * ROWS))
    backs = dot(high, backward_ref[: 2 * ROWS]) + dot(low, backward_ref[: 2 * ROWS]) + dot(high, backward_ref[2 * ROWS :])
    sum_even = jnp.zeros((FA, 2 * FB), F32)
    sum_odd = jnp.zeros((FA, 2 * FB), F32)
    lines_even = jnp.zeros((FA, 2 * FB), F32)
    lines_odd = jnp.zeros((FA, 2 * FB), F32)
    for group in range(PARTS):
        ref = blocks_of(group)
        sums = [jnp.zeros((FA, 2 * FB), F32)] * 2
        for kern in range(local):
            start = (group * local + kern) * tall
            c_part, s_part = backs[start : start + FA], backs[start + FA : start + tall]
            x_grad = c_part[:, : 2 * FB] - s_part[:, 2 * FB :]
            y_grad = s_part[:, : 2 * FB] + c_part[:, 2 * FB :]
            a_block, b_block = ref[2 * kern], ref[2 * kern + 1]
            sum_even = sum_even + x_grad * a_block - y_grad * b_block
            sum_odd = sum_odd + x_grad * b_block + y_grad * a_block
            back = turned[group * local + kern]
            for i in range(2):
                for piece in range(2):
                    whole = back[FA * i : FA * (i + 1), ROWS * piece : ROWS * (piece + 1)]
                    whole = jnp.sum(whole, axis=1, keepdims=True)
                    sums[i] = jnp.where(lane == 4 * kern + piece, whole, sums[i])
        lines_even = lines_even + sums[0] * extras_ref[group, 0] - sums[1] * extras_ref[group, 1]
        lines_odd = lines_odd + sums[0] * extras_ref[group, 1] + sums[1] * extras_ref[group, 0]
    value = jnp.where(first, sum_even + pltpu.roll(sum_even, 2 * FB - HALF, 1), sum_odd + pltpu.roll(sum_odd, HALF, 1))
    for place, columns in ((FA - 2, lines_even), (FA - 3, lines_odd)):
        column = jnp.sum(columns, axis=1, keepdims=True)
        line = jnp.sum(jnp.where((lane == row) & (row <= HALF), column, 0.0), axis=0, keepdims=True)
        value = jnp.where(row == place, line, value)
    out_ref[...] = value


def image_rows(packed, rows, turned_ref):
    high, low = split(jnp.concatenate(unpack(packed), axis=0))
    pair = dot(rows, jnp.concatenate([high, high, low], axis=0))
    count = pair.shape[0] // 2
    high, low = split(jnp.concatenate([pair[:count], pair[count:]], axis=1))
    return dot(high, turned_ref[0]) + dot(low, turned_ref[0]) + dot(high, turned_ref[1])


def edge_start(part_ref):
    return pl.multiple_of(jnp.where(part_of(part_ref) == PARTS - 1, ROWS - HALO, 0), HALO)


def gradient_kernel(part_ref, theta_ref, sum_ref, turned_ref, rows_ref, out_ref, edge_ref, scale_ref):
    part = part_of(part_ref)
    mask = jnp.tanh(mask_steep * theta_ref[...])
    scale = mask_steep * (1.0 - mask * mask)
    gradient = image_rows(sum_ref[...], rows_ref[0], turned_ref) * scale
    out_ref[...] = gradient
    last = part == PARTS - 1
    edge_ref[...] = jnp.where(last, gradient[ROWS - HALO :], gradient[:HALO])
    scale_ref[...] = jnp.where(last, scale[ROWS - HALO :], scale[:HALO])


def edge_kernel(part_ref, gradient_hbm, edge_ref, scale_ref, near_ref, turned_ref, rows_ref, out_hbm, stage, sem):
    rim = image_rows(near_ref[...], rows_ref[0], turned_ref) * scale_ref[...]
    stage[...] = edge_ref[...] + jnp.where(has_halo(part_ref), rim, 0.0)
    copy = pltpu.make_async_copy(stage, out_hbm.at[pl.ds(edge_start(part_ref), HALO)], sem)
    copy.start()
    copy.wait()


def whole_spec(array):
    rank = len(array.shape)
    return pl.BlockSpec(array.shape, lambda i, *refs: (0,) * rank)


def part_spec(array):
    rank = len(array.shape)
    return pl.BlockSpec((1,) + array.shape[1:], lambda i, part, *refs: (part_of(part),) + (0,) * (rank - 1))


def call(kernel, scalars, operands, specs, out_shapes, scratch=(), name=None, flops=1 << 28, out_specs=None, aliases=None):
    many = isinstance(out_shapes, list)
    if out_specs is None:
        out_specs = [whole_spec(shape) for shape in out_shapes] if many else whole_spec(out_shapes)
    return pl.pallas_call(
        kernel,
        grid_spec=pltpu.PrefetchScalarGridSpec(
            num_scalar_prefetch=len(scalars),
            grid=(1,),
            in_specs=specs,
            out_specs=out_specs,
            scratch_shapes=list(scratch),
        ),
        out_shape=out_shapes,
        input_output_aliases=aliases or {},
        compiler_params=pltpu.CompilerParams(vmem_limit_bytes=48 * 1024 * 1024),
        cost_estimate=pl.CostEstimate(flops=flops, bytes_accessed=1 << 20, transcendentals=0),
        name=name,
    )(*scalars, *operands)


def floats(*shape):
    return jax.ShapeDtypeStruct(shape, F32)


def shards(theta, target, kernel_real, kernel_imag, weights, thresholds):
    table = {name: jnp.asarray(value) for name, value in tables().items()}
    tiles = lax.axis_size("tile")
    part = lax.axis_index("cond")
    tile = lax.axis_index("tile")
    last = PARTS - 1
    above = ((part == 0) & (tile > 0)) | ((part == last) & (tile < tiles - 1))
    parts = (part + PARTS * above.astype(jnp.int32)).reshape(1).astype(jnp.int32)
    local_conds = kernel_real.shape[0]
    local = local_conds * KERNELS
    count = CONDS * KERNELS
    hbm = pl.BlockSpec(memory_space=pltpu.HBM)

    def across(value, down, up, within=()):
        pairs = [(PARTS * i + a, PARTS * i + b) for i in range(tiles) for a, b in within]
        pairs += [(PARTS * (i + 1) + down[0], PARTS * i + down[1]) for i in range(tiles - 1)]
        pairs += [(PARTS * i + up[0], PARTS * (i + 1) + up[1]) for i in range(tiles - 1)]
        if within:
            pairs += [(down[0], up[1]), (PARTS * (tiles - 1) + up[0], PARTS * (tiles - 1) + down[1])]
        return lax.ppermute(value, ("tile", "cond"), pairs)

    def partner(value, step):
        return lax.ppermute(value, "cond", [(i, i ^ step) for i in range(PARTS)])

    kernel_shape = (local_conds, KSUP, KERNELS, KSUP)
    own, shares, forward, backward = call(
        open_kernel,
        (parts,),
        tuple(
            pltpu.with_memory_space_constraint(value, pltpu.HBM)
            for value in (
                kernel_real.transpose(0, 2, 1, 3), kernel_imag.transpose(0, 2, 1, 3), thresholds, weights,
                table["forward"], table["backward"],
            )
        ),
        [hbm] * 6,
        [
            floats(2 * local, FA, 2 * FB),
            floats(CONDS, ROWS),
            jax.ShapeDtypeStruct(table["forward"].shape[1:], BF),
            jax.ShapeDtypeStruct(table["backward"].shape[1:], BF),
        ],
        scratch=(
            pltpu.VMEM(kernel_shape, F32),
            pltpu.VMEM(kernel_shape, F32),
            pltpu.SMEM(thresholds.shape, F32),
            pltpu.SMEM(weights.shape, jnp.int32),
            pltpu.VMEM((2 * local, 72, 2 * FB), F32),
            pltpu.SemaphoreType.DMA((6,)),
        ),
        name="open_parts",
    )
    rim = call(
        send_rim_kernel,
        (parts,),
        tuple(pltpu.with_memory_space_constraint(value, pltpu.HBM) for value in (theta, table["waves"])),
        [hbm, hbm],
        floats(HALO, 2 * FB),
        scratch=(
            pltpu.VMEM((HALO, TP), F32),
            pltpu.VMEM(table["waves"].shape, BF),
            pltpu.SemaphoreType.DMA((2,)),
        ),
        name="edge_columns",
    )
    rim = across(rim, (0, 0), (last, last))
    spectrum = call(
        spectrum_kernel,
        (parts,),
        (theta, table["column"], table["spectrum_rows"]),
        [whole_spec(theta), whole_spec(table["column"]), part_spec(table["spectrum_rows"])],
        floats(2, FA, 2 * FB),
        name="own_spectrum",
        flops=1 << 31,
    )
    side = partner(own, 3)
    spectrum = call(
        rim_kernel,
        (parts,),
        (spectrum, rim, table["rim_rows"]),
        [whole_spec(spectrum), whole_spec(rim), part_spec(table["rim_rows"])],
        floats(1, FA, 2 * FB),
        name="add_rim",
    )
    mixed = jnp.concatenate([own, side, spectrum + partner(spectrum, 3)], axis=0)
    adjoint = call(
        fields_kernel,
        (parts,),
        (mixed, partner(mixed, 1), shares, target, forward, backward, table["row"], table["row_turned"]),
        [
            whole_spec(mixed),
            whole_spec(mixed),
            whole_spec(shares),
            pl.BlockSpec((TP, ROWS), lambda i, part, *refs: (0, part_of(part))),
            whole_spec(forward),
            whole_spec(backward),
            whole_spec(table["row"]),
            whole_spec(table["row_turned"]),
        ],
        floats(FA, 2 * FB),
        scratch=(
            pltpu.VMEM((PARTS, 2, FA, 2 * FB), F32),
            pltpu.VMEM((CONDS, ROWS), F32),
            pltpu.VMEM((count * 2 * FA, 2 * FB), F32),
            pltpu.VMEM((count * 2 * FA, 2 * FB), F32),
            pltpu.VMEM((count, 6 * FA, 2 * ROWS), BF),
            pltpu.VMEM((count, TP, 2 * ROWS), F32),
            pltpu.VMEM((CONDS, TP, ROWS), F32),
            pltpu.VMEM((TP, ROWS), F32),
            pltpu.VMEM((TP, ROWS), F32),
            pltpu.VMEM((count, 2 * FA, 2 * ROWS), F32),
        ),
        name="coherent_fields",
        flops=1 << 33,
    )
    adjoint = adjoint + partner(adjoint, 1)
    adjoint = adjoint + partner(adjoint, 3)
    near = across(adjoint, (2, last), (1, 0), within=[(0, 1), (last, 2)])
    gradient, edge, scale = call(
        gradient_kernel,
        (parts,),
        (theta, adjoint, table["turned"], table["own_rows"]),
        [
            whole_spec(theta),
            whole_spec(adjoint),
            whole_spec(table["turned"]),
            part_spec(table["own_rows"]),
        ],
        [floats(ROWS, TP), floats(HALO, TP), floats(HALO, TP)],
        name="own_gradient",
        flops=1 << 31,
    )
    return call(
        edge_kernel,
        (parts,),
        (gradient, edge, scale, near, table["turned"], table["halo_rows"]),
        [
            hbm,
            whole_spec(edge),
            whole_spec(scale),
            whole_spec(near),
            whole_spec(table["turned"]),
            part_spec(table["halo_rows"]),
        ],
        floats(ROWS, TP),
        scratch=(pltpu.VMEM((HALO, TP), F32), pltpu.SemaphoreType.DMA),
        name="edge_gradient",
        out_specs=hbm,
        aliases={1: 0},
    )


def solution(mesh):
    in_specs = (
        P(("tile", "cond"), None),
        P("tile", None),
        P("cond", None, None, None),
        P("cond", None, None, None),
        P(),
        P("cond"),
    )
    out_specs = P(("tile", "cond"), None)
    return jax.shard_map(shards, mesh=mesh, in_specs=in_specs, out_specs=out_specs, check_vma=False)
```

```python
import functools

import jax
import jax.numpy as jnp
import ml_dtypes
import numpy as np
from jax import lax
from jax.experimental import pallas as pl
from jax.experimental.pallas import tpu as pltpu
from jax.sharding import PartitionSpec as P

TP = 512
HALO = 32
KSUP = 65
HALF = KSUP // 2
KERNELS = 2
CONDS = 8
FULL = TP + 2 * HALO
PARTS = 4
ROWS = TP // PARTS
FA = 40
FB = 64
SPARE = FA - HALF - 1
SPARE_BLOCKS = -(-(HALF + 1) // SPARE)
BF = jnp.bfloat16
F32 = jnp.float32

mask_steep = 2.0
resist_steep = 4.0
band_weight = 1.0


def waves(positions):
    angles = (np.outer(np.asarray(positions, np.int64), np.arange(HALF + 1)) % FULL) * (2.0 * np.pi / FULL)
    return np.cos(angles), np.sin(angles)


def halves(table):
    high = table.astype(np.float32).astype(ml_dtypes.bfloat16)
    low = (table - high.astype(np.float64)).astype(np.float32).astype(ml_dtypes.bfloat16)
    return high, low


def row_table(positions):
    cosine, sine = waves(positions)
    table = np.zeros((len(positions), 2 * FA))
    table[:, : HALF + 1] = cosine
    table[:, FA : FA + HALF + 1] = sine
    return table


def pair_table(positions):
    table = row_table(positions)
    return np.concatenate([table, np.concatenate([-table[:, FA:], table[:, :FA]], axis=1)])


def column_table(positions):
    cosine, sine = waves(positions)
    table = np.zeros((len(positions), 4 * FB))
    for block, values in enumerate((cosine, cosine, sine, -sine)):
        table[:, block * FB : block * FB + HALF] = values[:, 1:]
    table[:, HALF] = 1.0
    return table


@functools.cache
def tables():
    pixels = np.arange(TP) + HALO
    column = column_table(pixels)
    column_high, column_low = halves(column)
    turned = np.concatenate([column[:, : 2 * FB].T, column[:, 2 * FB :].T], axis=1)
    turned_high, turned_low = halves(turned)
    row = row_table(pixels)
    row_high, row_low = halves(row)
    out = {}
    out["column"] = np.stack([column_high, column_low])
    waves_only = np.s_[:, np.r_[0:FB, 2 * FB : 3 * FB]]
    out["waves"] = np.stack([column_high[waves_only], column_low[waves_only]])
    spectrum_rows = []
    rim_rows = []
    halo_rows = []
    own_rows = []
    forward = []
    backward = []
    for part in range(PARTS):
        own = np.arange(ROWS) + part * ROWS + HALO
        rim = np.arange(HALO) + (0 if part == PARTS - 1 else FULL - HALO)
        for rows, positions in ((spectrum_rows, own), (rim_rows, rim)):
            high, low = halves(row_table(positions).T)
            rows.append(np.concatenate([high, low, high], axis=1))
        high, low = halves(pair_table(rim))
        halo_rows.append(np.concatenate([high, low, high], axis=1))
        high, low = halves(pair_table(own))
        own_rows.append(np.concatenate([high, low, high], axis=1))
        cols = slice(part * ROWS, (part + 1) * ROWS)
        high = np.concatenate([turned_high[:, :TP][:, cols], turned_high[:, TP:][:, cols]], axis=1)
        low = np.concatenate([turned_low[:, :TP][:, cols], turned_low[:, TP:][:, cols]], axis=1)
        forward.append(np.concatenate([high, high, low]))
        backward.append(np.concatenate([column_high[cols], column_high[cols], column_low[cols]]))
    out["spectrum_rows"] = np.stack(spectrum_rows)
    out["own_rows"] = np.stack(own_rows)
    out["rim_rows"] = np.stack(rim_rows)
    out["halo_rows"] = np.stack(halo_rows)
    out["forward"] = np.stack(forward)
    out["backward"] = np.stack(backward)
    out["turned"] = np.stack([column_high.T, column_low.T])
    out["row"] = np.concatenate([row_high, row_low, row_high], axis=1)
    out["row_turned"] = np.concatenate([row_high.T, row_low.T])
    return out


def part_of(ref):
    return ref[0] % PARTS


def has_adjoint_halo(ref):
    return ref[0] // PARTS % 2 > 0


def has_mask_halo(ref):
    return ref[0] // (2 * PARTS) > 0


def dot(left, right):
    return jnp.dot(left, right, preferred_element_type=F32)


def split(value):
    high = value.astype(BF)
    return high, (value - high.astype(F32)).astype(BF)


def lanes_and_rows():
    shape = (FA, 2 * FB)
    return lax.broadcasted_iota(jnp.int32, shape, 1), lax.broadcasted_iota(jnp.int32, shape, 0)


def pack(even, odd):
    lane, row = lanes_and_rows()
    packed = jnp.where(lane % FB < HALF, even, pltpu.roll(odd, HALF, 1))
    for place, value in ((FA - 2, even), (FA - 3, odd)):
        line = jnp.sum(jnp.where(lane == row, value[:, HALF : HALF + 1], 0.0), axis=0, keepdims=True)
        packed = jnp.where(row == place, line, packed)
    return packed


def unpack(packed):
    lane, row = lanes_and_rows()
    values = []
    for place, value in ((FA - 2, packed), (FA - 3, pltpu.roll(packed, 2 * FB - HALF, 1))):
        column = jnp.sum(jnp.where((lane == row) & (row <= HALF), packed[place : place + 1], 0.0), axis=1, keepdims=True)
        value = jnp.where(lane == HALF, column, jnp.where(lane % FB < HALF, value, 0.0))
        values.append(jnp.where(row <= HALF, value, 0.0))
    return values


def columns_of(mask, column_ref):
    high, low = split(mask)
    return dot(high, column_ref[0]) + dot(low, column_ref[0]) + dot(high, column_ref[1])


def spectrum_of(across, rows):
    high, low = split(across)
    both = dot(rows, jnp.concatenate([high, high, low], axis=0))
    even = both[:FA, : 2 * FB] - both[FA:, 2 * FB :]
    odd = both[FA:, : 2 * FB] + both[:FA, 2 * FB :]
    return even, odd


def open_kernel(
    part_ref, real_hbm, imag_hbm, thresholds_hbm, weights_hbm, forward_hbm, backward_hbm,
    out_ref, shares_ref, forward_ref, backward_ref, real_ref, imag_ref, thresholds_ref, weights_ref, stage, sems,
):
    part = part_of(part_ref)
    moves = [
        (real_hbm, real_ref),
        (imag_hbm, imag_ref),
        (thresholds_hbm, thresholds_ref),
        (weights_hbm, weights_ref),
        (forward_hbm.at[part], forward_ref),
        (backward_hbm.at[part], backward_ref),
    ]
    copies = [pltpu.make_async_copy(source, target, sems.at[i]) for i, (source, target) in enumerate(moves)]
    for copy in copies:
        copy.start()
    local_conds = real_ref.shape[0]
    mats = local_conds * KERNELS * 2
    stage[...] = jnp.zeros_like(stage)
    for copy in copies[:4]:
        copy.wait()
    for cond in range(local_conds):
        for kern in range(KERNELS):
            for piece, ref in enumerate((real_ref, imag_ref)):
                stage[(cond * KERNELS + kern) * 2 + piece, :KSUP, :KSUP] = ref[cond, :, kern, :]
    rows = stage.shape[1]
    source = lax.broadcasted_iota(jnp.int32, (2 * FB, 4 * FB), 0)
    target = lax.broadcasted_iota(jnp.int32, (2 * FB, 4 * FB), 1)
    lane = target % FB
    block = target // FB
    plus = (block == 0) | (block == 3)
    freq = jnp.where(lane < HALF, lane + 1, 0)
    used = (lane < HALF) | ((lane == HALF) & (block % 2 == 0))
    pick = (used & (source == jnp.where(plus, HALF + freq, HALF - freq))).astype(F32).astype(BF)
    high, low = split(stage[...].reshape(mats * rows, 2 * FB))
    picked = [dot(piece, pick) for piece in (high, low)]
    source = lax.broadcasted_iota(jnp.int32, (FA, 2 * rows), 1) % rows
    target = lax.broadcasted_iota(jnp.int32, (FA, 2 * rows), 0)
    turn = ((source == HALF - target) & (target <= HALF)).astype(F32).astype(BF)
    lane = lax.broadcasted_iota(jnp.int32, (FA, 2 * FB), 1)
    row = lax.broadcasted_iota(jnp.int32, (FA, 2 * FB), 0)
    valid = (row <= HALF) & ((lane <= HALF) | ((row > 0) & (lane >= FB) & (lane < FB + HALF)))
    scale = 1.0 / (FULL * FULL)
    keep_top = jnp.where(valid, scale, 0.0)
    keep_bottom = jnp.where((row == 0) & (lane == HALF), 0.0, keep_top)
    first = lane % FB < HALF
    extra = jnp.zeros((FA, 2 * FB), F32)
    blocks = []
    for kern in range(local_conds * KERNELS):
        arrays = [[], []]
        for piece in range(2):
            start = (kern * 2 + piece) * rows
            top = picked[0][start + HALF : start + HALF + FA, : 2 * FB] + picked[1][start + HALF : start + HALF + FA, : 2 * FB]
            pieces = jnp.concatenate([half[start : start + rows, 2 * FB :] for half in picked], axis=0)
            bottom = dot(turn, pieces.astype(BF)) * keep_bottom
            top = top * keep_top
            arrays[0].append(top + bottom)
            arrays[1].append(top - bottom)
        for which, (real, imag) in enumerate(arrays):
            blocks.append(jnp.where(first, real, pltpu.roll(imag, HALF, 1)))
            for piece, value in enumerate((real, imag)):
                place = kern * 4 + which * 2 + piece
                extra = jnp.where(lane == place, pltpu.roll(value, (place - HALF) % (2 * FB), 1), extra)
    for i, block in enumerate(blocks):
        if i < SPARE_BLOCKS:
            block = jnp.concatenate([block[: HALF + 1], extra[SPARE * i : SPARE * (i + 1)]], axis=0)
        elif i < SPARE_BLOCKS + local_conds:
            block = jnp.where(row == FA - 1, thresholds_ref[i - SPARE_BLOCKS], block)
        out_ref[i] = block
    weight_sum = weights_ref[0]
    for i in range(1, CONDS):
        weight_sum = weight_sum + weights_ref[i]
    row = lax.broadcasted_iota(jnp.int32, shares_ref.shape, 0)
    shares = jnp.zeros(shares_ref.shape, F32)
    for group, step in enumerate((0, 3, 1, 2)):
        for i in range(local_conds):
            weight = weights_ref[lax.bitwise_xor(part, step) * local_conds + i]
            shares = jnp.where(row == group * local_conds + i, weight.astype(F32), shares)
    shares_ref[...] = shares / weight_sum.astype(F32)
    for copy in copies[4:]:
        copy.wait()


def send_rim_kernel(part_ref, theta_hbm, waves_hbm, out_ref, theta_ref, waves_ref, sems):
    rows = pl.ds(pl.multiple_of(jnp.where(part_of(part_ref) == 0, 0, ROWS - HALO), HALO), HALO)
    copies = [
        pltpu.make_async_copy(theta_hbm.at[rows], theta_ref, sems.at[0]),
        pltpu.make_async_copy(waves_hbm, waves_ref, sems.at[1]),
    ]
    for copy in copies:
        copy.start()
    copies[0].wait()
    mask = jnp.tanh(mask_steep * theta_ref[...])
    copies[1].wait()
    out_ref[...] = columns_of(mask, waves_ref)


def spectrum_kernel(part_ref, theta_ref, column_ref, rows_ref, out_ref):
    across = columns_of(jnp.tanh(mask_steep * theta_ref[...]), column_ref)
    even, odd = spectrum_of(across, rows_ref[0])
    out_ref[0] = even
    out_ref[1] = odd


def rim_kernel(part_ref, spectrum_ref, rim_ref, rows_ref, out_ref):
    rim = jnp.where(has_mask_halo(part_ref), rim_ref[...], 0.0)
    turned = pltpu.roll(rim, FB, 1)
    first = lax.broadcasted_iota(jnp.int32, rim.shape, 1) < FB
    across = jnp.concatenate([jnp.where(first, rim, turned), jnp.where(first, turned, -rim)], axis=1)
    even, odd = spectrum_of(across, rows_ref[0])
    out_ref[0] = pack(even + spectrum_ref[0], odd + spectrum_ref[1])


def fields_kernel(
    part_ref, mixed_ref, other_ref, shares_ref, target_ref, forward_ref, backward_ref, row_ref,
    row_turned_ref, out_ref, kernels_ref, levels_ref, lines, folded, amps, tanhs, total, signs, turned, backs,
):
    count = kernels_ref.shape[0]
    local = count // PARTS
    tall = 4 * FA
    each = 2 * local
    even, odd = unpack(mixed_ref[2 * each] + other_ref[2 * each])
    lane, row = lanes_and_rows()
    zero_lane = (lane == HALF) & (row <= HALF)
    for group in range(PARTS):
        ref = (mixed_ref, other_ref)[group // 2].at[pl.ds(group % 2 * each, each)]
        extra = [ref[i][HALF + 1 :] for i in range(SPARE_BLOCKS)]
        extra = jnp.concatenate(extra + [jnp.zeros((FA - SPARE * SPARE_BLOCKS, 2 * FB), F32)], axis=0)
        for i in range(CONDS // PARTS):
            place = group * (CONDS // PARTS) + i
            levels_ref[place : place + 1] = ref[SPARE_BLOCKS + i][FA - 1 :]
        for kern in range(local):
            values = []
            for which in range(2):
                packed = ref[2 * kern + which]
                for part, value in enumerate((packed, pltpu.roll(packed, 2 * FB - HALF, 1))):
                    place = kern * 4 + which * 2 + part
                    zeroth = pltpu.roll(extra, (HALF - place) % (2 * FB), 1)
                    value = jnp.where(zero_lane, zeroth, value)
                    kernels_ref[group * local + kern, which * 2 + part] = value
                    values.append(value)
            he_real, he_imag, ho_real, ho_imag = values
            start = (group * local + kern) * tall
            for i, value in enumerate(
                (
                    even * he_real + odd * ho_imag,
                    odd * he_real - even * ho_imag,
                    even * he_imag - odd * ho_real,
                    odd * he_imag + even * ho_real,
                )
            ):
                lines[start + i * FA : start + (i + 1) * FA] = value

    high, low = split(lines[...])
    lines_folded = dot(jnp.concatenate([high, low], axis=1), forward_ref[: 4 * FB]) + dot(high, forward_ref[4 * FB :])
    for kern in range(count):
        parts = []
        for i in range(2):
            x_part = lines_folded[tall * kern + 2 * FA * i : tall * kern + 2 * FA * i + FA]
            y_part = lines_folded[tall * kern + 2 * FA * i + FA : tall * kern + 2 * FA * (i + 1)]
            parts.append(
                jnp.concatenate(
                    [x_part[:, :ROWS] + y_part[:, ROWS:], y_part[:, :ROWS] - x_part[:, ROWS:]], axis=0
                )
            )
        high, low = split(jnp.concatenate(parts, axis=1))
        folded[kern] = jnp.concatenate([high, high, low], axis=0)
    total[...] = jnp.zeros_like(total)
    signs[...] = 1.0 - 2.0 * target_ref[...].astype(F32)

    def expose(cond, carry):
        intensity = None
        for kern in range(KERNELS):
            index = cond * KERNELS + kern
            amp = dot(row_ref[...], folded[index])
            amps[index] = amp
            power = amp[:, :ROWS] * amp[:, :ROWS] + amp[:, ROWS:] * amp[:, ROWS:]
            intensity = power if intensity is None else intensity + power
        level = levels_ref[pl.ds(cond, 1), :]
        value = jnp.tanh((0.5 * resist_steep) * (intensity - level))
        tanhs[cond] = value
        total[...] += value
        return carry

    lax.fori_loop(0, CONDS, expose, 0, unroll=4)
    total[...] = total[...] * (band_weight / (CONDS * CONDS))

    def drive(cond, carry):
        weight = shares_ref[pl.ds(cond, 1), :]
        value = tanhs[cond]
        slope = (weight + band_weight / CONDS) * value + weight * signs[...] - total[...]
        field = (0.5 * resist_steep) * (1.0 - value * value) * slope
        field = jnp.concatenate([field, field], axis=1)
        for kern in range(KERNELS):
            index = cond * KERNELS + kern
            high, low = split(field * amps[index])
            long = dot(row_turned_ref[...], high)
            back = long[: 2 * FA] + long[2 * FA :] + dot(row_turned_ref[: 2 * FA], low)
            turned[pl.ds(index * 2, 2)] = jnp.stack([back[:, :ROWS], back[:, ROWS:]])
        return carry

    lax.fori_loop(0, CONDS, drive, 0, unroll=4)
    high, low = split(turned[...].reshape(count * tall, ROWS))
    backs[...] = dot(jnp.concatenate([high, low], axis=1), backward_ref[: 2 * ROWS]) + dot(high, backward_ref[2 * ROWS :])

    sum_even = jnp.zeros((FA, 2 * FB), F32)
    sum_odd = jnp.zeros((FA, 2 * FB), F32)
    for kern in range(count):
        grads = []
        for i in range(2):
            c_part = backs[tall * kern + 2 * FA * i : tall * kern + 2 * FA * i + FA]
            s_part = backs[tall * kern + 2 * FA * i + FA : tall * kern + 2 * FA * (i + 1)]
            grads.append(
                (
                    c_part[:, : 2 * FB] - s_part[:, 2 * FB :],
                    s_part[:, : 2 * FB] + c_part[:, 2 * FB :],
                )
            )
        (x_real, y_real), (x_imag, y_imag) = grads
        he_real, he_imag, ho_real, ho_imag = (kernels_ref[kern, i] for i in range(4))
        sum_even = sum_even + x_real * he_real + x_imag * he_imag - y_real * ho_imag + y_imag * ho_real
        sum_odd = sum_odd + x_real * ho_imag - x_imag * ho_real + y_real * he_real + y_imag * he_imag
    out_ref[...] = pack(sum_even, sum_odd)


def image_rows(packed, rows, turned_ref):
    high, low = split(jnp.concatenate(unpack(packed), axis=0))
    pair = dot(rows, jnp.concatenate([high, high, low], axis=0))
    count = pair.shape[0] // 2
    high, low = split(jnp.concatenate([pair[:count], pair[count:]], axis=1))
    return dot(high, turned_ref[0]) + dot(low, turned_ref[0]) + dot(high, turned_ref[1])


def edge_start(part_ref):
    return pl.multiple_of(jnp.where(part_of(part_ref) == PARTS - 1, ROWS - HALO, 0), HALO)


def gradient_kernel(part_ref, theta_ref, sum_ref, turned_ref, rows_ref, out_ref, edge_ref, scale_ref):
    part = part_of(part_ref)
    mask = jnp.tanh(mask_steep * theta_ref[...])
    scale = mask_steep * (1.0 - mask * mask)
    gradient = image_rows(sum_ref[...], rows_ref[0], turned_ref) * scale
    out_ref[...] = gradient
    last = part == PARTS - 1
    edge_ref[...] = jnp.where(last, gradient[ROWS - HALO :], gradient[:HALO])
    scale_ref[...] = jnp.where(last, scale[ROWS - HALO :], scale[:HALO])


def edge_kernel(part_ref, gradient_hbm, edge_ref, scale_ref, near_ref, turned_ref, rows_ref, out_hbm, stage, sem):
    rim = image_rows(near_ref[...], rows_ref[0], turned_ref) * scale_ref[...]
    stage[...] = edge_ref[...] + jnp.where(has_adjoint_halo(part_ref), rim, 0.0)
    copy = pltpu.make_async_copy(stage, out_hbm.at[pl.ds(edge_start(part_ref), HALO)], sem)
    copy.start()
    copy.wait()


def whole_spec(array):
    rank = len(array.shape)
    return pl.BlockSpec(array.shape, lambda i, *refs: (0,) * rank)


def part_spec(array):
    rank = len(array.shape)
    return pl.BlockSpec((1,) + array.shape[1:], lambda i, part, *refs: (part_of(part),) + (0,) * (rank - 1))


def call(kernel, scalars, operands, specs, out_shapes, scratch=(), name=None, flops=1 << 28, out_specs=None, aliases=None):
    many = isinstance(out_shapes, list)
    if out_specs is None:
        out_specs = [whole_spec(shape) for shape in out_shapes] if many else whole_spec(out_shapes)
    return pl.pallas_call(
        kernel,
        grid_spec=pltpu.PrefetchScalarGridSpec(
            num_scalar_prefetch=len(scalars),
            grid=(1,),
            in_specs=specs,
            out_specs=out_specs,
            scratch_shapes=list(scratch),
        ),
        out_shape=out_shapes,
        input_output_aliases=aliases or {},
        compiler_params=pltpu.CompilerParams(vmem_limit_bytes=48 * 1024 * 1024),
        cost_estimate=pl.CostEstimate(flops=flops, bytes_accessed=1 << 20, transcendentals=0),
        name=name,
    )(*scalars, *operands)


def floats(*shape):
    return jax.ShapeDtypeStruct(shape, F32)


def shards(theta, target, kernel_real, kernel_imag, weights, thresholds):
    table = {name: jnp.asarray(value) for name, value in tables().items()}
    tiles = lax.axis_size("tile")
    part = lax.axis_index("cond")
    tile = lax.axis_index("tile")
    last = PARTS - 1
    above = ((part == 0) & (tile > 0)) | ((part == last) & (tile < tiles - 1))
    below = ((part == 0) & (tile < tiles - 1)) | ((part == last) & (tile > 0))
    parts = (part + PARTS * above.astype(jnp.int32) + 2 * PARTS * below.astype(jnp.int32)).reshape(1).astype(jnp.int32)
    local_conds = kernel_real.shape[0]
    local = local_conds * KERNELS
    count = CONDS * KERNELS
    hbm = pl.BlockSpec(memory_space=pltpu.HBM)

    def across(value, down, up, within):
        pairs = [(PARTS * i + a, PARTS * i + b) for i in range(tiles) for a, b in within]
        pairs += [(PARTS * (i + 1) + down[0], PARTS * i + down[1]) for i in range(tiles - 1)]
        pairs += [(PARTS * i + up[0], PARTS * (i + 1) + up[1]) for i in range(tiles - 1)]
        pairs += [(down[0], up[1]), (PARTS * (tiles - 1) + up[0], PARTS * (tiles - 1) + down[1])]
        return lax.ppermute(value, ("tile", "cond"), pairs)

    def partner(value, step):
        return lax.ppermute(value, "cond", [(i, i ^ step) for i in range(PARTS)])

    kernel_shape = (local_conds, KSUP, KERNELS, KSUP)
    own, shares, forward, backward = call(
        open_kernel,
        (parts,),
        tuple(
            pltpu.with_memory_space_constraint(value, pltpu.HBM)
            for value in (
                kernel_real.transpose(0, 2, 1, 3), kernel_imag.transpose(0, 2, 1, 3), thresholds, weights,
                table["forward"], table["backward"],
            )
        ),
        [hbm] * 6,
        [
            floats(2 * local, FA, 2 * FB),
            floats(CONDS, ROWS),
            jax.ShapeDtypeStruct(table["forward"].shape[1:], BF),
            jax.ShapeDtypeStruct(table["backward"].shape[1:], BF),
        ],
        scratch=(
            pltpu.VMEM(kernel_shape, F32),
            pltpu.VMEM(kernel_shape, F32),
            pltpu.SMEM(thresholds.shape, F32),
            pltpu.SMEM(weights.shape, jnp.int32),
            pltpu.VMEM((2 * local, 72, 2 * FB), F32),
            pltpu.SemaphoreType.DMA((6,)),
        ),
        name="open_parts",
    )
    rim = call(
        send_rim_kernel,
        (parts,),
        tuple(pltpu.with_memory_space_constraint(value, pltpu.HBM) for value in (theta, table["waves"])),
        [hbm, hbm],
        floats(HALO, 2 * FB),
        scratch=(
            pltpu.VMEM((HALO, TP), F32),
            pltpu.VMEM(table["waves"].shape, BF),
            pltpu.SemaphoreType.DMA((2,)),
        ),
        name="edge_columns",
    )
    rim = across(rim, (0, 0), (last, last), [(1, 2), (2, 1)])
    spectrum = call(
        spectrum_kernel,
        (parts,),
        (theta, table["column"], table["spectrum_rows"]),
        [whole_spec(theta), whole_spec(table["column"]), part_spec(table["spectrum_rows"])],
        floats(2, FA, 2 * FB),
        name="own_spectrum",
        flops=1 << 31,
    )
    side = partner(own, 3)
    spectrum = call(
        rim_kernel,
        (parts,),
        (spectrum, rim, table["rim_rows"]),
        [whole_spec(spectrum), whole_spec(rim), part_spec(table["rim_rows"])],
        floats(1, FA, 2 * FB),
        name="add_rim",
    )
    mixed = jnp.concatenate([own, side, spectrum + partner(spectrum, 3)], axis=0)
    adjoint = call(
        fields_kernel,
        (parts,),
        (mixed, partner(mixed, 1), shares, target, forward, backward, table["row"], table["row_turned"]),
        [
            whole_spec(mixed),
            whole_spec(mixed),
            whole_spec(shares),
            pl.BlockSpec((TP, ROWS), lambda i, part, *refs: (0, part_of(part))),
            whole_spec(forward),
            whole_spec(backward),
            whole_spec(table["row"]),
            whole_spec(table["row_turned"]),
        ],
        floats(FA, 2 * FB),
        scratch=(
            pltpu.VMEM((count, 4, FA, 2 * FB), F32),
            pltpu.VMEM((CONDS, ROWS), F32),
            pltpu.VMEM((count * 4 * FA, 2 * FB), F32),
            pltpu.VMEM((count, 6 * FA, 2 * ROWS), BF),
            pltpu.VMEM((count, TP, 2 * ROWS), F32),
            pltpu.VMEM((CONDS, TP, ROWS), F32),
            pltpu.VMEM((TP, ROWS), F32),
            pltpu.VMEM((TP, ROWS), F32),
            pltpu.VMEM((count * 2, 2 * FA, ROWS), F32),
            pltpu.VMEM((count * 4 * FA, 4 * FB), F32),
        ),
        name="coherent_fields",
        flops=1 << 33,
    )
    adjoint = adjoint + partner(adjoint, 1)
    adjoint = adjoint + partner(adjoint, 3)
    near = across(adjoint, (2, last), (1, 0), [(0, 1), (last, 2)])
    gradient, edge, scale = call(
        gradient_kernel,
        (parts,),
        (theta, adjoint, table["turned"], table["own_rows"]),
        [
            whole_spec(theta),
            whole_spec(adjoint),
            whole_spec(table["turned"]),
            part_spec(table["own_rows"]),
        ],
        [floats(ROWS, TP), floats(HALO, TP), floats(HALO, TP)],
        name="own_gradient",
        flops=1 << 31,
    )
    return call(
        edge_kernel,
        (parts,),
        (gradient, edge, scale, near, table["turned"], table["halo_rows"]),
        [
            hbm,
            whole_spec(edge),
            whole_spec(scale),
            whole_spec(near),
            whole_spec(table["turned"]),
            part_spec(table["halo_rows"]),
        ],
        floats(ROWS, TP),
        scratch=(pltpu.VMEM((HALO, TP), F32), pltpu.SemaphoreType.DMA),
        name="edge_gradient",
        out_specs=hbm,
        aliases={1: 0},
    )


def solution(mesh):
    in_specs = (
        P(("tile", "cond"), None),
        P("tile", None),
        P("cond", None, None, None),
        P("cond", None, None, None),
        P(),
        P("cond"),
    )
    out_specs = P(("tile", "cond"), None)
    return jax.shard_map(shards, mesh=mesh, in_specs=in_specs, out_specs=out_specs, check_vma=False)
```

```python
import functools

import jax
import jax.numpy as jnp
import ml_dtypes
import numpy as np
from jax import lax
from jax.experimental import pallas as pl
from jax.experimental.pallas import tpu as pltpu
from jax.sharding import PartitionSpec as P

TP = 512
HALO = 32
KSUP = 65
HALF = KSUP // 2
KERNELS = 2
CONDS = 8
FULL = TP + 2 * HALO
PARTS = 4
ROWS = TP // PARTS
FA = 40
FB = 64
SPARE = FA - HALF - 1
SPARE_BLOCKS = -(-(HALF + 1) // SPARE)
BF = jnp.bfloat16
F32 = jnp.float32

mask_steep = 2.0
resist_steep = 4.0
band_weight = 1.0


def waves(positions):
    angles = (np.outer(np.asarray(positions, np.int64), np.arange(HALF + 1)) % FULL) * (2.0 * np.pi / FULL)
    return np.cos(angles), np.sin(angles)


def halves(table):
    high = table.astype(np.float32).astype(ml_dtypes.bfloat16)
    low = (table - high.astype(np.float64)).astype(np.float32).astype(ml_dtypes.bfloat16)
    return high, low


def row_table(positions):
    cosine, sine = waves(positions)
    table = np.zeros((len(positions), 2 * FA))
    table[:, : HALF + 1] = cosine
    table[:, FA : FA + HALF + 1] = sine
    return table


def pair_table(positions):
    table = row_table(positions)
    return np.concatenate([table, np.concatenate([-table[:, FA:], table[:, :FA]], axis=1)])


def column_table(positions):
    cosine, sine = waves(positions)
    table = np.zeros((len(positions), 4 * FB))
    for block, values in enumerate((cosine, cosine, sine, -sine)):
        table[:, block * FB : block * FB + HALF] = values[:, 1:]
    table[:, HALF] = 1.0
    return table


@functools.cache
def tables():
    pixels = np.arange(TP) + HALO
    column = column_table(pixels)
    column_high, column_low = halves(column)
    turned = np.concatenate([column[:, : 2 * FB].T, column[:, 2 * FB :].T], axis=1)
    turned_high, turned_low = halves(turned)
    row = row_table(pixels)
    row_high, row_low = halves(row)
    out = {}
    out["column"] = np.stack([column_high, column_low])
    waves_only = np.s_[:, np.r_[0:FB, 2 * FB : 3 * FB]]
    out["waves"] = np.stack([column_high[waves_only], column_low[waves_only]])
    spectrum_rows = []
    rim_rows = []
    halo_rows = []
    own_rows = []
    forward = []
    backward = []
    for part in range(PARTS):
        own = np.arange(ROWS) + part * ROWS + HALO
        rim = np.arange(HALO) + (0 if part == PARTS - 1 else FULL - HALO)
        for rows, positions in ((spectrum_rows, own), (rim_rows, rim)):
            high, low = halves(row_table(positions).T)
            rows.append(np.concatenate([high, low, high], axis=1))
        high, low = halves(pair_table(rim))
        halo_rows.append(np.concatenate([high, low, high], axis=1))
        high, low = halves(pair_table(own))
        own_rows.append(np.concatenate([high, low, high], axis=1))
        cols = slice(part * ROWS, (part + 1) * ROWS)
        high = np.concatenate([turned_high[:, :TP][:, cols], turned_high[:, TP:][:, cols]], axis=1)
        low = np.concatenate([turned_low[:, :TP][:, cols], turned_low[:, TP:][:, cols]], axis=1)
        forward.append(np.concatenate([high, high, low]))
        backward.append(np.concatenate([column_high[cols], column_high[cols], column_low[cols]]))
    out["spectrum_rows"] = np.stack(spectrum_rows)
    out["own_rows"] = np.stack(own_rows)
    out["rim_rows"] = np.stack(rim_rows)
    out["halo_rows"] = np.stack(halo_rows)
    out["forward"] = np.stack(forward)
    out["backward"] = np.stack(backward)
    out["turned"] = np.stack([column_high.T, column_low.T])
    out["row"] = np.concatenate([row_high, row_low, row_high], axis=1)
    out["row_turned"] = np.concatenate([row_high.T, row_low.T])
    return out


def part_of(ref):
    return ref[0] % PARTS


def has_adjoint_halo(ref):
    return ref[0] // PARTS % 2 > 0


def has_mask_halo(ref):
    return ref[0] // (2 * PARTS) > 0


def dot(left, right):
    return jnp.dot(left, right, preferred_element_type=F32)


def split(value):
    high = value.astype(BF)
    return high, (value - high.astype(F32)).astype(BF)


def lanes_and_rows():
    shape = (FA, 2 * FB)
    return lax.broadcasted_iota(jnp.int32, shape, 1), lax.broadcasted_iota(jnp.int32, shape, 0)


def pack(even, odd):
    lane, row = lanes_and_rows()
    packed = jnp.where(lane % FB < HALF, even, pltpu.roll(odd, HALF, 1))
    for place, value in ((FA - 2, even), (FA - 3, odd)):
        line = jnp.sum(jnp.where(lane == row, value[:, HALF : HALF + 1], 0.0), axis=0, keepdims=True)
        packed = jnp.where(row == place, line, packed)
    return packed


def unpack(packed):
    lane, row = lanes_and_rows()
    values = []
    for place, value in ((FA - 2, packed), (FA - 3, pltpu.roll(packed, 2 * FB - HALF, 1))):
        column = jnp.sum(jnp.where((lane == row) & (row <= HALF), packed[place : place + 1], 0.0), axis=1, keepdims=True)
        value = jnp.where(lane == HALF, column, jnp.where(lane % FB < HALF, value, 0.0))
        values.append(jnp.where(row <= HALF, value, 0.0))
    return values


def columns_of(mask, column_ref):
    high, low = split(mask)
    return dot(high, column_ref[0]) + dot(low, column_ref[0]) + dot(high, column_ref[1])


def spectrum_of(across, rows):
    high, low = split(across)
    both = dot(rows, jnp.concatenate([high, high, low], axis=0))
    even = both[:FA, : 2 * FB] - both[FA:, 2 * FB :]
    odd = both[FA:, : 2 * FB] + both[:FA, 2 * FB :]
    return even, odd


def open_kernel(
    part_ref, real_hbm, imag_hbm, thresholds_hbm, weights_hbm, forward_hbm, backward_hbm,
    out_ref, shares_ref, forward_ref, backward_ref, real_ref, imag_ref, thresholds_ref, weights_ref, stage, sems,
):
    part = part_of(part_ref)
    moves = [
        (real_hbm, real_ref),
        (imag_hbm, imag_ref),
        (thresholds_hbm, thresholds_ref),
        (weights_hbm, weights_ref),
        (forward_hbm.at[part], forward_ref),
        (backward_hbm.at[part], backward_ref),
    ]
    copies = [pltpu.make_async_copy(source, target, sems.at[i]) for i, (source, target) in enumerate(moves)]
    for copy in copies:
        copy.start()
    local_conds = real_ref.shape[0]
    mats = local_conds * KERNELS * 2
    stage[...] = jnp.zeros_like(stage)
    for copy in copies[:4]:
        copy.wait()
    for cond in range(local_conds):
        for kern in range(KERNELS):
            for piece, ref in enumerate((real_ref, imag_ref)):
                stage[(cond * KERNELS + kern) * 2 + piece, :KSUP, :KSUP] = ref[cond, :, kern, :]
    rows = stage.shape[1]
    source = lax.broadcasted_iota(jnp.int32, (2 * FB, 4 * FB), 0)
    target = lax.broadcasted_iota(jnp.int32, (2 * FB, 4 * FB), 1)
    lane = target % FB
    block = target // FB
    plus = (block == 0) | (block == 3)
    freq = jnp.where(lane < HALF, lane + 1, 0)
    used = (lane < HALF) | ((lane == HALF) & (block % 2 == 0))
    pick = (used & (source == jnp.where(plus, HALF + freq, HALF - freq))).astype(F32).astype(BF)
    high, low = split(stage[...].reshape(mats * rows, 2 * FB))
    picked = [dot(piece, pick) for piece in (high, low)]
    source = lax.broadcasted_iota(jnp.int32, (FA, 2 * rows), 1) % rows
    target = lax.broadcasted_iota(jnp.int32, (FA, 2 * rows), 0)
    turn = ((source == HALF - target) & (target <= HALF)).astype(F32).astype(BF)
    lane = lax.broadcasted_iota(jnp.int32, (FA, 2 * FB), 1)
    row = lax.broadcasted_iota(jnp.int32, (FA, 2 * FB), 0)
    valid = (row <= HALF) & ((lane <= HALF) | ((row > 0) & (lane >= FB) & (lane < FB + HALF)))
    scale = 1.0 / (FULL * FULL)
    keep_top = jnp.where(valid, scale, 0.0)
    keep_bottom = jnp.where((row == 0) & (lane == HALF), 0.0, keep_top)
    first = lane % FB < HALF
    extra = jnp.zeros((FA, 2 * FB), F32)
    blocks = []
    for kern in range(local_conds * KERNELS):
        arrays = [[], []]
        for piece in range(2):
            start = (kern * 2 + piece) * rows
            top = picked[0][start + HALF : start + HALF + FA, : 2 * FB] + picked[1][start + HALF : start + HALF + FA, : 2 * FB]
            pieces = jnp.concatenate([half[start : start + rows, 2 * FB :] for half in picked], axis=0)
            bottom = dot(turn, pieces.astype(BF)) * keep_bottom
            top = top * keep_top
            arrays[0].append(top + bottom)
            arrays[1].append(top - bottom)
        for which, (real, imag) in enumerate(arrays):
            blocks.append(jnp.where(first, real, pltpu.roll(imag, HALF, 1)))
            for piece, value in enumerate((real, imag)):
                place = kern * 4 + which * 2 + piece
                extra = jnp.where(lane == place, pltpu.roll(value, (place - HALF) % (2 * FB), 1), extra)
    for i, block in enumerate(blocks):
        if i < SPARE_BLOCKS:
            block = jnp.concatenate([block[: HALF + 1], extra[SPARE * i : SPARE * (i + 1)]], axis=0)
        elif i < SPARE_BLOCKS + local_conds:
            block = jnp.where(row == FA - 1, thresholds_ref[i - SPARE_BLOCKS], block)
        out_ref[i] = block
    weight_sum = weights_ref[0]
    for i in range(1, CONDS):
        weight_sum = weight_sum + weights_ref[i]
    row = lax.broadcasted_iota(jnp.int32, shares_ref.shape, 0)
    shares = jnp.zeros(shares_ref.shape, F32)
    for group, step in enumerate((0, 3, 1, 2)):
        for i in range(local_conds):
            weight = weights_ref[lax.bitwise_xor(part, step) * local_conds + i]
            shares = jnp.where(row == group * local_conds + i, weight.astype(F32), shares)
    shares_ref[...] = shares / weight_sum.astype(F32)
    for copy in copies[4:]:
        copy.wait()


def send_rim_kernel(part_ref, theta_hbm, waves_hbm, out_ref, theta_ref, waves_ref, sems):
    rows = pl.ds(pl.multiple_of(jnp.where(part_of(part_ref) == 0, 0, ROWS - HALO), HALO), HALO)
    copies = [
        pltpu.make_async_copy(theta_hbm.at[rows], theta_ref, sems.at[0]),
        pltpu.make_async_copy(waves_hbm, waves_ref, sems.at[1]),
    ]
    for copy in copies:
        copy.start()
    copies[0].wait()
    mask = jnp.tanh(mask_steep * theta_ref[...])
    copies[1].wait()
    out_ref[...] = columns_of(mask, waves_ref)


def spectrum_kernel(part_ref, theta_ref, column_ref, rows_ref, out_ref):
    across = columns_of(jnp.tanh(mask_steep * theta_ref[...]), column_ref)
    even, odd = spectrum_of(across, rows_ref[part_of(part_ref)])
    out_ref[0] = even
    out_ref[1] = odd


def rim_kernel(part_ref, spectrum_ref, rim_ref, rows_ref, out_ref):
    rim = jnp.where(has_mask_halo(part_ref), rim_ref[...], 0.0)
    turned = pltpu.roll(rim, FB, 1)
    first = lax.broadcasted_iota(jnp.int32, rim.shape, 1) < FB
    across = jnp.concatenate([jnp.where(first, rim, turned), jnp.where(first, turned, -rim)], axis=1)
    even, odd = spectrum_of(across, rows_ref[part_of(part_ref)])
    out_ref[0] = pack(even + spectrum_ref[0], odd + spectrum_ref[1])


def fields_kernel(
    part_ref, mixed_ref, other_ref, shares_ref, target_ref, forward_ref, backward_ref, row_ref,
    row_turned_ref, out_ref, kernels_ref, levels_ref, lines, folded, amps, tanhs, total, signs, turned, backs,
):
    count = kernels_ref.shape[0]
    local = count // PARTS
    tall = 4 * FA
    each = 2 * local
    even, odd = unpack(mixed_ref[2 * each] + other_ref[2 * each])
    lane, row = lanes_and_rows()
    zero_lane = (lane == HALF) & (row <= HALF)
    for group in range(PARTS):
        ref = (mixed_ref, other_ref)[group // 2].at[pl.ds(group % 2 * each, each)]
        extra = [ref[i][HALF + 1 :] for i in range(SPARE_BLOCKS)]
        extra = jnp.concatenate(extra + [jnp.zeros((FA - SPARE * SPARE_BLOCKS, 2 * FB), F32)], axis=0)
        for i in range(CONDS // PARTS):
            place = group * (CONDS // PARTS) + i
            levels_ref[place : place + 1] = ref[SPARE_BLOCKS + i][FA - 1 :]
        for kern in range(local):
            values = []
            for which in range(2):
                packed = ref[2 * kern + which]
                for part, value in enumerate((packed, pltpu.roll(packed, 2 * FB - HALF, 1))):
                    place = kern * 4 + which * 2 + part
                    zeroth = pltpu.roll(extra, (HALF - place) % (2 * FB), 1)
                    value = jnp.where(zero_lane, zeroth, value)
                    kernels_ref[group * local + kern, which * 2 + part] = value
                    values.append(value)
            he_real, he_imag, ho_real, ho_imag = values
            start = (group * local + kern) * tall
            for i, value in enumerate(
                (
                    even * he_real + odd * ho_imag,
                    odd * he_real - even * ho_imag,
                    even * he_imag - odd * ho_real,
                    odd * he_imag + even * ho_real,
                )
            ):
                lines[start + i * FA : start + (i + 1) * FA] = value

    high, low = split(lines[...])
    lines_folded = dot(jnp.concatenate([high, low], axis=1), forward_ref[: 4 * FB]) + dot(high, forward_ref[4 * FB :])
    for kern in range(count):
        parts = []
        for i in range(2):
            x_part = lines_folded[tall * kern + 2 * FA * i : tall * kern + 2 * FA * i + FA]
            y_part = lines_folded[tall * kern + 2 * FA * i + FA : tall * kern + 2 * FA * (i + 1)]
            parts.append(
                jnp.concatenate(
                    [x_part[:, :ROWS] + y_part[:, ROWS:], y_part[:, :ROWS] - x_part[:, ROWS:]], axis=0
                )
            )
        high, low = split(jnp.concatenate(parts, axis=1))
        folded[kern] = jnp.concatenate([high, high, low], axis=0)
    total[...] = jnp.zeros_like(total)
    own = pl.ds(pl.multiple_of(part_of(part_ref) * ROWS, ROWS), ROWS)
    signs[...] = 1.0 - 2.0 * target_ref[:, own].astype(F32)

    def expose(cond, carry):
        intensity = None
        for kern in range(KERNELS):
            index = cond * KERNELS + kern
            amp = dot(row_ref[...], folded[index])
            amps[index] = amp
            power = amp[:, :ROWS] * amp[:, :ROWS] + amp[:, ROWS:] * amp[:, ROWS:]
            intensity = power if intensity is None else intensity + power
        level = levels_ref[pl.ds(cond, 1), :]
        value = jnp.tanh((0.5 * resist_steep) * (intensity - level))
        tanhs[cond] = value
        total[...] += value
        return carry

    lax.fori_loop(0, CONDS, expose, 0, unroll=4)
    total[...] = total[...] * (band_weight / (CONDS * CONDS))

    def drive(cond, carry):
        weight = shares_ref[pl.ds(cond, 1), :]
        value = tanhs[cond]
        slope = (weight + band_weight / CONDS) * value + weight * signs[...] - total[...]
        field = (0.5 * resist_steep) * (1.0 - value * value) * slope
        field = jnp.concatenate([field, field], axis=1)
        for kern in range(KERNELS):
            index = cond * KERNELS + kern
            high, low = split(field * amps[index])
            long = dot(row_turned_ref[...], high)
            back = long[: 2 * FA] + long[2 * FA :] + dot(row_turned_ref[: 2 * FA], low)
            turned[pl.ds(index * 2, 2)] = jnp.stack([back[:, :ROWS], back[:, ROWS:]])
        return carry

    lax.fori_loop(0, CONDS, drive, 0, unroll=4)
    high, low = split(turned[...].reshape(count * tall, ROWS))
    backs[...] = dot(jnp.concatenate([high, low], axis=1), backward_ref[: 2 * ROWS]) + dot(high, backward_ref[2 * ROWS :])

    sum_even = jnp.zeros((FA, 2 * FB), F32)
    sum_odd = jnp.zeros((FA, 2 * FB), F32)
    for kern in range(count):
        grads = []
        for i in range(2):
            c_part = backs[tall * kern + 2 * FA * i : tall * kern + 2 * FA * i + FA]
            s_part = backs[tall * kern + 2 * FA * i + FA : tall * kern + 2 * FA * (i + 1)]
            grads.append(
                (
                    c_part[:, : 2 * FB] - s_part[:, 2 * FB :],
                    s_part[:, : 2 * FB] + c_part[:, 2 * FB :],
                )
            )
        (x_real, y_real), (x_imag, y_imag) = grads
        he_real, he_imag, ho_real, ho_imag = (kernels_ref[kern, i] for i in range(4))
        sum_even = sum_even + x_real * he_real + x_imag * he_imag - y_real * ho_imag + y_imag * ho_real
        sum_odd = sum_odd + x_real * ho_imag - x_imag * ho_real + y_real * he_real + y_imag * he_imag
    out_ref[...] = pack(sum_even, sum_odd)


def image_rows(packed, rows, turned_ref):
    high, low = split(jnp.concatenate(unpack(packed), axis=0))
    pair = dot(rows, jnp.concatenate([high, high, low], axis=0))
    count = pair.shape[0] // 2
    high, low = split(jnp.concatenate([pair[:count], pair[count:]], axis=1))
    return dot(high, turned_ref[0]) + dot(low, turned_ref[0]) + dot(high, turned_ref[1])


def edge_start(part_ref):
    return pl.multiple_of(jnp.where(part_of(part_ref) == PARTS - 1, ROWS - HALO, 0), HALO)


def gradient_kernel(part_ref, theta_ref, sum_ref, turned_ref, rows_ref, out_ref, edge_ref, scale_ref):
    part = part_of(part_ref)
    mask = jnp.tanh(mask_steep * theta_ref[...])
    scale = mask_steep * (1.0 - mask * mask)
    gradient = image_rows(sum_ref[...], rows_ref[part], turned_ref) * scale
    out_ref[...] = gradient
    last = part == PARTS - 1
    edge_ref[...] = jnp.where(last, gradient[ROWS - HALO :], gradient[:HALO])
    scale_ref[...] = jnp.where(last, scale[ROWS - HALO :], scale[:HALO])


def edge_kernel(part_ref, gradient_hbm, edge_ref, scale_ref, near_ref, turned_ref, rows_ref, out_hbm, stage, sem):
    rim = image_rows(near_ref[...], rows_ref[part_of(part_ref)], turned_ref) * scale_ref[...]
    stage[...] = edge_ref[...] + jnp.where(has_adjoint_halo(part_ref), rim, 0.0)
    copy = pltpu.make_async_copy(stage, out_hbm.at[pl.ds(edge_start(part_ref), HALO)], sem)
    copy.start()
    copy.wait()


def whole_spec(array):
    del array
    return pl.BlockSpec(memory_space=pltpu.VMEM)


def call(kernel, scalars, operands, specs, out_shapes, scratch=(), name=None, flops=1 << 28, out_specs=None, aliases=None):
    many = isinstance(out_shapes, list)
    if out_specs is None:
        out_specs = [whole_spec(shape) for shape in out_shapes] if many else whole_spec(out_shapes)
    return pl.pallas_call(
        kernel,
        grid_spec=pltpu.PrefetchScalarGridSpec(
            num_scalar_prefetch=len(scalars),
            grid=(1,),
            in_specs=specs,
            out_specs=out_specs,
            scratch_shapes=list(scratch),
        ),
        out_shape=out_shapes,
        input_output_aliases=aliases or {},
        compiler_params=pltpu.CompilerParams(vmem_limit_bytes=48 * 1024 * 1024),
        cost_estimate=pl.CostEstimate(flops=flops, bytes_accessed=1 << 20, transcendentals=0),
        name=name,
    )(*scalars, *operands)


def floats(*shape):
    return jax.ShapeDtypeStruct(shape, F32)


def shards(theta, target, kernel_real, kernel_imag, weights, thresholds):
    table = {name: jnp.asarray(value) for name, value in tables().items()}
    tiles = lax.axis_size("tile")
    part = lax.axis_index("cond")
    tile = lax.axis_index("tile")
    last = PARTS - 1
    above = ((part == 0) & (tile > 0)) | ((part == last) & (tile < tiles - 1))
    below = ((part == 0) & (tile < tiles - 1)) | ((part == last) & (tile > 0))
    parts = (part + PARTS * above.astype(jnp.int32) + 2 * PARTS * below.astype(jnp.int32)).reshape(1).astype(jnp.int32)
    local_conds = kernel_real.shape[0]
    local = local_conds * KERNELS
    count = CONDS * KERNELS
    hbm = pl.BlockSpec(memory_space=pltpu.HBM)

    def across(value, down, up, within):
        pairs = [(PARTS * i + a, PARTS * i + b) for i in range(tiles) for a, b in within]
        pairs += [(PARTS * (i + 1) + down[0], PARTS * i + down[1]) for i in range(tiles - 1)]
        pairs += [(PARTS * i + up[0], PARTS * (i + 1) + up[1]) for i in range(tiles - 1)]
        pairs += [(down[0], up[1]), (PARTS * (tiles - 1) + up[0], PARTS * (tiles - 1) + down[1])]
        return lax.ppermute(value, ("tile", "cond"), pairs)

    def partner(value, step):
        return lax.ppermute(value, "cond", [(i, i ^ step) for i in range(PARTS)])

    kernel_shape = (local_conds, KSUP, KERNELS, KSUP)
    own, shares, forward, backward = call(
        open_kernel,
        (parts,),
        tuple(
            pltpu.with_memory_space_constraint(value, pltpu.HBM)
            for value in (
                kernel_real.transpose(0, 2, 1, 3), kernel_imag.transpose(0, 2, 1, 3), thresholds, weights,
                table["forward"], table["backward"],
            )
        ),
        [hbm] * 6,
        [
            floats(2 * local, FA, 2 * FB),
            floats(CONDS, ROWS),
            jax.ShapeDtypeStruct(table["forward"].shape[1:], BF),
            jax.ShapeDtypeStruct(table["backward"].shape[1:], BF),
        ],
        scratch=(
            pltpu.VMEM(kernel_shape, F32),
            pltpu.VMEM(kernel_shape, F32),
            pltpu.SMEM(thresholds.shape, F32),
            pltpu.SMEM(weights.shape, jnp.int32),
            pltpu.VMEM((2 * local, 72, 2 * FB), F32),
            pltpu.SemaphoreType.DMA((6,)),
        ),
        name="open_parts",
    )
    rim = call(
        send_rim_kernel,
        (parts,),
        tuple(pltpu.with_memory_space_constraint(value, pltpu.HBM) for value in (theta, table["waves"])),
        [hbm, hbm],
        floats(HALO, 2 * FB),
        scratch=(
            pltpu.VMEM((HALO, TP), F32),
            pltpu.VMEM(table["waves"].shape, BF),
            pltpu.SemaphoreType.DMA((2,)),
        ),
        name="edge_columns",
    )
    rim = across(rim, (0, 0), (last, last), [(1, 2), (2, 1)])
    spectrum = call(
        spectrum_kernel,
        (parts,),
        (theta, table["column"], table["spectrum_rows"]),
        [whole_spec(theta), whole_spec(table["column"]), whole_spec(table["spectrum_rows"])],
        floats(2, FA, 2 * FB),
        name="own_spectrum",
        flops=1 << 31,
    )
    side = partner(own, 3)
    spectrum = call(
        rim_kernel,
        (parts,),
        (spectrum, rim, table["rim_rows"]),
        [whole_spec(spectrum), whole_spec(rim), whole_spec(table["rim_rows"])],
        floats(1, FA, 2 * FB),
        name="add_rim",
    )
    mixed = jnp.concatenate([own, side, spectrum + partner(spectrum, 3)], axis=0)
    adjoint = call(
        fields_kernel,
        (parts,),
        (mixed, partner(mixed, 1), shares, target, forward, backward, table["row"], table["row_turned"]),
        [
            whole_spec(mixed),
            whole_spec(mixed),
            whole_spec(shares),
            whole_spec(target),
            whole_spec(forward),
            whole_spec(backward),
            whole_spec(table["row"]),
            whole_spec(table["row_turned"]),
        ],
        floats(FA, 2 * FB),
        scratch=(
            pltpu.VMEM((count, 4, FA, 2 * FB), F32),
            pltpu.VMEM((CONDS, ROWS), F32),
            pltpu.VMEM((count * 4 * FA, 2 * FB), F32),
            pltpu.VMEM((count, 6 * FA, 2 * ROWS), BF),
            pltpu.VMEM((count, TP, 2 * ROWS), F32),
            pltpu.VMEM((CONDS, TP, ROWS), F32),
            pltpu.VMEM((TP, ROWS), F32),
            pltpu.VMEM((TP, ROWS), F32),
            pltpu.VMEM((count * 2, 2 * FA, ROWS), F32),
            pltpu.VMEM((count * 4 * FA, 4 * FB), F32),
        ),
        name="coherent_fields",
        flops=1 << 33,
    )
    adjoint = adjoint + partner(adjoint, 1)
    adjoint = adjoint + partner(adjoint, 3)
    near = across(adjoint, (2, last), (1, 0), [(0, 1), (last, 2)])
    gradient, edge, scale = call(
        gradient_kernel,
        (parts,),
        (theta, adjoint, table["turned"], table["own_rows"]),
        [
            whole_spec(theta),
            whole_spec(adjoint),
            whole_spec(table["turned"]),
            whole_spec(table["own_rows"]),
        ],
        [floats(ROWS, TP), floats(HALO, TP), floats(HALO, TP)],
        out_specs=[
            pl.BlockSpec((ROWS, TP), lambda i, *refs: (0, 0)),
            whole_spec(adjoint),
            whole_spec(adjoint),
        ],
        name="own_gradient",
        flops=1 << 31,
    )
    return call(
        edge_kernel,
        (parts,),
        (gradient, edge, scale, near, table["turned"], table["halo_rows"]),
        [
            hbm,
            whole_spec(edge),
            whole_spec(scale),
            whole_spec(near),
            whole_spec(table["turned"]),
            whole_spec(table["halo_rows"]),
        ],
        floats(ROWS, TP),
        scratch=(pltpu.VMEM((HALO, TP), F32), pltpu.SemaphoreType.DMA),
        name="edge_gradient",
        out_specs=hbm,
        aliases={1: 0},
    )


def solution(mesh):
    in_specs = (
        P(("tile", "cond"), None),
        P("tile", None),
        P("cond", None, None, None),
        P("cond", None, None, None),
        P(),
        P("cond"),
    )
    out_specs = P(("tile", "cond"), None)
    return jax.shard_map(shards, mesh=mesh, in_specs=in_specs, out_specs=out_specs, check_vma=False)
```

```python
import functools

import jax
import jax.numpy as jnp
import ml_dtypes
import numpy as np
from jax import lax
from jax.experimental import pallas as pl
from jax.experimental.pallas import tpu as pltpu
from jax.sharding import PartitionSpec as P

TP = 512
HALO = 32
KSUP = 65
HALF = KSUP // 2
KERNELS = 2
CONDS = 8
FULL = TP + 2 * HALO
PARTS = 4
ROWS = TP // PARTS
FA = 40
FB = 64
SPARE = FA - HALF - 1
SPARE_BLOCKS = -(-(HALF + 1) // SPARE)
BF = jnp.bfloat16
F32 = jnp.float32

mask_steep = 2.0
resist_steep = 4.0
band_weight = 1.0


def waves(positions):
    angles = (np.outer(np.asarray(positions, np.int64), np.arange(HALF + 1)) % FULL) * (2.0 * np.pi / FULL)
    return np.cos(angles), np.sin(angles)


def halves(table):
    high = table.astype(np.float32).astype(ml_dtypes.bfloat16)
    low = (table - high.astype(np.float64)).astype(np.float32).astype(ml_dtypes.bfloat16)
    return high, low


def row_table(positions):
    cosine, sine = waves(positions)
    table = np.zeros((len(positions), 2 * FA))
    table[:, : HALF + 1] = cosine
    table[:, FA : FA + HALF + 1] = sine
    return table


def pair_table(positions):
    table = row_table(positions)
    return np.concatenate([table, np.concatenate([-table[:, FA:], table[:, :FA]], axis=1)])


def column_table(positions):
    cosine, sine = waves(positions)
    table = np.zeros((len(positions), 4 * FB))
    for block, values in enumerate((cosine, cosine, sine, -sine)):
        table[:, block * FB : block * FB + HALF] = values[:, 1:]
    table[:, HALF] = 1.0
    return table


@functools.cache
def tables():
    pixels = np.arange(TP) + HALO
    column = column_table(pixels)
    column_high, column_low = halves(column)
    turned = np.concatenate([column[:, : 2 * FB].T, column[:, 2 * FB :].T], axis=1)
    turned_high, turned_low = halves(turned)
    row = row_table(pixels)
    row_high, row_low = halves(row)
    out = {}
    out["column"] = np.stack([column_high, column_low])
    waves_only = np.s_[:, np.r_[0:FB, 2 * FB : 3 * FB]]
    out["waves"] = np.stack([column_high[waves_only], column_low[waves_only]])
    spectrum_rows = []
    rim_rows = []
    halo_rows = []
    own_rows = []
    forward = []
    backward = []
    for part in range(PARTS):
        own = np.arange(ROWS) + part * ROWS + HALO
        rim = np.arange(HALO) + (0 if part == PARTS - 1 else FULL - HALO)
        for rows, positions in ((spectrum_rows, own), (rim_rows, rim)):
            high, low = halves(row_table(positions).T)
            rows.append(np.concatenate([high, low, high], axis=1))
        high, low = halves(pair_table(rim))
        halo_rows.append(np.concatenate([high, low, high], axis=1))
        high, low = halves(pair_table(own))
        own_rows.append(np.concatenate([high, low, high], axis=1))
        cols = slice(part * ROWS, (part + 1) * ROWS)
        high = np.concatenate([turned_high[:, :TP][:, cols], turned_high[:, TP:][:, cols]], axis=1)
        low = np.concatenate([turned_low[:, :TP][:, cols], turned_low[:, TP:][:, cols]], axis=1)
        forward.append(np.concatenate([high, high, low]))
        backward.append(np.concatenate([column_high[cols], column_high[cols], column_low[cols]]))
    out["spectrum_rows"] = np.stack(spectrum_rows)
    out["own_rows"] = np.stack(own_rows)
    out["rim_rows"] = np.stack(rim_rows)
    out["halo_rows"] = np.stack(halo_rows)
    out["forward"] = np.stack(forward)
    out["backward"] = np.stack(backward)
    out["turned"] = np.stack([column_high.T, column_low.T])
    out["row"] = np.concatenate([row_high, row_low, row_high], axis=1)
    out["row_turned"] = np.concatenate([row_high.T, row_low.T])
    return out


def part_of(ref):
    return ref[0] % PARTS


def has_adjoint_halo(ref):
    return ref[0] // PARTS % 2 > 0


def has_mask_halo(ref):
    return ref[0] // (2 * PARTS) > 0


def dot(left, right):
    return jnp.dot(left, right, preferred_element_type=F32)


def split(value):
    high = value.astype(BF)
    return high, (value - high.astype(F32)).astype(BF)


def lanes_and_rows():
    shape = (FA, 2 * FB)
    return lax.broadcasted_iota(jnp.int32, shape, 1), lax.broadcasted_iota(jnp.int32, shape, 0)


def pack(even, odd):
    lane, row = lanes_and_rows()
    packed = jnp.where(lane % FB < HALF, even, pltpu.roll(odd, HALF, 1))
    for place, value in ((FA - 2, even), (FA - 3, odd)):
        line = jnp.sum(jnp.where(lane == row, value[:, HALF : HALF + 1], 0.0), axis=0, keepdims=True)
        packed = jnp.where(row == place, line, packed)
    return packed


def unpack(packed):
    lane, row = lanes_and_rows()
    values = []
    for place, value in ((FA - 2, packed), (FA - 3, pltpu.roll(packed, 2 * FB - HALF, 1))):
        column = jnp.sum(jnp.where((lane == row) & (row <= HALF), packed[place : place + 1], 0.0), axis=1, keepdims=True)
        value = jnp.where(lane == HALF, column, jnp.where(lane % FB < HALF, value, 0.0))
        values.append(jnp.where(row <= HALF, value, 0.0))
    return values


def columns_of(mask, column_ref):
    high, low = split(mask)
    return dot(high, column_ref[0]) + dot(low, column_ref[0]) + dot(high, column_ref[1])


def spectrum_of(across, rows):
    high, low = split(across)
    both = dot(rows, jnp.concatenate([high, high, low], axis=0))
    even = both[:FA, : 2 * FB] - both[FA:, 2 * FB :]
    odd = both[FA:, : 2 * FB] + both[:FA, 2 * FB :]
    return even, odd


def open_kernel(
    part_ref, real_hbm, imag_hbm, thresholds_hbm, weights_hbm, forward_hbm, backward_hbm,
    out_ref, shares_ref, forward_ref, backward_ref, real_ref, imag_ref, thresholds_ref, weights_ref, stage, sems,
):
    part = part_of(part_ref)
    moves = [
        (real_hbm, real_ref),
        (imag_hbm, imag_ref),
        (thresholds_hbm, thresholds_ref),
        (weights_hbm, weights_ref),
        (forward_hbm.at[part], forward_ref),
        (backward_hbm.at[part], backward_ref),
    ]
    copies = [pltpu.make_async_copy(source, target, sems.at[i]) for i, (source, target) in enumerate(moves)]
    for copy in copies:
        copy.start()
    local_conds = real_ref.shape[0]
    mats = local_conds * KERNELS * 2
    stage[...] = jnp.zeros_like(stage)
    rows = stage.shape[1]
    source = lax.broadcasted_iota(jnp.int32, (2 * FB, 4 * FB), 0)
    target = lax.broadcasted_iota(jnp.int32, (2 * FB, 4 * FB), 1)
    lane = target % FB
    block = target // FB
    plus = (block == 0) | (block == 3)
    freq = jnp.where(lane < HALF, lane + 1, 0)
    used = (lane < HALF) | ((lane == HALF) & (block % 2 == 0))
    pick = (used & (source == jnp.where(plus, HALF + freq, HALF - freq))).astype(F32).astype(BF)
    source = lax.broadcasted_iota(jnp.int32, (FA, 2 * rows), 1) % rows
    target = lax.broadcasted_iota(jnp.int32, (FA, 2 * rows), 0)
    turn = ((source == HALF - target) & (target <= HALF)).astype(F32).astype(BF)
    lane = lax.broadcasted_iota(jnp.int32, (FA, 2 * FB), 1)
    row = lax.broadcasted_iota(jnp.int32, (FA, 2 * FB), 0)
    valid = (row <= HALF) & ((lane <= HALF) | ((row > 0) & (lane >= FB) & (lane < FB + HALF)))
    scale = 1.0 / (FULL * FULL)
    keep_top = jnp.where(valid, scale, 0.0)
    keep_bottom = jnp.where((row == 0) & (lane == HALF), 0.0, keep_top)
    first = lane % FB < HALF
    for copy in copies[:4]:
        copy.wait()
    for cond in range(local_conds):
        for kern in range(KERNELS):
            for piece, ref in enumerate((real_ref, imag_ref)):
                stage[(cond * KERNELS + kern) * 2 + piece, :KSUP, :KSUP] = ref[cond, :, kern, :]
    high, low = split(stage[...].reshape(mats * rows, 2 * FB))
    picked = [dot(piece, pick) for piece in (high, low)]
    extra = jnp.zeros((FA, 2 * FB), F32)
    blocks = []
    for kern in range(local_conds * KERNELS):
        arrays = [[], []]
        for piece in range(2):
            start = (kern * 2 + piece) * rows
            top = picked[0][start + HALF : start + HALF + FA, : 2 * FB] + picked[1][start + HALF : start + HALF + FA, : 2 * FB]
            pieces = jnp.concatenate([half[start : start + rows, 2 * FB :] for half in picked], axis=0)
            bottom = dot(turn, pieces.astype(BF)) * keep_bottom
            top = top * keep_top
            arrays[0].append(top + bottom)
            arrays[1].append(top - bottom)
        for which, (real, imag) in enumerate(arrays):
            blocks.append(jnp.where(first, real, pltpu.roll(imag, HALF, 1)))
            for piece, value in enumerate((real, imag)):
                place = kern * 4 + which * 2 + piece
                extra = jnp.where(lane == place, pltpu.roll(value, (place - HALF) % (2 * FB), 1), extra)
    for i, block in enumerate(blocks):
        if i < SPARE_BLOCKS:
            block = jnp.concatenate([block[: HALF + 1], extra[SPARE * i : SPARE * (i + 1)]], axis=0)
        elif i < SPARE_BLOCKS + local_conds:
            block = jnp.where(row == FA - 1, thresholds_ref[i - SPARE_BLOCKS], block)
        out_ref[i] = block
    weight_sum = weights_ref[0]
    for i in range(1, CONDS):
        weight_sum = weight_sum + weights_ref[i]
    row = lax.broadcasted_iota(jnp.int32, shares_ref.shape, 0)
    shares = jnp.zeros(shares_ref.shape, F32)
    for group, step in enumerate((0, 3, 1, 2)):
        for i in range(local_conds):
            weight = weights_ref[lax.bitwise_xor(part, step) * local_conds + i]
            shares = jnp.where(row == group * local_conds + i, weight.astype(F32), shares)
    shares_ref[...] = shares / weight_sum.astype(F32)
    for copy in copies[4:]:
        copy.wait()


def send_rim_kernel(part_ref, theta_hbm, waves_hbm, out_ref, theta_ref, waves_ref, sems):
    rows = pl.ds(pl.multiple_of(jnp.where(part_of(part_ref) == 0, 0, ROWS - HALO), HALO), HALO)
    copies = [
        pltpu.make_async_copy(theta_hbm.at[rows], theta_ref, sems.at[0]),
        pltpu.make_async_copy(waves_hbm, waves_ref, sems.at[1]),
    ]
    for copy in copies:
        copy.start()
    copies[0].wait()
    mask = jnp.tanh(mask_steep * theta_ref[...])
    copies[1].wait()
    out_ref[...] = columns_of(mask, waves_ref)


def spectrum_kernel(part_ref, theta_ref, column_ref, rows_ref, out_ref):
    across = columns_of(jnp.tanh(mask_steep * theta_ref[...]), column_ref)
    even, odd = spectrum_of(across, rows_ref[part_of(part_ref)])
    out_ref[0] = even
    out_ref[1] = odd


def rim_kernel(part_ref, spectrum_ref, rim_ref, rows_ref, out_ref):
    rim = jnp.where(has_mask_halo(part_ref), rim_ref[...], 0.0)
    turned = pltpu.roll(rim, FB, 1)
    first = lax.broadcasted_iota(jnp.int32, rim.shape, 1) < FB
    across = jnp.concatenate([jnp.where(first, rim, turned), jnp.where(first, turned, -rim)], axis=1)
    even, odd = spectrum_of(across, rows_ref[part_of(part_ref)])
    out_ref[0] = pack(even + spectrum_ref[0], odd + spectrum_ref[1])


def unpack_group(ref, put):
    lane, row = lanes_and_rows()
    zero_lane = (lane == HALF) & (row <= HALF)
    extra = [ref[i][HALF + 1 :] for i in range(SPARE_BLOCKS)]
    extra = jnp.concatenate(extra + [jnp.zeros((FA - SPARE * SPARE_BLOCKS, 2 * FB), F32)], axis=0)
    for kern in range(ref.shape[0] // 2):
        values = []
        for which in range(2):
            packed = ref[2 * kern + which]
            for part, value in enumerate((packed, pltpu.roll(packed, 2 * FB - HALF, 1))):
                place = kern * 4 + which * 2 + part
                zeroth = pltpu.roll(extra, (HALF - place) % (2 * FB), 1)
                values.append(jnp.where(zero_lane, zeroth, value))
        put(kern, values)


def near_kernels_kernel(part_ref, mixed_ref, target_ref, near_ref, signs_ref):
    local = near_ref.shape[0] // 2
    for group in range(2):
        def put(kern, values, group=group):
            for i, value in enumerate(values):
                near_ref[group * local + kern, i] = value

        unpack_group(mixed_ref.at[pl.ds(group * 2 * local, 2 * local)], put)
    own = pl.ds(pl.multiple_of(part_of(part_ref) * ROWS, ROWS), ROWS)
    signs_ref[...] = 1.0 - 2.0 * target_ref[:, own].astype(F32)


def fields_kernel(
    part_ref, mixed_ref, other_ref, near_ref, signs, shares_ref, forward_ref, backward_ref, row_ref,
    row_turned_ref, out_ref, far_ref, levels_ref, lines, folded, amps, tanhs, total, turned, backs,
):
    count = 2 * far_ref.shape[0]
    local = count // PARTS
    tall = 4 * FA
    each = 2 * local
    even, odd = unpack(mixed_ref[2 * each] + other_ref[2 * each])

    def put_line(kern, values):
        he_real, he_imag, ho_real, ho_imag = values
        start = kern * tall
        for i, value in enumerate(
            (
                even * he_real + odd * ho_imag,
                odd * he_real - even * ho_imag,
                even * he_imag - odd * ho_real,
                odd * he_imag + even * ho_real,
            )
        ):
            lines[start + i * FA : start + (i + 1) * FA] = value

    def arrays_of(kern):
        ref = near_ref if kern < count // 2 else far_ref
        return [ref[kern % (count // 2), i] for i in range(4)]

    for group in range(PARTS):
        ref = (mixed_ref, other_ref)[group // 2].at[pl.ds(group % 2 * each, each)]
        for i in range(CONDS // PARTS):
            place = group * (CONDS // PARTS) + i
            levels_ref[place : place + 1] = ref[SPARE_BLOCKS + i][FA - 1 :]
        if group < 2:
            for kern in range(group * local, (group + 1) * local):
                put_line(kern, arrays_of(kern))
        else:
            def put(kern, values, group=group):
                for i, value in enumerate(values):
                    far_ref[(group - 2) * local + kern, i] = value
                put_line(group * local + kern, values)

            unpack_group(ref, put)

    high, low = split(lines[...])
    lines_folded = dot(jnp.concatenate([high, low], axis=1), forward_ref[: 4 * FB]) + dot(high, forward_ref[4 * FB :])
    for kern in range(count):
        parts = []
        for i in range(2):
            x_part = lines_folded[tall * kern + 2 * FA * i : tall * kern + 2 * FA * i + FA]
            y_part = lines_folded[tall * kern + 2 * FA * i + FA : tall * kern + 2 * FA * (i + 1)]
            parts.append(
                jnp.concatenate(
                    [x_part[:, :ROWS] + y_part[:, ROWS:], y_part[:, :ROWS] - x_part[:, ROWS:]], axis=0
                )
            )
        high, low = split(jnp.concatenate(parts, axis=1))
        folded[kern] = jnp.concatenate([high, high, low], axis=0)
    total[...] = jnp.zeros_like(total)

    def expose(cond, carry):
        intensity = None
        for kern in range(KERNELS):
            index = cond * KERNELS + kern
            amp = dot(row_ref[...], folded[index])
            amps[index] = amp
            power = amp[:, :ROWS] * amp[:, :ROWS] + amp[:, ROWS:] * amp[:, ROWS:]
            intensity = power if intensity is None else intensity + power
        level = levels_ref[pl.ds(cond, 1), :]
        value = jnp.tanh((0.5 * resist_steep) * (intensity - level))
        tanhs[cond] = value
        total[...] += value
        return carry

    lax.fori_loop(0, CONDS, expose, 0, unroll=4)
    total[...] = total[...] * (band_weight / (CONDS * CONDS))

    def drive(cond, carry):
        weight = shares_ref[pl.ds(cond, 1), :]
        value = tanhs[cond]
        slope = (weight + band_weight / CONDS) * value + weight * signs[...] - total[...]
        field = (0.5 * resist_steep) * (1.0 - value * value) * slope
        field = jnp.concatenate([field, field], axis=1)
        for kern in range(KERNELS):
            index = cond * KERNELS + kern
            high, low = split(field * amps[index])
            long = dot(row_turned_ref[...], high)
            back = long[: 2 * FA] + long[2 * FA :] + dot(row_turned_ref[: 2 * FA], low)
            turned[pl.ds(index * 2, 2)] = jnp.stack([back[:, :ROWS], back[:, ROWS:]])
        return carry

    lax.fori_loop(0, CONDS, drive, 0, unroll=4)
    high, low = split(turned[...].reshape(count * tall, ROWS))
    backs[...] = dot(jnp.concatenate([high, low], axis=1), backward_ref[: 2 * ROWS]) + dot(high, backward_ref[2 * ROWS :])

    sum_even = jnp.zeros((FA, 2 * FB), F32)
    sum_odd = jnp.zeros((FA, 2 * FB), F32)
    for kern in range(count):
        grads = []
        for i in range(2):
            c_part = backs[tall * kern + 2 * FA * i : tall * kern + 2 * FA * i + FA]
            s_part = backs[tall * kern + 2 * FA * i + FA : tall * kern + 2 * FA * (i + 1)]
            grads.append(
                (
                    c_part[:, : 2 * FB] - s_part[:, 2 * FB :],
                    s_part[:, : 2 * FB] + c_part[:, 2 * FB :],
                )
            )
        (x_real, y_real), (x_imag, y_imag) = grads
        he_real, he_imag, ho_real, ho_imag = arrays_of(kern)
        sum_even = sum_even + x_real * he_real + x_imag * he_imag - y_real * ho_imag + y_imag * ho_real
        sum_odd = sum_odd + x_real * ho_imag - x_imag * ho_real + y_real * he_real + y_imag * he_imag
    out_ref[...] = pack(sum_even, sum_odd)


def image_rows(packed, rows, turned_ref):
    high, low = split(jnp.concatenate(unpack(packed), axis=0))
    pair = dot(rows, jnp.concatenate([high, high, low], axis=0))
    count = pair.shape[0] // 2
    high, low = split(jnp.concatenate([pair[:count], pair[count:]], axis=1))
    return dot(high, turned_ref[0]) + dot(low, turned_ref[0]) + dot(high, turned_ref[1])


def edge_start(part_ref):
    return pl.multiple_of(jnp.where(part_of(part_ref) == PARTS - 1, ROWS - HALO, 0), HALO)


def gradient_kernel(part_ref, theta_ref, sum_ref, turned_ref, rows_ref, out_ref, edge_ref, scale_ref):
    part = part_of(part_ref)
    mask = jnp.tanh(mask_steep * theta_ref[...])
    scale = mask_steep * (1.0 - mask * mask)
    gradient = image_rows(sum_ref[...], rows_ref[part], turned_ref) * scale
    out_ref[...] = gradient
    last = part == PARTS - 1
    edge_ref[...] = jnp.where(last, gradient[ROWS - HALO :], gradient[:HALO])
    scale_ref[...] = jnp.where(last, scale[ROWS - HALO :], scale[:HALO])


def edge_kernel(part_ref, gradient_hbm, edge_ref, scale_ref, near_ref, turned_ref, rows_ref, out_hbm, stage, sem):
    @pl.when(has_adjoint_halo(part_ref))
    def _():
        rim = image_rows(near_ref[...], rows_ref[part_of(part_ref)], turned_ref)
        stage[...] = edge_ref[...] + rim * scale_ref[...]
        copy = pltpu.make_async_copy(stage, out_hbm.at[pl.ds(edge_start(part_ref), HALO)], sem)
        copy.start()
        copy.wait()


def whole_spec(array):
    del array
    return pl.BlockSpec(memory_space=pltpu.VMEM)


def call(kernel, scalars, operands, specs, out_shapes, scratch=(), name=None, flops=1 << 28, out_specs=None, aliases=None):
    many = isinstance(out_shapes, list)
    if out_specs is None:
        out_specs = [whole_spec(shape) for shape in out_shapes] if many else whole_spec(out_shapes)
    return pl.pallas_call(
        kernel,
        grid_spec=pltpu.PrefetchScalarGridSpec(
            num_scalar_prefetch=len(scalars),
            grid=(1,),
            in_specs=specs,
            out_specs=out_specs,
            scratch_shapes=list(scratch),
        ),
        out_shape=out_shapes,
        input_output_aliases=aliases or {},
        compiler_params=pltpu.CompilerParams(vmem_limit_bytes=48 * 1024 * 1024),
        cost_estimate=pl.CostEstimate(flops=flops, bytes_accessed=1 << 20, transcendentals=0),
        name=name,
    )(*scalars, *operands)


def floats(*shape):
    return jax.ShapeDtypeStruct(shape, F32)


def shards(theta, target, kernel_real, kernel_imag, weights, thresholds):
    table = {name: jnp.asarray(value) for name, value in tables().items()}
    tiles = lax.axis_size("tile")
    part = lax.axis_index("cond")
    tile = lax.axis_index("tile")
    last = PARTS - 1
    above = ((part == 0) & (tile > 0)) | ((part == last) & (tile < tiles - 1))
    below = ((part == 0) & (tile < tiles - 1)) | ((part == last) & (tile > 0))
    parts = (part + PARTS * above.astype(jnp.int32) + 2 * PARTS * below.astype(jnp.int32)).reshape(1).astype(jnp.int32)
    local_conds = kernel_real.shape[0]
    local = local_conds * KERNELS
    count = CONDS * KERNELS
    hbm = pl.BlockSpec(memory_space=pltpu.HBM)

    def across(value, down, up, within):
        pairs = [(PARTS * i + a, PARTS * i + b) for i in range(tiles) for a, b in within]
        pairs += [(PARTS * (i + 1) + down[0], PARTS * i + down[1]) for i in range(tiles - 1)]
        pairs += [(PARTS * i + up[0], PARTS * (i + 1) + up[1]) for i in range(tiles - 1)]
        pairs += [(down[0], up[1]), (PARTS * (tiles - 1) + up[0], PARTS * (tiles - 1) + down[1])]
        return lax.ppermute(value, ("tile", "cond"), pairs)

    def partner(value, step):
        return lax.ppermute(value, "cond", [(i, i ^ step) for i in range(PARTS)])

    kernel_shape = (local_conds, KSUP, KERNELS, KSUP)
    own, shares, forward, backward = call(
        open_kernel,
        (parts,),
        tuple(
            pltpu.with_memory_space_constraint(value, pltpu.HBM)
            for value in (
                kernel_real.transpose(0, 2, 1, 3), kernel_imag.transpose(0, 2, 1, 3), thresholds, weights,
                table["forward"], table["backward"],
            )
        ),
        [hbm] * 6,
        [
            floats(2 * local, FA, 2 * FB),
            floats(CONDS, ROWS),
            jax.ShapeDtypeStruct(table["forward"].shape[1:], BF),
            jax.ShapeDtypeStruct(table["backward"].shape[1:], BF),
        ],
        scratch=(
            pltpu.VMEM(kernel_shape, F32),
            pltpu.VMEM(kernel_shape, F32),
            pltpu.SMEM(thresholds.shape, F32),
            pltpu.SMEM(weights.shape, jnp.int32),
            pltpu.VMEM((2 * local, 72, 2 * FB), F32),
            pltpu.SemaphoreType.DMA((6,)),
        ),
        name="open_parts",
    )
    rim = call(
        send_rim_kernel,
        (parts,),
        tuple(pltpu.with_memory_space_constraint(value, pltpu.HBM) for value in (theta, table["waves"])),
        [hbm, hbm],
        floats(HALO, 2 * FB),
        scratch=(
            pltpu.VMEM((HALO, TP), F32),
            pltpu.VMEM(table["waves"].shape, BF),
            pltpu.SemaphoreType.DMA((2,)),
        ),
        name="edge_columns",
    )
    rim = across(rim, (0, 0), (last, last), [(1, 2), (2, 1)])
    spectrum = call(
        spectrum_kernel,
        (parts,),
        (theta, table["column"], table["spectrum_rows"]),
        [whole_spec(theta), whole_spec(table["column"]), whole_spec(table["spectrum_rows"])],
        floats(2, FA, 2 * FB),
        name="own_spectrum",
        flops=1 << 31,
    )
    side = partner(own, 3)
    spectrum = call(
        rim_kernel,
        (parts,),
        (spectrum, rim, table["rim_rows"]),
        [whole_spec(spectrum), whole_spec(rim), whole_spec(table["rim_rows"])],
        floats(1, FA, 2 * FB),
        name="add_rim",
    )
    mixed = jnp.concatenate([own, side, spectrum + partner(spectrum, 3)], axis=0)
    near_kernels, signs = call(
        near_kernels_kernel,
        (parts,),
        (mixed, target),
        [whole_spec(mixed), whole_spec(target)],
        [floats(count // 2, 4, FA, 2 * FB), floats(TP, ROWS)],
        name="near_kernels",
        flops=1 << 30,
    )
    adjoint = call(
        fields_kernel,
        (parts,),
        (
            mixed, partner(mixed, 1), near_kernels, signs, shares, forward, backward, table["row"], table["row_turned"],
        ),
        [
            whole_spec(mixed),
            whole_spec(mixed),
            whole_spec(near_kernels),
            whole_spec(signs),
            whole_spec(shares),
            whole_spec(forward),
            whole_spec(backward),
            whole_spec(table["row"]),
            whole_spec(table["row_turned"]),
        ],
        floats(FA, 2 * FB),
        scratch=(
            pltpu.VMEM((count // 2, 4, FA, 2 * FB), F32),
            pltpu.VMEM((CONDS, ROWS), F32),
            pltpu.VMEM((count * 4 * FA, 2 * FB), F32),
            pltpu.VMEM((count, 6 * FA, 2 * ROWS), BF),
            pltpu.VMEM((count, TP, 2 * ROWS), F32),
            pltpu.VMEM((CONDS, TP, ROWS), F32),
            pltpu.VMEM((TP, ROWS), F32),
            pltpu.VMEM((count * 2, 2 * FA, ROWS), F32),
            pltpu.VMEM((count * 4 * FA, 4 * FB), F32),
        ),
        name="coherent_fields",
        flops=1 << 33,
    )
    adjoint = adjoint + partner(adjoint, 1)
    adjoint = adjoint + partner(adjoint, 3)
    near = across(adjoint, (2, last), (1, 0), [(0, 1), (last, 2)])
    gradient, edge, scale = call(
        gradient_kernel,
        (parts,),
        (theta, adjoint, table["turned"], table["own_rows"]),
        [
            whole_spec(theta),
            whole_spec(adjoint),
            whole_spec(table["turned"]),
            whole_spec(table["own_rows"]),
        ],
        [floats(ROWS, TP), floats(HALO, TP), floats(HALO, TP)],
        out_specs=[
            pl.BlockSpec((ROWS, TP), lambda i, *refs: (0, 0)),
            whole_spec(adjoint),
            whole_spec(adjoint),
        ],
        name="own_gradient",
        flops=1 << 31,
    )
    return call(
        edge_kernel,
        (parts,),
        (gradient, edge, scale, near, table["turned"], table["halo_rows"]),
        [
            hbm,
            whole_spec(edge),
            whole_spec(scale),
            whole_spec(near),
            whole_spec(table["turned"]),
            whole_spec(table["halo_rows"]),
        ],
        floats(ROWS, TP),
        scratch=(pltpu.VMEM((HALO, TP), F32), pltpu.SemaphoreType.DMA),
        name="edge_gradient",
        out_specs=hbm,
        aliases={1: 0},
    )


def solution(mesh):
    in_specs = (
        P(("tile", "cond"), None),
        P("tile", None),
        P("cond", None, None, None),
        P("cond", None, None, None),
        P(),
        P("cond"),
    )
    out_specs = P(("tile", "cond"), None)
    return jax.shard_map(shards, mesh=mesh, in_specs=in_specs, out_specs=out_specs, check_vma=False)
```

```python
import functools

import jax
import jax.numpy as jnp
import ml_dtypes
import numpy as np
from jax import lax
from jax.experimental import pallas as pl
from jax.experimental.pallas import tpu as pltpu
from jax.sharding import PartitionSpec as P

TP = 512
HALO = 32
KSUP = 65
HALF = KSUP // 2
KERNELS = 2
CONDS = 8
FULL = TP + 2 * HALO
PARTS = 4
ROWS = TP // PARTS
FA = 40
FB = 64
SPARE = FA - HALF - 1
DEPTH = 256
CHUNK = 64
SPARE_BLOCKS = -(-(HALF + 1) // SPARE)
BF = jnp.bfloat16
F32 = jnp.float32

mask_steep = 2.0
resist_steep = 4.0
band_weight = 1.0


def waves(positions):
    angles = (np.outer(np.asarray(positions, np.int64), np.arange(HALF + 1)) % FULL) * (2.0 * np.pi / FULL)
    return np.cos(angles), np.sin(angles)


def halves(table):
    high = table.astype(np.float32).astype(ml_dtypes.bfloat16)
    low = (table - high.astype(np.float64)).astype(np.float32).astype(ml_dtypes.bfloat16)
    return high, low


def row_table(positions):
    cosine, sine = waves(positions)
    table = np.zeros((len(positions), 2 * FA))
    table[:, : HALF + 1] = cosine
    table[:, FA : FA + HALF + 1] = sine
    return table


def pair_table(positions):
    table = row_table(positions)
    return np.concatenate([table, np.concatenate([-table[:, FA:], table[:, :FA]], axis=1)])


def column_table(positions):
    cosine, sine = waves(positions)
    table = np.zeros((len(positions), 4 * FB))
    for block, values in enumerate((cosine, cosine, sine, -sine)):
        table[:, block * FB : block * FB + HALF] = values[:, 1:]
    table[:, HALF] = 1.0
    return table


@functools.cache
def tables():
    pixels = np.arange(TP) + HALO
    column = column_table(pixels)
    column_high, column_low = halves(column)
    turned = np.concatenate([column[:, : 2 * FB].T, column[:, 2 * FB :].T], axis=1)
    turned_high, turned_low = halves(turned)
    row = row_table(pixels)
    row_high, row_low = halves(row)
    out = {}
    out["column"] = np.stack([column_high, column_low])
    waves_only = np.s_[:, np.r_[0:FB, 2 * FB : 3 * FB]]
    out["waves"] = np.stack([column_high[waves_only], column_low[waves_only]])
    spectrum_rows = []
    rim_rows = []
    halo_rows = []
    own_rows = []
    forward = []
    backward = []
    for part in range(PARTS):
        own = np.arange(ROWS) + part * ROWS + HALO
        rim = np.arange(HALO) + (0 if part == PARTS - 1 else FULL - HALO)
        for rows, positions in ((spectrum_rows, own), (rim_rows, rim)):
            high, low = halves(row_table(positions).T)
            rows.append(np.concatenate([high, low, high], axis=1))
        high, low = halves(pair_table(rim))
        halo_rows.append(np.concatenate([high, low, high], axis=1))
        high, low = halves(pair_table(own))
        own_rows.append(np.concatenate([high, low, high], axis=1))
        cols = slice(part * ROWS, (part + 1) * ROWS)
        high = np.concatenate([turned_high[:, :TP][:, cols], turned_high[:, TP:][:, cols]], axis=1)
        low = np.concatenate([turned_low[:, :TP][:, cols], turned_low[:, TP:][:, cols]], axis=1)
        forward.append(np.concatenate([high, high, low]))
        backward.append(np.concatenate([column_high[cols], column_high[cols], column_low[cols]]))
    out["spectrum_rows"] = np.stack(spectrum_rows)
    out["own_rows"] = np.stack(own_rows)
    out["rim_rows"] = np.stack(rim_rows)
    out["halo_rows"] = np.stack(halo_rows)
    out["forward"] = np.stack(forward)
    out["backward"] = np.stack(backward)
    out["turned"] = np.stack([column_high.T, column_low.T])
    out["row"] = np.concatenate([row_high, row_low, row_high, np.zeros((TP, DEPTH - 6 * FA), row_high.dtype)], axis=1)
    out["row_turned"] = np.concatenate([row_high.T, row_low.T])
    return out


def part_of(ref):
    return ref[0] % PARTS


def has_adjoint_halo(ref):
    return ref[0] // PARTS % 2 > 0


def has_mask_halo(ref):
    return ref[0] // (2 * PARTS) > 0


def dot(left, right):
    return jnp.dot(left, right, preferred_element_type=F32)


def split(value):
    high = value.astype(BF)
    return high, (value - high.astype(F32)).astype(BF)


def lanes_and_rows():
    shape = (FA, 2 * FB)
    return lax.broadcasted_iota(jnp.int32, shape, 1), lax.broadcasted_iota(jnp.int32, shape, 0)


def pack(even, odd):
    lane, row = lanes_and_rows()
    packed = jnp.where(lane % FB < HALF, even, pltpu.roll(odd, HALF, 1))
    for place, value in ((FA - 2, even), (FA - 3, odd)):
        line = jnp.sum(jnp.where(lane == row, value[:, HALF : HALF + 1], 0.0), axis=0, keepdims=True)
        packed = jnp.where(row == place, line, packed)
    return packed


def unpack(packed):
    lane, row = lanes_and_rows()
    values = []
    for place, value in ((FA - 2, packed), (FA - 3, pltpu.roll(packed, 2 * FB - HALF, 1))):
        column = jnp.sum(jnp.where((lane == row) & (row <= HALF), packed[place : place + 1], 0.0), axis=1, keepdims=True)
        value = jnp.where(lane == HALF, column, jnp.where(lane % FB < HALF, value, 0.0))
        values.append(jnp.where(row <= HALF, value, 0.0))
    return values


def columns_of(mask, column_ref):
    high, low = split(mask)
    return dot(high, column_ref[0]) + dot(low, column_ref[0]) + dot(high, column_ref[1])


def spectrum_of(across, rows):
    high, low = split(across)
    both = dot(rows, jnp.concatenate([high, high, low], axis=0))
    even = both[:FA, : 2 * FB] - both[FA:, 2 * FB :]
    odd = both[FA:, : 2 * FB] + both[:FA, 2 * FB :]
    return even, odd


def open_kernel(
    part_ref, real_hbm, imag_hbm, thresholds_hbm, weights_hbm, forward_hbm, backward_hbm,
    out_ref, shares_ref, forward_ref, backward_ref, real_ref, imag_ref, thresholds_ref, weights_ref, stage, sems,
):
    part = part_of(part_ref)
    moves = [
        (real_hbm, real_ref),
        (imag_hbm, imag_ref),
        (thresholds_hbm, thresholds_ref),
        (weights_hbm, weights_ref),
        (forward_hbm.at[part], forward_ref),
        (backward_hbm.at[part], backward_ref),
    ]
    copies = [pltpu.make_async_copy(source, target, sems.at[i]) for i, (source, target) in enumerate(moves)]
    for copy in copies:
        copy.start()
    local_conds = real_ref.shape[0]
    mats = local_conds * KERNELS * 2
    stage[...] = jnp.zeros_like(stage)
    rows = stage.shape[1]
    source = lax.broadcasted_iota(jnp.int32, (2 * FB, 4 * FB), 0)
    target = lax.broadcasted_iota(jnp.int32, (2 * FB, 4 * FB), 1)
    lane = target % FB
    block = target // FB
    plus = (block == 0) | (block == 3)
    freq = jnp.where(lane < HALF, lane + 1, 0)
    used = (lane < HALF) | ((lane == HALF) & (block % 2 == 0))
    pick = (used & (source == jnp.where(plus, HALF + freq, HALF - freq))).astype(F32).astype(BF)
    source = lax.broadcasted_iota(jnp.int32, (FA, 2 * rows), 1) % rows
    target = lax.broadcasted_iota(jnp.int32, (FA, 2 * rows), 0)
    turn = ((source == HALF - target) & (target <= HALF)).astype(F32).astype(BF)
    lane = lax.broadcasted_iota(jnp.int32, (FA, 2 * FB), 1)
    row = lax.broadcasted_iota(jnp.int32, (FA, 2 * FB), 0)
    valid = (row <= HALF) & ((lane <= HALF) | ((row > 0) & (lane >= FB) & (lane < FB + HALF)))
    scale = 1.0 / (FULL * FULL)
    keep_top = jnp.where(valid, scale, 0.0)
    keep_bottom = jnp.where((row == 0) & (lane == HALF), 0.0, keep_top)
    first = lane % FB < HALF
    for copy in copies[:4]:
        copy.wait()
    for cond in range(local_conds):
        for kern in range(KERNELS):
            for piece, ref in enumerate((real_ref, imag_ref)):
                stage[(cond * KERNELS + kern) * 2 + piece, :KSUP, :KSUP] = ref[cond, :, kern, :]
    high, low = split(stage[...].reshape(mats * rows, 2 * FB))
    picked = [dot(piece, pick) for piece in (high, low)]
    extra = jnp.zeros((FA, 2 * FB), F32)
    blocks = []
    for kern in range(local_conds * KERNELS):
        arrays = [[], []]
        for piece in range(2):
            start = (kern * 2 + piece) * rows
            top = picked[0][start + HALF : start + HALF + FA, : 2 * FB] + picked[1][start + HALF : start + HALF + FA, : 2 * FB]
            pieces = jnp.concatenate([half[start : start + rows, 2 * FB :] for half in picked], axis=0)
            bottom = dot(turn, pieces.astype(BF)) * keep_bottom
            top = top * keep_top
            arrays[0].append(top + bottom)
            arrays[1].append(top - bottom)
        for which, (real, imag) in enumerate(arrays):
            blocks.append(jnp.where(first, real, pltpu.roll(imag, HALF, 1)))
            for piece, value in enumerate((real, imag)):
                place = kern * 4 + which * 2 + piece
                extra = jnp.where(lane == place, pltpu.roll(value, (place - HALF) % (2 * FB), 1), extra)
    for i, block in enumerate(blocks):
        if i < SPARE_BLOCKS:
            block = jnp.concatenate([block[: HALF + 1], extra[SPARE * i : SPARE * (i + 1)]], axis=0)
        elif i < SPARE_BLOCKS + local_conds:
            block = jnp.where(row == FA - 1, thresholds_ref[i - SPARE_BLOCKS], block)
        out_ref[i] = block
    weight_sum = weights_ref[0]
    for i in range(1, CONDS):
        weight_sum = weight_sum + weights_ref[i]
    row = lax.broadcasted_iota(jnp.int32, shares_ref.shape, 0)
    shares = jnp.zeros(shares_ref.shape, F32)
    for group, step in enumerate((0, 3, 1, 2)):
        for i in range(local_conds):
            weight = weights_ref[lax.bitwise_xor(part, step) * local_conds + i]
            shares = jnp.where(row == group * local_conds + i, weight.astype(F32), shares)
    shares_ref[...] = shares / weight_sum.astype(F32)
    for copy in copies[4:]:
        copy.wait()


def send_rim_kernel(part_ref, theta_hbm, waves_hbm, out_ref, theta_ref, waves_ref, sems):
    rows = pl.ds(pl.multiple_of(jnp.where(part_of(part_ref) == 0, 0, ROWS - HALO), HALO), HALO)
    copies = [
        pltpu.make_async_copy(theta_hbm.at[rows], theta_ref, sems.at[0]),
        pltpu.make_async_copy(waves_hbm, waves_ref, sems.at[1]),
    ]
    for copy in copies:
        copy.start()
    copies[0].wait()
    mask = jnp.tanh(mask_steep * theta_ref[...])
    copies[1].wait()
    out_ref[...] = columns_of(mask, waves_ref)


def spectrum_kernel(part_ref, theta_ref, column_ref, rows_ref, out_ref):
    across = columns_of(jnp.tanh(mask_steep * theta_ref[...]), column_ref)
    even, odd = spectrum_of(across, rows_ref[part_of(part_ref)])
    out_ref[0] = even
    out_ref[1] = odd


def rim_kernel(part_ref, spectrum_ref, rim_ref, rows_ref, out_ref):
    rim = jnp.where(has_mask_halo(part_ref), rim_ref[...], 0.0)
    turned = pltpu.roll(rim, FB, 1)
    first = lax.broadcasted_iota(jnp.int32, rim.shape, 1) < FB
    across = jnp.concatenate([jnp.where(first, rim, turned), jnp.where(first, turned, -rim)], axis=1)
    even, odd = spectrum_of(across, rows_ref[part_of(part_ref)])
    out_ref[0] = pack(even + spectrum_ref[0], odd + spectrum_ref[1])


def unpack_group(ref, put):
    lane, row = lanes_and_rows()
    zero_lane = (lane == HALF) & (row <= HALF)
    extra = [ref[i][HALF + 1 :] for i in range(SPARE_BLOCKS)]
    extra = jnp.concatenate(extra + [jnp.zeros((FA - SPARE * SPARE_BLOCKS, 2 * FB), F32)], axis=0)
    for kern in range(ref.shape[0] // 2):
        values = []
        for which in range(2):
            packed = ref[2 * kern + which]
            for part, value in enumerate((packed, pltpu.roll(packed, 2 * FB - HALF, 1))):
                place = kern * 4 + which * 2 + part
                zeroth = pltpu.roll(extra, (HALF - place) % (2 * FB), 1)
                values.append(jnp.where(zero_lane, zeroth, value))
        put(kern, values)


def near_kernels_kernel(part_ref, mixed_ref, target_ref, near_ref, signs_ref):
    local = near_ref.shape[0] // 2
    for group in range(2):
        def put(kern, values, group=group):
            for i, value in enumerate(values):
                near_ref[group * local + kern, i] = value

        unpack_group(mixed_ref.at[pl.ds(group * 2 * local, 2 * local)], put)
    own = pl.ds(pl.multiple_of(part_of(part_ref) * ROWS, ROWS), ROWS)
    signs_ref[...] = 1.0 - 2.0 * target_ref[:, own].astype(F32)


def fields_kernel(
    part_ref, mixed_ref, other_ref, near_ref, signs, shares_ref, forward_ref, backward_ref, row_ref,
    row_turned_ref, out_ref, far_ref, levels_ref, lines, folded, amps, highs, lows, tanhs, total, turned, backs,
):
    count = 2 * far_ref.shape[0]
    local = count // PARTS
    tall = 4 * FA
    each = 2 * local
    even, odd = unpack(mixed_ref[2 * each] + other_ref[2 * each])

    def put_line(kern, values):
        he_real, he_imag, ho_real, ho_imag = values
        start = kern * tall
        for i, value in enumerate(
            (
                even * he_real + odd * ho_imag,
                odd * he_real - even * ho_imag,
                even * he_imag - odd * ho_real,
                odd * he_imag + even * ho_real,
            )
        ):
            lines[start + i * FA : start + (i + 1) * FA] = value

    def arrays_of(kern):
        ref = near_ref if kern < count // 2 else far_ref
        return [ref[kern % (count // 2), i] for i in range(4)]

    for group in range(PARTS):
        ref = (mixed_ref, other_ref)[group // 2].at[pl.ds(group % 2 * each, each)]
        for i in range(CONDS // PARTS):
            place = group * (CONDS // PARTS) + i
            levels_ref[place : place + 1] = ref[SPARE_BLOCKS + i][FA - 1 :]
        if group < 2:
            for kern in range(group * local, (group + 1) * local):
                put_line(kern, arrays_of(kern))
        else:
            def put(kern, values, group=group):
                for i, value in enumerate(values):
                    far_ref[(group - 2) * local + kern, i] = value
                put_line(group * local + kern, values)

            unpack_group(ref, put)

    high, low = split(lines[...])
    lines_folded = dot(jnp.concatenate([high, low], axis=1), forward_ref[: 4 * FB]) + dot(high, forward_ref[4 * FB :])
    for kern in range(count):
        parts = []
        for i in range(2):
            x_part = lines_folded[tall * kern + 2 * FA * i : tall * kern + 2 * FA * i + FA]
            y_part = lines_folded[tall * kern + 2 * FA * i + FA : tall * kern + 2 * FA * (i + 1)]
            parts.append(
                jnp.concatenate(
                    [x_part[:, :ROWS] + y_part[:, ROWS:], y_part[:, :ROWS] - x_part[:, ROWS:]], axis=0
                )
            )
        high, low = split(jnp.concatenate(parts, axis=1))
        folded[kern] = jnp.concatenate([high, high, low, jnp.zeros((DEPTH - 6 * FA, 2 * ROWS), BF)], axis=0)
    total[...] = jnp.zeros_like(total)

    def expose(cond, carry):
        for kern in range(KERNELS):
            amps[cond * KERNELS + kern] = dot(row_ref[...], folded[cond * KERNELS + kern])
        level = levels_ref[pl.ds(cond, 1), :]
        for start in range(0, TP, CHUNK):
            rows = slice(start, start + CHUNK)
            intensity = None
            for kern in range(KERNELS):
                amp = amps[cond * KERNELS + kern, rows]
                power = amp[:, :ROWS] * amp[:, :ROWS] + amp[:, ROWS:] * amp[:, ROWS:]
                intensity = power if intensity is None else intensity + power
            value = jnp.tanh((0.5 * resist_steep) * (intensity - level))
            tanhs[cond, rows] = value
            total[rows] += value
        return carry

    lax.fori_loop(0, CONDS, expose, 0, unroll=4)

    def drive(cond, carry):
        weight = shares_ref[pl.ds(cond, 1), :]
        for start in range(0, TP, CHUNK):
            rows = slice(start, start + CHUNK)
            value = tanhs[cond, rows]
            slope = (weight + band_weight / CONDS) * value + weight * signs[rows]
            slope = slope - total[rows] * (band_weight / (CONDS * CONDS))
            field = (0.5 * resist_steep) * (1.0 - value * value) * slope
            field = jnp.concatenate([field, field], axis=1)
            for kern in range(KERNELS):
                index = cond * KERNELS + kern
                high, low = split(field * amps[index, rows])
                highs[index, rows] = high
                lows[index, rows] = low
        for kern in range(KERNELS):
            index = cond * KERNELS + kern
            long = dot(row_turned_ref[...], highs[index])
            back = long[: 2 * FA] + long[2 * FA :] + dot(row_turned_ref[: 2 * FA], lows[index])
            turned[pl.ds(index * 2, 2)] = jnp.stack([back[:, :ROWS], back[:, ROWS:]])
        return carry

    lax.fori_loop(0, CONDS, drive, 0, unroll=4)
    high, low = split(turned[...].reshape(count * tall, ROWS))
    backs[...] = dot(jnp.concatenate([high, low], axis=1), backward_ref[: 2 * ROWS]) + dot(high, backward_ref[2 * ROWS :])

    sum_even = jnp.zeros((FA, 2 * FB), F32)
    sum_odd = jnp.zeros((FA, 2 * FB), F32)
    for kern in range(count):
        grads = []
        for i in range(2):
            c_part = backs[tall * kern + 2 * FA * i : tall * kern + 2 * FA * i + FA]
            s_part = backs[tall * kern + 2 * FA * i + FA : tall * kern + 2 * FA * (i + 1)]
            grads.append(
                (
                    c_part[:, : 2 * FB] - s_part[:, 2 * FB :],
                    s_part[:, : 2 * FB] + c_part[:, 2 * FB :],
                )
            )
        (x_real, y_real), (x_imag, y_imag) = grads
        he_real, he_imag, ho_real, ho_imag = arrays_of(kern)
        sum_even = sum_even + x_real * he_real + x_imag * he_imag - y_real * ho_imag + y_imag * ho_real
        sum_odd = sum_odd + x_real * ho_imag - x_imag * ho_real + y_real * he_real + y_imag * he_imag
    out_ref[...] = pack(sum_even, sum_odd)


def image_rows(packed, rows, turned_ref):
    high, low = split(jnp.concatenate(unpack(packed), axis=0))
    pair = dot(rows, jnp.concatenate([high, high, low], axis=0))
    count = pair.shape[0] // 2
    high, low = split(jnp.concatenate([pair[:count], pair[count:]], axis=1))
    return dot(high, turned_ref[0]) + dot(low, turned_ref[0]) + dot(high, turned_ref[1])


def edge_start(part_ref):
    return pl.multiple_of(jnp.where(part_of(part_ref) == PARTS - 1, ROWS - HALO, 0), HALO)


def gradient_kernel(part_ref, theta_ref, sum_ref, turned_ref, rows_ref, out_ref, edge_ref, scale_ref):
    part = part_of(part_ref)
    mask = jnp.tanh(mask_steep * theta_ref[...])
    scale = mask_steep * (1.0 - mask * mask)
    gradient = image_rows(sum_ref[...], rows_ref[part], turned_ref) * scale
    out_ref[...] = gradient
    last = part == PARTS - 1
    edge_ref[...] = jnp.where(last, gradient[ROWS - HALO :], gradient[:HALO])
    scale_ref[...] = jnp.where(last, scale[ROWS - HALO :], scale[:HALO])


def edge_kernel(part_ref, gradient_hbm, edge_ref, scale_ref, near_ref, turned_ref, rows_ref, out_hbm, stage, sem):
    @pl.when(has_adjoint_halo(part_ref))
    def _():
        rim = image_rows(near_ref[...], rows_ref[part_of(part_ref)], turned_ref)
        stage[...] = edge_ref[...] + rim * scale_ref[...]
        copy = pltpu.make_async_copy(stage, out_hbm.at[pl.ds(edge_start(part_ref), HALO)], sem)
        copy.start()
        copy.wait()


def whole_spec(array):
    del array
    return pl.BlockSpec(memory_space=pltpu.VMEM)


def call(kernel, scalars, operands, specs, out_shapes, scratch=(), name=None, flops=1 << 28, out_specs=None, aliases=None):
    many = isinstance(out_shapes, list)
    if out_specs is None:
        out_specs = [whole_spec(shape) for shape in out_shapes] if many else whole_spec(out_shapes)
    return pl.pallas_call(
        kernel,
        grid_spec=pltpu.PrefetchScalarGridSpec(
            num_scalar_prefetch=len(scalars),
            grid=(1,),
            in_specs=specs,
            out_specs=out_specs,
            scratch_shapes=list(scratch),
        ),
        out_shape=out_shapes,
        input_output_aliases=aliases or {},
        compiler_params=pltpu.CompilerParams(vmem_limit_bytes=48 * 1024 * 1024),
        cost_estimate=pl.CostEstimate(flops=flops, bytes_accessed=1 << 20, transcendentals=0),
        name=name,
    )(*scalars, *operands)


def floats(*shape):
    return jax.ShapeDtypeStruct(shape, F32)


def shards(theta, target, kernel_real, kernel_imag, weights, thresholds):
    table = {name: jnp.asarray(value) for name, value in tables().items()}
    tiles = lax.axis_size("tile")
    part = lax.axis_index("cond")
    tile = lax.axis_index("tile")
    last = PARTS - 1
    above = ((part == 0) & (tile > 0)) | ((part == last) & (tile < tiles - 1))
    below = ((part == 0) & (tile < tiles - 1)) | ((part == last) & (tile > 0))
    parts = (part + PARTS * above.astype(jnp.int32) + 2 * PARTS * below.astype(jnp.int32)).reshape(1).astype(jnp.int32)
    local_conds = kernel_real.shape[0]
    local = local_conds * KERNELS
    count = CONDS * KERNELS
    hbm = pl.BlockSpec(memory_space=pltpu.HBM)

    def across(value, down, up, within):
        pairs = [(PARTS * i + a, PARTS * i + b) for i in range(tiles) for a, b in within]
        pairs += [(PARTS * (i + 1) + down[0], PARTS * i + down[1]) for i in range(tiles - 1)]
        pairs += [(PARTS * i + up[0], PARTS * (i + 1) + up[1]) for i in range(tiles - 1)]
        pairs += [(down[0], up[1]), (PARTS * (tiles - 1) + up[0], PARTS * (tiles - 1) + down[1])]
        return lax.ppermute(value, ("tile", "cond"), pairs)

    def partner(value, step):
        return lax.ppermute(value, "cond", [(i, i ^ step) for i in range(PARTS)])

    kernel_shape = (local_conds, KSUP, KERNELS, KSUP)
    own, shares, forward, backward = call(
        open_kernel,
        (parts,),
        tuple(
            pltpu.with_memory_space_constraint(value, pltpu.HBM)
            for value in (
                kernel_real.transpose(0, 2, 1, 3), kernel_imag.transpose(0, 2, 1, 3), thresholds, weights,
                table["forward"], table["backward"],
            )
        ),
        [hbm] * 6,
        [
            floats(2 * local, FA, 2 * FB),
            floats(CONDS, ROWS),
            jax.ShapeDtypeStruct(table["forward"].shape[1:], BF),
            jax.ShapeDtypeStruct(table["backward"].shape[1:], BF),
        ],
        scratch=(
            pltpu.VMEM(kernel_shape, F32),
            pltpu.VMEM(kernel_shape, F32),
            pltpu.SMEM(thresholds.shape, F32),
            pltpu.SMEM(weights.shape, jnp.int32),
            pltpu.VMEM((2 * local, 72, 2 * FB), F32),
            pltpu.SemaphoreType.DMA((6,)),
        ),
        name="open_parts",
    )
    rim = call(
        send_rim_kernel,
        (parts,),
        tuple(pltpu.with_memory_space_constraint(value, pltpu.HBM) for value in (theta, table["waves"])),
        [hbm, hbm],
        floats(HALO, 2 * FB),
        scratch=(
            pltpu.VMEM((HALO, TP), F32),
            pltpu.VMEM(table["waves"].shape, BF),
            pltpu.SemaphoreType.DMA((2,)),
        ),
        name="edge_columns",
    )
    rim = across(rim, (0, 0), (last, last), [(1, 2), (2, 1)])
    spectrum = call(
        spectrum_kernel,
        (parts,),
        (theta, table["column"], table["spectrum_rows"]),
        [whole_spec(theta), whole_spec(table["column"]), whole_spec(table["spectrum_rows"])],
        floats(2, FA, 2 * FB),
        name="own_spectrum",
        flops=1 << 31,
    )
    side = partner(own, 3)
    spectrum = call(
        rim_kernel,
        (parts,),
        (spectrum, rim, table["rim_rows"]),
        [whole_spec(spectrum), whole_spec(rim), whole_spec(table["rim_rows"])],
        floats(1, FA, 2 * FB),
        name="add_rim",
    )
    mixed = jnp.concatenate([own, side, spectrum + partner(spectrum, 3)], axis=0)
    near_kernels, signs = call(
        near_kernels_kernel,
        (parts,),
        (mixed, target),
        [whole_spec(mixed), whole_spec(target)],
        [floats(count // 2, 4, FA, 2 * FB), floats(TP, ROWS)],
        name="near_kernels",
        flops=1 << 30,
    )
    adjoint = call(
        fields_kernel,
        (parts,),
        (
            mixed, partner(mixed, 1), near_kernels, signs, shares, forward, backward, table["row"], table["row_turned"],
        ),
        [
            whole_spec(mixed),
            whole_spec(mixed),
            whole_spec(near_kernels),
            whole_spec(signs),
            whole_spec(shares),
            whole_spec(forward),
            whole_spec(backward),
            whole_spec(table["row"]),
            whole_spec(table["row_turned"]),
        ],
        floats(FA, 2 * FB),
        scratch=(
            pltpu.VMEM((count // 2, 4, FA, 2 * FB), F32),
            pltpu.VMEM((CONDS, ROWS), F32),
            pltpu.VMEM((count * 4 * FA, 2 * FB), F32),
            pltpu.VMEM((count, DEPTH, 2 * ROWS), BF),
            pltpu.VMEM((count, TP, 2 * ROWS), F32),
            pltpu.VMEM((count, TP, 2 * ROWS), BF),
            pltpu.VMEM((count, TP, 2 * ROWS), BF),
            pltpu.VMEM((CONDS, TP, ROWS), F32),
            pltpu.VMEM((TP, ROWS), F32),
            pltpu.VMEM((count * 2, 2 * FA, ROWS), F32),
            pltpu.VMEM((count * 4 * FA, 4 * FB), F32),
        ),
        name="coherent_fields",
        flops=1 << 33,
    )
    adjoint = adjoint + partner(adjoint, 1)
    adjoint = adjoint + partner(adjoint, 3)
    near = across(adjoint, (2, last), (1, 0), [(0, 1), (last, 2)])
    gradient, edge, scale = call(
        gradient_kernel,
        (parts,),
        (theta, adjoint, table["turned"], table["own_rows"]),
        [
            whole_spec(theta),
            whole_spec(adjoint),
            whole_spec(table["turned"]),
            whole_spec(table["own_rows"]),
        ],
        [floats(ROWS, TP), floats(HALO, TP), floats(HALO, TP)],
        out_specs=[
            pl.BlockSpec((ROWS, TP), lambda i, *refs: (0, 0)),
            whole_spec(adjoint),
            whole_spec(adjoint),
        ],
        name="own_gradient",
        flops=1 << 31,
    )
    return call(
        edge_kernel,
        (parts,),
        (gradient, edge, scale, near, table["turned"], table["halo_rows"]),
        [
            hbm,
            whole_spec(edge),
            whole_spec(scale),
            whole_spec(near),
            whole_spec(table["turned"]),
            whole_spec(table["halo_rows"]),
        ],
        floats(ROWS, TP),
        scratch=(pltpu.VMEM((HALO, TP), F32), pltpu.SemaphoreType.DMA),
        name="edge_gradient",
        out_specs=hbm,
        aliases={1: 0},
    )


def solution(mesh):
    in_specs = (
        P(("tile", "cond"), None),
        P("tile", None),
        P("cond", None, None, None),
        P("cond", None, None, None),
        P(),
        P("cond"),
    )
    out_specs = P(("tile", "cond"), None)
    return jax.shard_map(shards, mesh=mesh, in_specs=in_specs, out_specs=out_specs, check_vma=False)
```

```python
import functools

import jax
import jax.numpy as jnp
import ml_dtypes
import numpy as np
from jax import lax
from jax.experimental import pallas as pl
from jax.experimental.pallas import tpu as pltpu
from jax.sharding import PartitionSpec as P

TP = 512
HALO = 32
KSUP = 65
HALF = KSUP // 2
KERNELS = 2
CONDS = 8
FULL = TP + 2 * HALO
PARTS = 4
ROWS = TP // PARTS
FA = 40
FB = 64
SPARE = FA - HALF - 1
SPARE_BLOCKS = -(-(HALF + 1) // SPARE)
BF = jnp.bfloat16
F32 = jnp.float32

mask_steep = 2.0
resist_steep = 4.0
band_weight = 1.0


def waves(positions):
    angles = (np.outer(np.asarray(positions, np.int64), np.arange(HALF + 1)) % FULL) * (2.0 * np.pi / FULL)
    return np.cos(angles), np.sin(angles)


def halves(table):
    high = table.astype(np.float32).astype(ml_dtypes.bfloat16)
    low = (table - high.astype(np.float64)).astype(np.float32).astype(ml_dtypes.bfloat16)
    return high, low


def row_table(positions):
    cosine, sine = waves(positions)
    table = np.zeros((len(positions), 2 * FA))
    table[:, : HALF + 1] = cosine
    table[:, FA : FA + HALF + 1] = sine
    return table


def pair_table(positions):
    table = row_table(positions)
    return np.concatenate([table, np.concatenate([-table[:, FA:], table[:, :FA]], axis=1)])


def column_table(positions):
    cosine, sine = waves(positions)
    table = np.zeros((len(positions), 4 * FB))
    for block, values in enumerate((cosine, cosine, sine, -sine)):
        table[:, block * FB : block * FB + HALF] = values[:, 1:]
    table[:, HALF] = 1.0
    return table


@functools.cache
def tables():
    pixels = np.arange(TP) + HALO
    column = column_table(pixels)
    column_high, column_low = halves(column)
    turned = np.concatenate([column[:, : 2 * FB].T, column[:, 2 * FB :].T], axis=1)
    turned_high, turned_low = halves(turned)
    row = row_table(pixels)
    row_high, row_low = halves(row)
    out = {}
    out["column"] = np.stack([column_high, column_low])
    waves_only = np.s_[:, np.r_[0:FB, 2 * FB : 3 * FB]]
    out["waves"] = np.stack([column_high[waves_only], column_low[waves_only]])
    spectrum_rows = []
    rim_rows = []
    halo_rows = []
    own_rows = []
    forward = []
    backward = []
    for part in range(PARTS):
        own = np.arange(ROWS) + part * ROWS + HALO
        rim = np.arange(HALO) + (0 if part == PARTS - 1 else FULL - HALO)
        for rows, positions in ((spectrum_rows, own), (rim_rows, rim)):
            high, low = halves(row_table(positions).T)
            rows.append(np.concatenate([high, low, high], axis=1))
        high, low = halves(pair_table(rim))
        halo_rows.append(np.concatenate([high, low, high], axis=1))
        high, low = halves(pair_table(own))
        own_rows.append(np.concatenate([high, low, high], axis=1))
        cols = slice(part * ROWS, (part + 1) * ROWS)
        high = np.concatenate([turned_high[:, :TP][:, cols], turned_high[:, TP:][:, cols]], axis=1)
        low = np.concatenate([turned_low[:, :TP][:, cols], turned_low[:, TP:][:, cols]], axis=1)
        forward.append(np.concatenate([high, high, low]))
        backward.append(np.concatenate([column_high[cols], column_high[cols], column_low[cols]]))
    out["spectrum_rows"] = np.stack(spectrum_rows)
    out["own_rows"] = np.stack(own_rows)
    out["rim_rows"] = np.stack(rim_rows)
    out["halo_rows"] = np.stack(halo_rows)
    out["forward"] = np.stack(forward)
    out["backward"] = np.stack(backward)
    out["turned"] = np.stack([column_high.T, column_low.T])
    out["row"] = np.concatenate([row_high, row_low, row_high], axis=1)
    out["row_turned"] = np.concatenate([row_high.T, row_low.T])
    return out


def part_of(ref):
    return ref[0] % PARTS


def has_adjoint_halo(ref):
    return ref[0] // PARTS % 2 > 0


def has_mask_halo(ref):
    return ref[0] // (2 * PARTS) > 0


def dot(left, right):
    return jnp.dot(left, right, preferred_element_type=F32)


def split(value):
    high = value.astype(BF)
    return high, (value - high.astype(F32)).astype(BF)


def lanes_and_rows():
    shape = (FA, 2 * FB)
    return lax.broadcasted_iota(jnp.int32, shape, 1), lax.broadcasted_iota(jnp.int32, shape, 0)


def pack(even, odd):
    lane, row = lanes_and_rows()
    packed = jnp.where(lane % FB < HALF, even, pltpu.roll(odd, HALF, 1))
    for place, value in ((FA - 2, even), (FA - 3, odd)):
        line = jnp.sum(jnp.where(lane == row, value[:, HALF : HALF + 1], 0.0), axis=0, keepdims=True)
        packed = jnp.where(row == place, line, packed)
    return packed


def unpack(packed):
    lane, row = lanes_and_rows()
    values = []
    for place, value in ((FA - 2, packed), (FA - 3, pltpu.roll(packed, 2 * FB - HALF, 1))):
        column = jnp.sum(jnp.where((lane == row) & (row <= HALF), packed[place : place + 1], 0.0), axis=1, keepdims=True)
        value = jnp.where(lane == HALF, column, jnp.where(lane % FB < HALF, value, 0.0))
        values.append(jnp.where(row <= HALF, value, 0.0))
    return values


def columns_of(mask, column_ref):
    high, low = split(mask)
    return dot(high, column_ref[0]) + dot(low, column_ref[0]) + dot(high, column_ref[1])


def spectrum_of(across, rows):
    high, low = split(across)
    both = dot(rows, jnp.concatenate([high, high, low], axis=0))
    even = both[:FA, : 2 * FB] - both[FA:, 2 * FB :]
    odd = both[FA:, : 2 * FB] + both[:FA, 2 * FB :]
    return even, odd


def open_kernel(
    part_ref, real_hbm, imag_hbm, thresholds_hbm, weights_hbm, forward_hbm, backward_hbm,
    out_ref, shares_ref, forward_ref, backward_ref, real_ref, imag_ref, thresholds_ref, weights_ref, stage, sems,
):
    part = part_of(part_ref)
    moves = [
        (real_hbm, real_ref),
        (imag_hbm, imag_ref),
        (thresholds_hbm, thresholds_ref),
        (weights_hbm, weights_ref),
        (forward_hbm.at[part], forward_ref),
        (backward_hbm.at[part], backward_ref),
    ]
    copies = [pltpu.make_async_copy(source, target, sems.at[i]) for i, (source, target) in enumerate(moves)]
    for copy in copies:
        copy.start()
    local_conds = real_ref.shape[0]
    mats = local_conds * KERNELS * 2
    stage[...] = jnp.zeros_like(stage)
    rows = stage.shape[1]
    source = lax.broadcasted_iota(jnp.int32, (2 * FB, 4 * FB), 0)
    target = lax.broadcasted_iota(jnp.int32, (2 * FB, 4 * FB), 1)
    lane = target % FB
    block = target // FB
    plus = (block == 0) | (block == 3)
    freq = jnp.where(lane < HALF, lane + 1, 0)
    used = (lane < HALF) | ((lane == HALF) & (block % 2 == 0))
    pick = (used & (source == jnp.where(plus, HALF + freq, HALF - freq))).astype(F32).astype(BF)
    source = lax.broadcasted_iota(jnp.int32, (FA, 2 * rows), 1) % rows
    target = lax.broadcasted_iota(jnp.int32, (FA, 2 * rows), 0)
    turn = ((source == HALF - target) & (target <= HALF)).astype(F32).astype(BF)
    lane = lax.broadcasted_iota(jnp.int32, (FA, 2 * FB), 1)
    row = lax.broadcasted_iota(jnp.int32, (FA, 2 * FB), 0)
    valid = (row <= HALF) & ((lane <= HALF) | ((row > 0) & (lane >= FB) & (lane < FB + HALF)))
    scale = 1.0 / (FULL * FULL)
    keep_top = jnp.where(valid, scale, 0.0)
    keep_bottom = jnp.where((row == 0) & (lane == HALF), 0.0, keep_top)
    first = lane % FB < HALF
    for copy in copies[:4]:
        copy.wait()
    for cond in range(local_conds):
        for kern in range(KERNELS):
            for piece, ref in enumerate((real_ref, imag_ref)):
                stage[(cond * KERNELS + kern) * 2 + piece, :KSUP, :KSUP] = ref[cond, :, kern, :]
    high, low = split(stage[...].reshape(mats * rows, 2 * FB))
    picked = [dot(piece, pick) for piece in (high, low)]
    extra = jnp.zeros((FA, 2 * FB), F32)
    blocks = []
    for kern in range(local_conds * KERNELS):
        arrays = [[], []]
        for piece in range(2):
            start = (kern * 2 + piece) * rows
            top = picked[0][start + HALF : start + HALF + FA, : 2 * FB] + picked[1][start + HALF : start + HALF + FA, : 2 * FB]
            pieces = jnp.concatenate([half[start : start + rows, 2 * FB :] for half in picked], axis=0)
            bottom = dot(turn, pieces.astype(BF)) * keep_bottom
            top = top * keep_top
            arrays[0].append(top + bottom)
            arrays[1].append(top - bottom)
        for which, (real, imag) in enumerate(arrays):
            blocks.append(jnp.where(first, real, pltpu.roll(imag, HALF, 1)))
            for piece, value in enumerate((real, imag)):
                place = kern * 4 + which * 2 + piece
                extra = jnp.where(lane == place, pltpu.roll(value, (place - HALF) % (2 * FB), 1), extra)
    for i, block in enumerate(blocks):
        if i < SPARE_BLOCKS:
            block = jnp.concatenate([block[: HALF + 1], extra[SPARE * i : SPARE * (i + 1)]], axis=0)
        elif i < SPARE_BLOCKS + local_conds:
            block = jnp.where(row == FA - 1, thresholds_ref[i - SPARE_BLOCKS], block)
        out_ref[i] = block
    weight_sum = weights_ref[0]
    for i in range(1, CONDS):
        weight_sum = weight_sum + weights_ref[i]
    row = lax.broadcasted_iota(jnp.int32, shares_ref.shape, 0)
    shares = jnp.zeros(shares_ref.shape, F32)
    for group, step in enumerate((0, 3, 1, 2)):
        for i in range(local_conds):
            weight = weights_ref[lax.bitwise_xor(part, step) * local_conds + i]
            shares = jnp.where(row == group * local_conds + i, weight.astype(F32), shares)
    shares_ref[...] = shares / weight_sum.astype(F32)
    for copy in copies[4:]:
        copy.wait()


def send_rim_kernel(part_ref, theta_hbm, waves_hbm, out_ref, theta_ref, waves_ref, sems):
    rows = pl.ds(pl.multiple_of(jnp.where(part_of(part_ref) == 0, 0, ROWS - HALO), HALO), HALO)
    copies = [
        pltpu.make_async_copy(theta_hbm.at[rows], theta_ref, sems.at[0]),
        pltpu.make_async_copy(waves_hbm, waves_ref, sems.at[1]),
    ]
    for copy in copies:
        copy.start()
    copies[0].wait()
    mask = jnp.tanh(mask_steep * theta_ref[...])
    copies[1].wait()
    out_ref[...] = columns_of(mask, waves_ref)


def spectrum_kernel(part_ref, theta_ref, column_ref, rows_ref, out_ref):
    across = columns_of(jnp.tanh(mask_steep * theta_ref[...]), column_ref)
    even, odd = spectrum_of(across, rows_ref[part_of(part_ref)])
    out_ref[0] = even
    out_ref[1] = odd


def rim_kernel(part_ref, spectrum_ref, rim_ref, rows_ref, out_ref):
    rim = jnp.where(has_mask_halo(part_ref), rim_ref[...], 0.0)
    turned = pltpu.roll(rim, FB, 1)
    first = lax.broadcasted_iota(jnp.int32, rim.shape, 1) < FB
    across = jnp.concatenate([jnp.where(first, rim, turned), jnp.where(first, turned, -rim)], axis=1)
    even, odd = spectrum_of(across, rows_ref[part_of(part_ref)])
    out_ref[0] = pack(even + spectrum_ref[0], odd + spectrum_ref[1])


def unpack_group(ref, put):
    lane, row = lanes_and_rows()
    zero_lane = (lane == HALF) & (row <= HALF)
    extra = [ref[i][HALF + 1 :] for i in range(SPARE_BLOCKS)]
    extra = jnp.concatenate(extra + [jnp.zeros((FA - SPARE * SPARE_BLOCKS, 2 * FB), F32)], axis=0)
    for kern in range(ref.shape[0] // 2):
        values = []
        for which in range(2):
            packed = ref[2 * kern + which]
            for part, value in enumerate((packed, pltpu.roll(packed, 2 * FB - HALF, 1))):
                place = kern * 4 + which * 2 + part
                zeroth = pltpu.roll(extra, (HALF - place) % (2 * FB), 1)
                values.append(jnp.where(zero_lane, zeroth, value))
        put(kern, values)


def near_kernels_kernel(part_ref, mixed_ref, target_ref, near_ref, signs_ref):
    local = near_ref.shape[0] // 2
    for group in range(2):
        def put(kern, values, group=group):
            for i, value in enumerate(values):
                near_ref[group * local + kern, i] = value

        unpack_group(mixed_ref.at[pl.ds(group * 2 * local, 2 * local)], put)
    own = pl.ds(pl.multiple_of(part_of(part_ref) * ROWS, ROWS), ROWS)
    signs_ref[...] = 1.0 - 2.0 * target_ref[:, own].astype(F32)


def fields_kernel(
    part_ref, mixed_ref, other_ref, near_ref, signs, shares_ref, forward_ref, backward_ref, row_ref,
    row_turned_ref, out_ref, far_ref, levels_ref, lines, folded, amps, tanhs, total, turned, backs,
):
    count = 2 * far_ref.shape[0]
    local = count // PARTS
    tall = 4 * FA
    each = 2 * local
    even, odd = unpack(mixed_ref[2 * each] + other_ref[2 * each])

    def put_line(kern, values):
        he_real, he_imag, ho_real, ho_imag = values
        start = kern * tall
        for i, value in enumerate(
            (
                even * he_real + odd * ho_imag,
                odd * he_real - even * ho_imag,
                even * he_imag - odd * ho_real,
                odd * he_imag + even * ho_real,
            )
        ):
            lines[start + i * FA : start + (i + 1) * FA] = value

    def arrays_of(kern):
        ref = near_ref if kern < count // 2 else far_ref
        return [ref[kern % (count // 2), i] for i in range(4)]

    for group in range(PARTS):
        ref = (mixed_ref, other_ref)[group // 2].at[pl.ds(group % 2 * each, each)]
        for i in range(CONDS // PARTS):
            place = group * (CONDS // PARTS) + i
            levels_ref[place : place + 1] = ref[SPARE_BLOCKS + i][FA - 1 :]
        if group < 2:
            for kern in range(group * local, (group + 1) * local):
                put_line(kern, arrays_of(kern))
        else:
            def put(kern, values, group=group):
                for i, value in enumerate(values):
                    far_ref[(group - 2) * local + kern, i] = value
                put_line(group * local + kern, values)

            unpack_group(ref, put)

    high, low = split(lines[...])
    lines_folded = dot(jnp.concatenate([high, low], axis=1), forward_ref[: 4 * FB]) + dot(high, forward_ref[4 * FB :])
    for kern in range(count):
        parts = []
        for i in range(2):
            x_part = lines_folded[tall * kern + 2 * FA * i : tall * kern + 2 * FA * i + FA]
            y_part = lines_folded[tall * kern + 2 * FA * i + FA : tall * kern + 2 * FA * (i + 1)]
            parts.append(
                jnp.concatenate(
                    [x_part[:, :ROWS] + y_part[:, ROWS:], y_part[:, :ROWS] - x_part[:, ROWS:]], axis=0
                )
            )
        high, low = split(jnp.concatenate(parts, axis=1))
        lanes = slice(kern % KERNELS * 2 * ROWS, (kern % KERNELS + 1) * 2 * ROWS)
        folded[kern // KERNELS, :, lanes] = jnp.concatenate([high, high, low], axis=0)
    total[...] = jnp.zeros_like(total)

    def expose(cond, carry):
        amp = dot(row_ref[...], folded[cond])
        amps[cond] = amp
        intensity = sum(amp[:, i * ROWS : (i + 1) * ROWS] * amp[:, i * ROWS : (i + 1) * ROWS] for i in range(2 * KERNELS))
        level = levels_ref[pl.ds(cond, 1), :]
        value = jnp.tanh((0.5 * resist_steep) * (intensity - level))
        tanhs[cond] = value
        total[...] += value
        return carry

    lax.fori_loop(0, CONDS, expose, 0, unroll=4)
    total[...] = total[...] * (band_weight / (CONDS * CONDS))

    def drive(cond, carry):
        weight = shares_ref[pl.ds(cond, 1), :]
        value = tanhs[cond]
        slope = (weight + band_weight / CONDS) * value + weight * signs[...] - total[...]
        field = (0.5 * resist_steep) * (1.0 - value * value) * slope
        high, low = split(jnp.concatenate([field] * (2 * KERNELS), axis=1) * amps[cond])
        long = dot(row_turned_ref[...], high)
        back = long[: 2 * FA] + long[2 * FA :] + dot(row_turned_ref[: 2 * FA], low)
        for i in range(2 * KERNELS):
            turned[cond * 2 * KERNELS + i] = back[:, i * ROWS : (i + 1) * ROWS]
        return carry

    lax.fori_loop(0, CONDS, drive, 0, unroll=4)
    high, low = split(turned[...].reshape(count * tall, ROWS))
    backs[...] = dot(jnp.concatenate([high, low], axis=1), backward_ref[: 2 * ROWS]) + dot(high, backward_ref[2 * ROWS :])

    sum_even = jnp.zeros((FA, 2 * FB), F32)
    sum_odd = jnp.zeros((FA, 2 * FB), F32)
    for kern in range(count):
        grads = []
        for i in range(2):
            c_part = backs[tall * kern + 2 * FA * i : tall * kern + 2 * FA * i + FA]
            s_part = backs[tall * kern + 2 * FA * i + FA : tall * kern + 2 * FA * (i + 1)]
            grads.append(
                (
                    c_part[:, : 2 * FB] - s_part[:, 2 * FB :],
                    s_part[:, : 2 * FB] + c_part[:, 2 * FB :],
                )
            )
        (x_real, y_real), (x_imag, y_imag) = grads
        he_real, he_imag, ho_real, ho_imag = arrays_of(kern)
        sum_even = sum_even + x_real * he_real + x_imag * he_imag - y_real * ho_imag + y_imag * ho_real
        sum_odd = sum_odd + x_real * ho_imag - x_imag * ho_real + y_real * he_real + y_imag * he_imag
    out_ref[...] = pack(sum_even, sum_odd)


def image_rows(packed, rows, turned_ref):
    high, low = split(jnp.concatenate(unpack(packed), axis=0))
    pair = dot(rows, jnp.concatenate([high, high, low], axis=0))
    count = pair.shape[0] // 2
    high, low = split(jnp.concatenate([pair[:count], pair[count:]], axis=1))
    return dot(high, turned_ref[0]) + dot(low, turned_ref[0]) + dot(high, turned_ref[1])


def edge_start(part_ref):
    return pl.multiple_of(jnp.where(part_of(part_ref) == PARTS - 1, ROWS - HALO, 0), HALO)


def gradient_kernel(part_ref, theta_ref, sum_ref, turned_ref, rows_ref, out_ref, edge_ref, scale_ref):
    part = part_of(part_ref)
    mask = jnp.tanh(mask_steep * theta_ref[...])
    scale = mask_steep * (1.0 - mask * mask)
    gradient = image_rows(sum_ref[...], rows_ref[part], turned_ref) * scale
    out_ref[...] = gradient
    last = part == PARTS - 1
    edge_ref[...] = jnp.where(last, gradient[ROWS - HALO :], gradient[:HALO])
    scale_ref[...] = jnp.where(last, scale[ROWS - HALO :], scale[:HALO])


def edge_kernel(part_ref, gradient_hbm, edge_ref, scale_ref, near_ref, turned_ref, rows_ref, out_hbm, stage, sem):
    @pl.when(has_adjoint_halo(part_ref))
    def _():
        rim = image_rows(near_ref[...], rows_ref[part_of(part_ref)], turned_ref)
        stage[...] = edge_ref[...] + rim * scale_ref[...]
        copy = pltpu.make_async_copy(stage, out_hbm.at[pl.ds(edge_start(part_ref), HALO)], sem)
        copy.start()
        copy.wait()


def whole_spec(array):
    del array
    return pl.BlockSpec(memory_space=pltpu.VMEM)


def call(kernel, scalars, operands, specs, out_shapes, scratch=(), name=None, flops=1 << 28, out_specs=None, aliases=None):
    many = isinstance(out_shapes, list)
    if out_specs is None:
        out_specs = [whole_spec(shape) for shape in out_shapes] if many else whole_spec(out_shapes)
    return pl.pallas_call(
        kernel,
        grid_spec=pltpu.PrefetchScalarGridSpec(
            num_scalar_prefetch=len(scalars),
            grid=(1,),
            in_specs=specs,
            out_specs=out_specs,
            scratch_shapes=list(scratch),
        ),
        out_shape=out_shapes,
        input_output_aliases=aliases or {},
        compiler_params=pltpu.CompilerParams(vmem_limit_bytes=48 * 1024 * 1024),
        cost_estimate=pl.CostEstimate(flops=flops, bytes_accessed=1 << 20, transcendentals=0),
        name=name,
    )(*scalars, *operands)


def floats(*shape):
    return jax.ShapeDtypeStruct(shape, F32)


def shards(theta, target, kernel_real, kernel_imag, weights, thresholds):
    table = {name: jnp.asarray(value) for name, value in tables().items()}
    tiles = lax.axis_size("tile")
    part = lax.axis_index("cond")
    tile = lax.axis_index("tile")
    last = PARTS - 1
    above = ((part == 0) & (tile > 0)) | ((part == last) & (tile < tiles - 1))
    below = ((part == 0) & (tile < tiles - 1)) | ((part == last) & (tile > 0))
    parts = (part + PARTS * above.astype(jnp.int32) + 2 * PARTS * below.astype(jnp.int32)).reshape(1).astype(jnp.int32)
    local_conds = kernel_real.shape[0]
    local = local_conds * KERNELS
    count = CONDS * KERNELS
    hbm = pl.BlockSpec(memory_space=pltpu.HBM)

    def across(value, down, up, within):
        pairs = [(PARTS * i + a, PARTS * i + b) for i in range(tiles) for a, b in within]
        pairs += [(PARTS * (i + 1) + down[0], PARTS * i + down[1]) for i in range(tiles - 1)]
        pairs += [(PARTS * i + up[0], PARTS * (i + 1) + up[1]) for i in range(tiles - 1)]
        pairs += [(down[0], up[1]), (PARTS * (tiles - 1) + up[0], PARTS * (tiles - 1) + down[1])]
        return lax.ppermute(value, ("tile", "cond"), pairs)

    def partner(value, step):
        return lax.ppermute(value, "cond", [(i, i ^ step) for i in range(PARTS)])

    kernel_shape = (local_conds, KSUP, KERNELS, KSUP)
    own, shares, forward, backward = call(
        open_kernel,
        (parts,),
        tuple(
            pltpu.with_memory_space_constraint(value, pltpu.HBM)
            for value in (
                kernel_real.transpose(0, 2, 1, 3), kernel_imag.transpose(0, 2, 1, 3), thresholds, weights,
                table["forward"], table["backward"],
            )
        ),
        [hbm] * 6,
        [
            floats(2 * local, FA, 2 * FB),
            floats(CONDS, ROWS),
            jax.ShapeDtypeStruct(table["forward"].shape[1:], BF),
            jax.ShapeDtypeStruct(table["backward"].shape[1:], BF),
        ],
        scratch=(
            pltpu.VMEM(kernel_shape, F32),
            pltpu.VMEM(kernel_shape, F32),
            pltpu.SMEM(thresholds.shape, F32),
            pltpu.SMEM(weights.shape, jnp.int32),
            pltpu.VMEM((2 * local, 72, 2 * FB), F32),
            pltpu.SemaphoreType.DMA((6,)),
        ),
        name="open_parts",
    )
    rim = call(
        send_rim_kernel,
        (parts,),
        tuple(pltpu.with_memory_space_constraint(value, pltpu.HBM) for value in (theta, table["waves"])),
        [hbm, hbm],
        floats(HALO, 2 * FB),
        scratch=(
            pltpu.VMEM((HALO, TP), F32),
            pltpu.VMEM(table["waves"].shape, BF),
            pltpu.SemaphoreType.DMA((2,)),
        ),
        name="edge_columns",
    )
    rim = across(rim, (0, 0), (last, last), [(1, 2), (2, 1)])
    spectrum = call(
        spectrum_kernel,
        (parts,),
        (theta, table["column"], table["spectrum_rows"]),
        [whole_spec(theta), whole_spec(table["column"]), whole_spec(table["spectrum_rows"])],
        floats(2, FA, 2 * FB),
        name="own_spectrum",
        flops=1 << 31,
    )
    side = partner(own, 3)
    spectrum = call(
        rim_kernel,
        (parts,),
        (spectrum, rim, table["rim_rows"]),
        [whole_spec(spectrum), whole_spec(rim), whole_spec(table["rim_rows"])],
        floats(1, FA, 2 * FB),
        name="add_rim",
    )
    mixed = jnp.concatenate([own, side, spectrum + partner(spectrum, 3)], axis=0)
    near_kernels, signs = call(
        near_kernels_kernel,
        (parts,),
        (mixed, target),
        [whole_spec(mixed), whole_spec(target)],
        [floats(count // 2, 4, FA, 2 * FB), floats(TP, ROWS)],
        name="near_kernels",
        flops=1 << 30,
    )
    adjoint = call(
        fields_kernel,
        (parts,),
        (
            mixed, partner(mixed, 1), near_kernels, signs, shares, forward, backward, table["row"], table["row_turned"],
        ),
        [
            whole_spec(mixed),
            whole_spec(mixed),
            whole_spec(near_kernels),
            whole_spec(signs),
            whole_spec(shares),
            whole_spec(forward),
            whole_spec(backward),
            whole_spec(table["row"]),
            whole_spec(table["row_turned"]),
        ],
        floats(FA, 2 * FB),
        scratch=(
            pltpu.VMEM((count // 2, 4, FA, 2 * FB), F32),
            pltpu.VMEM((CONDS, ROWS), F32),
            pltpu.VMEM((count * 4 * FA, 2 * FB), F32),
            pltpu.VMEM((CONDS, 6 * FA, 2 * KERNELS * ROWS), BF),
            pltpu.VMEM((CONDS, TP, 2 * KERNELS * ROWS), F32),
            pltpu.VMEM((CONDS, TP, ROWS), F32),
            pltpu.VMEM((TP, ROWS), F32),
            pltpu.VMEM((count * 2, 2 * FA, ROWS), F32),
            pltpu.VMEM((count * 4 * FA, 4 * FB), F32),
        ),
        name="coherent_fields",
        flops=1 << 33,
    )
    adjoint = adjoint + partner(adjoint, 1)
    adjoint = adjoint + partner(adjoint, 3)
    near = across(adjoint, (2, last), (1, 0), [(0, 1), (last, 2)])
    gradient, edge, scale = call(
        gradient_kernel,
        (parts,),
        (theta, adjoint, table["turned"], table["own_rows"]),
        [
            whole_spec(theta),
            whole_spec(adjoint),
            whole_spec(table["turned"]),
            whole_spec(table["own_rows"]),
        ],
        [floats(ROWS, TP), floats(HALO, TP), floats(HALO, TP)],
        out_specs=[
            pl.BlockSpec((ROWS, TP), lambda i, *refs: (0, 0)),
            whole_spec(adjoint),
            whole_spec(adjoint),
        ],
        name="own_gradient",
        flops=1 << 31,
    )
    return call(
        edge_kernel,
        (parts,),
        (gradient, edge, scale, near, table["turned"], table["halo_rows"]),
        [
            hbm,
            whole_spec(edge),
            whole_spec(scale),
            whole_spec(near),
            whole_spec(table["turned"]),
            whole_spec(table["halo_rows"]),
        ],
        floats(ROWS, TP),
        scratch=(pltpu.VMEM((HALO, TP), F32), pltpu.SemaphoreType.DMA),
        name="edge_gradient",
        out_specs=hbm,
        aliases={1: 0},
    )


def solution(mesh):
    in_specs = (
        P(("tile", "cond"), None),
        P("tile", None),
        P("cond", None, None, None),
        P("cond", None, None, None),
        P(),
        P("cond"),
    )
    out_specs = P(("tile", "cond"), None)
    return jax.shard_map(shards, mesh=mesh, in_specs=in_specs, out_specs=out_specs, check_vma=False)
```

```python
import functools

import jax
import jax.numpy as jnp
import ml_dtypes
import numpy as np
from jax import lax
from jax.experimental import pallas as pl
from jax.experimental.pallas import tpu as pltpu
from jax.sharding import PartitionSpec as P

TP = 512
HALO = 32
KSUP = 65
HALF = KSUP // 2
KERNELS = 2
CONDS = 8
FULL = TP + 2 * HALO
PARTS = 4
ROWS = TP // PARTS
FA = 40
FB = 64
SPARE = FA - HALF - 1
SPARE_BLOCKS = -(-(HALF + 1) // SPARE)
BF = jnp.bfloat16
F32 = jnp.float32

mask_steep = 2.0
resist_steep = 4.0
band_weight = 1.0


def waves(positions):
    angles = (np.outer(np.asarray(positions, np.int64), np.arange(HALF + 1)) % FULL) * (2.0 * np.pi / FULL)
    return np.cos(angles), np.sin(angles)


def halves(table):
    high = table.astype(np.float32).astype(ml_dtypes.bfloat16)
    low = (table - high.astype(np.float64)).astype(np.float32).astype(ml_dtypes.bfloat16)
    return high, low


def row_table(positions):
    cosine, sine = waves(positions)
    table = np.zeros((len(positions), 2 * FA))
    table[:, : HALF + 1] = cosine
    table[:, FA : FA + HALF + 1] = sine
    return table


def pair_table(positions):
    table = row_table(positions)
    return np.concatenate([table, np.concatenate([-table[:, FA:], table[:, :FA]], axis=1)])


def column_table(positions):
    cosine, sine = waves(positions)
    table = np.zeros((len(positions), 4 * FB))
    for block, values in enumerate((cosine, cosine, sine, -sine)):
        table[:, block * FB : block * FB + HALF] = values[:, 1:]
    table[:, HALF] = 1.0
    return table


@functools.cache
def tables():
    pixels = np.arange(TP) + HALO
    column = column_table(pixels)
    column_high, column_low = halves(column)
    turned = np.concatenate([column[:, : 2 * FB].T, column[:, 2 * FB :].T], axis=1)
    turned_high, turned_low = halves(turned)
    row = row_table(pixels)
    row_high, row_low = halves(row)
    out = {}
    out["column"] = np.stack([column_high, column_low])
    waves_only = np.s_[:, np.r_[0:FB, 2 * FB : 3 * FB]]
    out["waves"] = np.stack([column_high[waves_only], column_low[waves_only]])
    spectrum_rows = []
    rim_rows = []
    halo_rows = []
    own_rows = []
    forward = []
    backward = []
    for part in range(PARTS):
        own = np.arange(ROWS) + part * ROWS + HALO
        rim = np.arange(HALO) + (0 if part == PARTS - 1 else FULL - HALO)
        for rows, positions in ((spectrum_rows, own), (rim_rows, rim)):
            high, low = halves(row_table(positions).T)
            rows.append(np.concatenate([high, low, high], axis=1))
        high, low = halves(pair_table(rim))
        halo_rows.append(np.concatenate([high, low, high], axis=1))
        high, low = halves(pair_table(own))
        own_rows.append(np.concatenate([high, low, high], axis=1))
        cols = slice(part * ROWS, (part + 1) * ROWS)
        high = np.concatenate([turned_high[:, :TP][:, cols], turned_high[:, TP:][:, cols]], axis=1)
        low = np.concatenate([turned_low[:, :TP][:, cols], turned_low[:, TP:][:, cols]], axis=1)
        forward.append(np.concatenate([high, high, low]))
        backward.append(np.concatenate([column_high[cols], column_high[cols], column_low[cols]]))
    out["spectrum_rows"] = np.stack(spectrum_rows)
    out["own_rows"] = np.stack(own_rows)
    out["rim_rows"] = np.stack(rim_rows)
    out["halo_rows"] = np.stack(halo_rows)
    out["forward"] = np.stack(forward)
    out["backward"] = np.stack(backward)
    out["turned"] = np.stack([column_high.T, column_low.T])
    out["row"] = np.concatenate([row_high, row_low, row_high], axis=1)
    out["row_turned"] = np.concatenate([row_high.T, row_low.T])
    return out


def part_of(ref):
    return ref[0] % PARTS


def has_adjoint_halo(ref):
    return ref[0] // PARTS % 2 > 0


def has_mask_halo(ref):
    return ref[0] // (2 * PARTS) > 0


def dot(left, right):
    return jnp.dot(left, right, preferred_element_type=F32)


def split(value):
    high = value.astype(BF)
    return high, (value - high.astype(F32)).astype(BF)


def lanes_and_rows():
    shape = (FA, 2 * FB)
    return lax.broadcasted_iota(jnp.int32, shape, 1), lax.broadcasted_iota(jnp.int32, shape, 0)


def pack(even, odd):
    lane, row = lanes_and_rows()
    packed = jnp.where(lane % FB < HALF, even, pltpu.roll(odd, HALF, 1))
    for place, value in ((FA - 2, even), (FA - 3, odd)):
        line = jnp.sum(jnp.where(lane == row, value[:, HALF : HALF + 1], 0.0), axis=0, keepdims=True)
        packed = jnp.where(row == place, line, packed)
    return packed


def unpack(packed):
    lane, row = lanes_and_rows()
    values = []
    for place, value in ((FA - 2, packed), (FA - 3, pltpu.roll(packed, 2 * FB - HALF, 1))):
        column = jnp.sum(jnp.where((lane == row) & (row <= HALF), packed[place : place + 1], 0.0), axis=1, keepdims=True)
        value = jnp.where(lane == HALF, column, jnp.where(lane % FB < HALF, value, 0.0))
        values.append(jnp.where(row <= HALF, value, 0.0))
    return values


def columns_of(mask, column_ref):
    high, low = split(mask)
    return dot(high, column_ref[0]) + dot(low, column_ref[0]) + dot(high, column_ref[1])


def spectrum_of(across, rows):
    high, low = split(across)
    both = dot(rows, jnp.concatenate([high, high, low], axis=0))
    even = both[:FA, : 2 * FB] - both[FA:, 2 * FB :]
    odd = both[FA:, : 2 * FB] + both[:FA, 2 * FB :]
    return even, odd


def open_kernel(
    part_ref, theta_hbm, waves_hbm, real_hbm, imag_hbm, thresholds_hbm, weights_hbm, forward_hbm, backward_hbm,
    out_ref, rim_ref, shares_ref, forward_ref, backward_ref, theta_ref, waves_ref, real_ref, imag_ref, thresholds_ref,
    weights_ref, stage, sems,
):
    part = part_of(part_ref)
    edge = pl.ds(pl.multiple_of(jnp.where(part == 0, 0, ROWS - HALO), HALO), HALO)
    moves = [
        (theta_hbm.at[edge], theta_ref),
        (waves_hbm, waves_ref),
        (real_hbm, real_ref),
        (imag_hbm, imag_ref),
        (thresholds_hbm, thresholds_ref),
        (weights_hbm, weights_ref),
        (forward_hbm.at[part], forward_ref),
        (backward_hbm.at[part], backward_ref),
    ]
    copies = [pltpu.make_async_copy(source, target, sems.at[i]) for i, (source, target) in enumerate(moves)]
    for copy in copies:
        copy.start()
    local_conds = real_ref.shape[0]
    mats = local_conds * KERNELS * 2
    stage[...] = jnp.zeros_like(stage)
    rows = stage.shape[1]
    source = lax.broadcasted_iota(jnp.int32, (2 * FB, 4 * FB), 0)
    target = lax.broadcasted_iota(jnp.int32, (2 * FB, 4 * FB), 1)
    lane = target % FB
    block = target // FB
    plus = (block == 0) | (block == 3)
    freq = jnp.where(lane < HALF, lane + 1, 0)
    used = (lane < HALF) | ((lane == HALF) & (block % 2 == 0))
    pick = (used & (source == jnp.where(plus, HALF + freq, HALF - freq))).astype(F32).astype(BF)
    source = lax.broadcasted_iota(jnp.int32, (FA, 2 * rows), 1) % rows
    target = lax.broadcasted_iota(jnp.int32, (FA, 2 * rows), 0)
    turn = ((source == HALF - target) & (target <= HALF)).astype(F32).astype(BF)
    lane = lax.broadcasted_iota(jnp.int32, (FA, 2 * FB), 1)
    row = lax.broadcasted_iota(jnp.int32, (FA, 2 * FB), 0)
    valid = (row <= HALF) & ((lane <= HALF) | ((row > 0) & (lane >= FB) & (lane < FB + HALF)))
    scale = 1.0 / (FULL * FULL)
    keep_top = jnp.where(valid, scale, 0.0)
    keep_bottom = jnp.where((row == 0) & (lane == HALF), 0.0, keep_top)
    first = lane % FB < HALF
    for copy in copies[:6]:
        copy.wait()
    rim_ref[...] = columns_of(jnp.tanh(mask_steep * theta_ref[...]), waves_ref)
    for cond in range(local_conds):
        for kern in range(KERNELS):
            for piece, ref in enumerate((real_ref, imag_ref)):
                stage[(cond * KERNELS + kern) * 2 + piece, :KSUP, :KSUP] = ref[cond, :, kern, :]
    high, low = split(stage[...].reshape(mats * rows, 2 * FB))
    picked = [dot(piece, pick) for piece in (high, low)]
    extra = jnp.zeros((FA, 2 * FB), F32)
    blocks = []
    for kern in range(local_conds * KERNELS):
        arrays = [[], []]
        for piece in range(2):
            start = (kern * 2 + piece) * rows
            top = picked[0][start + HALF : start + HALF + FA, : 2 * FB] + picked[1][start + HALF : start + HALF + FA, : 2 * FB]
            pieces = jnp.concatenate([half[start : start + rows, 2 * FB :] for half in picked], axis=0)
            bottom = dot(turn, pieces.astype(BF)) * keep_bottom
            top = top * keep_top
            arrays[0].append(top + bottom)
            arrays[1].append(top - bottom)
        for which, (real, imag) in enumerate(arrays):
            blocks.append(jnp.where(first, real, pltpu.roll(imag, HALF, 1)))
            for piece, value in enumerate((real, imag)):
                place = kern * 4 + which * 2 + piece
                extra = jnp.where(lane == place, pltpu.roll(value, (place - HALF) % (2 * FB), 1), extra)
    for i, block in enumerate(blocks):
        if i < SPARE_BLOCKS:
            block = jnp.concatenate([block[: HALF + 1], extra[SPARE * i : SPARE * (i + 1)]], axis=0)
        elif i < SPARE_BLOCKS + local_conds:
            block = jnp.where(row == FA - 1, thresholds_ref[i - SPARE_BLOCKS], block)
        out_ref[i] = block
    weight_sum = weights_ref[0]
    for i in range(1, CONDS):
        weight_sum = weight_sum + weights_ref[i]
    row = lax.broadcasted_iota(jnp.int32, shares_ref.shape, 0)
    shares = jnp.zeros(shares_ref.shape, F32)
    for group, step in enumerate((0, 3, 1, 2)):
        for i in range(local_conds):
            weight = weights_ref[lax.bitwise_xor(part, step) * local_conds + i]
            shares = jnp.where(row == group * local_conds + i, weight.astype(F32), shares)
    shares_ref[...] = shares / weight_sum.astype(F32)
    for copy in copies[6:]:
        copy.wait()


def spectrum_kernel(part_ref, theta_ref, column_ref, rows_ref, out_ref):
    across = columns_of(jnp.tanh(mask_steep * theta_ref[...]), column_ref)
    even, odd = spectrum_of(across, rows_ref[part_of(part_ref)])
    out_ref[0] = even
    out_ref[1] = odd


def rim_kernel(part_ref, spectrum_ref, rim_ref, rows_ref, out_ref):
    rim = jnp.where(has_mask_halo(part_ref), rim_ref[...], 0.0)
    turned = pltpu.roll(rim, FB, 1)
    first = lax.broadcasted_iota(jnp.int32, rim.shape, 1) < FB
    across = jnp.concatenate([jnp.where(first, rim, turned), jnp.where(first, turned, -rim)], axis=1)
    even, odd = spectrum_of(across, rows_ref[part_of(part_ref)])
    out_ref[0] = pack(even + spectrum_ref[0], odd + spectrum_ref[1])


def unpack_group(ref, put):
    lane, row = lanes_and_rows()
    zero_lane = (lane == HALF) & (row <= HALF)
    extra = [ref[i][HALF + 1 :] for i in range(SPARE_BLOCKS)]
    extra = jnp.concatenate(extra + [jnp.zeros((FA - SPARE * SPARE_BLOCKS, 2 * FB), F32)], axis=0)
    for kern in range(ref.shape[0] // 2):
        values = []
        for which in range(2):
            packed = ref[2 * kern + which]
            for part, value in enumerate((packed, pltpu.roll(packed, 2 * FB - HALF, 1))):
                place = kern * 4 + which * 2 + part
                zeroth = pltpu.roll(extra, (HALF - place) % (2 * FB), 1)
                values.append(jnp.where(zero_lane, zeroth, value))
        put(kern, values)


def near_kernels_kernel(part_ref, mixed_ref, target_ref, near_ref, signs_ref):
    local = near_ref.shape[0] // 2
    for group in range(2):
        def put(kern, values, group=group):
            for i, value in enumerate(values):
                near_ref[group * local + kern, i] = value

        unpack_group(mixed_ref.at[pl.ds(group * 2 * local, 2 * local)], put)
    own = pl.ds(pl.multiple_of(part_of(part_ref) * ROWS, ROWS), ROWS)
    signs_ref[...] = 1.0 - 2.0 * target_ref[:, own].astype(F32)


def fields_kernel(
    part_ref, mixed_ref, other_ref, near_ref, signs, shares_ref, forward_ref, backward_ref, row_ref,
    row_turned_ref, out_ref, far_ref, levels_ref, lines, folded, amps, tanhs, total, turned, backs,
):
    count = 2 * far_ref.shape[0]
    local = count // PARTS
    tall = 4 * FA
    each = 2 * local
    even, odd = unpack(mixed_ref[2 * each] + other_ref[2 * each])

    def put_line(kern, values):
        he_real, he_imag, ho_real, ho_imag = values
        start = kern * tall
        for i, value in enumerate(
            (
                even * he_real + odd * ho_imag,
                odd * he_real - even * ho_imag,
                even * he_imag - odd * ho_real,
                odd * he_imag + even * ho_real,
            )
        ):
            lines[start + i * FA : start + (i + 1) * FA] = value

    def arrays_of(kern):
        ref = near_ref if kern < count // 2 else far_ref
        return [ref[kern % (count // 2), i] for i in range(4)]

    for group in range(PARTS):
        ref = (mixed_ref, other_ref)[group // 2].at[pl.ds(group % 2 * each, each)]
        for i in range(CONDS // PARTS):
            place = group * (CONDS // PARTS) + i
            levels_ref[place : place + 1] = ref[SPARE_BLOCKS + i][FA - 1 :]
        if group < 2:
            for kern in range(group * local, (group + 1) * local):
                put_line(kern, arrays_of(kern))
        else:
            def put(kern, values, group=group):
                for i, value in enumerate(values):
                    far_ref[(group - 2) * local + kern, i] = value
                put_line(group * local + kern, values)

            unpack_group(ref, put)

    high, low = split(lines[...])
    lines_folded = dot(jnp.concatenate([high, low], axis=1), forward_ref[: 4 * FB]) + dot(high, forward_ref[4 * FB :])
    for kern in range(count):
        parts = []
        for i in range(2):
            x_part = lines_folded[tall * kern + 2 * FA * i : tall * kern + 2 * FA * i + FA]
            y_part = lines_folded[tall * kern + 2 * FA * i + FA : tall * kern + 2 * FA * (i + 1)]
            parts.append(
                jnp.concatenate(
                    [x_part[:, :ROWS] + y_part[:, ROWS:], y_part[:, :ROWS] - x_part[:, ROWS:]], axis=0
                )
            )
        high, low = split(jnp.concatenate(parts, axis=1))
        folded[kern] = jnp.concatenate([high, high, low], axis=0)
    total[...] = jnp.zeros_like(total)

    def expose(cond, carry):
        intensity = None
        for kern in range(KERNELS):
            index = cond * KERNELS + kern
            amp = dot(row_ref[...], folded[index])
            amps[index] = amp
            power = amp[:, :ROWS] * amp[:, :ROWS] + amp[:, ROWS:] * amp[:, ROWS:]
            intensity = power if intensity is None else intensity + power
        level = levels_ref[pl.ds(cond, 1), :]
        value = jnp.tanh((0.5 * resist_steep) * (intensity - level))
        tanhs[cond] = value
        total[...] += value
        return carry

    lax.fori_loop(0, CONDS, expose, 0, unroll=4)
    total[...] = total[...] * (band_weight / (CONDS * CONDS))

    def drive(cond, carry):
        weight = shares_ref[pl.ds(cond, 1), :]
        value = tanhs[cond]
        slope = (weight + band_weight / CONDS) * value + weight * signs[...] - total[...]
        field = (0.5 * resist_steep) * (1.0 - value * value) * slope
        field = jnp.concatenate([field, field], axis=1)
        for kern in range(KERNELS):
            index = cond * KERNELS + kern
            high, low = split(field * amps[index])
            long = dot(row_turned_ref[...], high)
            back = long[: 2 * FA] + long[2 * FA :] + dot(row_turned_ref[: 2 * FA], low)
            turned[pl.ds(index * 2, 2)] = jnp.stack([back[:, :ROWS], back[:, ROWS:]])
        return carry

    lax.fori_loop(0, CONDS, drive, 0, unroll=4)
    high, low = split(turned[...].reshape(count * tall, ROWS))
    backs[...] = dot(jnp.concatenate([high, low], axis=1), backward_ref[: 2 * ROWS]) + dot(high, backward_ref[2 * ROWS :])

    sum_even = jnp.zeros((FA, 2 * FB), F32)
    sum_odd = jnp.zeros((FA, 2 * FB), F32)
    for kern in range(count):
        grads = []
        for i in range(2):
            c_part = backs[tall * kern + 2 * FA * i : tall * kern + 2 * FA * i + FA]
            s_part = backs[tall * kern + 2 * FA * i + FA : tall * kern + 2 * FA * (i + 1)]
            grads.append(
                (
                    c_part[:, : 2 * FB] - s_part[:, 2 * FB :],
                    s_part[:, : 2 * FB] + c_part[:, 2 * FB :],
                )
            )
        (x_real, y_real), (x_imag, y_imag) = grads
        he_real, he_imag, ho_real, ho_imag = arrays_of(kern)
        sum_even = sum_even + x_real * he_real + x_imag * he_imag - y_real * ho_imag + y_imag * ho_real
        sum_odd = sum_odd + x_real * ho_imag - x_imag * ho_real + y_real * he_real + y_imag * he_imag
    out_ref[...] = pack(sum_even, sum_odd)


def image_rows(packed, rows, turned_ref):
    high, low = split(jnp.concatenate(unpack(packed), axis=0))
    pair = dot(rows, jnp.concatenate([high, high, low], axis=0))
    count = pair.shape[0] // 2
    high, low = split(jnp.concatenate([pair[:count], pair[count:]], axis=1))
    return dot(high, turned_ref[0]) + dot(low, turned_ref[0]) + dot(high, turned_ref[1])


def edge_start(part_ref):
    return pl.multiple_of(jnp.where(part_of(part_ref) == PARTS - 1, ROWS - HALO, 0), HALO)


def gradient_kernel(part_ref, theta_ref, sum_ref, turned_ref, rows_ref, out_ref, edge_ref, scale_ref):
    part = part_of(part_ref)
    mask = jnp.tanh(mask_steep * theta_ref[...])
    scale = mask_steep * (1.0 - mask * mask)
    gradient = image_rows(sum_ref[...], rows_ref[part], turned_ref) * scale
    out_ref[...] = gradient
    last = part == PARTS - 1
    edge_ref[...] = jnp.where(last, gradient[ROWS - HALO :], gradient[:HALO])
    scale_ref[...] = jnp.where(last, scale[ROWS - HALO :], scale[:HALO])


def edge_kernel(part_ref, gradient_hbm, edge_ref, scale_ref, near_ref, turned_ref, rows_ref, out_hbm, stage, sem):
    @pl.when(has_adjoint_halo(part_ref))
    def _():
        rim = image_rows(near_ref[...], rows_ref[part_of(part_ref)], turned_ref)
        stage[...] = edge_ref[...] + rim * scale_ref[...]
        copy = pltpu.make_async_copy(stage, out_hbm.at[pl.ds(edge_start(part_ref), HALO)], sem)
        copy.start()
        copy.wait()


def whole_spec(array):
    del array
    return pl.BlockSpec(memory_space=pltpu.VMEM)


def call(kernel, scalars, operands, specs, out_shapes, scratch=(), name=None, flops=1 << 28, out_specs=None, aliases=None):
    many = isinstance(out_shapes, list)
    if out_specs is None:
        out_specs = [whole_spec(shape) for shape in out_shapes] if many else whole_spec(out_shapes)
    return pl.pallas_call(
        kernel,
        grid_spec=pltpu.PrefetchScalarGridSpec(
            num_scalar_prefetch=len(scalars),
            grid=(1,),
            in_specs=specs,
            out_specs=out_specs,
            scratch_shapes=list(scratch),
        ),
        out_shape=out_shapes,
        input_output_aliases=aliases or {},
        compiler_params=pltpu.CompilerParams(vmem_limit_bytes=48 * 1024 * 1024),
        cost_estimate=pl.CostEstimate(flops=flops, bytes_accessed=1 << 20, transcendentals=0),
        name=name,
    )(*scalars, *operands)


def floats(*shape):
    return jax.ShapeDtypeStruct(shape, F32)


def shards(theta, target, kernel_real, kernel_imag, weights, thresholds):
    table = {name: jnp.asarray(value) for name, value in tables().items()}
    tiles = lax.axis_size("tile")
    part = lax.axis_index("cond")
    tile = lax.axis_index("tile")
    last = PARTS - 1
    above = ((part == 0) & (tile > 0)) | ((part == last) & (tile < tiles - 1))
    below = ((part == 0) & (tile < tiles - 1)) | ((part == last) & (tile > 0))
    parts = (part + PARTS * above.astype(jnp.int32) + 2 * PARTS * below.astype(jnp.int32)).reshape(1).astype(jnp.int32)
    local_conds = kernel_real.shape[0]
    local = local_conds * KERNELS
    count = CONDS * KERNELS
    hbm = pl.BlockSpec(memory_space=pltpu.HBM)

    def across(value, down, up, within):
        pairs = [(PARTS * i + a, PARTS * i + b) for i in range(tiles) for a, b in within]
        pairs += [(PARTS * (i + 1) + down[0], PARTS * i + down[1]) for i in range(tiles - 1)]
        pairs += [(PARTS * i + up[0], PARTS * (i + 1) + up[1]) for i in range(tiles - 1)]
        pairs += [(down[0], up[1]), (PARTS * (tiles - 1) + up[0], PARTS * (tiles - 1) + down[1])]
        return lax.ppermute(value, ("tile", "cond"), pairs)

    def partner(value, step):
        return lax.ppermute(value, "cond", [(i, i ^ step) for i in range(PARTS)])

    kernel_shape = (local_conds, KSUP, KERNELS, KSUP)
    own, rim, shares, forward, backward = call(
        open_kernel,
        (parts,),
        tuple(
            pltpu.with_memory_space_constraint(value, pltpu.HBM)
            for value in (
                theta, table["waves"], kernel_real.transpose(0, 2, 1, 3), kernel_imag.transpose(0, 2, 1, 3), thresholds, weights,
                table["forward"], table["backward"],
            )
        ),
        [hbm] * 8,
        [
            floats(2 * local, FA, 2 * FB),
            floats(HALO, 2 * FB),
            floats(CONDS, ROWS),
            jax.ShapeDtypeStruct(table["forward"].shape[1:], BF),
            jax.ShapeDtypeStruct(table["backward"].shape[1:], BF),
        ],
        scratch=(
            pltpu.VMEM((HALO, TP), F32),
            pltpu.VMEM(table["waves"].shape, BF),
            pltpu.VMEM(kernel_shape, F32),
            pltpu.VMEM(kernel_shape, F32),
            pltpu.SMEM(thresholds.shape, F32),
            pltpu.SMEM(weights.shape, jnp.int32),
            pltpu.VMEM((2 * local, 72, 2 * FB), F32),
            pltpu.SemaphoreType.DMA((8,)),
        ),
        name="open_parts",
    )
    rim = across(rim, (0, 0), (last, last), [(1, 2), (2, 1)])
    spectrum = call(
        spectrum_kernel,
        (parts,),
        (theta, table["column"], table["spectrum_rows"]),
        [whole_spec(theta), whole_spec(table["column"]), whole_spec(table["spectrum_rows"])],
        floats(2, FA, 2 * FB),
        name="own_spectrum",
        flops=1 << 31,
    )
    side = partner(own, 3)
    spectrum = call(
        rim_kernel,
        (parts,),
        (spectrum, rim, table["rim_rows"]),
        [whole_spec(spectrum), whole_spec(rim), whole_spec(table["rim_rows"])],
        floats(1, FA, 2 * FB),
        name="add_rim",
    )
    mixed = jnp.concatenate([own, side, spectrum + partner(spectrum, 3)], axis=0)
    near_kernels, signs = call(
        near_kernels_kernel,
        (parts,),
        (mixed, target),
        [whole_spec(mixed), whole_spec(target)],
        [floats(count // 2, 4, FA, 2 * FB), floats(TP, ROWS)],
        name="near_kernels",
        flops=1 << 30,
    )
    adjoint = call(
        fields_kernel,
        (parts,),
        (
            mixed, partner(mixed, 1), near_kernels, signs, shares, forward, backward, table["row"], table["row_turned"],
        ),
        [
            whole_spec(mixed),
            whole_spec(mixed),
            whole_spec(near_kernels),
            whole_spec(signs),
            whole_spec(shares),
            whole_spec(forward),
            whole_spec(backward),
            whole_spec(table["row"]),
            whole_spec(table["row_turned"]),
        ],
        floats(FA, 2 * FB),
        scratch=(
            pltpu.VMEM((count // 2, 4, FA, 2 * FB), F32),
            pltpu.VMEM((CONDS, ROWS), F32),
            pltpu.VMEM((count * 4 * FA, 2 * FB), F32),
            pltpu.VMEM((count, 6 * FA, 2 * ROWS), BF),
            pltpu.VMEM((count, TP, 2 * ROWS), F32),
            pltpu.VMEM((CONDS, TP, ROWS), F32),
            pltpu.VMEM((TP, ROWS), F32),
            pltpu.VMEM((count * 2, 2 * FA, ROWS), F32),
            pltpu.VMEM((count * 4 * FA, 4 * FB), F32),
        ),
        name="coherent_fields",
        flops=1 << 33,
    )
    adjoint = adjoint + partner(adjoint, 1)
    adjoint = adjoint + partner(adjoint, 3)
    near = across(adjoint, (2, last), (1, 0), [(0, 1), (last, 2)])
    gradient, edge, scale = call(
        gradient_kernel,
        (parts,),
        (theta, adjoint, table["turned"], table["own_rows"]),
        [
            whole_spec(theta),
            whole_spec(adjoint),
            whole_spec(table["turned"]),
            whole_spec(table["own_rows"]),
        ],
        [floats(ROWS, TP), floats(HALO, TP), floats(HALO, TP)],
        out_specs=[
            pl.BlockSpec((ROWS, TP), lambda i, *refs: (0, 0)),
            whole_spec(adjoint),
            whole_spec(adjoint),
        ],
        name="own_gradient",
        flops=1 << 31,
    )
    return call(
        edge_kernel,
        (parts,),
        (gradient, edge, scale, near, table["turned"], table["halo_rows"]),
        [
            hbm,
            whole_spec(edge),
            whole_spec(scale),
            whole_spec(near),
            whole_spec(table["turned"]),
            whole_spec(table["halo_rows"]),
        ],
        floats(ROWS, TP),
        scratch=(pltpu.VMEM((HALO, TP), F32), pltpu.SemaphoreType.DMA),
        name="edge_gradient",
        out_specs=hbm,
        aliases={1: 0},
    )


def solution(mesh):
    in_specs = (
        P(("tile", "cond"), None),
        P("tile", None),
        P("cond", None, None, None),
        P("cond", None, None, None),
        P(),
        P("cond"),
    )
    out_specs = P(("tile", "cond"), None)
    return jax.shard_map(shards, mesh=mesh, in_specs=in_specs, out_specs=out_specs, check_vma=False)
```

```python
import functools

import jax
import jax.numpy as jnp
import ml_dtypes
import numpy as np
from jax import lax
from jax.experimental import pallas as pl
from jax.experimental.pallas import tpu as pltpu
from jax.sharding import PartitionSpec as P

TP = 512
HALO = 32
KSUP = 65
HALF = KSUP // 2
KERNELS = 2
CONDS = 8
FULL = TP + 2 * HALO
PARTS = 4
ROWS = TP // PARTS
FA = 40
FB = 64
SPARE = FA - HALF - 1
SPARE_BLOCKS = -(-(HALF + 1) // SPARE)
BF = jnp.bfloat16
F32 = jnp.float32

mask_steep = 2.0
resist_steep = 4.0
band_weight = 1.0


def waves(positions):
    angles = (np.outer(np.asarray(positions, np.int64), np.arange(HALF + 1)) % FULL) * (2.0 * np.pi / FULL)
    return np.cos(angles), np.sin(angles)


def halves(table):
    high = table.astype(np.float32).astype(ml_dtypes.bfloat16)
    low = (table - high.astype(np.float64)).astype(np.float32).astype(ml_dtypes.bfloat16)
    return high, low


def row_table(positions):
    cosine, sine = waves(positions)
    table = np.zeros((len(positions), 2 * FA))
    table[:, : HALF + 1] = cosine
    table[:, FA : FA + HALF + 1] = sine
    return table


def pair_table(positions):
    table = row_table(positions)
    return np.concatenate([table, np.concatenate([-table[:, FA:], table[:, :FA]], axis=1)])


def column_table(positions):
    cosine, sine = waves(positions)
    table = np.zeros((len(positions), 4 * FB))
    for block, values in enumerate((cosine, cosine, sine, -sine)):
        table[:, block * FB : block * FB + HALF] = values[:, 1:]
    table[:, HALF] = 1.0
    return table


@functools.cache
def tables():
    pixels = np.arange(TP) + HALO
    column = column_table(pixels)
    column_high, column_low = halves(column)
    turned = np.concatenate([column[:, : 2 * FB].T, column[:, 2 * FB :].T], axis=1)
    turned_high, turned_low = halves(turned)
    row = row_table(pixels)
    row_high, row_low = halves(row)
    out = {}
    out["column"] = np.stack([column_high, column_low])
    waves_only = np.s_[:, np.r_[0:FB, 2 * FB : 3 * FB]]
    out["waves"] = np.stack([column_high[waves_only], column_low[waves_only]])
    spectrum_rows = []
    rim_rows = []
    halo_rows = []
    own_rows = []
    forward = []
    backward = []
    for part in range(PARTS):
        own = np.arange(ROWS) + part * ROWS + HALO
        rim = np.arange(HALO) + (0 if part == PARTS - 1 else FULL - HALO)
        for rows, positions in ((spectrum_rows, own), (rim_rows, rim)):
            high, low = halves(row_table(positions).T)
            rows.append(np.concatenate([high, low, high], axis=1))
        high, low = halves(pair_table(rim))
        halo_rows.append(np.concatenate([high, low, high], axis=1))
        high, low = halves(pair_table(own))
        own_rows.append(np.concatenate([high, low, high], axis=1))
        cols = slice(part * ROWS, (part + 1) * ROWS)
        high = np.concatenate([turned_high[:, :TP][:, cols], turned_high[:, TP:][:, cols]], axis=1)
        low = np.concatenate([turned_low[:, :TP][:, cols], turned_low[:, TP:][:, cols]], axis=1)
        forward.append(np.concatenate([high, high, low]))
        backward.append(np.concatenate([column_high[cols], column_high[cols], column_low[cols]]))
    out["spectrum_rows"] = np.stack(spectrum_rows)
    out["own_rows"] = np.stack(own_rows)
    out["rim_rows"] = np.stack(rim_rows)
    out["halo_rows"] = np.stack(halo_rows)
    out["forward"] = np.stack(forward)
    out["backward"] = np.stack(backward)
    out["turned"] = np.stack([column_high.T, column_low.T])
    out["row"] = np.concatenate([row_high, row_low, row_high], axis=1)
    out["row_turned"] = np.concatenate([row_high.T, row_low.T])
    return out


def part_of(ref):
    return ref[0] % PARTS


def has_adjoint_halo(ref):
    return ref[0] // PARTS % 2 > 0


def has_mask_halo(ref):
    return ref[0] // (2 * PARTS) > 0


def dot(left, right):
    return jnp.dot(left, right, preferred_element_type=F32)


def split(value):
    high = value.astype(BF)
    return high, (value - high.astype(F32)).astype(BF)


def lanes_and_rows():
    shape = (FA, 2 * FB)
    return lax.broadcasted_iota(jnp.int32, shape, 1), lax.broadcasted_iota(jnp.int32, shape, 0)


def pack(even, odd):
    lane, row = lanes_and_rows()
    packed = jnp.where(lane % FB < HALF, even, pltpu.roll(odd, HALF, 1))
    for place, value in ((FA - 2, even), (FA - 3, odd)):
        line = jnp.sum(jnp.where(lane == row, value[:, HALF : HALF + 1], 0.0), axis=0, keepdims=True)
        packed = jnp.where(row == place, line, packed)
    return packed


def unpack(packed):
    lane, row = lanes_and_rows()
    values = []
    for place, value in ((FA - 2, packed), (FA - 3, pltpu.roll(packed, 2 * FB - HALF, 1))):
        column = jnp.sum(jnp.where((lane == row) & (row <= HALF), packed[place : place + 1], 0.0), axis=1, keepdims=True)
        value = jnp.where(lane == HALF, column, jnp.where(lane % FB < HALF, value, 0.0))
        values.append(jnp.where(row <= HALF, value, 0.0))
    return values


def columns_of(mask, column_ref):
    high, low = split(mask)
    return dot(high, column_ref[0]) + dot(low, column_ref[0]) + dot(high, column_ref[1])


def spectrum_of(across, rows):
    high, low = split(across)
    both = dot(rows, jnp.concatenate([high, high, low], axis=0))
    even = both[:FA, : 2 * FB] - both[FA:, 2 * FB :]
    odd = both[FA:, : 2 * FB] + both[:FA, 2 * FB :]
    return even, odd


def open_kernel(
    part_ref, theta_hbm, waves_hbm, real_hbm, imag_hbm, thresholds_hbm, weights_hbm, forward_hbm, backward_hbm,
    out_ref, rim_ref, shares_ref, forward_ref, backward_ref, theta_ref, waves_ref, real_ref, imag_ref, thresholds_ref,
    weights_ref, stage, sems,
):
    part = part_of(part_ref)
    edge = pl.ds(pl.multiple_of(jnp.where(part == 0, 0, ROWS - HALO), HALO), HALO)
    moves = [
        (theta_hbm.at[edge], theta_ref),
        (waves_hbm, waves_ref),
        (real_hbm, real_ref),
        (imag_hbm, imag_ref),
        (thresholds_hbm, thresholds_ref),
        (weights_hbm, weights_ref),
        (forward_hbm.at[part], forward_ref),
        (backward_hbm.at[part], backward_ref),
    ]
    copies = [pltpu.make_async_copy(source, target, sems.at[i]) for i, (source, target) in enumerate(moves)]
    for copy in copies:
        copy.start()
    local_conds = real_ref.shape[0]
    mats = local_conds * KERNELS * 2
    stage[...] = jnp.zeros_like(stage)
    rows = stage.shape[1]
    source = lax.broadcasted_iota(jnp.int32, (2 * FB, 4 * FB), 0)
    target = lax.broadcasted_iota(jnp.int32, (2 * FB, 4 * FB), 1)
    lane = target % FB
    block = target // FB
    plus = (block == 0) | (block == 3)
    freq = jnp.where(lane < HALF, lane + 1, 0)
    used = (lane < HALF) | ((lane == HALF) & (block % 2 == 0))
    pick = (used & (source == jnp.where(plus, HALF + freq, HALF - freq))).astype(F32).astype(BF)
    source = lax.broadcasted_iota(jnp.int32, (FA, 2 * rows), 1) % rows
    target = lax.broadcasted_iota(jnp.int32, (FA, 2 * rows), 0)
    turn = ((source == HALF - target) & (target <= HALF)).astype(F32).astype(BF)
    lane = lax.broadcasted_iota(jnp.int32, (FA, 2 * FB), 1)
    row = lax.broadcasted_iota(jnp.int32, (FA, 2 * FB), 0)
    valid = (row <= HALF) & ((lane <= HALF) | ((row > 0) & (lane >= FB) & (lane < FB + HALF)))
    scale = 1.0 / (FULL * FULL)
    keep_top = jnp.where(valid, scale, 0.0)
    keep_bottom = jnp.where((row == 0) & (lane == HALF), 0.0, keep_top)
    first = lane % FB < HALF
    for copy in copies[:6]:
        copy.wait()
    rim_ref[...] = columns_of(jnp.tanh(mask_steep * theta_ref[...]), waves_ref)
    for cond in range(local_conds):
        for kern in range(KERNELS):
            for piece, ref in enumerate((real_ref, imag_ref)):
                stage[(cond * KERNELS + kern) * 2 + piece, :KSUP, :KSUP] = ref[cond, :, kern, :]
    high, low = split(stage[...].reshape(mats * rows, 2 * FB))
    picked = [dot(piece, pick) for piece in (high, low)]
    extra = jnp.zeros((FA, 2 * FB), F32)
    blocks = []
    for kern in range(local_conds * KERNELS):
        arrays = [[], []]
        for piece in range(2):
            start = (kern * 2 + piece) * rows
            top = picked[0][start + HALF : start + HALF + FA, : 2 * FB] + picked[1][start + HALF : start + HALF + FA, : 2 * FB]
            pieces = jnp.concatenate([half[start : start + rows, 2 * FB :] for half in picked], axis=0)
            bottom = dot(turn, pieces.astype(BF)) * keep_bottom
            top = top * keep_top
            arrays[0].append(top + bottom)
            arrays[1].append(top - bottom)
        for which, (real, imag) in enumerate(arrays):
            blocks.append(jnp.where(first, real, pltpu.roll(imag, HALF, 1)))
            for piece, value in enumerate((real, imag)):
                place = kern * 4 + which * 2 + piece
                extra = jnp.where(lane == place, pltpu.roll(value, (place - HALF) % (2 * FB), 1), extra)
    for i, block in enumerate(blocks):
        if i < SPARE_BLOCKS:
            block = jnp.concatenate([block[: HALF + 1], extra[SPARE * i : SPARE * (i + 1)]], axis=0)
        elif i < SPARE_BLOCKS + local_conds:
            block = jnp.where(row == FA - 1, thresholds_ref[i - SPARE_BLOCKS], block)
        out_ref[i] = block
    weight_sum = weights_ref[0]
    for i in range(1, CONDS):
        weight_sum = weight_sum + weights_ref[i]
    row = lax.broadcasted_iota(jnp.int32, shares_ref.shape, 0)
    shares = jnp.zeros(shares_ref.shape, F32)
    for group, step in enumerate((0, 3, 1, 2)):
        for i in range(local_conds):
            weight = weights_ref[lax.bitwise_xor(part, step) * local_conds + i]
            shares = jnp.where(row == group * local_conds + i, weight.astype(F32), shares)
    shares_ref[...] = shares / weight_sum.astype(F32)
    for copy in copies[6:]:
        copy.wait()


def spectrum_kernel(part_ref, theta_ref, column_ref, rows_ref, out_ref):
    across = columns_of(jnp.tanh(mask_steep * theta_ref[...]), column_ref)
    even, odd = spectrum_of(across, rows_ref[part_of(part_ref)])
    out_ref[0] = even
    out_ref[1] = odd


def rim_kernel(part_ref, spectrum_ref, rim_ref, rows_ref, out_ref):
    rim = jnp.where(has_mask_halo(part_ref), rim_ref[...], 0.0)
    turned = pltpu.roll(rim, FB, 1)
    first = lax.broadcasted_iota(jnp.int32, rim.shape, 1) < FB
    across = jnp.concatenate([jnp.where(first, rim, turned), jnp.where(first, turned, -rim)], axis=1)
    even, odd = spectrum_of(across, rows_ref[part_of(part_ref)])
    out_ref[0] = pack(even + spectrum_ref[0], odd + spectrum_ref[1])


def unpack_group(ref, put):
    lane, row = lanes_and_rows()
    zero_lane = (lane == HALF) & (row <= HALF)
    extra = [ref[i][HALF + 1 :] for i in range(SPARE_BLOCKS)]
    extra = jnp.concatenate(extra + [jnp.zeros((FA - SPARE * SPARE_BLOCKS, 2 * FB), F32)], axis=0)
    for kern in range(ref.shape[0] // 2):
        values = []
        for which in range(2):
            packed = ref[2 * kern + which]
            for part, value in enumerate((packed, pltpu.roll(packed, 2 * FB - HALF, 1))):
                place = kern * 4 + which * 2 + part
                zeroth = pltpu.roll(extra, (HALF - place) % (2 * FB), 1)
                values.append(jnp.where(zero_lane, zeroth, value))
        put(kern, values)


def near_kernels_kernel(part_ref, mixed_ref, target_ref, near_ref, signs_ref):
    local = near_ref.shape[0] // 2
    for group in range(2):
        def put(kern, values, group=group):
            for i, value in enumerate(values):
                near_ref[group * local + kern, i] = value

        unpack_group(mixed_ref.at[pl.ds(group * 2 * local, 2 * local)], put)
    own = pl.ds(pl.multiple_of(part_of(part_ref) * ROWS, ROWS), ROWS)
    signs_ref[...] = 1.0 - 2.0 * target_ref[:, own].astype(F32)


def fields_kernel(
    part_ref, mixed_ref, other_ref, near_ref, signs, shares_ref, forward_ref, backward_ref, row_ref,
    row_turned_ref, out_ref, far_ref, levels_ref, lines, folded, amps, tanhs, total, turned, backs,
):
    count = 2 * far_ref.shape[0]
    local = count // PARTS
    tall = 4 * FA
    each = 2 * local
    even, odd = unpack(mixed_ref[2 * each] + other_ref[2 * each])

    def write_lines(ref, offset):
        def body(kern, carry):
            he_real, he_imag, ho_real, ho_imag = (ref[kern, i] for i in range(4))
            start = (kern + offset) * tall
            for i, value in enumerate(
                (
                    even * he_real + odd * ho_imag,
                    odd * he_real - even * ho_imag,
                    even * he_imag - odd * ho_real,
                    odd * he_imag + even * ho_real,
                )
            ):
                lines[pl.ds(pl.multiple_of(start + i * FA, FA), FA)] = value
            return carry

        lax.fori_loop(0, count // 2, body, 0, unroll=2)

    for group in range(PARTS):
        ref = (mixed_ref, other_ref)[group // 2].at[pl.ds(group % 2 * each, each)]
        for i in range(CONDS // PARTS):
            place = group * (CONDS // PARTS) + i
            levels_ref[place : place + 1] = ref[SPARE_BLOCKS + i][FA - 1 :]
        if group >= 2:

            def put(kern, values, group=group):
                for i, value in enumerate(values):
                    far_ref[(group - 2) * local + kern, i] = value

            unpack_group(ref, put)
    write_lines(near_ref, 0)
    write_lines(far_ref, count // 2)

    high, low = split(lines[...])
    backs[...] = dot(jnp.concatenate([high, low], axis=1), forward_ref[: 4 * FB]) + dot(high, forward_ref[4 * FB :])

    def rows_of(kern, i):
        start = kern * tall + 2 * FA * i
        return (backs[pl.ds(pl.multiple_of(start + j * FA, FA), FA)] for j in range(2))

    def fold(kern, carry):
        parts = []
        for i in range(2):
            x_part, y_part = rows_of(kern, i)
            parts.append(
                jnp.concatenate(
                    [x_part[:, :ROWS] + y_part[:, ROWS:], y_part[:, :ROWS] - x_part[:, ROWS:]], axis=0
                )
            )
        high, low = split(jnp.concatenate(parts, axis=1))
        folded[kern] = jnp.concatenate([high, high, low], axis=0)
        return carry

    lax.fori_loop(0, count, fold, 0, unroll=2)
    total[...] = jnp.zeros_like(total)

    def expose(cond, carry):
        intensity = None
        for kern in range(KERNELS):
            index = cond * KERNELS + kern
            amp = dot(row_ref[...], folded[index])
            amps[index] = amp
            power = amp[:, :ROWS] * amp[:, :ROWS] + amp[:, ROWS:] * amp[:, ROWS:]
            intensity = power if intensity is None else intensity + power
        level = levels_ref[pl.ds(cond, 1), :]
        value = jnp.tanh((0.5 * resist_steep) * (intensity - level))
        tanhs[cond] = value
        total[...] += value
        return carry

    lax.fori_loop(0, CONDS, expose, 0, unroll=4)
    total[...] = total[...] * (band_weight / (CONDS * CONDS))

    def drive(cond, carry):
        weight = shares_ref[pl.ds(cond, 1), :]
        value = tanhs[cond]
        slope = (weight + band_weight / CONDS) * value + weight * signs[...] - total[...]
        field = (0.5 * resist_steep) * (1.0 - value * value) * slope
        field = jnp.concatenate([field, field], axis=1)
        for kern in range(KERNELS):
            index = cond * KERNELS + kern
            high, low = split(field * amps[index])
            long = dot(row_turned_ref[...], high)
            back = long[: 2 * FA] + long[2 * FA :] + dot(row_turned_ref[: 2 * FA], low)
            turned[pl.ds(index * 2, 2)] = jnp.stack([back[:, :ROWS], back[:, ROWS:]])
        return carry

    lax.fori_loop(0, CONDS, drive, 0, unroll=4)
    high, low = split(turned[...].reshape(count * tall, ROWS))
    backs[...] = dot(jnp.concatenate([high, low], axis=1), backward_ref[: 2 * ROWS]) + dot(high, backward_ref[2 * ROWS :])

    sums = (jnp.zeros((FA, 2 * FB), F32),) * 2
    for offset, ref in ((0, near_ref), (count // 2, far_ref)):

        def gather(kern, carry, offset=offset, ref=ref):
            sum_even, sum_odd = carry
            grads = []
            for i in range(2):
                c_part, s_part = rows_of(kern + offset, i)
                grads.append(
                    (
                        c_part[:, : 2 * FB] - s_part[:, 2 * FB :],
                        s_part[:, : 2 * FB] + c_part[:, 2 * FB :],
                    )
                )
            (x_real, y_real), (x_imag, y_imag) = grads
            he_real, he_imag, ho_real, ho_imag = (ref[kern, i] for i in range(4))
            sum_even = sum_even + x_real * he_real + x_imag * he_imag - y_real * ho_imag + y_imag * ho_real
            sum_odd = sum_odd + x_real * ho_imag - x_imag * ho_real + y_real * he_real + y_imag * he_imag
            return sum_even, sum_odd

        sums = lax.fori_loop(0, count // 2, gather, sums, unroll=2)
    sum_even, sum_odd = sums
    out_ref[...] = pack(sum_even, sum_odd)


def image_rows(packed, rows, turned_ref):
    high, low = split(jnp.concatenate(unpack(packed), axis=0))
    pair = dot(rows, jnp.concatenate([high, high, low], axis=0))
    count = pair.shape[0] // 2
    high, low = split(jnp.concatenate([pair[:count], pair[count:]], axis=1))
    return dot(high, turned_ref[0]) + dot(low, turned_ref[0]) + dot(high, turned_ref[1])


def edge_start(part_ref):
    return pl.multiple_of(jnp.where(part_of(part_ref) == PARTS - 1, ROWS - HALO, 0), HALO)


def gradient_kernel(part_ref, theta_ref, sum_ref, turned_ref, rows_ref, out_ref, edge_ref, scale_ref):
    part = part_of(part_ref)
    mask = jnp.tanh(mask_steep * theta_ref[...])
    scale = mask_steep * (1.0 - mask * mask)
    gradient = image_rows(sum_ref[...], rows_ref[part], turned_ref) * scale
    out_ref[...] = gradient
    last = part == PARTS - 1
    edge_ref[...] = jnp.where(last, gradient[ROWS - HALO :], gradient[:HALO])
    scale_ref[...] = jnp.where(last, scale[ROWS - HALO :], scale[:HALO])


def edge_kernel(part_ref, gradient_hbm, edge_ref, scale_ref, near_ref, turned_ref, rows_ref, out_hbm, stage, sem):
    @pl.when(has_adjoint_halo(part_ref))
    def _():
        rim = image_rows(near_ref[...], rows_ref[part_of(part_ref)], turned_ref)
        stage[...] = edge_ref[...] + rim * scale_ref[...]
        copy = pltpu.make_async_copy(stage, out_hbm.at[pl.ds(edge_start(part_ref), HALO)], sem)
        copy.start()
        copy.wait()


def whole_spec(array):
    del array
    return pl.BlockSpec(memory_space=pltpu.VMEM)


def call(kernel, scalars, operands, specs, out_shapes, scratch=(), name=None, flops=1 << 28, out_specs=None, aliases=None):
    many = isinstance(out_shapes, list)
    if out_specs is None:
        out_specs = [whole_spec(shape) for shape in out_shapes] if many else whole_spec(out_shapes)
    return pl.pallas_call(
        kernel,
        grid_spec=pltpu.PrefetchScalarGridSpec(
            num_scalar_prefetch=len(scalars),
            grid=(1,),
            in_specs=specs,
            out_specs=out_specs,
            scratch_shapes=list(scratch),
        ),
        out_shape=out_shapes,
        input_output_aliases=aliases or {},
        compiler_params=pltpu.CompilerParams(vmem_limit_bytes=48 * 1024 * 1024),
        cost_estimate=pl.CostEstimate(flops=flops, bytes_accessed=1 << 20, transcendentals=0),
        name=name,
    )(*scalars, *operands)


def floats(*shape):
    return jax.ShapeDtypeStruct(shape, F32)


def shards(theta, target, kernel_real, kernel_imag, weights, thresholds):
    table = {name: jnp.asarray(value) for name, value in tables().items()}
    tiles = lax.axis_size("tile")
    part = lax.axis_index("cond")
    tile = lax.axis_index("tile")
    last = PARTS - 1
    above = ((part == 0) & (tile > 0)) | ((part == last) & (tile < tiles - 1))
    below = ((part == 0) & (tile < tiles - 1)) | ((part == last) & (tile > 0))
    parts = (part + PARTS * above.astype(jnp.int32) + 2 * PARTS * below.astype(jnp.int32)).reshape(1).astype(jnp.int32)
    local_conds = kernel_real.shape[0]
    local = local_conds * KERNELS
    count = CONDS * KERNELS
    hbm = pl.BlockSpec(memory_space=pltpu.HBM)

    def across(value, down, up, within):
        pairs = [(PARTS * i + a, PARTS * i + b) for i in range(tiles) for a, b in within]
        pairs += [(PARTS * (i + 1) + down[0], PARTS * i + down[1]) for i in range(tiles - 1)]
        pairs += [(PARTS * i + up[0], PARTS * (i + 1) + up[1]) for i in range(tiles - 1)]
        pairs += [(down[0], up[1]), (PARTS * (tiles - 1) + up[0], PARTS * (tiles - 1) + down[1])]
        return lax.ppermute(value, ("tile", "cond"), pairs)

    def partner(value, step):
        return lax.ppermute(value, "cond", [(i, i ^ step) for i in range(PARTS)])

    kernel_shape = (local_conds, KSUP, KERNELS, KSUP)
    own, rim, shares, forward, backward = call(
        open_kernel,
        (parts,),
        tuple(
            pltpu.with_memory_space_constraint(value, pltpu.HBM)
            for value in (
                theta, table["waves"], kernel_real.transpose(0, 2, 1, 3), kernel_imag.transpose(0, 2, 1, 3), thresholds, weights,
                table["forward"], table["backward"],
            )
        ),
        [hbm] * 8,
        [
            floats(2 * local, FA, 2 * FB),
            floats(HALO, 2 * FB),
            floats(CONDS, ROWS),
            jax.ShapeDtypeStruct(table["forward"].shape[1:], BF),
            jax.ShapeDtypeStruct(table["backward"].shape[1:], BF),
        ],
        scratch=(
            pltpu.VMEM((HALO, TP), F32),
            pltpu.VMEM(table["waves"].shape, BF),
            pltpu.VMEM(kernel_shape, F32),
            pltpu.VMEM(kernel_shape, F32),
            pltpu.SMEM(thresholds.shape, F32),
            pltpu.SMEM(weights.shape, jnp.int32),
            pltpu.VMEM((2 * local, 72, 2 * FB), F32),
            pltpu.SemaphoreType.DMA((8,)),
        ),
        name="open_parts",
    )
    rim = across(rim, (0, 0), (last, last), [(1, 2), (2, 1)])
    spectrum = call(
        spectrum_kernel,
        (parts,),
        (theta, table["column"], table["spectrum_rows"]),
        [whole_spec(theta), whole_spec(table["column"]), whole_spec(table["spectrum_rows"])],
        floats(2, FA, 2 * FB),
        name="own_spectrum",
        flops=1 << 31,
    )
    side = partner(own, 3)
    spectrum = call(
        rim_kernel,
        (parts,),
        (spectrum, rim, table["rim_rows"]),
        [whole_spec(spectrum), whole_spec(rim), whole_spec(table["rim_rows"])],
        floats(1, FA, 2 * FB),
        name="add_rim",
    )
    mixed = jnp.concatenate([own, side, spectrum + partner(spectrum, 3)], axis=0)
    near_kernels, signs = call(
        near_kernels_kernel,
        (parts,),
        (mixed, target),
        [whole_spec(mixed), whole_spec(target)],
        [floats(count // 2, 4, FA, 2 * FB), floats(TP, ROWS)],
        name="near_kernels",
        flops=1 << 30,
    )
    adjoint = call(
        fields_kernel,
        (parts,),
        (
            mixed, partner(mixed, 1), near_kernels, signs, shares, forward, backward, table["row"], table["row_turned"],
        ),
        [
            whole_spec(mixed),
            whole_spec(mixed),
            whole_spec(near_kernels),
            whole_spec(signs),
            whole_spec(shares),
            whole_spec(forward),
            whole_spec(backward),
            whole_spec(table["row"]),
            whole_spec(table["row_turned"]),
        ],
        floats(FA, 2 * FB),
        scratch=(
            pltpu.VMEM((count // 2, 4, FA, 2 * FB), F32),
            pltpu.VMEM((CONDS, ROWS), F32),
            pltpu.VMEM((count * 4 * FA, 2 * FB), F32),
            pltpu.VMEM((count, 6 * FA, 2 * ROWS), BF),
            pltpu.VMEM((count, TP, 2 * ROWS), F32),
            pltpu.VMEM((CONDS, TP, ROWS), F32),
            pltpu.VMEM((TP, ROWS), F32),
            pltpu.VMEM((count * 2, 2 * FA, ROWS), F32),
            pltpu.VMEM((count * 4 * FA, 4 * FB), F32),
        ),
        name="coherent_fields",
        flops=1 << 33,
    )
    adjoint = adjoint + partner(adjoint, 1)
    adjoint = adjoint + partner(adjoint, 3)
    near = across(adjoint, (2, last), (1, 0), [(0, 1), (last, 2)])
    gradient, edge, scale = call(
        gradient_kernel,
        (parts,),
        (theta, adjoint, table["turned"], table["own_rows"]),
        [
            whole_spec(theta),
            whole_spec(adjoint),
            whole_spec(table["turned"]),
            whole_spec(table["own_rows"]),
        ],
        [floats(ROWS, TP), floats(HALO, TP), floats(HALO, TP)],
        out_specs=[
            pl.BlockSpec((ROWS, TP), lambda i, *refs: (0, 0)),
            whole_spec(adjoint),
            whole_spec(adjoint),
        ],
        name="own_gradient",
        flops=1 << 31,
    )
    return call(
        edge_kernel,
        (parts,),
        (gradient, edge, scale, near, table["turned"], table["halo_rows"]),
        [
            hbm,
            whole_spec(edge),
            whole_spec(scale),
            whole_spec(near),
            whole_spec(table["turned"]),
            whole_spec(table["halo_rows"]),
        ],
        floats(ROWS, TP),
        scratch=(pltpu.VMEM((HALO, TP), F32), pltpu.SemaphoreType.DMA),
        name="edge_gradient",
        out_specs=hbm,
        aliases={1: 0},
    )


def solution(mesh):
    in_specs = (
        P(("tile", "cond"), None),
        P("tile", None),
        P("cond", None, None, None),
        P("cond", None, None, None),
        P(),
        P("cond"),
    )
    out_specs = P(("tile", "cond"), None)
    return jax.shard_map(shards, mesh=mesh, in_specs=in_specs, out_specs=out_specs, check_vma=False)
```

```python
import functools

import jax
import jax.numpy as jnp
import ml_dtypes
import numpy as np
from jax import lax
from jax.experimental import pallas as pl
from jax.experimental.pallas import tpu as pltpu
from jax.sharding import PartitionSpec as P

TP = 512
HALO = 32
KSUP = 65
HALF = KSUP // 2
KERNELS = 2
CONDS = 8
FULL = TP + 2 * HALO
PARTS = 4
ROWS = TP // PARTS
FA = 40
FB = 64
SPARE = FA - HALF - 1
SPARE_BLOCKS = -(-(HALF + 1) // SPARE)
BF = jnp.bfloat16
F32 = jnp.float32

mask_steep = 2.0
resist_steep = 4.0
band_weight = 1.0


def waves(positions):
    angles = (np.outer(np.asarray(positions, np.int64), np.arange(HALF + 1)) % FULL) * (2.0 * np.pi / FULL)
    return np.cos(angles), np.sin(angles)


def halves(table):
    high = table.astype(np.float32).astype(ml_dtypes.bfloat16)
    low = (table - high.astype(np.float64)).astype(np.float32).astype(ml_dtypes.bfloat16)
    return high, low


def row_table(positions):
    cosine, sine = waves(positions)
    table = np.zeros((len(positions), 2 * FA))
    table[:, : HALF + 1] = cosine
    table[:, FA : FA + HALF + 1] = sine
    return table


def pair_table(positions):
    table = row_table(positions)
    return np.concatenate([table, np.concatenate([-table[:, FA:], table[:, :FA]], axis=1)])


def column_table(positions):
    cosine, sine = waves(positions)
    table = np.zeros((len(positions), 4 * FB))
    for block, values in enumerate((cosine, cosine, sine, -sine)):
        table[:, block * FB : block * FB + HALF] = values[:, 1:]
    table[:, HALF] = 1.0
    return table


@functools.cache
def tables():
    pixels = np.arange(TP) + HALO
    column = column_table(pixels)
    column_high, column_low = halves(column)
    turned = np.concatenate([column[:, : 2 * FB].T, column[:, 2 * FB :].T], axis=1)
    turned_high, turned_low = halves(turned)
    row = row_table(pixels)
    row_high, row_low = halves(row)
    out = {}
    out["column"] = np.stack([column_high, column_low])
    waves_only = np.s_[:, np.r_[0:FB, 2 * FB : 3 * FB]]
    out["waves"] = np.stack([column_high[waves_only], column_low[waves_only]])
    spectrum_rows = []
    rim_rows = []
    halo_rows = []
    own_rows = []
    forward = []
    backward = []
    for part in range(PARTS):
        own = np.arange(ROWS) + part * ROWS + HALO
        rim = np.arange(HALO) + (0 if part == PARTS - 1 else FULL - HALO)
        for rows, positions in ((spectrum_rows, own), (rim_rows, rim)):
            high, low = halves(row_table(positions).T)
            rows.append(np.concatenate([high, low, high], axis=1))
        high, low = halves(pair_table(rim))
        halo_rows.append(np.concatenate([high, low, high], axis=1))
        high, low = halves(pair_table(own))
        own_rows.append(np.concatenate([high, low, high], axis=1))
        cols = slice(part * ROWS, (part + 1) * ROWS)
        high = np.concatenate([turned_high[:, :TP][:, cols], turned_high[:, TP:][:, cols]], axis=1)
        low = np.concatenate([turned_low[:, :TP][:, cols], turned_low[:, TP:][:, cols]], axis=1)
        forward.append(np.concatenate([high, high, low]))
        backward.append(np.concatenate([column_high[cols], column_high[cols], column_low[cols]]))
    out["spectrum_rows"] = np.stack(spectrum_rows)
    out["own_rows"] = np.stack(own_rows)
    out["rim_rows"] = np.stack(rim_rows)
    out["halo_rows"] = np.stack(halo_rows)
    out["forward"] = np.stack(forward)
    out["backward"] = np.stack(backward)
    out["turned"] = np.stack([column_high.T, column_low.T])
    out["row"] = np.concatenate([row_high, row_low, row_high], axis=1)
    out["row_turned"] = np.concatenate([row_high.T, row_low.T])
    return out


def part_of(ref):
    return ref[0] % PARTS


def has_adjoint_halo(ref):
    return ref[0] // PARTS % 2 > 0


def has_mask_halo(ref):
    return ref[0] // (2 * PARTS) > 0


def dot(left, right):
    return jnp.dot(left, right, preferred_element_type=F32)


def split(value):
    high = value.astype(BF)
    return high, (value - high.astype(F32)).astype(BF)


def lanes_and_rows():
    shape = (FA, 2 * FB)
    return lax.broadcasted_iota(jnp.int32, shape, 1), lax.broadcasted_iota(jnp.int32, shape, 0)


def pack(even, odd):
    lane, row = lanes_and_rows()
    packed = jnp.where(lane % FB < HALF, even, pltpu.roll(odd, HALF, 1))
    for place, value in ((FA - 2, even), (FA - 3, odd)):
        line = jnp.sum(jnp.where(lane == row, value[:, HALF : HALF + 1], 0.0), axis=0, keepdims=True)
        packed = jnp.where(row == place, line, packed)
    return packed


def unpack(packed):
    lane, row = lanes_and_rows()
    values = []
    for place, value in ((FA - 2, packed), (FA - 3, pltpu.roll(packed, 2 * FB - HALF, 1))):
        column = jnp.sum(jnp.where((lane == row) & (row <= HALF), packed[place : place + 1], 0.0), axis=1, keepdims=True)
        value = jnp.where(lane == HALF, column, jnp.where(lane % FB < HALF, value, 0.0))
        values.append(jnp.where(row <= HALF, value, 0.0))
    return values


def columns_of(mask, column_ref):
    high, low = split(mask)
    return dot(high, column_ref[0]) + dot(low, column_ref[0]) + dot(high, column_ref[1])


def spectrum_of(across, rows):
    high, low = split(across)
    both = dot(rows, jnp.concatenate([high, high, low], axis=0))
    even = both[:FA, : 2 * FB] - both[FA:, 2 * FB :]
    odd = both[FA:, : 2 * FB] + both[:FA, 2 * FB :]
    return even, odd


def open_kernel(
    part_ref, theta_hbm, waves_hbm, real_hbm, imag_hbm, thresholds_hbm, weights_hbm, forward_hbm, backward_hbm,
    out_ref, rim_ref, shares_ref, forward_ref, backward_ref, theta_ref, waves_ref, real_ref, imag_ref, thresholds_ref,
    weights_ref, stage, sems,
):
    part = part_of(part_ref)
    edge = pl.ds(pl.multiple_of(jnp.where(part == 0, 0, ROWS - HALO), HALO), HALO)
    moves = [
        (theta_hbm.at[edge], theta_ref),
        (waves_hbm, waves_ref),
        (real_hbm, real_ref),
        (imag_hbm, imag_ref),
        (thresholds_hbm, thresholds_ref),
        (weights_hbm, weights_ref),
        (forward_hbm.at[part], forward_ref),
        (backward_hbm.at[part], backward_ref),
    ]
    copies = [pltpu.make_async_copy(source, target, sems.at[i]) for i, (source, target) in enumerate(moves)]
    for copy in copies:
        copy.start()
    local_conds = real_ref.shape[0]
    mats = local_conds * KERNELS * 2
    stage[...] = jnp.zeros_like(stage)
    rows = stage.shape[1]
    source = lax.broadcasted_iota(jnp.int32, (2 * FB, 4 * FB), 0)
    target = lax.broadcasted_iota(jnp.int32, (2 * FB, 4 * FB), 1)
    lane = target % FB
    block = target // FB
    plus = (block == 0) | (block == 3)
    freq = jnp.where(lane < HALF, lane + 1, 0)
    used = (lane < HALF) | ((lane == HALF) & (block % 2 == 0))
    pick = (used & (source == jnp.where(plus, HALF + freq, HALF - freq))).astype(F32).astype(BF)
    source = lax.broadcasted_iota(jnp.int32, (FA, 2 * rows), 1) % rows
    target = lax.broadcasted_iota(jnp.int32, (FA, 2 * rows), 0)
    turn = ((source == HALF - target) & (target <= HALF)).astype(F32).astype(BF)
    lane = lax.broadcasted_iota(jnp.int32, (FA, 2 * FB), 1)
    row = lax.broadcasted_iota(jnp.int32, (FA, 2 * FB), 0)
    valid = (row <= HALF) & ((lane <= HALF) | ((row > 0) & (lane >= FB) & (lane < FB + HALF)))
    scale = 1.0 / (FULL * FULL)
    keep_top = jnp.where(valid, scale, 0.0)
    keep_bottom = jnp.where((row == 0) & (lane == HALF), 0.0, keep_top)
    first = lane % FB < HALF
    for copy in copies[:2]:
        copy.wait()
    rim_ref[...] = columns_of(jnp.tanh(mask_steep * theta_ref[...]), waves_ref)
    for copy in copies[2:6]:
        copy.wait()
    for cond in range(local_conds):
        for kern in range(KERNELS):
            for piece, ref in enumerate((real_ref, imag_ref)):
                stage[(cond * KERNELS + kern) * 2 + piece, :KSUP, :KSUP] = ref[cond, :, kern, :]
    high, low = split(stage[...].reshape(mats * rows, 2 * FB))
    picked = [dot(piece, pick) for piece in (high, low)]
    extra = jnp.zeros((FA, 2 * FB), F32)
    blocks = []
    for kern in range(local_conds * KERNELS):
        arrays = [[], []]
        for piece in range(2):
            start = (kern * 2 + piece) * rows
            top = picked[0][start + HALF : start + HALF + FA, : 2 * FB] + picked[1][start + HALF : start + HALF + FA, : 2 * FB]
            pieces = jnp.concatenate([half[start : start + rows, 2 * FB :] for half in picked], axis=0)
            bottom = dot(turn, pieces.astype(BF)) * keep_bottom
            top = top * keep_top
            arrays[0].append(top + bottom)
            arrays[1].append(top - bottom)
        for which, (real, imag) in enumerate(arrays):
            blocks.append(jnp.where(first, real, pltpu.roll(imag, HALF, 1)))
            for piece, value in enumerate((real, imag)):
                place = kern * 4 + which * 2 + piece
                extra = jnp.where(lane == place, pltpu.roll(value, (place - HALF) % (2 * FB), 1), extra)
    for i, block in enumerate(blocks):
        if i < SPARE_BLOCKS:
            block = jnp.concatenate([block[: HALF + 1], extra[SPARE * i : SPARE * (i + 1)]], axis=0)
        elif i < SPARE_BLOCKS + local_conds:
            block = jnp.where(row == FA - 1, thresholds_ref[i - SPARE_BLOCKS], block)
        out_ref[i] = block
    weight_sum = weights_ref[0]
    for i in range(1, CONDS):
        weight_sum = weight_sum + weights_ref[i]
    row = lax.broadcasted_iota(jnp.int32, shares_ref.shape, 0)
    shares = jnp.zeros(shares_ref.shape, F32)
    for group, step in enumerate((0, 3, 1, 2)):
        for i in range(local_conds):
            weight = weights_ref[lax.bitwise_xor(part, step) * local_conds + i]
            shares = jnp.where(row == group * local_conds + i, weight.astype(F32), shares)
    shares_ref[...] = shares / weight_sum.astype(F32)
    for copy in copies[6:]:
        copy.wait()


def spectrum_kernel(part_ref, theta_ref, column_ref, rows_ref, out_ref):
    across = columns_of(jnp.tanh(mask_steep * theta_ref[...]), column_ref)
    even, odd = spectrum_of(across, rows_ref[part_of(part_ref)])
    out_ref[0] = even
    out_ref[1] = odd


def rim_kernel(part_ref, spectrum_ref, rim_ref, rows_ref, out_ref):
    rim = jnp.where(has_mask_halo(part_ref), rim_ref[...], 0.0)
    turned = pltpu.roll(rim, FB, 1)
    first = lax.broadcasted_iota(jnp.int32, rim.shape, 1) < FB
    across = jnp.concatenate([jnp.where(first, rim, turned), jnp.where(first, turned, -rim)], axis=1)
    even, odd = spectrum_of(across, rows_ref[part_of(part_ref)])
    out_ref[0] = pack(even + spectrum_ref[0], odd + spectrum_ref[1])


def unpack_group(ref, put):
    lane, row = lanes_and_rows()
    zero_lane = (lane == HALF) & (row <= HALF)
    extra = [ref[i][HALF + 1 :] for i in range(SPARE_BLOCKS)]
    extra = jnp.concatenate(extra + [jnp.zeros((FA - SPARE * SPARE_BLOCKS, 2 * FB), F32)], axis=0)
    for kern in range(ref.shape[0] // 2):
        values = []
        for which in range(2):
            packed = ref[2 * kern + which]
            for part, value in enumerate((packed, pltpu.roll(packed, 2 * FB - HALF, 1))):
                place = kern * 4 + which * 2 + part
                zeroth = pltpu.roll(extra, (HALF - place) % (2 * FB), 1)
                values.append(jnp.where(zero_lane, zeroth, value))
        put(kern, values)


def near_kernels_kernel(part_ref, mixed_ref, target_ref, near_ref, signs_ref):
    local = near_ref.shape[0] // 2
    for group in range(2):
        def put(kern, values, group=group):
            for i, value in enumerate(values):
                near_ref[group * local + kern, i] = value

        unpack_group(mixed_ref.at[pl.ds(group * 2 * local, 2 * local)], put)
    own = pl.ds(pl.multiple_of(part_of(part_ref) * ROWS, ROWS), ROWS)
    signs_ref[...] = 1.0 - 2.0 * target_ref[:, own].astype(F32)


def fields_kernel(
    part_ref, mixed_ref, other_ref, near_ref, signs, shares_ref, forward_ref, backward_ref, row_ref,
    row_turned_ref, out_ref, far_ref, levels_ref, lines, folded, amps, tanhs, total, turned, backs,
):
    count = 2 * far_ref.shape[0]
    local = count // PARTS
    tall = 4 * FA
    each = 2 * local
    even, odd = unpack(mixed_ref[2 * each] + other_ref[2 * each])

    def put_line(kern, values):
        he_real, he_imag, ho_real, ho_imag = values
        start = kern * tall
        for i, value in enumerate(
            (
                even * he_real + odd * ho_imag,
                odd * he_real - even * ho_imag,
                even * he_imag - odd * ho_real,
                odd * he_imag + even * ho_real,
            )
        ):
            lines[start + i * FA : start + (i + 1) * FA] = value

    def arrays_of(kern):
        ref = near_ref if kern < count // 2 else far_ref
        return [ref[kern % (count // 2), i] for i in range(4)]

    for group in range(PARTS):
        ref = (mixed_ref, other_ref)[group // 2].at[pl.ds(group % 2 * each, each)]
        for i in range(CONDS // PARTS):
            place = group * (CONDS // PARTS) + i
            levels_ref[place : place + 1] = ref[SPARE_BLOCKS + i][FA - 1 :]
        if group < 2:
            for kern in range(group * local, (group + 1) * local):
                put_line(kern, arrays_of(kern))
        else:
            def put(kern, values, group=group):
                for i, value in enumerate(values):
                    far_ref[(group - 2) * local + kern, i] = value
                put_line(group * local + kern, values)

            unpack_group(ref, put)

    high, low = split(lines[...])
    lines_folded = dot(jnp.concatenate([high, low], axis=1), forward_ref[: 4 * FB]) + dot(high, forward_ref[4 * FB :])
    for kern in range(count):
        parts = []
        for i in range(2):
            x_part = lines_folded[tall * kern + 2 * FA * i : tall * kern + 2 * FA * i + FA]
            y_part = lines_folded[tall * kern + 2 * FA * i + FA : tall * kern + 2 * FA * (i + 1)]
            parts.append(
                jnp.concatenate(
                    [x_part[:, :ROWS] + y_part[:, ROWS:], y_part[:, :ROWS] - x_part[:, ROWS:]], axis=0
                )
            )
        high, low = split(jnp.concatenate(parts, axis=1))
        folded[kern] = jnp.concatenate([high, high, low], axis=0)
    total[...] = jnp.zeros_like(total)

    def expose(cond, carry):
        intensity = None
        for kern in range(KERNELS):
            index = cond * KERNELS + kern
            amp = dot(row_ref[...], folded[index])
            amps[index] = amp
            power = amp[:, :ROWS] * amp[:, :ROWS] + amp[:, ROWS:] * amp[:, ROWS:]
            intensity = power if intensity is None else intensity + power
        level = levels_ref[pl.ds(cond, 1), :]
        value = jnp.tanh((0.5 * resist_steep) * (intensity - level))
        tanhs[cond] = value
        total[...] += value
        return carry

    lax.fori_loop(0, CONDS, expose, 0, unroll=8)
    total[...] = total[...] * (band_weight / (CONDS * CONDS))

    def drive(cond, carry):
        weight = shares_ref[pl.ds(cond, 1), :]
        value = tanhs[cond]
        slope = (weight + band_weight / CONDS) * value + weight * signs[...] - total[...]
        field = (0.5 * resist_steep) * (1.0 - value * value) * slope
        field = jnp.concatenate([field, field], axis=1)
        for kern in range(KERNELS):
            index = cond * KERNELS + kern
            high, low = split(field * amps[index])
            long = dot(row_turned_ref[...], high)
            back = long[: 2 * FA] + long[2 * FA :] + dot(row_turned_ref[: 2 * FA], low)
            turned[pl.ds(index * 2, 2)] = jnp.stack([back[:, :ROWS], back[:, ROWS:]])
        return carry

    lax.fori_loop(0, CONDS, drive, 0, unroll=4)
    high, low = split(turned[...].reshape(count * tall, ROWS))
    backs[...] = dot(jnp.concatenate([high, low], axis=1), backward_ref[: 2 * ROWS]) + dot(high, backward_ref[2 * ROWS :])

    sum_even = jnp.zeros((FA, 2 * FB), F32)
    sum_odd = jnp.zeros((FA, 2 * FB), F32)
    for kern in range(count):
        grads = []
        for i in range(2):
            c_part = backs[tall * kern + 2 * FA * i : tall * kern + 2 * FA * i + FA]
            s_part = backs[tall * kern + 2 * FA * i + FA : tall * kern + 2 * FA * (i + 1)]
            grads.append(
                (
                    c_part[:, : 2 * FB] - s_part[:, 2 * FB :],
                    s_part[:, : 2 * FB] + c_part[:, 2 * FB :],
                )
            )
        (x_real, y_real), (x_imag, y_imag) = grads
        he_real, he_imag, ho_real, ho_imag = arrays_of(kern)
        sum_even = sum_even + x_real * he_real + x_imag * he_imag - y_real * ho_imag + y_imag * ho_real
        sum_odd = sum_odd + x_real * ho_imag - x_imag * ho_real + y_real * he_real + y_imag * he_imag
    out_ref[...] = pack(sum_even, sum_odd)


def image_rows(packed, rows, turned_ref):
    high, low = split(jnp.concatenate(unpack(packed), axis=0))
    pair = dot(rows, jnp.concatenate([high, high, low], axis=0))
    count = pair.shape[0] // 2
    high, low = split(jnp.concatenate([pair[:count], pair[count:]], axis=1))
    return dot(high, turned_ref[0]) + dot(low, turned_ref[0]) + dot(high, turned_ref[1])


def edge_start(part_ref):
    return pl.multiple_of(jnp.where(part_of(part_ref) == PARTS - 1, ROWS - HALO, 0), HALO)


def gradient_kernel(part_ref, theta_ref, sum_ref, turned_ref, rows_ref, out_ref, edge_ref, scale_ref):
    part = part_of(part_ref)
    mask = jnp.tanh(mask_steep * theta_ref[...])
    scale = mask_steep * (1.0 - mask * mask)
    gradient = image_rows(sum_ref[...], rows_ref[part], turned_ref) * scale
    out_ref[...] = gradient
    last = part == PARTS - 1
    edge_ref[...] = jnp.where(last, gradient[ROWS - HALO :], gradient[:HALO])
    scale_ref[...] = jnp.where(last, scale[ROWS - HALO :], scale[:HALO])


def edge_kernel(part_ref, gradient_hbm, edge_ref, scale_ref, near_ref, turned_ref, rows_ref, out_hbm, stage, sem):
    @pl.when(has_adjoint_halo(part_ref))
    def _():
        rim = image_rows(near_ref[...], rows_ref[part_of(part_ref)], turned_ref)
        stage[...] = edge_ref[...] + rim * scale_ref[...]
        copy = pltpu.make_async_copy(stage, out_hbm.at[pl.ds(edge_start(part_ref), HALO)], sem)
        copy.start()
        copy.wait()


def whole_spec(array):
    del array
    return pl.BlockSpec(memory_space=pltpu.VMEM)


def call(kernel, scalars, operands, specs, out_shapes, scratch=(), name=None, flops=1 << 28, out_specs=None, aliases=None):
    many = isinstance(out_shapes, list)
    if out_specs is None:
        out_specs = [whole_spec(shape) for shape in out_shapes] if many else whole_spec(out_shapes)
    return pl.pallas_call(
        kernel,
        grid_spec=pltpu.PrefetchScalarGridSpec(
            num_scalar_prefetch=len(scalars),
            grid=(1,),
            in_specs=specs,
            out_specs=out_specs,
            scratch_shapes=list(scratch),
        ),
        out_shape=out_shapes,
        input_output_aliases=aliases or {},
        compiler_params=pltpu.CompilerParams(vmem_limit_bytes=48 * 1024 * 1024),
        cost_estimate=pl.CostEstimate(flops=flops, bytes_accessed=1 << 20, transcendentals=0),
        name=name,
    )(*scalars, *operands)


def floats(*shape):
    return jax.ShapeDtypeStruct(shape, F32)


def shards(theta, target, kernel_real, kernel_imag, weights, thresholds):
    table = {name: jnp.asarray(value) for name, value in tables().items()}
    tiles = lax.axis_size("tile")
    part = lax.axis_index("cond")
    tile = lax.axis_index("tile")
    last = PARTS - 1
    above = ((part == 0) & (tile > 0)) | ((part == last) & (tile < tiles - 1))
    below = ((part == 0) & (tile < tiles - 1)) | ((part == last) & (tile > 0))
    parts = (part + PARTS * above.astype(jnp.int32) + 2 * PARTS * below.astype(jnp.int32)).reshape(1).astype(jnp.int32)
    local_conds = kernel_real.shape[0]
    local = local_conds * KERNELS
    count = CONDS * KERNELS
    hbm = pl.BlockSpec(memory_space=pltpu.HBM)

    def across(value, down, up, within):
        pairs = [(PARTS * i + a, PARTS * i + b) for i in range(tiles) for a, b in within]
        pairs += [(PARTS * (i + 1) + down[0], PARTS * i + down[1]) for i in range(tiles - 1)]
        pairs += [(PARTS * i + up[0], PARTS * (i + 1) + up[1]) for i in range(tiles - 1)]
        pairs += [(down[0], up[1]), (PARTS * (tiles - 1) + up[0], PARTS * (tiles - 1) + down[1])]
        return lax.ppermute(value, ("tile", "cond"), pairs)

    def partner(value, step):
        return lax.ppermute(value, "cond", [(i, i ^ step) for i in range(PARTS)])

    kernel_shape = (local_conds, KSUP, KERNELS, KSUP)
    own, rim, shares, forward, backward = call(
        open_kernel,
        (parts,),
        tuple(
            pltpu.with_memory_space_constraint(value, pltpu.HBM)
            for value in (
                theta, table["waves"], kernel_real.transpose(0, 2, 1, 3), kernel_imag.transpose(0, 2, 1, 3), thresholds, weights,
                table["forward"], table["backward"],
            )
        ),
        [hbm] * 8,
        [
            floats(2 * local, FA, 2 * FB),
            floats(HALO, 2 * FB),
            floats(CONDS, ROWS),
            jax.ShapeDtypeStruct(table["forward"].shape[1:], BF),
            jax.ShapeDtypeStruct(table["backward"].shape[1:], BF),
        ],
        scratch=(
            pltpu.VMEM((HALO, TP), F32),
            pltpu.VMEM(table["waves"].shape, BF),
            pltpu.VMEM(kernel_shape, F32),
            pltpu.VMEM(kernel_shape, F32),
            pltpu.SMEM(thresholds.shape, F32),
            pltpu.SMEM(weights.shape, jnp.int32),
            pltpu.VMEM((2 * local, 72, 2 * FB), F32),
            pltpu.SemaphoreType.DMA((8,)),
        ),
        name="open_parts",
    )
    rim = across(rim, (0, 0), (last, last), [(1, 2), (2, 1)])
    spectrum = call(
        spectrum_kernel,
        (parts,),
        (theta, table["column"], table["spectrum_rows"]),
        [whole_spec(theta), whole_spec(table["column"]), whole_spec(table["spectrum_rows"])],
        floats(2, FA, 2 * FB),
        name="own_spectrum",
        flops=1 << 31,
    )
    side = partner(own, 3)
    spectrum = call(
        rim_kernel,
        (parts,),
        (spectrum, rim, table["rim_rows"]),
        [whole_spec(spectrum), whole_spec(rim), whole_spec(table["rim_rows"])],
        floats(1, FA, 2 * FB),
        name="add_rim",
    )
    mixed = jnp.concatenate([own, side, spectrum + partner(spectrum, 3)], axis=0)
    near_kernels, signs = call(
        near_kernels_kernel,
        (parts,),
        (mixed, target),
        [whole_spec(mixed), whole_spec(target)],
        [floats(count // 2, 4, FA, 2 * FB), floats(TP, ROWS)],
        name="near_kernels",
        flops=1 << 30,
    )
    adjoint = call(
        fields_kernel,
        (parts,),
        (
            mixed, partner(mixed, 1), near_kernels, signs, shares, forward, backward, table["row"], table["row_turned"],
        ),
        [
            whole_spec(mixed),
            whole_spec(mixed),
            whole_spec(near_kernels),
            whole_spec(signs),
            whole_spec(shares),
            whole_spec(forward),
            whole_spec(backward),
            whole_spec(table["row"]),
            whole_spec(table["row_turned"]),
        ],
        floats(FA, 2 * FB),
        scratch=(
            pltpu.VMEM((count // 2, 4, FA, 2 * FB), F32),
            pltpu.VMEM((CONDS, ROWS), F32),
            pltpu.VMEM((count * 4 * FA, 2 * FB), F32),
            pltpu.VMEM((count, 6 * FA, 2 * ROWS), BF),
            pltpu.VMEM((count, TP, 2 * ROWS), F32),
            pltpu.VMEM((CONDS, TP, ROWS), F32),
            pltpu.VMEM((TP, ROWS), F32),
            pltpu.VMEM((count * 2, 2 * FA, ROWS), F32),
            pltpu.VMEM((count * 4 * FA, 4 * FB), F32),
        ),
        name="coherent_fields",
        flops=1 << 33,
    )
    adjoint = adjoint + partner(adjoint, 1)
    adjoint = adjoint + partner(adjoint, 3)
    near = across(adjoint, (2, last), (1, 0), [(0, 1), (last, 2)])
    gradient, edge, scale = call(
        gradient_kernel,
        (parts,),
        (theta, adjoint, table["turned"], table["own_rows"]),
        [
            whole_spec(theta),
            whole_spec(adjoint),
            whole_spec(table["turned"]),
            whole_spec(table["own_rows"]),
        ],
        [floats(ROWS, TP), floats(HALO, TP), floats(HALO, TP)],
        out_specs=[
            pl.BlockSpec((ROWS, TP), lambda i, *refs: (0, 0)),
            whole_spec(adjoint),
            whole_spec(adjoint),
        ],
        name="own_gradient",
        flops=1 << 31,
    )
    return call(
        edge_kernel,
        (parts,),
        (gradient, edge, scale, near, table["turned"], table["halo_rows"]),
        [
            hbm,
            whole_spec(edge),
            whole_spec(scale),
            whole_spec(near),
            whole_spec(table["turned"]),
            whole_spec(table["halo_rows"]),
        ],
        floats(ROWS, TP),
        scratch=(pltpu.VMEM((HALO, TP), F32), pltpu.SemaphoreType.DMA),
        name="edge_gradient",
        out_specs=hbm,
        aliases={1: 0},
    )


def solution(mesh):
    in_specs = (
        P(("tile", "cond"), None),
        P("tile", None),
        P("cond", None, None, None),
        P("cond", None, None, None),
        P(),
        P("cond"),
    )
    out_specs = P(("tile", "cond"), None)
    return jax.shard_map(shards, mesh=mesh, in_specs=in_specs, out_specs=out_specs, check_vma=False)
```

```python
import functools

import jax
import jax.numpy as jnp
import ml_dtypes
import numpy as np
from jax import lax
from jax.experimental import pallas as pl
from jax.experimental.pallas import tpu as pltpu
from jax.sharding import PartitionSpec as P

TP = 512
HALO = 32
KSUP = 65
HALF = KSUP // 2
KERNELS = 2
CONDS = 8
FULL = TP + 2 * HALO
PARTS = 4
ROWS = TP // PARTS
FA = 40
FB = 64
SPARE = FA - HALF - 1
SPARE_BLOCKS = -(-(HALF + 1) // SPARE)
BF = jnp.bfloat16
F32 = jnp.float32

mask_steep = 2.0
resist_steep = 4.0
band_weight = 1.0


def waves(positions):
    angles = (np.outer(np.asarray(positions, np.int64), np.arange(HALF + 1)) % FULL) * (2.0 * np.pi / FULL)
    return np.cos(angles), np.sin(angles)


def halves(table):
    high = table.astype(np.float32).astype(ml_dtypes.bfloat16)
    low = (table - high.astype(np.float64)).astype(np.float32).astype(ml_dtypes.bfloat16)
    return high, low


def row_table(positions):
    cosine, sine = waves(positions)
    table = np.zeros((len(positions), 2 * FA))
    table[:, : HALF + 1] = cosine
    table[:, FA : FA + HALF + 1] = sine
    return table


def pair_table(positions):
    table = row_table(positions)
    return np.concatenate([table, np.concatenate([-table[:, FA:], table[:, :FA]], axis=1)])


def column_table(positions):
    cosine, sine = waves(positions)
    table = np.zeros((len(positions), 4 * FB))
    for block, values in enumerate((cosine, cosine, sine, -sine)):
        table[:, block * FB : block * FB + HALF] = values[:, 1:]
    table[:, HALF] = 1.0
    return table


@functools.cache
def tables():
    pixels = np.arange(TP) + HALO
    column = column_table(pixels)
    column_high, column_low = halves(column)
    turned = np.concatenate([column[:, : 2 * FB].T, column[:, 2 * FB :].T], axis=1)
    turned_high, turned_low = halves(turned)
    row = row_table(pixels)
    row_high, row_low = halves(row)
    out = {}
    out["column"] = np.stack([column_high, column_low])
    waves_only = np.s_[:, np.r_[0:FB, 2 * FB : 3 * FB]]
    out["waves"] = np.stack([column_high[waves_only], column_low[waves_only]])
    spectrum_rows = []
    rim_rows = []
    halo_rows = []
    own_rows = []
    forward = []
    backward = []
    for part in range(PARTS):
        own = np.arange(ROWS) + part * ROWS + HALO
        rim = np.arange(HALO) + (0 if part == PARTS - 1 else FULL - HALO)
        for rows, positions in ((spectrum_rows, own), (rim_rows, rim)):
            high, low = halves(row_table(positions).T)
            rows.append(np.concatenate([high, low, high], axis=1))
        high, low = halves(pair_table(rim))
        halo_rows.append(np.concatenate([high, low, high], axis=1))
        high, low = halves(pair_table(own))
        own_rows.append(np.concatenate([high, low, high], axis=1))
        cols = slice(part * ROWS, (part + 1) * ROWS)
        high = np.concatenate([turned_high[:, :TP][:, cols], turned_high[:, TP:][:, cols]], axis=1)
        low = np.concatenate([turned_low[:, :TP][:, cols], turned_low[:, TP:][:, cols]], axis=1)
        forward.append(np.concatenate([high, high, low]))
        backward.append(np.concatenate([column_high[cols], column_high[cols], column_low[cols]]))
    out["spectrum_rows"] = np.stack(spectrum_rows)
    out["own_rows"] = np.stack(own_rows)
    out["rim_rows"] = np.stack(rim_rows)
    out["halo_rows"] = np.stack(halo_rows)
    out["forward"] = np.stack(forward)
    out["backward"] = np.stack(backward)
    out["turned"] = np.stack([column_high.T, column_low.T])
    out["row"] = np.concatenate([row_high, row_low, row_high], axis=1)
    out["row_turned"] = np.concatenate([row_high.T, row_low.T])
    return out


def part_of(ref):
    return ref[0] % PARTS


def has_adjoint_halo(ref):
    return ref[0] // PARTS % 2 > 0


def has_mask_halo(ref):
    return ref[0] // (2 * PARTS) > 0


def dot(left, right):
    return jnp.dot(left, right, preferred_element_type=F32)


def split(value):
    high = value.astype(BF)
    return high, (value - high.astype(F32)).astype(BF)


def lanes_and_rows():
    shape = (FA, 2 * FB)
    return lax.broadcasted_iota(jnp.int32, shape, 1), lax.broadcasted_iota(jnp.int32, shape, 0)


def pack(even, odd):
    lane, row = lanes_and_rows()
    packed = jnp.where(lane % FB < HALF, even, pltpu.roll(odd, HALF, 1))
    for place, value in ((FA - 2, even), (FA - 3, odd)):
        line = jnp.sum(jnp.where(lane == row, value[:, HALF : HALF + 1], 0.0), axis=0, keepdims=True)
        packed = jnp.where(row == place, line, packed)
    return packed


def unpack(packed):
    lane, row = lanes_and_rows()
    values = []
    for place, value in ((FA - 2, packed), (FA - 3, pltpu.roll(packed, 2 * FB - HALF, 1))):
        column = jnp.sum(jnp.where((lane == row) & (row <= HALF), packed[place : place + 1], 0.0), axis=1, keepdims=True)
        value = jnp.where(lane == HALF, column, jnp.where(lane % FB < HALF, value, 0.0))
        values.append(jnp.where(row <= HALF, value, 0.0))
    return values


def columns_of(mask, column_ref):
    high, low = split(mask)
    return dot(high, column_ref[0]) + dot(low, column_ref[0]) + dot(high, column_ref[1])


def spectrum_of(across, rows):
    high, low = split(across)
    both = dot(rows, jnp.concatenate([high, high, low], axis=0))
    even = both[:FA, : 2 * FB] - both[FA:, 2 * FB :]
    odd = both[FA:, : 2 * FB] + both[:FA, 2 * FB :]
    return even, odd


def open_kernel(
    part_ref, theta_hbm, waves_hbm, real_hbm, imag_hbm, thresholds_hbm, weights_hbm, forward_hbm, backward_hbm,
    out_ref, rim_ref, shares_ref, forward_ref, backward_ref, theta_ref, waves_ref, real_ref, imag_ref, thresholds_ref,
    weights_ref, stage, sems,
):
    part = part_of(part_ref)
    edge = pl.ds(pl.multiple_of(jnp.where(part == 0, 0, ROWS - HALO), HALO), HALO)
    moves = [
        (theta_hbm.at[edge], theta_ref),
        (waves_hbm, waves_ref),
        (real_hbm, real_ref),
        (imag_hbm, imag_ref),
        (thresholds_hbm, thresholds_ref),
        (weights_hbm, weights_ref),
        (forward_hbm.at[part], forward_ref),
        (backward_hbm.at[part], backward_ref),
    ]
    copies = [pltpu.make_async_copy(source, target, sems.at[i]) for i, (source, target) in enumerate(moves)]
    for copy in copies:
        copy.start()
    local_conds = real_ref.shape[0]
    mats = local_conds * KERNELS * 2
    stage[...] = jnp.zeros_like(stage)
    rows = stage.shape[1]
    source = lax.broadcasted_iota(jnp.int32, (2 * FB, 4 * FB), 0)
    target = lax.broadcasted_iota(jnp.int32, (2 * FB, 4 * FB), 1)
    lane = target % FB
    block = target // FB
    plus = (block == 0) | (block == 3)
    freq = jnp.where(lane < HALF, lane + 1, 0)
    used = (lane < HALF) | ((lane == HALF) & (block % 2 == 0))
    pick = (used & (source == jnp.where(plus, HALF + freq, HALF - freq))).astype(F32).astype(BF)
    source = lax.broadcasted_iota(jnp.int32, (FA, 2 * rows), 1) % rows
    target = lax.broadcasted_iota(jnp.int32, (FA, 2 * rows), 0)
    turn = ((source == HALF - target) & (target <= HALF)).astype(F32).astype(BF)
    lane = lax.broadcasted_iota(jnp.int32, (FA, 2 * FB), 1)
    row = lax.broadcasted_iota(jnp.int32, (FA, 2 * FB), 0)
    valid = (row <= HALF) & ((lane <= HALF) | ((row > 0) & (lane >= FB) & (lane < FB + HALF)))
    scale = 1.0 / (FULL * FULL)
    keep_top = jnp.where(valid, scale, 0.0)
    keep_bottom = jnp.where((row == 0) & (lane == HALF), 0.0, keep_top)
    first = lane % FB < HALF
    for copy in copies[:6]:
        copy.wait()
    rim_ref[...] = columns_of(jnp.tanh(mask_steep * theta_ref[...]), waves_ref)
    for cond in range(local_conds):
        for kern in range(KERNELS):
            for piece, ref in enumerate((real_ref, imag_ref)):
                stage[(cond * KERNELS + kern) * 2 + piece, :KSUP, :KSUP] = ref[cond, :, kern, :]
    high, low = split(stage[...].reshape(mats * rows, 2 * FB))
    picked = [dot(piece, pick) for piece in (high, low)]
    extra = jnp.zeros((FA, 2 * FB), F32)
    blocks = []
    for kern in range(local_conds * KERNELS):
        arrays = [[], []]
        for piece in range(2):
            start = (kern * 2 + piece) * rows
            top = picked[0][start + HALF : start + HALF + FA, : 2 * FB] + picked[1][start + HALF : start + HALF + FA, : 2 * FB]
            pieces = jnp.concatenate([half[start : start + rows, 2 * FB :] for half in picked], axis=0)
            bottom = dot(turn, pieces.astype(BF)) * keep_bottom
            top = top * keep_top
            arrays[0].append(top + bottom)
            arrays[1].append(top - bottom)
        for which, (real, imag) in enumerate(arrays):
            blocks.append(jnp.where(first, real, pltpu.roll(imag, HALF, 1)))
            for piece, value in enumerate((real, imag)):
                place = kern * 4 + which * 2 + piece
                extra = jnp.where(lane == place, pltpu.roll(value, (place - HALF) % (2 * FB), 1), extra)
    for i, block in enumerate(blocks):
        if i < SPARE_BLOCKS:
            block = jnp.concatenate([block[: HALF + 1], extra[SPARE * i : SPARE * (i + 1)]], axis=0)
        elif i < SPARE_BLOCKS + local_conds:
            block = jnp.where(row == FA - 1, thresholds_ref[i - SPARE_BLOCKS], block)
        out_ref[i] = block
    weight_sum = weights_ref[0]
    for i in range(1, CONDS):
        weight_sum = weight_sum + weights_ref[i]
    row = lax.broadcasted_iota(jnp.int32, shares_ref.shape, 0)
    shares = jnp.zeros(shares_ref.shape, F32)
    for group, step in enumerate((0, 3, 1, 2)):
        for i in range(local_conds):
            weight = weights_ref[lax.bitwise_xor(part, step) * local_conds + i]
            shares = jnp.where(row == group * local_conds + i, weight.astype(F32), shares)
    shares_ref[...] = shares / weight_sum.astype(F32)
    for copy in copies[6:]:
        copy.wait()


def spectrum_kernel(part_ref, theta_ref, column_ref, rows_ref, out_ref):
    across = columns_of(jnp.tanh(mask_steep * theta_ref[...]), column_ref)
    even, odd = spectrum_of(across, rows_ref[part_of(part_ref)])
    out_ref[0] = even
    out_ref[1] = odd


def rim_kernel(part_ref, spectrum_ref, rim_ref, rows_ref, out_ref):
    rim = jnp.where(has_mask_halo(part_ref), rim_ref[...], 0.0)
    turned = pltpu.roll(rim, FB, 1)
    first = lax.broadcasted_iota(jnp.int32, rim.shape, 1) < FB
    across = jnp.concatenate([jnp.where(first, rim, turned), jnp.where(first, turned, -rim)], axis=1)
    even, odd = spectrum_of(across, rows_ref[part_of(part_ref)])
    out_ref[0] = pack(even + spectrum_ref[0], odd + spectrum_ref[1])


def unpack_group(ref, put):
    lane, row = lanes_and_rows()
    zero_lane = (lane == HALF) & (row <= HALF)
    extra = [ref[i][HALF + 1 :] for i in range(SPARE_BLOCKS)]
    extra = jnp.concatenate(extra + [jnp.zeros((FA - SPARE * SPARE_BLOCKS, 2 * FB), F32)], axis=0)
    for kern in range(ref.shape[0] // 2):
        values = []
        for which in range(2):
            packed = ref[2 * kern + which]
            for part, value in enumerate((packed, pltpu.roll(packed, 2 * FB - HALF, 1))):
                place = kern * 4 + which * 2 + part
                zeroth = pltpu.roll(extra, (HALF - place) % (2 * FB), 1)
                values.append(jnp.where(zero_lane, zeroth, value))
        put(kern, values)


def near_kernels_kernel(part_ref, mixed_ref, target_ref, near_ref, signs_ref):
    local = near_ref.shape[0] // 2
    for group in range(2):
        def put(kern, values, group=group):
            for i, value in enumerate(values):
                near_ref[group * local + kern, i] = value

        unpack_group(mixed_ref.at[pl.ds(group * 2 * local, 2 * local)], put)
    own = pl.ds(pl.multiple_of(part_of(part_ref) * ROWS, ROWS), ROWS)
    signs_ref[...] = 1.0 - 2.0 * target_ref[:, own].astype(F32)


def fields_kernel(
    part_ref, mixed_ref, other_ref, near_ref, signs, shares_ref, forward_ref, backward_ref, row_ref,
    row_turned_ref, out_ref, far_ref, levels_ref, lines, folded, amps, tanhs, total, turned, backs,
):
    count = 2 * far_ref.shape[0]
    local = count // PARTS
    tall = 4 * FA
    each = 2 * local
    even, odd = unpack(mixed_ref[2 * each] + other_ref[2 * each])

    def put_line(kern, values):
        he_real, he_imag, ho_real, ho_imag = values
        start = kern * tall
        for i, value in enumerate(
            (
                even * he_real + odd * ho_imag,
                odd * he_real - even * ho_imag,
                even * he_imag - odd * ho_real,
                odd * he_imag + even * ho_real,
            )
        ):
            lines[start + i * FA : start + (i + 1) * FA] = value

    def arrays_of(kern):
        ref = near_ref if kern < count // 2 else far_ref
        return [ref[kern % (count // 2), i] for i in range(4)]

    for group in range(PARTS):
        ref = (mixed_ref, other_ref)[group // 2].at[pl.ds(group % 2 * each, each)]
        for i in range(CONDS // PARTS):
            place = group * (CONDS // PARTS) + i
            levels_ref[place : place + 1] = ref[SPARE_BLOCKS + i][FA - 1 :]
        if group < 2:
            for kern in range(group * local, (group + 1) * local):
                put_line(kern, arrays_of(kern))
        else:
            def put(kern, values, group=group):
                for i, value in enumerate(values):
                    far_ref[(group - 2) * local + kern, i] = value
                put_line(group * local + kern, values)

            unpack_group(ref, put)

    high, low = split(lines[...])
    lines_folded = dot(jnp.concatenate([high, low], axis=1), forward_ref[: 4 * FB]) + dot(high, forward_ref[4 * FB :])
    for kern in range(count):
        parts = []
        for i in range(2):
            x_part = lines_folded[tall * kern + 2 * FA * i : tall * kern + 2 * FA * i + FA]
            y_part = lines_folded[tall * kern + 2 * FA * i + FA : tall * kern + 2 * FA * (i + 1)]
            parts.append(
                jnp.concatenate(
                    [x_part[:, :ROWS] + y_part[:, ROWS:], y_part[:, :ROWS] - x_part[:, ROWS:]], axis=0
                )
            )
        high, low = split(jnp.concatenate(parts, axis=1))
        folded[kern] = jnp.concatenate([high, high, low], axis=0)
    total[...] = jnp.zeros_like(total)

    def expose(cond, carry):
        intensity = None
        for kern in range(KERNELS):
            index = cond * KERNELS + kern
            amp = dot(row_ref[...], folded[index])
            amps[index] = amp
            power = amp[:, :ROWS] * amp[:, :ROWS] + amp[:, ROWS:] * amp[:, ROWS:]
            intensity = power if intensity is None else intensity + power
        level = levels_ref[pl.ds(cond, 1), :]
        value = jnp.tanh((0.5 * resist_steep) * (intensity - level))
        tanhs[cond] = value
        total[...] += value
        return carry

    lax.fori_loop(0, CONDS, expose, 0, unroll=2)
    total[...] = total[...] * (band_weight / (CONDS * CONDS))

    def drive(cond, carry):
        weight = shares_ref[pl.ds(cond, 1), :]
        value = tanhs[cond]
        slope = (weight + band_weight / CONDS) * value + weight * signs[...] - total[...]
        field = (0.5 * resist_steep) * (1.0 - value * value) * slope
        field = jnp.concatenate([field, field], axis=1)
        for kern in range(KERNELS):
            index = cond * KERNELS + kern
            high, low = split(field * amps[index])
            long = dot(row_turned_ref[...], high)
            back = long[: 2 * FA] + long[2 * FA :] + dot(row_turned_ref[: 2 * FA], low)
            turned[pl.ds(index * 2, 2)] = jnp.stack([back[:, :ROWS], back[:, ROWS:]])
        return carry

    lax.fori_loop(0, CONDS, drive, 0, unroll=4)
    high, low = split(turned[...].reshape(count * tall, ROWS))
    backs[...] = dot(jnp.concatenate([high, low], axis=1), backward_ref[: 2 * ROWS]) + dot(high, backward_ref[2 * ROWS :])

    sum_even = jnp.zeros((FA, 2 * FB), F32)
    sum_odd = jnp.zeros((FA, 2 * FB), F32)
    for kern in range(count):
        grads = []
        for i in range(2):
            c_part = backs[tall * kern + 2 * FA * i : tall * kern + 2 * FA * i + FA]
            s_part = backs[tall * kern + 2 * FA * i + FA : tall * kern + 2 * FA * (i + 1)]
            grads.append(
                (
                    c_part[:, : 2 * FB] - s_part[:, 2 * FB :],
                    s_part[:, : 2 * FB] + c_part[:, 2 * FB :],
                )
            )
        (x_real, y_real), (x_imag, y_imag) = grads
        he_real, he_imag, ho_real, ho_imag = arrays_of(kern)
        sum_even = sum_even + x_real * he_real + x_imag * he_imag - y_real * ho_imag + y_imag * ho_real
        sum_odd = sum_odd + x_real * ho_imag - x_imag * ho_real + y_real * he_real + y_imag * he_imag
    out_ref[...] = pack(sum_even, sum_odd)


def image_rows(packed, rows, turned_ref):
    high, low = split(jnp.concatenate(unpack(packed), axis=0))
    pair = dot(rows, jnp.concatenate([high, high, low], axis=0))
    count = pair.shape[0] // 2
    high, low = split(jnp.concatenate([pair[:count], pair[count:]], axis=1))
    return dot(high, turned_ref[0]) + dot(low, turned_ref[0]) + dot(high, turned_ref[1])


def edge_start(part_ref):
    return pl.multiple_of(jnp.where(part_of(part_ref) == PARTS - 1, ROWS - HALO, 0), HALO)


def gradient_kernel(part_ref, theta_ref, sum_ref, turned_ref, rows_ref, out_ref, edge_ref, scale_ref):
    part = part_of(part_ref)
    mask = jnp.tanh(mask_steep * theta_ref[...])
    scale = mask_steep * (1.0 - mask * mask)
    gradient = image_rows(sum_ref[...], rows_ref[part], turned_ref) * scale
    out_ref[...] = gradient
    last = part == PARTS - 1
    edge_ref[...] = jnp.where(last, gradient[ROWS - HALO :], gradient[:HALO])
    scale_ref[...] = jnp.where(last, scale[ROWS - HALO :], scale[:HALO])


def edge_kernel(part_ref, gradient_hbm, edge_ref, scale_ref, near_ref, turned_ref, rows_ref, out_hbm, stage, sem):
    @pl.when(has_adjoint_halo(part_ref))
    def _():
        rim = image_rows(near_ref[...], rows_ref[part_of(part_ref)], turned_ref)
        stage[...] = edge_ref[...] + rim * scale_ref[...]
        copy = pltpu.make_async_copy(stage, out_hbm.at[pl.ds(edge_start(part_ref), HALO)], sem)
        copy.start()
        copy.wait()


def whole_spec(array):
    del array
    return pl.BlockSpec(memory_space=pltpu.VMEM)


def call(kernel, scalars, operands, specs, out_shapes, scratch=(), name=None, flops=1 << 28, out_specs=None, aliases=None):
    many = isinstance(out_shapes, list)
    if out_specs is None:
        out_specs = [whole_spec(shape) for shape in out_shapes] if many else whole_spec(out_shapes)
    return pl.pallas_call(
        kernel,
        grid_spec=pltpu.PrefetchScalarGridSpec(
            num_scalar_prefetch=len(scalars),
            grid=(1,),
            in_specs=specs,
            out_specs=out_specs,
            scratch_shapes=list(scratch),
        ),
        out_shape=out_shapes,
        input_output_aliases=aliases or {},
        compiler_params=pltpu.CompilerParams(vmem_limit_bytes=48 * 1024 * 1024),
        cost_estimate=pl.CostEstimate(flops=flops, bytes_accessed=1 << 20, transcendentals=0),
        name=name,
    )(*scalars, *operands)


def floats(*shape):
    return jax.ShapeDtypeStruct(shape, F32)


def shards(theta, target, kernel_real, kernel_imag, weights, thresholds):
    table = {name: jnp.asarray(value) for name, value in tables().items()}
    tiles = lax.axis_size("tile")
    part = lax.axis_index("cond")
    tile = lax.axis_index("tile")
    last = PARTS - 1
    above = ((part == 0) & (tile > 0)) | ((part == last) & (tile < tiles - 1))
    below = ((part == 0) & (tile < tiles - 1)) | ((part == last) & (tile > 0))
    parts = (part + PARTS * above.astype(jnp.int32) + 2 * PARTS * below.astype(jnp.int32)).reshape(1).astype(jnp.int32)
    local_conds = kernel_real.shape[0]
    local = local_conds * KERNELS
    count = CONDS * KERNELS
    hbm = pl.BlockSpec(memory_space=pltpu.HBM)

    def across(value, down, up, within):
        pairs = [(PARTS * i + a, PARTS * i + b) for i in range(tiles) for a, b in within]
        pairs += [(PARTS * (i + 1) + down[0], PARTS * i + down[1]) for i in range(tiles - 1)]
        pairs += [(PARTS * i + up[0], PARTS * (i + 1) + up[1]) for i in range(tiles - 1)]
        pairs += [(down[0], up[1]), (PARTS * (tiles - 1) + up[0], PARTS * (tiles - 1) + down[1])]
        return lax.ppermute(value, ("tile", "cond"), pairs)

    def partner(value, step):
        return lax.ppermute(value, "cond", [(i, i ^ step) for i in range(PARTS)])

    kernel_shape = (local_conds, KSUP, KERNELS, KSUP)
    own, rim, shares, forward, backward = call(
        open_kernel,
        (parts,),
        tuple(
            pltpu.with_memory_space_constraint(value, pltpu.HBM)
            for value in (
                theta, table["waves"], kernel_real.transpose(0, 2, 1, 3), kernel_imag.transpose(0, 2, 1, 3), thresholds, weights,
                table["forward"], table["backward"],
            )
        ),
        [hbm] * 8,
        [
            floats(2 * local, FA, 2 * FB),
            floats(HALO, 2 * FB),
            floats(CONDS, ROWS),
            jax.ShapeDtypeStruct(table["forward"].shape[1:], BF),
            jax.ShapeDtypeStruct(table["backward"].shape[1:], BF),
        ],
        scratch=(
            pltpu.VMEM((HALO, TP), F32),
            pltpu.VMEM(table["waves"].shape, BF),
            pltpu.VMEM(kernel_shape, F32),
            pltpu.VMEM(kernel_shape, F32),
            pltpu.SMEM(thresholds.shape, F32),
            pltpu.SMEM(weights.shape, jnp.int32),
            pltpu.VMEM((2 * local, 72, 2 * FB), F32),
            pltpu.SemaphoreType.DMA((8,)),
        ),
        name="open_parts",
    )
    rim = across(rim, (0, 0), (last, last), [(1, 2), (2, 1)])
    spectrum = call(
        spectrum_kernel,
        (parts,),
        (theta, table["column"], table["spectrum_rows"]),
        [whole_spec(theta), whole_spec(table["column"]), whole_spec(table["spectrum_rows"])],
        floats(2, FA, 2 * FB),
        name="own_spectrum",
        flops=1 << 31,
    )
    side = partner(own, 3)
    spectrum = call(
        rim_kernel,
        (parts,),
        (spectrum, rim, table["rim_rows"]),
        [whole_spec(spectrum), whole_spec(rim), whole_spec(table["rim_rows"])],
        floats(1, FA, 2 * FB),
        name="add_rim",
    )
    mixed = jnp.concatenate([own, side, spectrum + partner(spectrum, 3)], axis=0)
    near_kernels, signs = call(
        near_kernels_kernel,
        (parts,),
        (mixed, target),
        [whole_spec(mixed), whole_spec(target)],
        [floats(count // 2, 4, FA, 2 * FB), floats(TP, ROWS)],
        name="near_kernels",
        flops=1 << 30,
    )
    adjoint = call(
        fields_kernel,
        (parts,),
        (
            mixed, partner(mixed, 1), near_kernels, signs, shares, forward, backward, table["row"], table["row_turned"],
        ),
        [
            whole_spec(mixed),
            whole_spec(mixed),
            whole_spec(near_kernels),
            whole_spec(signs),
            whole_spec(shares),
            whole_spec(forward),
            whole_spec(backward),
            whole_spec(table["row"]),
            whole_spec(table["row_turned"]),
        ],
        floats(FA, 2 * FB),
        scratch=(
            pltpu.VMEM((count // 2, 4, FA, 2 * FB), F32),
            pltpu.VMEM((CONDS, ROWS), F32),
            pltpu.VMEM((count * 4 * FA, 2 * FB), F32),
            pltpu.VMEM((count, 6 * FA, 2 * ROWS), BF),
            pltpu.VMEM((count, TP, 2 * ROWS), F32),
            pltpu.VMEM((CONDS, TP, ROWS), F32),
            pltpu.VMEM((TP, ROWS), F32),
            pltpu.VMEM((count * 2, 2 * FA, ROWS), F32),
            pltpu.VMEM((count * 4 * FA, 4 * FB), F32),
        ),
        name="coherent_fields",
        flops=1 << 33,
    )
    adjoint = adjoint + partner(adjoint, 1)
    adjoint = adjoint + partner(adjoint, 3)
    near = across(adjoint, (2, last), (1, 0), [(0, 1), (last, 2)])
    gradient, edge, scale = call(
        gradient_kernel,
        (parts,),
        (theta, adjoint, table["turned"], table["own_rows"]),
        [
            whole_spec(theta),
            whole_spec(adjoint),
            whole_spec(table["turned"]),
            whole_spec(table["own_rows"]),
        ],
        [floats(ROWS, TP), floats(HALO, TP), floats(HALO, TP)],
        out_specs=[
            pl.BlockSpec((ROWS, TP), lambda i, *refs: (0, 0)),
            whole_spec(adjoint),
            whole_spec(adjoint),
        ],
        name="own_gradient",
        flops=1 << 31,
    )
    return call(
        edge_kernel,
        (parts,),
        (gradient, edge, scale, near, table["turned"], table["halo_rows"]),
        [
            hbm,
            whole_spec(edge),
            whole_spec(scale),
            whole_spec(near),
            whole_spec(table["turned"]),
            whole_spec(table["halo_rows"]),
        ],
        floats(ROWS, TP),
        scratch=(pltpu.VMEM((HALO, TP), F32), pltpu.SemaphoreType.DMA),
        name="edge_gradient",
        out_specs=hbm,
        aliases={1: 0},
    )


def solution(mesh):
    in_specs = (
        P(("tile", "cond"), None),
        P("tile", None),
        P("cond", None, None, None),
        P("cond", None, None, None),
        P(),
        P("cond"),
    )
    out_specs = P(("tile", "cond"), None)
    return jax.shard_map(shards, mesh=mesh, in_specs=in_specs, out_specs=out_specs, check_vma=False)
```

```python
import functools

import jax
import jax.numpy as jnp
import ml_dtypes
import numpy as np
from jax import lax
from jax.experimental import pallas as pl
from jax.experimental.pallas import tpu as pltpu
from jax.sharding import PartitionSpec as P

TP = 512
HALO = 32
KSUP = 65
HALF = KSUP // 2
KERNELS = 2
CONDS = 8
FULL = TP + 2 * HALO
PARTS = 4
ROWS = TP // PARTS
FA = 40
FB = 64
SPARE = FA - HALF - 1
SPARE_BLOCKS = -(-(HALF + 1) // SPARE)
BF = jnp.bfloat16
F32 = jnp.float32

mask_steep = 2.0
resist_steep = 4.0
band_weight = 1.0


def waves(positions):
    angles = (np.outer(np.asarray(positions, np.int64), np.arange(HALF + 1)) % FULL) * (2.0 * np.pi / FULL)
    return np.cos(angles), np.sin(angles)


def halves(table):
    high = table.astype(np.float32).astype(ml_dtypes.bfloat16)
    low = (table - high.astype(np.float64)).astype(np.float32).astype(ml_dtypes.bfloat16)
    return high, low


def row_table(positions):
    cosine, sine = waves(positions)
    table = np.zeros((len(positions), 2 * FA))
    table[:, : HALF + 1] = cosine
    table[:, FA : FA + HALF + 1] = sine
    return table


def pair_table(positions):
    table = row_table(positions)
    return np.concatenate([table, np.concatenate([-table[:, FA:], table[:, :FA]], axis=1)])


def column_table(positions):
    cosine, sine = waves(positions)
    table = np.zeros((len(positions), 4 * FB))
    for block, values in enumerate((cosine, cosine, sine, -sine)):
        table[:, block * FB : block * FB + HALF] = values[:, 1:]
    table[:, HALF] = 1.0
    return table


@functools.cache
def tables():
    pixels = np.arange(TP) + HALO
    column = column_table(pixels)
    column_high, column_low = halves(column)
    turned = np.concatenate([column[:, : 2 * FB].T, column[:, 2 * FB :].T], axis=1)
    turned_high, turned_low = halves(turned)
    row = row_table(pixels)
    row_high, row_low = halves(row)
    out = {}
    out["column"] = np.stack([column_high, column_low])
    waves_only = np.s_[:, np.r_[0:FB, 2 * FB : 3 * FB]]
    out["waves"] = np.stack([column_high[waves_only], column_low[waves_only]])
    spectrum_rows = []
    rim_rows = []
    halo_rows = []
    own_rows = []
    forward = []
    backward = []
    for part in range(PARTS):
        own = np.arange(ROWS) + part * ROWS + HALO
        rim = np.arange(HALO) + (0 if part == PARTS - 1 else FULL - HALO)
        for rows, positions in ((spectrum_rows, own), (rim_rows, rim)):
            high, low = halves(row_table(positions).T)
            rows.append(np.concatenate([high, low, high], axis=1))
        high, low = halves(pair_table(rim))
        halo_rows.append(np.concatenate([high, low, high], axis=1))
        high, low = halves(pair_table(own))
        own_rows.append(np.concatenate([high, low, high], axis=1))
        cols = slice(part * ROWS, (part + 1) * ROWS)
        high = np.concatenate([turned_high[:, :TP][:, cols], turned_high[:, TP:][:, cols]], axis=1)
        low = np.concatenate([turned_low[:, :TP][:, cols], turned_low[:, TP:][:, cols]], axis=1)
        forward.append(np.concatenate([high, high, low]))
        backward.append(np.concatenate([column_high[cols], column_high[cols], column_low[cols]]))
    out["spectrum_rows"] = np.stack(spectrum_rows)
    out["own_rows"] = np.stack(own_rows)
    out["rim_rows"] = np.stack(rim_rows)
    out["halo_rows"] = np.stack(halo_rows)
    out["forward"] = np.stack(forward)
    out["backward"] = np.stack(backward)
    out["turned"] = np.stack([column_high.T, column_low.T])
    out["row"] = np.concatenate([row_high, row_low, row_high], axis=1)
    out["row_turned"] = np.concatenate([row_high.T, row_low.T])
    return out


def part_of(ref):
    return ref[0] % PARTS


def has_adjoint_halo(ref):
    return ref[0] // PARTS % 2 > 0


def has_mask_halo(ref):
    return ref[0] // (2 * PARTS) > 0


def dot(left, right):
    return jnp.dot(left, right, preferred_element_type=F32)


def split(value):
    high = value.astype(BF)
    return high, (value - high.astype(F32)).astype(BF)


def lanes_and_rows():
    shape = (FA, 2 * FB)
    return lax.broadcasted_iota(jnp.int32, shape, 1), lax.broadcasted_iota(jnp.int32, shape, 0)


def pack(even, odd):
    lane, row = lanes_and_rows()
    packed = jnp.where(lane % FB < HALF, even, pltpu.roll(odd, HALF, 1))
    for place, value in ((FA - 2, even), (FA - 3, odd)):
        line = jnp.sum(jnp.where(lane == row, value[:, HALF : HALF + 1], 0.0), axis=0, keepdims=True)
        packed = jnp.where(row == place, line, packed)
    return packed


def unpack(packed):
    lane, row = lanes_and_rows()
    values = []
    for place, value in ((FA - 2, packed), (FA - 3, pltpu.roll(packed, 2 * FB - HALF, 1))):
        column = jnp.sum(jnp.where((lane == row) & (row <= HALF), packed[place : place + 1], 0.0), axis=1, keepdims=True)
        value = jnp.where(lane == HALF, column, jnp.where(lane % FB < HALF, value, 0.0))
        values.append(jnp.where(row <= HALF, value, 0.0))
    return values


def columns_of(mask, column_ref):
    high, low = split(mask)
    return dot(high, column_ref[0]) + dot(low, column_ref[0]) + dot(high, column_ref[1])


def spectrum_of(across, rows):
    high, low = split(across)
    both = dot(rows, jnp.concatenate([high, high, low], axis=0))
    even = both[:FA, : 2 * FB] - both[FA:, 2 * FB :]
    odd = both[FA:, : 2 * FB] + both[:FA, 2 * FB :]
    return even, odd


def open_kernel(
    part_ref, theta_hbm, waves_hbm, real_hbm, imag_hbm, thresholds_hbm, weights_hbm, forward_hbm, backward_hbm,
    out_ref, rim_ref, shares_ref, forward_ref, backward_ref, theta_ref, waves_ref, real_ref, imag_ref, thresholds_ref,
    weights_ref, stage, sems,
):
    part = part_of(part_ref)
    edge = pl.ds(pl.multiple_of(jnp.where(part == 0, 0, ROWS - HALO), HALO), HALO)
    moves = [
        (theta_hbm.at[edge], theta_ref),
        (waves_hbm, waves_ref),
        (real_hbm, real_ref),
        (imag_hbm, imag_ref),
        (thresholds_hbm, thresholds_ref),
        (weights_hbm, weights_ref),
        (forward_hbm.at[part], forward_ref),
        (backward_hbm.at[part], backward_ref),
    ]
    copies = [pltpu.make_async_copy(source, target, sems.at[i]) for i, (source, target) in enumerate(moves)]
    for copy in copies:
        copy.start()
    local_conds = real_ref.shape[0]
    mats = local_conds * KERNELS * 2
    stage[...] = jnp.zeros_like(stage)
    rows = stage.shape[1]
    source = lax.broadcasted_iota(jnp.int32, (2 * FB, 4 * FB), 0)
    target = lax.broadcasted_iota(jnp.int32, (2 * FB, 4 * FB), 1)
    lane = target % FB
    block = target // FB
    plus = (block == 0) | (block == 3)
    freq = jnp.where(lane < HALF, lane + 1, 0)
    used = (lane < HALF) | ((lane == HALF) & (block % 2 == 0))
    pick = (used & (source == jnp.where(plus, HALF + freq, HALF - freq))).astype(F32).astype(BF)
    source = lax.broadcasted_iota(jnp.int32, (FA, 2 * rows), 1) % rows
    target = lax.broadcasted_iota(jnp.int32, (FA, 2 * rows), 0)
    turn = ((source == HALF - target) & (target <= HALF)).astype(F32).astype(BF)
    lane = lax.broadcasted_iota(jnp.int32, (FA, 2 * FB), 1)
    row = lax.broadcasted_iota(jnp.int32, (FA, 2 * FB), 0)
    valid = (row <= HALF) & ((lane <= HALF) | ((row > 0) & (lane >= FB) & (lane < FB + HALF)))
    scale = 1.0 / (FULL * FULL)
    keep_top = jnp.where(valid, scale, 0.0)
    keep_bottom = jnp.where((row == 0) & (lane == HALF), 0.0, keep_top)
    first = lane % FB < HALF
    for copy in copies[:6]:
        copy.wait()
    rim_ref[...] = columns_of(jnp.tanh(mask_steep * theta_ref[...]), waves_ref)
    for cond in range(local_conds):
        for kern in range(KERNELS):
            for piece, ref in enumerate((real_ref, imag_ref)):
                stage[(cond * KERNELS + kern) * 2 + piece, :KSUP, :KSUP] = ref[cond, :, kern, :]
    high, low = split(stage[...].reshape(mats * rows, 2 * FB))
    picked = [dot(piece, pick) for piece in (high, low)]
    extra = jnp.zeros((FA, 2 * FB), F32)
    blocks = []
    for kern in range(local_conds * KERNELS):
        arrays = [[], []]
        for piece in range(2):
            start = (kern * 2 + piece) * rows
            top = picked[0][start + HALF : start + HALF + FA, : 2 * FB] + picked[1][start + HALF : start + HALF + FA, : 2 * FB]
            pieces = jnp.concatenate([half[start : start + rows, 2 * FB :] for half in picked], axis=0)
            bottom = dot(turn, pieces.astype(BF)) * keep_bottom
            top = top * keep_top
            arrays[0].append(top + bottom)
            arrays[1].append(top - bottom)
        for which, (real, imag) in enumerate(arrays):
            blocks.append(jnp.where(first, real, pltpu.roll(imag, HALF, 1)))
            for piece, value in enumerate((real, imag)):
                place = kern * 4 + which * 2 + piece
                extra = jnp.where(lane == place, pltpu.roll(value, (place - HALF) % (2 * FB), 1), extra)
    for i, block in enumerate(blocks):
        if i < SPARE_BLOCKS:
            block = jnp.concatenate([block[: HALF + 1], extra[SPARE * i : SPARE * (i + 1)]], axis=0)
        elif i < SPARE_BLOCKS + local_conds:
            block = jnp.where(row == FA - 1, thresholds_ref[i - SPARE_BLOCKS], block)
        out_ref[i] = block
    weight_sum = weights_ref[0]
    for i in range(1, CONDS):
        weight_sum = weight_sum + weights_ref[i]
    row = lax.broadcasted_iota(jnp.int32, shares_ref.shape, 0)
    shares = jnp.zeros(shares_ref.shape, F32)
    for group, step in enumerate((0, 3, 1, 2)):
        for i in range(local_conds):
            weight = weights_ref[lax.bitwise_xor(part, step) * local_conds + i]
            shares = jnp.where(row == group * local_conds + i, weight.astype(F32), shares)
    shares_ref[...] = shares / weight_sum.astype(F32)
    for copy in copies[6:]:
        copy.wait()


def spectrum_kernel(part_ref, theta_ref, column_ref, rows_ref, out_ref):
    across = columns_of(jnp.tanh(mask_steep * theta_ref[...]), column_ref)
    even, odd = spectrum_of(across, rows_ref[part_of(part_ref)])
    out_ref[0] = even
    out_ref[1] = odd


def rim_kernel(part_ref, spectrum_ref, rim_ref, rows_ref, out_ref):
    rim = jnp.where(has_mask_halo(part_ref), rim_ref[...], 0.0)
    turned = pltpu.roll(rim, FB, 1)
    first = lax.broadcasted_iota(jnp.int32, rim.shape, 1) < FB
    across = jnp.concatenate([jnp.where(first, rim, turned), jnp.where(first, turned, -rim)], axis=1)
    even, odd = spectrum_of(across, rows_ref[part_of(part_ref)])
    out_ref[0] = pack(even + spectrum_ref[0], odd + spectrum_ref[1])


def unpack_group(ref, put):
    lane, row = lanes_and_rows()
    zero_lane = (lane == HALF) & (row <= HALF)
    extra = [ref[i][HALF + 1 :] for i in range(SPARE_BLOCKS)]
    extra = jnp.concatenate(extra + [jnp.zeros((FA - SPARE * SPARE_BLOCKS, 2 * FB), F32)], axis=0)
    for kern in range(ref.shape[0] // 2):
        values = []
        for which in range(2):
            packed = ref[2 * kern + which]
            for part, value in enumerate((packed, pltpu.roll(packed, 2 * FB - HALF, 1))):
                place = kern * 4 + which * 2 + part
                zeroth = pltpu.roll(extra, (HALF - place) % (2 * FB), 1)
                values.append(jnp.where(zero_lane, zeroth, value))
        put(kern, values)


def near_kernels_kernel(part_ref, mixed_ref, target_ref, near_ref, signs_ref):
    local = near_ref.shape[0] // 2
    for group in range(2):
        def put(kern, values, group=group):
            for i, value in enumerate(values):
                near_ref[group * local + kern, i] = value

        unpack_group(mixed_ref.at[pl.ds(group * 2 * local, 2 * local)], put)
    own = pl.ds(pl.multiple_of(part_of(part_ref) * ROWS, ROWS), ROWS)
    signs_ref[...] = 1.0 - 2.0 * target_ref[:, own].astype(F32)


def fields_kernel(
    part_ref, mixed_ref, other_ref, near_ref, signs, shares_ref, forward_ref, backward_ref, row_ref,
    row_turned_ref, out_ref, far_ref, levels_ref, lines, folded, amps, tanhs, total, turned, backs,
):
    count = 2 * far_ref.shape[0]
    local = count // PARTS
    tall = 4 * FA
    each = 2 * local
    even, odd = unpack(mixed_ref[2 * each] + other_ref[2 * each])

    def put_line(kern, values):
        he_real, he_imag, ho_real, ho_imag = values
        start = kern * tall
        for i, value in enumerate(
            (
                even * he_real + odd * ho_imag,
                odd * he_real - even * ho_imag,
                even * he_imag - odd * ho_real,
                odd * he_imag + even * ho_real,
            )
        ):
            lines[start + i * FA : start + (i + 1) * FA] = value

    def arrays_of(kern):
        ref = near_ref if kern < count // 2 else far_ref
        return [ref[kern % (count // 2), i] for i in range(4)]

    for group in range(PARTS):
        ref = (mixed_ref, other_ref)[group // 2].at[pl.ds(group % 2 * each, each)]
        for i in range(CONDS // PARTS):
            place = group * (CONDS // PARTS) + i
            levels_ref[place : place + 1] = ref[SPARE_BLOCKS + i][FA - 1 :]
        if group < 2:
            for kern in range(group * local, (group + 1) * local):
                put_line(kern, arrays_of(kern))
        else:
            def put(kern, values, group=group):
                for i, value in enumerate(values):
                    far_ref[(group - 2) * local + kern, i] = value
                put_line(group * local + kern, values)

            unpack_group(ref, put)

    high, low = split(lines[...])
    lines_folded = dot(jnp.concatenate([high, low], axis=1), forward_ref[: 4 * FB]) + dot(high, forward_ref[4 * FB :])
    for kern in range(count):
        parts = []
        for i in range(2):
            x_part = lines_folded[tall * kern + 2 * FA * i : tall * kern + 2 * FA * i + FA]
            y_part = lines_folded[tall * kern + 2 * FA * i + FA : tall * kern + 2 * FA * (i + 1)]
            parts.append(
                jnp.concatenate(
                    [x_part[:, :ROWS] + y_part[:, ROWS:], y_part[:, :ROWS] - x_part[:, ROWS:]], axis=0
                )
            )
        high, low = split(jnp.concatenate(parts, axis=1))
        folded[kern] = jnp.concatenate([high, high, low], axis=0)
    total[...] = jnp.zeros_like(total)

    def expose(cond, carry):
        intensity = None
        for kern in range(KERNELS):
            index = cond * KERNELS + kern
            amp = dot(row_ref[...], folded[index])
            amps[index] = amp
            power = amp[:, :ROWS] * amp[:, :ROWS] + amp[:, ROWS:] * amp[:, ROWS:]
            intensity = power if intensity is None else intensity + power
        level = levels_ref[pl.ds(cond, 1), :]
        value = jnp.tanh((0.5 * resist_steep) * (intensity - level))
        tanhs[cond] = value
        total[...] += value
        return carry

    lax.fori_loop(0, CONDS, expose, 0, unroll=4)
    total[...] = total[...] * (band_weight / (CONDS * CONDS))

    def drive(cond, carry):
        weight = shares_ref[pl.ds(cond, 1), :]
        value = tanhs[cond]
        slope = (weight + band_weight / CONDS) * value + weight * signs[...] - total[...]
        field = (0.5 * resist_steep) * (1.0 - value * value) * slope
        field = jnp.concatenate([field, field], axis=1)
        for kern in range(KERNELS):
            index = cond * KERNELS + kern
            high, low = split(field * amps[index])
            long = dot(row_turned_ref[...], high)
            back = long[: 2 * FA] + long[2 * FA :] + dot(row_turned_ref[: 2 * FA], low)
            turned[pl.ds(index * 2, 2)] = jnp.stack([back[:, :ROWS], back[:, ROWS:]])
        return carry

    lax.fori_loop(0, CONDS, drive, 0, unroll=8)
    high, low = split(turned[...].reshape(count * tall, ROWS))
    backs[...] = dot(jnp.concatenate([high, low], axis=1), backward_ref[: 2 * ROWS]) + dot(high, backward_ref[2 * ROWS :])

    sum_even = jnp.zeros((FA, 2 * FB), F32)
    sum_odd = jnp.zeros((FA, 2 * FB), F32)
    for kern in range(count):
        grads = []
        for i in range(2):
            c_part = backs[tall * kern + 2 * FA * i : tall * kern + 2 * FA * i + FA]
            s_part = backs[tall * kern + 2 * FA * i + FA : tall * kern + 2 * FA * (i + 1)]
            grads.append(
                (
                    c_part[:, : 2 * FB] - s_part[:, 2 * FB :],
                    s_part[:, : 2 * FB] + c_part[:, 2 * FB :],
                )
            )
        (x_real, y_real), (x_imag, y_imag) = grads
        he_real, he_imag, ho_real, ho_imag = arrays_of(kern)
        sum_even = sum_even + x_real * he_real + x_imag * he_imag - y_real * ho_imag + y_imag * ho_real
        sum_odd = sum_odd + x_real * ho_imag - x_imag * ho_real + y_real * he_real + y_imag * he_imag
    out_ref[...] = pack(sum_even, sum_odd)


def image_rows(packed, rows, turned_ref):
    high, low = split(jnp.concatenate(unpack(packed), axis=0))
    pair = dot(rows, jnp.concatenate([high, high, low], axis=0))
    count = pair.shape[0] // 2
    high, low = split(jnp.concatenate([pair[:count], pair[count:]], axis=1))
    return dot(high, turned_ref[0]) + dot(low, turned_ref[0]) + dot(high, turned_ref[1])


def edge_start(part_ref):
    return pl.multiple_of(jnp.where(part_of(part_ref) == PARTS - 1, ROWS - HALO, 0), HALO)


def gradient_kernel(part_ref, theta_ref, sum_ref, turned_ref, rows_ref, out_ref, edge_ref, scale_ref):
    part = part_of(part_ref)
    mask = jnp.tanh(mask_steep * theta_ref[...])
    scale = mask_steep * (1.0 - mask * mask)
    gradient = image_rows(sum_ref[...], rows_ref[part], turned_ref) * scale
    out_ref[...] = gradient
    last = part == PARTS - 1
    edge_ref[...] = jnp.where(last, gradient[ROWS - HALO :], gradient[:HALO])
    scale_ref[...] = jnp.where(last, scale[ROWS - HALO :], scale[:HALO])


def edge_kernel(part_ref, gradient_hbm, edge_ref, scale_ref, near_ref, turned_ref, rows_ref, out_hbm, stage, sem):
    @pl.when(has_adjoint_halo(part_ref))
    def _():
        rim = image_rows(near_ref[...], rows_ref[part_of(part_ref)], turned_ref)
        stage[...] = edge_ref[...] + rim * scale_ref[...]
        copy = pltpu.make_async_copy(stage, out_hbm.at[pl.ds(edge_start(part_ref), HALO)], sem)
        copy.start()
        copy.wait()


def whole_spec(array):
    del array
    return pl.BlockSpec(memory_space=pltpu.VMEM)


def call(kernel, scalars, operands, specs, out_shapes, scratch=(), name=None, flops=1 << 28, out_specs=None, aliases=None):
    many = isinstance(out_shapes, list)
    if out_specs is None:
        out_specs = [whole_spec(shape) for shape in out_shapes] if many else whole_spec(out_shapes)
    return pl.pallas_call(
        kernel,
        grid_spec=pltpu.PrefetchScalarGridSpec(
            num_scalar_prefetch=len(scalars),
            grid=(1,),
            in_specs=specs,
            out_specs=out_specs,
            scratch_shapes=list(scratch),
        ),
        out_shape=out_shapes,
        input_output_aliases=aliases or {},
        compiler_params=pltpu.CompilerParams(vmem_limit_bytes=48 * 1024 * 1024),
        cost_estimate=pl.CostEstimate(flops=flops, bytes_accessed=1 << 20, transcendentals=0),
        name=name,
    )(*scalars, *operands)


def floats(*shape):
    return jax.ShapeDtypeStruct(shape, F32)


def shards(theta, target, kernel_real, kernel_imag, weights, thresholds):
    table = {name: jnp.asarray(value) for name, value in tables().items()}
    tiles = lax.axis_size("tile")
    part = lax.axis_index("cond")
    tile = lax.axis_index("tile")
    last = PARTS - 1
    above = ((part == 0) & (tile > 0)) | ((part == last) & (tile < tiles - 1))
    below = ((part == 0) & (tile < tiles - 1)) | ((part == last) & (tile > 0))
    parts = (part + PARTS * above.astype(jnp.int32) + 2 * PARTS * below.astype(jnp.int32)).reshape(1).astype(jnp.int32)
    local_conds = kernel_real.shape[0]
    local = local_conds * KERNELS
    count = CONDS * KERNELS
    hbm = pl.BlockSpec(memory_space=pltpu.HBM)

    def across(value, down, up, within):
        pairs = [(PARTS * i + a, PARTS * i + b) for i in range(tiles) for a, b in within]
        pairs += [(PARTS * (i + 1) + down[0], PARTS * i + down[1]) for i in range(tiles - 1)]
        pairs += [(PARTS * i + up[0], PARTS * (i + 1) + up[1]) for i in range(tiles - 1)]
        pairs += [(down[0], up[1]), (PARTS * (tiles - 1) + up[0], PARTS * (tiles - 1) + down[1])]
        return lax.ppermute(value, ("tile", "cond"), pairs)

    def partner(value, step):
        return lax.ppermute(value, "cond", [(i, i ^ step) for i in range(PARTS)])

    kernel_shape = (local_conds, KSUP, KERNELS, KSUP)
    own, rim, shares, forward, backward = call(
        open_kernel,
        (parts,),
        tuple(
            pltpu.with_memory_space_constraint(value, pltpu.HBM)
            for value in (
                theta, table["waves"], kernel_real.transpose(0, 2, 1, 3), kernel_imag.transpose(0, 2, 1, 3), thresholds, weights,
                table["forward"], table["backward"],
            )
        ),
        [hbm] * 8,
        [
            floats(2 * local, FA, 2 * FB),
            floats(HALO, 2 * FB),
            floats(CONDS, ROWS),
            jax.ShapeDtypeStruct(table["forward"].shape[1:], BF),
            jax.ShapeDtypeStruct(table["backward"].shape[1:], BF),
        ],
        scratch=(
            pltpu.VMEM((HALO, TP), F32),
            pltpu.VMEM(table["waves"].shape, BF),
            pltpu.VMEM(kernel_shape, F32),
            pltpu.VMEM(kernel_shape, F32),
            pltpu.SMEM(thresholds.shape, F32),
            pltpu.SMEM(weights.shape, jnp.int32),
            pltpu.VMEM((2 * local, 72, 2 * FB), F32),
            pltpu.SemaphoreType.DMA((8,)),
        ),
        name="open_parts",
    )
    rim = across(rim, (0, 0), (last, last), [(1, 2), (2, 1)])
    spectrum = call(
        spectrum_kernel,
        (parts,),
        (theta, table["column"], table["spectrum_rows"]),
        [whole_spec(theta), whole_spec(table["column"]), whole_spec(table["spectrum_rows"])],
        floats(2, FA, 2 * FB),
        name="own_spectrum",
        flops=1 << 31,
    )
    side = partner(own, 3)
    spectrum = call(
        rim_kernel,
        (parts,),
        (spectrum, rim, table["rim_rows"]),
        [whole_spec(spectrum), whole_spec(rim), whole_spec(table["rim_rows"])],
        floats(1, FA, 2 * FB),
        name="add_rim",
    )
    mixed = jnp.concatenate([own, side, spectrum + partner(spectrum, 3)], axis=0)
    near_kernels, signs = call(
        near_kernels_kernel,
        (parts,),
        (mixed, target),
        [whole_spec(mixed), whole_spec(target)],
        [floats(count // 2, 4, FA, 2 * FB), floats(TP, ROWS)],
        name="near_kernels",
        flops=1 << 30,
    )
    adjoint = call(
        fields_kernel,
        (parts,),
        (
            mixed, partner(mixed, 1), near_kernels, signs, shares, forward, backward, table["row"], table["row_turned"],
        ),
        [
            whole_spec(mixed),
            whole_spec(mixed),
            whole_spec(near_kernels),
            whole_spec(signs),
            whole_spec(shares),
            whole_spec(forward),
            whole_spec(backward),
            whole_spec(table["row"]),
            whole_spec(table["row_turned"]),
        ],
        floats(FA, 2 * FB),
        scratch=(
            pltpu.VMEM((count // 2, 4, FA, 2 * FB), F32),
            pltpu.VMEM((CONDS, ROWS), F32),
            pltpu.VMEM((count * 4 * FA, 2 * FB), F32),
            pltpu.VMEM((count, 6 * FA, 2 * ROWS), BF),
            pltpu.VMEM((count, TP, 2 * ROWS), F32),
            pltpu.VMEM((CONDS, TP, ROWS), F32),
            pltpu.VMEM((TP, ROWS), F32),
            pltpu.VMEM((count * 2, 2 * FA, ROWS), F32),
            pltpu.VMEM((count * 4 * FA, 4 * FB), F32),
        ),
        name="coherent_fields",
        flops=1 << 33,
    )
    adjoint = adjoint + partner(adjoint, 1)
    adjoint = adjoint + partner(adjoint, 3)
    near = across(adjoint, (2, last), (1, 0), [(0, 1), (last, 2)])
    gradient, edge, scale = call(
        gradient_kernel,
        (parts,),
        (theta, adjoint, table["turned"], table["own_rows"]),
        [
            whole_spec(theta),
            whole_spec(adjoint),
            whole_spec(table["turned"]),
            whole_spec(table["own_rows"]),
        ],
        [floats(ROWS, TP), floats(HALO, TP), floats(HALO, TP)],
        out_specs=[
            pl.BlockSpec((ROWS, TP), lambda i, *refs: (0, 0)),
            whole_spec(adjoint),
            whole_spec(adjoint),
        ],
        name="own_gradient",
        flops=1 << 31,
    )
    return call(
        edge_kernel,
        (parts,),
        (gradient, edge, scale, near, table["turned"], table["halo_rows"]),
        [
            hbm,
            whole_spec(edge),
            whole_spec(scale),
            whole_spec(near),
            whole_spec(table["turned"]),
            whole_spec(table["halo_rows"]),
        ],
        floats(ROWS, TP),
        scratch=(pltpu.VMEM((HALO, TP), F32), pltpu.SemaphoreType.DMA),
        name="edge_gradient",
        out_specs=hbm,
        aliases={1: 0},
    )


def solution(mesh):
    in_specs = (
        P(("tile", "cond"), None),
        P("tile", None),
        P("cond", None, None, None),
        P("cond", None, None, None),
        P(),
        P("cond"),
    )
    out_specs = P(("tile", "cond"), None)
    return jax.shard_map(shards, mesh=mesh, in_specs=in_specs, out_specs=out_specs, check_vma=False)
```

```python
import functools

import jax
import jax.numpy as jnp
import ml_dtypes
import numpy as np
from jax import lax
from jax.experimental import pallas as pl
from jax.experimental.pallas import tpu as pltpu
from jax.sharding import PartitionSpec as P

TP = 512
HALO = 32
KSUP = 65
HALF = KSUP // 2
KERNELS = 2
CONDS = 8
FULL = TP + 2 * HALO
PARTS = 4
ROWS = TP // PARTS
FA = 40
FB = 64
SPARE = FA - HALF - 1
SPARE_BLOCKS = -(-(HALF + 1) // SPARE)
BF = jnp.bfloat16
F32 = jnp.float32

mask_steep = 2.0
resist_steep = 4.0
band_weight = 1.0


def waves(positions):
    angles = (np.outer(np.asarray(positions, np.int64), np.arange(HALF + 1)) % FULL) * (2.0 * np.pi / FULL)
    return np.cos(angles), np.sin(angles)


def halves(table):
    high = table.astype(np.float32).astype(ml_dtypes.bfloat16)
    low = (table - high.astype(np.float64)).astype(np.float32).astype(ml_dtypes.bfloat16)
    return high, low


def row_table(positions):
    cosine, sine = waves(positions)
    table = np.zeros((len(positions), 2 * FA))
    table[:, : HALF + 1] = cosine
    table[:, FA : FA + HALF + 1] = sine
    return table


def pair_table(positions):
    table = row_table(positions)
    return np.concatenate([table, np.concatenate([-table[:, FA:], table[:, :FA]], axis=1)])


def column_table(positions):
    cosine, sine = waves(positions)
    table = np.zeros((len(positions), 4 * FB))
    for block, values in enumerate((cosine, cosine, sine, -sine)):
        table[:, block * FB : block * FB + HALF] = values[:, 1:]
    table[:, HALF] = 1.0
    return table


@functools.cache
def tables():
    pixels = np.arange(TP) + HALO
    column = column_table(pixels)
    column_high, column_low = halves(column)
    turned = np.concatenate([column[:, : 2 * FB].T, column[:, 2 * FB :].T], axis=1)
    turned_high, turned_low = halves(turned)
    row = row_table(pixels)
    row_high, row_low = halves(row)
    out = {}
    out["column"] = np.stack([column_high, column_low])
    waves_only = np.s_[:, np.r_[0:FB, 2 * FB : 3 * FB]]
    out["waves"] = np.stack([column_high[waves_only], column_low[waves_only]])
    spectrum_rows = []
    rim_rows = []
    halo_rows = []
    own_rows = []
    forward = []
    backward = []
    for part in range(PARTS):
        own = np.arange(ROWS) + part * ROWS + HALO
        rim = np.arange(HALO) + (0 if part == PARTS - 1 else FULL - HALO)
        for rows, positions in ((spectrum_rows, own), (rim_rows, rim)):
            high, low = halves(row_table(positions).T)
            rows.append(np.concatenate([high, low, high], axis=1))
        high, low = halves(pair_table(rim))
        halo_rows.append(np.concatenate([high, low, high], axis=1))
        high, low = halves(pair_table(own))
        own_rows.append(np.concatenate([high, low, high], axis=1))
        cols = slice(part * ROWS, (part + 1) * ROWS)
        high = np.concatenate([turned_high[:, :TP][:, cols], turned_high[:, TP:][:, cols]], axis=1)
        low = np.concatenate([turned_low[:, :TP][:, cols], turned_low[:, TP:][:, cols]], axis=1)
        forward.append(np.concatenate([high, high, low]))
        backward.append(np.concatenate([column_high[cols], column_high[cols], column_low[cols]]))
    out["spectrum_rows"] = np.stack(spectrum_rows)
    out["own_rows"] = np.stack(own_rows)
    out["rim_rows"] = np.stack(rim_rows)
    out["halo_rows"] = np.stack(halo_rows)
    out["forward"] = np.stack(forward)
    out["backward"] = np.stack(backward)
    out["turned"] = np.stack([column_high.T, column_low.T])
    out["row"] = np.concatenate([row_high, row_low, row_high], axis=1)
    out["row_turned"] = np.concatenate([row_high.T, row_low.T])
    return out


def part_of(ref):
    return ref[0] % PARTS


def has_adjoint_halo(ref):
    return ref[0] // PARTS % 2 > 0


def has_mask_halo(ref):
    return ref[0] // (2 * PARTS) > 0


def dot(left, right):
    return jnp.dot(left, right, preferred_element_type=F32)


def split(value):
    high = value.astype(BF)
    return high, (value - high.astype(F32)).astype(BF)


def lanes_and_rows():
    shape = (FA, 2 * FB)
    return lax.broadcasted_iota(jnp.int32, shape, 1), lax.broadcasted_iota(jnp.int32, shape, 0)


def pack(even, odd):
    lane, row = lanes_and_rows()
    packed = jnp.where(lane % FB < HALF, even, pltpu.roll(odd, HALF, 1))
    for place, value in ((FA - 2, even), (FA - 3, odd)):
        line = jnp.sum(jnp.where(lane == row, value[:, HALF : HALF + 1], 0.0), axis=0, keepdims=True)
        packed = jnp.where(row == place, line, packed)
    return packed


def unpack(packed):
    lane, row = lanes_and_rows()
    values = []
    for place, value in ((FA - 2, packed), (FA - 3, pltpu.roll(packed, 2 * FB - HALF, 1))):
        column = jnp.sum(jnp.where((lane == row) & (row <= HALF), packed[place : place + 1], 0.0), axis=1, keepdims=True)
        value = jnp.where(lane == HALF, column, jnp.where(lane % FB < HALF, value, 0.0))
        values.append(jnp.where(row <= HALF, value, 0.0))
    return values


def columns_of(mask, column_ref):
    high, low = split(mask)
    return dot(high, column_ref[0]) + dot(low, column_ref[0]) + dot(high, column_ref[1])


def spectrum_of(across, rows):
    high, low = split(across)
    both = dot(rows, jnp.concatenate([high, high, low], axis=0))
    even = both[:FA, : 2 * FB] - both[FA:, 2 * FB :]
    odd = both[FA:, : 2 * FB] + both[:FA, 2 * FB :]
    return even, odd


def open_kernel(
    part_ref, theta_hbm, waves_hbm, real_hbm, imag_hbm, thresholds_hbm, weights_hbm, forward_hbm, backward_hbm,
    out_ref, rim_ref, shares_ref, forward_ref, backward_ref, theta_ref, waves_ref, real_ref, imag_ref, thresholds_ref,
    weights_ref, stage, sems,
):
    part = part_of(part_ref)
    edge = pl.ds(pl.multiple_of(jnp.where(part == 0, 0, ROWS - HALO), HALO), HALO)
    moves = [
        (theta_hbm.at[edge], theta_ref),
        (waves_hbm, waves_ref),
        (real_hbm, real_ref),
        (imag_hbm, imag_ref),
        (thresholds_hbm, thresholds_ref),
        (weights_hbm, weights_ref),
        (forward_hbm.at[part], forward_ref),
        (backward_hbm.at[part], backward_ref),
    ]
    copies = [pltpu.make_async_copy(source, target, sems.at[i]) for i, (source, target) in enumerate(moves)]
    for copy in copies:
        copy.start()
    local_conds = real_ref.shape[0]
    mats = local_conds * KERNELS * 2
    stage[...] = jnp.zeros_like(stage)
    rows = stage.shape[1]
    source = lax.broadcasted_iota(jnp.int32, (2 * FB, 4 * FB), 0)
    target = lax.broadcasted_iota(jnp.int32, (2 * FB, 4 * FB), 1)
    lane = target % FB
    block = target // FB
    plus = (block == 0) | (block == 3)
    freq = jnp.where(lane < HALF, lane + 1, 0)
    used = (lane < HALF) | ((lane == HALF) & (block % 2 == 0))
    pick = (used & (source == jnp.where(plus, HALF + freq, HALF - freq))).astype(F32).astype(BF)
    source = lax.broadcasted_iota(jnp.int32, (FA, 2 * rows), 1) % rows
    target = lax.broadcasted_iota(jnp.int32, (FA, 2 * rows), 0)
    turn = ((source == HALF - target) & (target <= HALF)).astype(F32).astype(BF)
    lane = lax.broadcasted_iota(jnp.int32, (FA, 2 * FB), 1)
    row = lax.broadcasted_iota(jnp.int32, (FA, 2 * FB), 0)
    valid = (row <= HALF) & ((lane <= HALF) | ((row > 0) & (lane >= FB) & (lane < FB + HALF)))
    scale = 1.0 / (FULL * FULL)
    keep_top = jnp.where(valid, scale, 0.0)
    keep_bottom = jnp.where((row == 0) & (lane == HALF), 0.0, keep_top)
    first = lane % FB < HALF
    for copy in copies[:6]:
        copy.wait()
    rim_ref[...] = columns_of(jnp.tanh(mask_steep * theta_ref[...]), waves_ref)
    for cond in range(local_conds):
        for kern in range(KERNELS):
            for piece, ref in enumerate((real_ref, imag_ref)):
                stage[(cond * KERNELS + kern) * 2 + piece, :KSUP, :KSUP] = ref[cond, :, kern, :]
    high, low = split(stage[...].reshape(mats * rows, 2 * FB))
    picked = [dot(piece, pick) for piece in (high, low)]
    extra = jnp.zeros((FA, 2 * FB), F32)
    blocks = []
    for kern in range(local_conds * KERNELS):
        arrays = [[], []]
        for piece in range(2):
            start = (kern * 2 + piece) * rows
            top = picked[0][start + HALF : start + HALF + FA, : 2 * FB] + picked[1][start + HALF : start + HALF + FA, : 2 * FB]
            pieces = jnp.concatenate([half[start : start + rows, 2 * FB :] for half in picked], axis=0)
            bottom = dot(turn, pieces.astype(BF)) * keep_bottom
            top = top * keep_top
            arrays[0].append(top + bottom)
            arrays[1].append(top - bottom)
        for which, (real, imag) in enumerate(arrays):
            blocks.append(jnp.where(first, real, pltpu.roll(imag, HALF, 1)))
            for piece, value in enumerate((real, imag)):
                place = kern * 4 + which * 2 + piece
                extra = jnp.where(lane == place, pltpu.roll(value, (place - HALF) % (2 * FB), 1), extra)
    for i, block in enumerate(blocks):
        if i < SPARE_BLOCKS:
            block = jnp.concatenate([block[: HALF + 1], extra[SPARE * i : SPARE * (i + 1)]], axis=0)
        elif i < SPARE_BLOCKS + local_conds:
            block = jnp.where(row == FA - 1, thresholds_ref[i - SPARE_BLOCKS], block)
        out_ref[i] = block
    weight_sum = weights_ref[0]
    for i in range(1, CONDS):
        weight_sum = weight_sum + weights_ref[i]
    row = lax.broadcasted_iota(jnp.int32, shares_ref.shape, 0)
    shares = jnp.zeros(shares_ref.shape, F32)
    for group, step in enumerate((0, 3, 1, 2)):
        for i in range(local_conds):
            weight = weights_ref[lax.bitwise_xor(part, step) * local_conds + i]
            shares = jnp.where(row == group * local_conds + i, weight.astype(F32), shares)
    shares_ref[...] = shares / weight_sum.astype(F32)
    for copy in copies[6:]:
        copy.wait()


def spectrum_kernel(part_ref, theta_ref, column_ref, rows_ref, out_ref):
    across = columns_of(jnp.tanh(mask_steep * theta_ref[...]), column_ref)
    even, odd = spectrum_of(across, rows_ref[part_of(part_ref)])
    out_ref[0] = even
    out_ref[1] = odd


def rim_kernel(part_ref, spectrum_ref, rim_ref, rows_ref, out_ref):
    rim = jnp.where(has_mask_halo(part_ref), rim_ref[...], 0.0)
    turned = pltpu.roll(rim, FB, 1)
    first = lax.broadcasted_iota(jnp.int32, rim.shape, 1) < FB
    across = jnp.concatenate([jnp.where(first, rim, turned), jnp.where(first, turned, -rim)], axis=1)
    even, odd = spectrum_of(across, rows_ref[part_of(part_ref)])
    out_ref[0] = pack(even + spectrum_ref[0], odd + spectrum_ref[1])


def unpack_group(ref, put):
    lane, row = lanes_and_rows()
    zero_lane = (lane == HALF) & (row <= HALF)
    extra = [ref[i][HALF + 1 :] for i in range(SPARE_BLOCKS)]
    extra = jnp.concatenate(extra + [jnp.zeros((FA - SPARE * SPARE_BLOCKS, 2 * FB), F32)], axis=0)
    for kern in range(ref.shape[0] // 2):
        values = []
        for which in range(2):
            packed = ref[2 * kern + which]
            for part, value in enumerate((packed, pltpu.roll(packed, 2 * FB - HALF, 1))):
                place = kern * 4 + which * 2 + part
                zeroth = pltpu.roll(extra, (HALF - place) % (2 * FB), 1)
                values.append(jnp.where(zero_lane, zeroth, value))
        put(kern, values)


def near_kernels_kernel(part_ref, mixed_ref, target_ref, near_ref, signs_ref):
    local = near_ref.shape[0] // 2
    for group in range(2):
        def put(kern, values, group=group):
            for i, value in enumerate(values):
                near_ref[group * local + kern, i] = value

        unpack_group(mixed_ref.at[pl.ds(group * 2 * local, 2 * local)], put)
    own = pl.ds(pl.multiple_of(part_of(part_ref) * ROWS, ROWS), ROWS)
    signs_ref[...] = 1.0 - 2.0 * target_ref[:, own].astype(F32)


def fields_kernel(
    part_ref, mixed_ref, other_ref, near_ref, signs, shares_ref, forward_ref, backward_ref, row_ref,
    row_turned_ref, out_ref, far_ref, levels_ref, lines, folded, amps, tanhs, total, turned, backs,
):
    count = 2 * far_ref.shape[0]
    local = count // PARTS
    tall = 4 * FA
    each = 2 * local
    even, odd = unpack(mixed_ref[2 * each] + other_ref[2 * each])

    def put_line(kern, values):
        he_real, he_imag, ho_real, ho_imag = values
        start = kern * tall
        for i, value in enumerate(
            (
                even * he_real + odd * ho_imag,
                odd * he_real - even * ho_imag,
                even * he_imag - odd * ho_real,
                odd * he_imag + even * ho_real,
            )
        ):
            lines[start + i * FA : start + (i + 1) * FA] = value

    def arrays_of(kern):
        ref = near_ref if kern < count // 2 else far_ref
        return [ref[kern % (count // 2), i] for i in range(4)]

    for group in range(PARTS):
        ref = (mixed_ref, other_ref)[group // 2].at[pl.ds(group % 2 * each, each)]
        for i in range(CONDS // PARTS):
            place = group * (CONDS // PARTS) + i
            levels_ref[place : place + 1] = ref[SPARE_BLOCKS + i][FA - 1 :]
        if group < 2:
            for kern in range(group * local, (group + 1) * local):
                put_line(kern, arrays_of(kern))
        else:
            def put(kern, values, group=group):
                for i, value in enumerate(values):
                    far_ref[(group - 2) * local + kern, i] = value
                put_line(group * local + kern, values)

            unpack_group(ref, put)

    high, low = split(lines[...])
    lines_folded = dot(jnp.concatenate([high, low], axis=1), forward_ref[: 4 * FB]) + dot(high, forward_ref[4 * FB :])
    for kern in range(count):
        parts = []
        for i in range(2):
            x_part = lines_folded[tall * kern + 2 * FA * i : tall * kern + 2 * FA * i + FA]
            y_part = lines_folded[tall * kern + 2 * FA * i + FA : tall * kern + 2 * FA * (i + 1)]
            parts.append(
                jnp.concatenate(
                    [x_part[:, :ROWS] + y_part[:, ROWS:], y_part[:, :ROWS] - x_part[:, ROWS:]], axis=0
                )
            )
        high, low = split(jnp.concatenate(parts, axis=1))
        lanes = slice(kern % KERNELS * 2 * ROWS, (kern % KERNELS + 1) * 2 * ROWS)
        folded[kern // KERNELS, :, lanes] = jnp.concatenate([high, high, low], axis=0)
    total[...] = jnp.zeros_like(total)

    def expose(cond, carry):
        amp = dot(row_ref[...], folded[cond])
        amps[cond] = amp
        intensity = sum(amp[:, i * ROWS : (i + 1) * ROWS] * amp[:, i * ROWS : (i + 1) * ROWS] for i in range(2 * KERNELS))
        level = levels_ref[pl.ds(cond, 1), :]
        value = jnp.tanh((0.5 * resist_steep) * (intensity - level))
        tanhs[cond] = value
        total[...] += value
        return carry

    lax.fori_loop(0, CONDS, expose, 0, unroll=4)
    total[...] = total[...] * (band_weight / (CONDS * CONDS))

    def drive(cond, carry):
        weight = shares_ref[pl.ds(cond, 1), :]
        value = tanhs[cond]
        slope = (weight + band_weight / CONDS) * value + weight * signs[...] - total[...]
        field = (0.5 * resist_steep) * (1.0 - value * value) * slope
        high, low = split(jnp.concatenate([field] * (2 * KERNELS), axis=1) * amps[cond])
        long = dot(row_turned_ref[...], high)
        back = long[: 2 * FA] + long[2 * FA :] + dot(row_turned_ref[: 2 * FA], low)
        for i in range(2 * KERNELS):
            turned[cond * 2 * KERNELS + i] = back[:, i * ROWS : (i + 1) * ROWS]
        return carry

    lax.fori_loop(0, CONDS, drive, 0, unroll=8)
    high, low = split(turned[...].reshape(count * tall, ROWS))
    backs[...] = dot(jnp.concatenate([high, low], axis=1), backward_ref[: 2 * ROWS]) + dot(high, backward_ref[2 * ROWS :])

    sum_even = jnp.zeros((FA, 2 * FB), F32)
    sum_odd = jnp.zeros((FA, 2 * FB), F32)
    for kern in range(count):
        grads = []
        for i in range(2):
            c_part = backs[tall * kern + 2 * FA * i : tall * kern + 2 * FA * i + FA]
            s_part = backs[tall * kern + 2 * FA * i + FA : tall * kern + 2 * FA * (i + 1)]
            grads.append(
                (
                    c_part[:, : 2 * FB] - s_part[:, 2 * FB :],
                    s_part[:, : 2 * FB] + c_part[:, 2 * FB :],
                )
            )
        (x_real, y_real), (x_imag, y_imag) = grads
        he_real, he_imag, ho_real, ho_imag = arrays_of(kern)
        sum_even = sum_even + x_real * he_real + x_imag * he_imag - y_real * ho_imag + y_imag * ho_real
        sum_odd = sum_odd + x_real * ho_imag - x_imag * ho_real + y_real * he_real + y_imag * he_imag
    out_ref[...] = pack(sum_even, sum_odd)


def image_rows(packed, rows, turned_ref):
    high, low = split(jnp.concatenate(unpack(packed), axis=0))
    pair = dot(rows, jnp.concatenate([high, high, low], axis=0))
    count = pair.shape[0] // 2
    high, low = split(jnp.concatenate([pair[:count], pair[count:]], axis=1))
    return dot(high, turned_ref[0]) + dot(low, turned_ref[0]) + dot(high, turned_ref[1])


def edge_start(part_ref):
    return pl.multiple_of(jnp.where(part_of(part_ref) == PARTS - 1, ROWS - HALO, 0), HALO)


def gradient_kernel(part_ref, theta_ref, sum_ref, turned_ref, rows_ref, out_ref, edge_ref, scale_ref):
    part = part_of(part_ref)
    mask = jnp.tanh(mask_steep * theta_ref[...])
    scale = mask_steep * (1.0 - mask * mask)
    gradient = image_rows(sum_ref[...], rows_ref[part], turned_ref) * scale
    out_ref[...] = gradient
    last = part == PARTS - 1
    edge_ref[...] = jnp.where(last, gradient[ROWS - HALO :], gradient[:HALO])
    scale_ref[...] = jnp.where(last, scale[ROWS - HALO :], scale[:HALO])


def edge_kernel(part_ref, gradient_hbm, edge_ref, scale_ref, near_ref, turned_ref, rows_ref, out_hbm, stage, sem):
    @pl.when(has_adjoint_halo(part_ref))
    def _():
        rim = image_rows(near_ref[...], rows_ref[part_of(part_ref)], turned_ref)
        stage[...] = edge_ref[...] + rim * scale_ref[...]
        copy = pltpu.make_async_copy(stage, out_hbm.at[pl.ds(edge_start(part_ref), HALO)], sem)
        copy.start()
        copy.wait()


def whole_spec(array):
    del array
    return pl.BlockSpec(memory_space=pltpu.VMEM)


def call(kernel, scalars, operands, specs, out_shapes, scratch=(), name=None, flops=1 << 28, out_specs=None, aliases=None):
    many = isinstance(out_shapes, list)
    if out_specs is None:
        out_specs = [whole_spec(shape) for shape in out_shapes] if many else whole_spec(out_shapes)
    return pl.pallas_call(
        kernel,
        grid_spec=pltpu.PrefetchScalarGridSpec(
            num_scalar_prefetch=len(scalars),
            grid=(1,),
            in_specs=specs,
            out_specs=out_specs,
            scratch_shapes=list(scratch),
        ),
        out_shape=out_shapes,
        input_output_aliases=aliases or {},
        compiler_params=pltpu.CompilerParams(vmem_limit_bytes=48 * 1024 * 1024),
        cost_estimate=pl.CostEstimate(flops=flops, bytes_accessed=1 << 20, transcendentals=0),
        name=name,
    )(*scalars, *operands)


def floats(*shape):
    return jax.ShapeDtypeStruct(shape, F32)


def shards(theta, target, kernel_real, kernel_imag, weights, thresholds):
    table = {name: jnp.asarray(value) for name, value in tables().items()}
    tiles = lax.axis_size("tile")
    part = lax.axis_index("cond")
    tile = lax.axis_index("tile")
    last = PARTS - 1
    above = ((part == 0) & (tile > 0)) | ((part == last) & (tile < tiles - 1))
    below = ((part == 0) & (tile < tiles - 1)) | ((part == last) & (tile > 0))
    parts = (part + PARTS * above.astype(jnp.int32) + 2 * PARTS * below.astype(jnp.int32)).reshape(1).astype(jnp.int32)
    local_conds = kernel_real.shape[0]
    local = local_conds * KERNELS
    count = CONDS * KERNELS
    hbm = pl.BlockSpec(memory_space=pltpu.HBM)

    def across(value, down, up, within):
        pairs = [(PARTS * i + a, PARTS * i + b) for i in range(tiles) for a, b in within]
        pairs += [(PARTS * (i + 1) + down[0], PARTS * i + down[1]) for i in range(tiles - 1)]
        pairs += [(PARTS * i + up[0], PARTS * (i + 1) + up[1]) for i in range(tiles - 1)]
        pairs += [(down[0], up[1]), (PARTS * (tiles - 1) + up[0], PARTS * (tiles - 1) + down[1])]
        return lax.ppermute(value, ("tile", "cond"), pairs)

    def partner(value, step):
        return lax.ppermute(value, "cond", [(i, i ^ step) for i in range(PARTS)])

    kernel_shape = (local_conds, KSUP, KERNELS, KSUP)
    own, rim, shares, forward, backward = call(
        open_kernel,
        (parts,),
        tuple(
            pltpu.with_memory_space_constraint(value, pltpu.HBM)
            for value in (
                theta, table["waves"], kernel_real.transpose(0, 2, 1, 3), kernel_imag.transpose(0, 2, 1, 3), thresholds, weights,
                table["forward"], table["backward"],
            )
        ),
        [hbm] * 8,
        [
            floats(2 * local, FA, 2 * FB),
            floats(HALO, 2 * FB),
            floats(CONDS, ROWS),
            jax.ShapeDtypeStruct(table["forward"].shape[1:], BF),
            jax.ShapeDtypeStruct(table["backward"].shape[1:], BF),
        ],
        scratch=(
            pltpu.VMEM((HALO, TP), F32),
            pltpu.VMEM(table["waves"].shape, BF),
            pltpu.VMEM(kernel_shape, F32),
            pltpu.VMEM(kernel_shape, F32),
            pltpu.SMEM(thresholds.shape, F32),
            pltpu.SMEM(weights.shape, jnp.int32),
            pltpu.VMEM((2 * local, 72, 2 * FB), F32),
            pltpu.SemaphoreType.DMA((8,)),
        ),
        name="open_parts",
    )
    rim = across(rim, (0, 0), (last, last), [(1, 2), (2, 1)])
    spectrum = call(
        spectrum_kernel,
        (parts,),
        (theta, table["column"], table["spectrum_rows"]),
        [whole_spec(theta), whole_spec(table["column"]), whole_spec(table["spectrum_rows"])],
        floats(2, FA, 2 * FB),
        name="own_spectrum",
        flops=1 << 31,
    )
    side = partner(own, 3)
    spectrum = call(
        rim_kernel,
        (parts,),
        (spectrum, rim, table["rim_rows"]),
        [whole_spec(spectrum), whole_spec(rim), whole_spec(table["rim_rows"])],
        floats(1, FA, 2 * FB),
        name="add_rim",
    )
    mixed = jnp.concatenate([own, side, spectrum + partner(spectrum, 3)], axis=0)
    near_kernels, signs = call(
        near_kernels_kernel,
        (parts,),
        (mixed, target),
        [whole_spec(mixed), whole_spec(target)],
        [floats(count // 2, 4, FA, 2 * FB), floats(TP, ROWS)],
        name="near_kernels",
        flops=1 << 30,
    )
    adjoint = call(
        fields_kernel,
        (parts,),
        (
            mixed, partner(mixed, 1), near_kernels, signs, shares, forward, backward, table["row"], table["row_turned"],
        ),
        [
            whole_spec(mixed),
            whole_spec(mixed),
            whole_spec(near_kernels),
            whole_spec(signs),
            whole_spec(shares),
            whole_spec(forward),
            whole_spec(backward),
            whole_spec(table["row"]),
            whole_spec(table["row_turned"]),
        ],
        floats(FA, 2 * FB),
        scratch=(
            pltpu.VMEM((count // 2, 4, FA, 2 * FB), F32),
            pltpu.VMEM((CONDS, ROWS), F32),
            pltpu.VMEM((count * 4 * FA, 2 * FB), F32),
            pltpu.VMEM((CONDS, 6 * FA, 2 * KERNELS * ROWS), BF),
            pltpu.VMEM((CONDS, TP, 2 * KERNELS * ROWS), F32),
            pltpu.VMEM((CONDS, TP, ROWS), F32),
            pltpu.VMEM((TP, ROWS), F32),
            pltpu.VMEM((count * 2, 2 * FA, ROWS), F32),
            pltpu.VMEM((count * 4 * FA, 4 * FB), F32),
        ),
        name="coherent_fields",
        flops=1 << 33,
    )
    adjoint = adjoint + partner(adjoint, 1)
    adjoint = adjoint + partner(adjoint, 3)
    near = across(adjoint, (2, last), (1, 0), [(0, 1), (last, 2)])
    gradient, edge, scale = call(
        gradient_kernel,
        (parts,),
        (theta, adjoint, table["turned"], table["own_rows"]),
        [
            whole_spec(theta),
            whole_spec(adjoint),
            whole_spec(table["turned"]),
            whole_spec(table["own_rows"]),
        ],
        [floats(ROWS, TP), floats(HALO, TP), floats(HALO, TP)],
        out_specs=[
            pl.BlockSpec((ROWS, TP), lambda i, *refs: (0, 0)),
            whole_spec(adjoint),
            whole_spec(adjoint),
        ],
        name="own_gradient",
        flops=1 << 31,
    )
    return call(
        edge_kernel,
        (parts,),
        (gradient, edge, scale, near, table["turned"], table["halo_rows"]),
        [
            hbm,
            whole_spec(edge),
            whole_spec(scale),
            whole_spec(near),
            whole_spec(table["turned"]),
            whole_spec(table["halo_rows"]),
        ],
        floats(ROWS, TP),
        scratch=(pltpu.VMEM((HALO, TP), F32), pltpu.SemaphoreType.DMA),
        name="edge_gradient",
        out_specs=hbm,
        aliases={1: 0},
    )


def solution(mesh):
    in_specs = (
        P(("tile", "cond"), None),
        P("tile", None),
        P("cond", None, None, None),
        P("cond", None, None, None),
        P(),
        P("cond"),
    )
    out_specs = P(("tile", "cond"), None)
    return jax.shard_map(shards, mesh=mesh, in_specs=in_specs, out_specs=out_specs, check_vma=False)
```

```python
import functools

import jax
import jax.numpy as jnp
import ml_dtypes
import numpy as np
from jax import lax
from jax.experimental import pallas as pl
from jax.experimental.pallas import tpu as pltpu
from jax.sharding import PartitionSpec as P

TP = 512
HALO = 32
KSUP = 65
HALF = KSUP // 2
KERNELS = 2
CONDS = 8
FULL = TP + 2 * HALO
PARTS = 4
ROWS = TP // PARTS
FA = 40
FB = 64
SPARE = FA - HALF - 1
SPARE_BLOCKS = -(-(HALF + 1) // SPARE)
BF = jnp.bfloat16
F32 = jnp.float32

mask_steep = 2.0
resist_steep = 4.0
band_weight = 1.0


def waves(positions):
    angles = (np.outer(np.asarray(positions, np.int64), np.arange(HALF + 1)) % FULL) * (2.0 * np.pi / FULL)
    return np.cos(angles), np.sin(angles)


def halves(table):
    high = table.astype(np.float32).astype(ml_dtypes.bfloat16)
    low = (table - high.astype(np.float64)).astype(np.float32).astype(ml_dtypes.bfloat16)
    return high, low


def row_table(positions):
    cosine, sine = waves(positions)
    table = np.zeros((len(positions), 2 * FA))
    table[:, : HALF + 1] = cosine
    table[:, FA : FA + HALF + 1] = sine
    return table


def pair_table(positions):
    table = row_table(positions)
    return np.concatenate([table, np.concatenate([-table[:, FA:], table[:, :FA]], axis=1)])


def column_table(positions):
    cosine, sine = waves(positions)
    table = np.zeros((len(positions), 4 * FB))
    for block, values in enumerate((cosine, cosine, sine, -sine)):
        table[:, block * FB : block * FB + HALF] = values[:, 1:]
    table[:, HALF] = 1.0
    return table


@functools.cache
def tables():
    pixels = np.arange(TP) + HALO
    column = column_table(pixels)
    column_high, column_low = halves(column)
    turned = np.concatenate([column[:, : 2 * FB].T, column[:, 2 * FB :].T], axis=1)
    turned_high, turned_low = halves(turned)
    row = row_table(pixels)
    row_high, row_low = halves(row)
    out = {}
    out["column"] = np.stack([column_high, column_low])
    waves_only = np.s_[:, np.r_[0:FB, 2 * FB : 3 * FB]]
    out["waves"] = np.stack([column_high[waves_only], column_low[waves_only]])
    spectrum_rows = []
    rim_rows = []
    halo_rows = []
    own_rows = []
    forward = []
    backward = []
    for part in range(PARTS):
        own = np.arange(ROWS) + part * ROWS + HALO
        rim = np.arange(HALO) + (0 if part == PARTS - 1 else FULL - HALO)
        for rows, positions in ((spectrum_rows, own), (rim_rows, rim)):
            high, low = halves(row_table(positions).T)
            rows.append(np.concatenate([high, low, high], axis=1))
        high, low = halves(pair_table(rim))
        halo_rows.append(np.concatenate([high, low, high], axis=1))
        high, low = halves(pair_table(own))
        own_rows.append(np.concatenate([high, low, high], axis=1))
        cols = slice(part * ROWS, (part + 1) * ROWS)
        high = np.concatenate([turned_high[:, :TP][:, cols], turned_high[:, TP:][:, cols]], axis=1)
        low = np.concatenate([turned_low[:, :TP][:, cols], turned_low[:, TP:][:, cols]], axis=1)
        forward.append(np.concatenate([high, high, low]))
        backward.append(np.concatenate([column_high[cols], column_high[cols], column_low[cols]]))
    out["spectrum_rows"] = np.stack(spectrum_rows)
    out["own_rows"] = np.stack(own_rows)
    out["rim_rows"] = np.stack(rim_rows)
    out["halo_rows"] = np.stack(halo_rows)
    out["forward"] = np.stack(forward)
    out["backward"] = np.stack(backward)
    out["turned"] = np.stack([column_high.T, column_low.T])
    out["row"] = np.concatenate([row_high, row_low, row_high], axis=1)
    out["row_turned"] = np.concatenate([row_high.T, row_low.T])
    return out


def part_of(ref):
    return ref[0] % PARTS


def has_adjoint_halo(ref):
    return ref[0] // PARTS % 2 > 0


def has_mask_halo(ref):
    return ref[0] // (2 * PARTS) > 0


def dot(left, right):
    return jnp.dot(left, right, preferred_element_type=F32)


def split(value):
    high = value.astype(BF)
    return high, (value - high.astype(F32)).astype(BF)


def lanes_and_rows():
    shape = (FA, 2 * FB)
    return lax.broadcasted_iota(jnp.int32, shape, 1), lax.broadcasted_iota(jnp.int32, shape, 0)


def pack(even, odd):
    lane, row = lanes_and_rows()
    packed = jnp.where(lane % FB < HALF, even, pltpu.roll(odd, HALF, 1))
    for place, value in ((FA - 2, even), (FA - 3, odd)):
        line = jnp.sum(jnp.where(lane == row, value[:, HALF : HALF + 1], 0.0), axis=0, keepdims=True)
        packed = jnp.where(row == place, line, packed)
    return packed


def unpack(packed):
    lane, row = lanes_and_rows()
    values = []
    for place, value in ((FA - 2, packed), (FA - 3, pltpu.roll(packed, 2 * FB - HALF, 1))):
        column = jnp.sum(jnp.where((lane == row) & (row <= HALF), packed[place : place + 1], 0.0), axis=1, keepdims=True)
        value = jnp.where(lane == HALF, column, jnp.where(lane % FB < HALF, value, 0.0))
        values.append(jnp.where(row <= HALF, value, 0.0))
    return values


def columns_of(mask, column_ref):
    high, low = split(mask)
    return dot(high, column_ref[0]) + dot(low, column_ref[0]) + dot(high, column_ref[1])


def spectrum_of(across, rows):
    high, low = split(across)
    both = dot(rows, jnp.concatenate([high, high, low], axis=0))
    even = both[:FA, : 2 * FB] - both[FA:, 2 * FB :]
    odd = both[FA:, : 2 * FB] + both[:FA, 2 * FB :]
    return even, odd


def open_kernel(
    part_ref, theta_hbm, waves_hbm, real_hbm, imag_hbm, thresholds_hbm, weights_hbm, forward_hbm, backward_hbm,
    out_ref, rim_ref, shares_ref, forward_ref, backward_ref, theta_ref, waves_ref, real_ref, imag_ref, thresholds_ref,
    weights_ref, stage, sems,
):
    part = part_of(part_ref)
    edge = pl.ds(pl.multiple_of(jnp.where(part == 0, 0, ROWS - HALO), HALO), HALO)
    moves = [
        (theta_hbm.at[edge], theta_ref),
        (waves_hbm, waves_ref),
        (real_hbm, real_ref),
        (imag_hbm, imag_ref),
        (thresholds_hbm, thresholds_ref),
        (weights_hbm, weights_ref),
        (forward_hbm.at[part], forward_ref),
        (backward_hbm.at[part], backward_ref),
    ]
    copies = [pltpu.make_async_copy(source, target, sems.at[i]) for i, (source, target) in enumerate(moves)]
    for copy in copies:
        copy.start()
    local_conds = real_ref.shape[0]
    mats = local_conds * KERNELS * 2
    stage[...] = jnp.zeros_like(stage)
    rows = stage.shape[1]
    source = lax.broadcasted_iota(jnp.int32, (2 * FB, 4 * FB), 0)
    target = lax.broadcasted_iota(jnp.int32, (2 * FB, 4 * FB), 1)
    lane = target % FB
    block = target // FB
    plus = (block == 0) | (block == 3)
    freq = jnp.where(lane < HALF, lane + 1, 0)
    used = (lane < HALF) | ((lane == HALF) & (block % 2 == 0))
    pick = (used & (source == jnp.where(plus, HALF + freq, HALF - freq))).astype(F32).astype(BF)
    source = lax.broadcasted_iota(jnp.int32, (FA, 2 * rows), 1) % rows
    target = lax.broadcasted_iota(jnp.int32, (FA, 2 * rows), 0)
    turn = ((source == HALF - target) & (target <= HALF)).astype(F32).astype(BF)
    lane = lax.broadcasted_iota(jnp.int32, (FA, 2 * FB), 1)
    row = lax.broadcasted_iota(jnp.int32, (FA, 2 * FB), 0)
    valid = (row <= HALF) & ((lane <= HALF) | ((row > 0) & (lane >= FB) & (lane < FB + HALF)))
    scale = 1.0 / (FULL * FULL)
    keep_top = jnp.where(valid, scale, 0.0)
    keep_bottom = jnp.where((row == 0) & (lane == HALF), 0.0, keep_top)
    first = lane % FB < HALF
    for copy in copies[:6]:
        copy.wait()
    rim_ref[...] = columns_of(jnp.tanh(mask_steep * theta_ref[...]), waves_ref)
    for cond in range(local_conds):
        for kern in range(KERNELS):
            for piece, ref in enumerate((real_ref, imag_ref)):
                stage[(cond * KERNELS + kern) * 2 + piece, :KSUP, :KSUP] = ref[cond, :, kern, :]
    high, low = split(stage[...].reshape(mats * rows, 2 * FB))
    picked = [dot(piece, pick) for piece in (high, low)]
    extra = jnp.zeros((FA, 2 * FB), F32)
    blocks = []
    for kern in range(local_conds * KERNELS):
        arrays = [[], []]
        for piece in range(2):
            start = (kern * 2 + piece) * rows
            top = picked[0][start + HALF : start + HALF + FA, : 2 * FB] + picked[1][start + HALF : start + HALF + FA, : 2 * FB]
            pieces = jnp.concatenate([half[start : start + rows, 2 * FB :] for half in picked], axis=0)
            bottom = dot(turn, pieces.astype(BF)) * keep_bottom
            top = top * keep_top
            arrays[0].append(top + bottom)
            arrays[1].append(top - bottom)
        for which, (real, imag) in enumerate(arrays):
            blocks.append(jnp.where(first, real, pltpu.roll(imag, HALF, 1)))
            for piece, value in enumerate((real, imag)):
                place = kern * 4 + which * 2 + piece
                extra = jnp.where(lane == place, pltpu.roll(value, (place - HALF) % (2 * FB), 1), extra)
    for i, block in enumerate(blocks):
        if i < SPARE_BLOCKS:
            block = jnp.concatenate([block[: HALF + 1], extra[SPARE * i : SPARE * (i + 1)]], axis=0)
        elif i < SPARE_BLOCKS + local_conds:
            block = jnp.where(row == FA - 1, thresholds_ref[i - SPARE_BLOCKS], block)
        out_ref[i] = block
    weight_sum = weights_ref[0]
    for i in range(1, CONDS):
        weight_sum = weight_sum + weights_ref[i]
    row = lax.broadcasted_iota(jnp.int32, shares_ref.shape, 0)
    shares = jnp.zeros(shares_ref.shape, F32)
    for group, step in enumerate((0, 3, 1, 2)):
        for i in range(local_conds):
            weight = weights_ref[lax.bitwise_xor(part, step) * local_conds + i]
            shares = jnp.where(row == group * local_conds + i, weight.astype(F32), shares)
    shares_ref[...] = shares / weight_sum.astype(F32)
    for copy in copies[6:]:
        copy.wait()


def spectrum_kernel(part_ref, theta_ref, column_ref, rows_ref, out_ref):
    across = columns_of(jnp.tanh(mask_steep * theta_ref[...]), column_ref)
    even, odd = spectrum_of(across, rows_ref[part_of(part_ref)])
    out_ref[0] = even
    out_ref[1] = odd


def rim_kernel(part_ref, spectrum_ref, rim_ref, rows_ref, out_ref):
    rim = jnp.where(has_mask_halo(part_ref), rim_ref[...], 0.0)
    turned = pltpu.roll(rim, FB, 1)
    first = lax.broadcasted_iota(jnp.int32, rim.shape, 1) < FB
    across = jnp.concatenate([jnp.where(first, rim, turned), jnp.where(first, turned, -rim)], axis=1)
    even, odd = spectrum_of(across, rows_ref[part_of(part_ref)])
    out_ref[0] = pack(even + spectrum_ref[0], odd + spectrum_ref[1])


def unpack_group(ref, put):
    lane, row = lanes_and_rows()
    zero_lane = (lane == HALF) & (row <= HALF)
    extra = [ref[i][HALF + 1 :] for i in range(SPARE_BLOCKS)]
    extra = jnp.concatenate(extra + [jnp.zeros((FA - SPARE * SPARE_BLOCKS, 2 * FB), F32)], axis=0)
    for kern in range(ref.shape[0] // 2):
        values = []
        for which in range(2):
            packed = ref[2 * kern + which]
            for part, value in enumerate((packed, pltpu.roll(packed, 2 * FB - HALF, 1))):
                place = kern * 4 + which * 2 + part
                zeroth = pltpu.roll(extra, (HALF - place) % (2 * FB), 1)
                values.append(jnp.where(zero_lane, zeroth, value))
        put(kern, values)


def near_kernels_kernel(part_ref, mixed_ref, target_ref, near_ref, signs_ref):
    local = near_ref.shape[0] // 2
    for group in range(2):
        def put(kern, values, group=group):
            for i, value in enumerate(values):
                near_ref[group * local + kern, i] = value

        unpack_group(mixed_ref.at[pl.ds(group * 2 * local, 2 * local)], put)
    own = pl.ds(pl.multiple_of(part_of(part_ref) * ROWS, ROWS), ROWS)
    signs_ref[...] = 1.0 - 2.0 * target_ref[:, own].astype(F32)


def fields_kernel(
    part_ref, mixed_ref, other_ref, near_ref, signs, shares_ref, forward_ref, backward_ref, row_ref,
    row_turned_ref, out_ref, far_ref, levels_ref, lines, folded, amps, tanhs, total, turned, backs,
):
    count = 2 * far_ref.shape[0]
    local = count // PARTS
    tall = 4 * FA
    each = 2 * local
    even, odd = unpack(mixed_ref[2 * each] + other_ref[2 * each])

    def put_line(kern, values):
        he_real, he_imag, ho_real, ho_imag = values
        start = kern * tall
        for i, value in enumerate(
            (
                even * he_real + odd * ho_imag,
                odd * he_real - even * ho_imag,
                even * he_imag - odd * ho_real,
                odd * he_imag + even * ho_real,
            )
        ):
            lines[start + i * FA : start + (i + 1) * FA] = value

    def arrays_of(kern):
        ref = near_ref if kern < count // 2 else far_ref
        return [ref[kern % (count // 2), i] for i in range(4)]

    for group in range(PARTS):
        ref = (mixed_ref, other_ref)[group // 2].at[pl.ds(group % 2 * each, each)]
        for i in range(CONDS // PARTS):
            place = group * (CONDS // PARTS) + i
            levels_ref[place : place + 1] = ref[SPARE_BLOCKS + i][FA - 1 :]
        if group < 2:
            for kern in range(group * local, (group + 1) * local):
                put_line(kern, arrays_of(kern))
        else:
            def put(kern, values, group=group):
                for i, value in enumerate(values):
                    far_ref[(group - 2) * local + kern, i] = value
                put_line(group * local + kern, values)

            unpack_group(ref, put)

    high, low = split(lines[...])
    lines_folded = dot(jnp.concatenate([high, low], axis=1), forward_ref[: 4 * FB]) + dot(high, forward_ref[4 * FB :])
    for kern in range(count):
        parts = []
        for i in range(2):
            x_part = lines_folded[tall * kern + 2 * FA * i : tall * kern + 2 * FA * i + FA]
            y_part = lines_folded[tall * kern + 2 * FA * i + FA : tall * kern + 2 * FA * (i + 1)]
            parts.append(
                jnp.concatenate(
                    [x_part[:, :ROWS] + y_part[:, ROWS:], y_part[:, :ROWS] - x_part[:, ROWS:]], axis=0
                )
            )
        high, low = split(jnp.concatenate(parts, axis=1))
        folded[kern] = jnp.concatenate([high, high, low], axis=0)
    total[...] = jnp.zeros_like(total)

    def expose(cond, carry):
        intensity = None
        for kern in range(KERNELS):
            index = cond * KERNELS + kern
            amp = dot(row_ref[...], folded[index])
            amps[index] = amp
            power = amp[:, :ROWS] * amp[:, :ROWS] + amp[:, ROWS:] * amp[:, ROWS:]
            intensity = power if intensity is None else intensity + power
        level = levels_ref[pl.ds(cond, 1), :]
        value = jnp.tanh((0.5 * resist_steep) * (intensity - level))
        tanhs[cond] = value
        total[...] += value
        return carry

    lax.fori_loop(0, CONDS, expose, 0, unroll=4)
    total[...] = total[...] * (band_weight / (CONDS * CONDS))

    def drive(cond, carry):
        weight = shares_ref[pl.ds(cond, 1), :]
        value = tanhs[cond]
        slope = (weight + band_weight / CONDS) * value + weight * signs[...] - total[...]
        field = (0.5 * resist_steep) * (1.0 - value * value) * slope
        field = jnp.concatenate([field, field], axis=1)
        for kern in range(KERNELS):
            index = cond * KERNELS + kern
            high, low = split(field * amps[index])
            long = dot(row_turned_ref[...], high)
            back = long[: 2 * FA] + long[2 * FA :] + dot(row_turned_ref[: 2 * FA], low)
            turned[pl.ds(index * 2, 2)] = jnp.stack([back[:, :ROWS], back[:, ROWS:]])
        return carry

    for half in range(2):
        for cond in range(half * CONDS // 2, (half + 1) * CONDS // 2):
            drive(cond, 0)
        high, low = split(turned[half * count : (half + 1) * count].reshape(count // 2 * tall, ROWS))
        backs[half * count // 2 * tall : (half + 1) * count // 2 * tall] = dot(
            jnp.concatenate([high, low], axis=1), backward_ref[: 2 * ROWS]
        ) + dot(high, backward_ref[2 * ROWS :])

    sum_even = jnp.zeros((FA, 2 * FB), F32)
    sum_odd = jnp.zeros((FA, 2 * FB), F32)
    for kern in range(count):
        grads = []
        for i in range(2):
            c_part = backs[tall * kern + 2 * FA * i : tall * kern + 2 * FA * i + FA]
            s_part = backs[tall * kern + 2 * FA * i + FA : tall * kern + 2 * FA * (i + 1)]
            grads.append(
                (
                    c_part[:, : 2 * FB] - s_part[:, 2 * FB :],
                    s_part[:, : 2 * FB] + c_part[:, 2 * FB :],
                )
            )
        (x_real, y_real), (x_imag, y_imag) = grads
        he_real, he_imag, ho_real, ho_imag = arrays_of(kern)
        sum_even = sum_even + x_real * he_real + x_imag * he_imag - y_real * ho_imag + y_imag * ho_real
        sum_odd = sum_odd + x_real * ho_imag - x_imag * ho_real + y_real * he_real + y_imag * he_imag
    out_ref[...] = pack(sum_even, sum_odd)


def image_rows(packed, rows, turned_ref):
    high, low = split(jnp.concatenate(unpack(packed), axis=0))
    pair = dot(rows, jnp.concatenate([high, high, low], axis=0))
    count = pair.shape[0] // 2
    high, low = split(jnp.concatenate([pair[:count], pair[count:]], axis=1))
    return dot(high, turned_ref[0]) + dot(low, turned_ref[0]) + dot(high, turned_ref[1])


def edge_start(part_ref):
    return pl.multiple_of(jnp.where(part_of(part_ref) == PARTS - 1, ROWS - HALO, 0), HALO)


def gradient_kernel(part_ref, theta_ref, sum_ref, turned_ref, rows_ref, out_ref, edge_ref, scale_ref):
    part = part_of(part_ref)
    mask = jnp.tanh(mask_steep * theta_ref[...])
    scale = mask_steep * (1.0 - mask * mask)
    gradient = image_rows(sum_ref[...], rows_ref[part], turned_ref) * scale
    out_ref[...] = gradient
    last = part == PARTS - 1
    edge_ref[...] = jnp.where(last, gradient[ROWS - HALO :], gradient[:HALO])
    scale_ref[...] = jnp.where(last, scale[ROWS - HALO :], scale[:HALO])


def edge_kernel(part_ref, gradient_hbm, edge_ref, scale_ref, near_ref, turned_ref, rows_ref, out_hbm, stage, sem):
    @pl.when(has_adjoint_halo(part_ref))
    def _():
        rim = image_rows(near_ref[...], rows_ref[part_of(part_ref)], turned_ref)
        stage[...] = edge_ref[...] + rim * scale_ref[...]
        copy = pltpu.make_async_copy(stage, out_hbm.at[pl.ds(edge_start(part_ref), HALO)], sem)
        copy.start()
        copy.wait()


def whole_spec(array):
    del array
    return pl.BlockSpec(memory_space=pltpu.VMEM)


def call(kernel, scalars, operands, specs, out_shapes, scratch=(), name=None, flops=1 << 28, out_specs=None, aliases=None):
    many = isinstance(out_shapes, list)
    if out_specs is None:
        out_specs = [whole_spec(shape) for shape in out_shapes] if many else whole_spec(out_shapes)
    return pl.pallas_call(
        kernel,
        grid_spec=pltpu.PrefetchScalarGridSpec(
            num_scalar_prefetch=len(scalars),
            grid=(1,),
            in_specs=specs,
            out_specs=out_specs,
            scratch_shapes=list(scratch),
        ),
        out_shape=out_shapes,
        input_output_aliases=aliases or {},
        compiler_params=pltpu.CompilerParams(vmem_limit_bytes=48 * 1024 * 1024),
        cost_estimate=pl.CostEstimate(flops=flops, bytes_accessed=1 << 20, transcendentals=0),
        name=name,
    )(*scalars, *operands)


def floats(*shape):
    return jax.ShapeDtypeStruct(shape, F32)


def shards(theta, target, kernel_real, kernel_imag, weights, thresholds):
    table = {name: jnp.asarray(value) for name, value in tables().items()}
    tiles = lax.axis_size("tile")
    part = lax.axis_index("cond")
    tile = lax.axis_index("tile")
    last = PARTS - 1
    above = ((part == 0) & (tile > 0)) | ((part == last) & (tile < tiles - 1))
    below = ((part == 0) & (tile < tiles - 1)) | ((part == last) & (tile > 0))
    parts = (part + PARTS * above.astype(jnp.int32) + 2 * PARTS * below.astype(jnp.int32)).reshape(1).astype(jnp.int32)
    local_conds = kernel_real.shape[0]
    local = local_conds * KERNELS
    count = CONDS * KERNELS
    hbm = pl.BlockSpec(memory_space=pltpu.HBM)

    def across(value, down, up, within):
        pairs = [(PARTS * i + a, PARTS * i + b) for i in range(tiles) for a, b in within]
        pairs += [(PARTS * (i + 1) + down[0], PARTS * i + down[1]) for i in range(tiles - 1)]
        pairs += [(PARTS * i + up[0], PARTS * (i + 1) + up[1]) for i in range(tiles - 1)]
        pairs += [(down[0], up[1]), (PARTS * (tiles - 1) + up[0], PARTS * (tiles - 1) + down[1])]
        return lax.ppermute(value, ("tile", "cond"), pairs)

    def partner(value, step):
        return lax.ppermute(value, "cond", [(i, i ^ step) for i in range(PARTS)])

    kernel_shape = (local_conds, KSUP, KERNELS, KSUP)
    own, rim, shares, forward, backward = call(
        open_kernel,
        (parts,),
        tuple(
            pltpu.with_memory_space_constraint(value, pltpu.HBM)
            for value in (
                theta, table["waves"], kernel_real.transpose(0, 2, 1, 3), kernel_imag.transpose(0, 2, 1, 3), thresholds, weights,
                table["forward"], table["backward"],
            )
        ),
        [hbm] * 8,
        [
            floats(2 * local, FA, 2 * FB),
            floats(HALO, 2 * FB),
            floats(CONDS, ROWS),
            jax.ShapeDtypeStruct(table["forward"].shape[1:], BF),
            jax.ShapeDtypeStruct(table["backward"].shape[1:], BF),
        ],
        scratch=(
            pltpu.VMEM((HALO, TP), F32),
            pltpu.VMEM(table["waves"].shape, BF),
            pltpu.VMEM(kernel_shape, F32),
            pltpu.VMEM(kernel_shape, F32),
            pltpu.SMEM(thresholds.shape, F32),
            pltpu.SMEM(weights.shape, jnp.int32),
            pltpu.VMEM((2 * local, 72, 2 * FB), F32),
            pltpu.SemaphoreType.DMA((8,)),
        ),
        name="open_parts",
    )
    rim = across(rim, (0, 0), (last, last), [(1, 2), (2, 1)])
    spectrum = call(
        spectrum_kernel,
        (parts,),
        (theta, table["column"], table["spectrum_rows"]),
        [whole_spec(theta), whole_spec(table["column"]), whole_spec(table["spectrum_rows"])],
        floats(2, FA, 2 * FB),
        name="own_spectrum",
        flops=1 << 31,
    )
    side = partner(own, 3)
    spectrum = call(
        rim_kernel,
        (parts,),
        (spectrum, rim, table["rim_rows"]),
        [whole_spec(spectrum), whole_spec(rim), whole_spec(table["rim_rows"])],
        floats(1, FA, 2 * FB),
        name="add_rim",
    )
    mixed = jnp.concatenate([own, side, spectrum + partner(spectrum, 3)], axis=0)
    near_kernels, signs = call(
        near_kernels_kernel,
        (parts,),
        (mixed, target),
        [whole_spec(mixed), whole_spec(target)],
        [floats(count // 2, 4, FA, 2 * FB), floats(TP, ROWS)],
        name="near_kernels",
        flops=1 << 30,
    )
    adjoint = call(
        fields_kernel,
        (parts,),
        (
            mixed, partner(mixed, 1), near_kernels, signs, shares, forward, backward, table["row"], table["row_turned"],
        ),
        [
            whole_spec(mixed),
            whole_spec(mixed),
            whole_spec(near_kernels),
            whole_spec(signs),
            whole_spec(shares),
            whole_spec(forward),
            whole_spec(backward),
            whole_spec(table["row"]),
            whole_spec(table["row_turned"]),
        ],
        floats(FA, 2 * FB),
        scratch=(
            pltpu.VMEM((count // 2, 4, FA, 2 * FB), F32),
            pltpu.VMEM((CONDS, ROWS), F32),
            pltpu.VMEM((count * 4 * FA, 2 * FB), F32),
            pltpu.VMEM((count, 6 * FA, 2 * ROWS), BF),
            pltpu.VMEM((count, TP, 2 * ROWS), F32),
            pltpu.VMEM((CONDS, TP, ROWS), F32),
            pltpu.VMEM((TP, ROWS), F32),
            pltpu.VMEM((count * 2, 2 * FA, ROWS), F32),
            pltpu.VMEM((count * 4 * FA, 4 * FB), F32),
        ),
        name="coherent_fields",
        flops=1 << 33,
    )
    adjoint = adjoint + partner(adjoint, 1)
    adjoint = adjoint + partner(adjoint, 3)
    near = across(adjoint, (2, last), (1, 0), [(0, 1), (last, 2)])
    gradient, edge, scale = call(
        gradient_kernel,
        (parts,),
        (theta, adjoint, table["turned"], table["own_rows"]),
        [
            whole_spec(theta),
            whole_spec(adjoint),
            whole_spec(table["turned"]),
            whole_spec(table["own_rows"]),
        ],
        [floats(ROWS, TP), floats(HALO, TP), floats(HALO, TP)],
        out_specs=[
            pl.BlockSpec((ROWS, TP), lambda i, *refs: (0, 0)),
            whole_spec(adjoint),
            whole_spec(adjoint),
        ],
        name="own_gradient",
        flops=1 << 31,
    )
    return call(
        edge_kernel,
        (parts,),
        (gradient, edge, scale, near, table["turned"], table["halo_rows"]),
        [
            hbm,
            whole_spec(edge),
            whole_spec(scale),
            whole_spec(near),
            whole_spec(table["turned"]),
            whole_spec(table["halo_rows"]),
        ],
        floats(ROWS, TP),
        scratch=(pltpu.VMEM((HALO, TP), F32), pltpu.SemaphoreType.DMA),
        name="edge_gradient",
        out_specs=hbm,
        aliases={1: 0},
    )


def solution(mesh):
    in_specs = (
        P(("tile", "cond"), None),
        P("tile", None),
        P("cond", None, None, None),
        P("cond", None, None, None),
        P(),
        P("cond"),
    )
    out_specs = P(("tile", "cond"), None)
    return jax.shard_map(shards, mesh=mesh, in_specs=in_specs, out_specs=out_specs, check_vma=False)
```

```python
import functools

import jax
import jax.numpy as jnp
import ml_dtypes
import numpy as np
from jax import lax
from jax.experimental import pallas as pl
from jax.experimental.pallas import tpu as pltpu
from jax.sharding import PartitionSpec as P

TP = 512
HALO = 32
KSUP = 65
HALF = KSUP // 2
KERNELS = 2
CONDS = 8
FULL = TP + 2 * HALO
PARTS = 4
ROWS = TP // PARTS
FA = 40
FB = 64
SPARE = FA - HALF - 1
SPARE_BLOCKS = -(-(HALF + 1) // SPARE)
BF = jnp.bfloat16
F32 = jnp.float32

mask_steep = 2.0
resist_steep = 4.0
band_weight = 1.0


def waves(positions):
    angles = (np.outer(np.asarray(positions, np.int64), np.arange(HALF + 1)) % FULL) * (2.0 * np.pi / FULL)
    return np.cos(angles), np.sin(angles)


def halves(table):
    high = table.astype(np.float32).astype(ml_dtypes.bfloat16)
    low = (table - high.astype(np.float64)).astype(np.float32).astype(ml_dtypes.bfloat16)
    return high, low


def row_table(positions):
    cosine, sine = waves(positions)
    table = np.zeros((len(positions), 2 * FA))
    table[:, : HALF + 1] = cosine
    table[:, FA : FA + HALF + 1] = sine
    return table


def pair_table(positions):
    table = row_table(positions)
    return np.concatenate([table, np.concatenate([-table[:, FA:], table[:, :FA]], axis=1)])


def column_table(positions):
    cosine, sine = waves(positions)
    table = np.zeros((len(positions), 4 * FB))
    for block, values in enumerate((cosine, cosine, sine, -sine)):
        table[:, block * FB : block * FB + HALF] = values[:, 1:]
    table[:, HALF] = 1.0
    return table


@functools.cache
def tables():
    pixels = np.arange(TP) + HALO
    column = column_table(pixels)
    column_high, column_low = halves(column)
    turned = np.concatenate([column[:, : 2 * FB].T, column[:, 2 * FB :].T], axis=1)
    turned_high, turned_low = halves(turned)
    row = row_table(pixels)
    row_high, row_low = halves(row)
    out = {}
    out["column"] = np.stack([column_high, column_low])
    waves_only = np.s_[:, np.r_[0:FB, 2 * FB : 3 * FB]]
    out["waves"] = np.stack([column_high[waves_only], column_low[waves_only]])
    spectrum_rows = []
    rim_rows = []
    halo_rows = []
    own_rows = []
    forward = []
    backward = []
    for part in range(PARTS):
        own = np.arange(ROWS) + part * ROWS + HALO
        rim = np.arange(HALO) + (0 if part == PARTS - 1 else FULL - HALO)
        for rows, positions in ((spectrum_rows, own), (rim_rows, rim)):
            high, low = halves(row_table(positions).T)
            rows.append(np.concatenate([high, low, high], axis=1))
        high, low = halves(pair_table(rim))
        halo_rows.append(np.concatenate([high, low, high], axis=1))
        high, low = halves(pair_table(own))
        own_rows.append(np.concatenate([high, low, high], axis=1))
        cols = slice(part * ROWS, (part + 1) * ROWS)
        high = np.concatenate([turned_high[:, :TP][:, cols], turned_high[:, TP:][:, cols]], axis=1)
        low = np.concatenate([turned_low[:, :TP][:, cols], turned_low[:, TP:][:, cols]], axis=1)
        forward.append(np.concatenate([high, high, low]))
        backward.append(np.concatenate([column_high[cols], column_high[cols], column_low[cols]]))
    out["spectrum_rows"] = np.stack(spectrum_rows)
    out["own_rows"] = np.stack(own_rows)
    out["rim_rows"] = np.stack(rim_rows)
    out["halo_rows"] = np.stack(halo_rows)
    out["forward"] = np.stack(forward)
    out["backward"] = np.stack(backward)
    out["turned"] = np.stack([column_high.T, column_low.T])
    out["row"] = np.concatenate([row_high, row_low, row_high], axis=1)
    out["row_turned"] = np.concatenate([row_high.T, row_low.T])
    return out


def part_of(ref):
    return ref[0] % PARTS


def has_adjoint_halo(ref):
    return ref[0] // PARTS % 2 > 0


def has_mask_halo(ref):
    return ref[0] // (2 * PARTS) > 0


def dot(left, right):
    return jnp.dot(left, right, preferred_element_type=F32)


def split(value):
    high = value.astype(BF)
    return high, (value - high.astype(F32)).astype(BF)


def lanes_and_rows():
    shape = (FA, 2 * FB)
    return lax.broadcasted_iota(jnp.int32, shape, 1), lax.broadcasted_iota(jnp.int32, shape, 0)


def pack(even, odd):
    lane, row = lanes_and_rows()
    packed = jnp.where(lane % FB < HALF, even, pltpu.roll(odd, HALF, 1))
    for place, value in ((FA - 2, even), (FA - 3, odd)):
        line = jnp.sum(jnp.where(lane == row, value[:, HALF : HALF + 1], 0.0), axis=0, keepdims=True)
        packed = jnp.where(row == place, line, packed)
    return packed


def unpack(packed):
    lane, row = lanes_and_rows()
    values = []
    for place, value in ((FA - 2, packed), (FA - 3, pltpu.roll(packed, 2 * FB - HALF, 1))):
        column = jnp.sum(jnp.where((lane == row) & (row <= HALF), packed[place : place + 1], 0.0), axis=1, keepdims=True)
        value = jnp.where(lane == HALF, column, jnp.where(lane % FB < HALF, value, 0.0))
        values.append(jnp.where(row <= HALF, value, 0.0))
    return values


def columns_of(mask, column_ref):
    high, low = split(mask)
    return dot(high, column_ref[0]) + dot(low, column_ref[0]) + dot(high, column_ref[1])


def spectrum_of(across, rows):
    high, low = split(across)
    both = dot(rows, jnp.concatenate([high, high, low], axis=0))
    even = both[:FA, : 2 * FB] - both[FA:, 2 * FB :]
    odd = both[FA:, : 2 * FB] + both[:FA, 2 * FB :]
    return even, odd


def open_kernel(
    part_ref, theta_hbm, waves_hbm, real_hbm, imag_hbm, thresholds_hbm, weights_hbm, forward_hbm, backward_hbm,
    out_ref, rim_ref, shares_ref, forward_ref, backward_ref, theta_ref, waves_ref, real_ref, imag_ref, thresholds_ref,
    weights_ref, stage, sems,
):
    part = part_of(part_ref)
    edge = pl.ds(pl.multiple_of(jnp.where(part == 0, 0, ROWS - HALO), HALO), HALO)
    moves = [
        (theta_hbm.at[edge], theta_ref),
        (waves_hbm, waves_ref),
        (real_hbm, real_ref),
        (imag_hbm, imag_ref),
        (thresholds_hbm, thresholds_ref),
        (weights_hbm, weights_ref),
        (forward_hbm.at[part], forward_ref),
        (backward_hbm.at[part], backward_ref),
    ]
    copies = [pltpu.make_async_copy(source, target, sems.at[i]) for i, (source, target) in enumerate(moves)]
    for copy in copies:
        copy.start()
    local_conds = real_ref.shape[0]
    mats = local_conds * KERNELS * 2
    stage[...] = jnp.zeros_like(stage)
    rows = stage.shape[1]
    source = lax.broadcasted_iota(jnp.int32, (2 * FB, 4 * FB), 0)
    target = lax.broadcasted_iota(jnp.int32, (2 * FB, 4 * FB), 1)
    lane = target % FB
    block = target // FB
    plus = (block == 0) | (block == 3)
    freq = jnp.where(lane < HALF, lane + 1, 0)
    used = (lane < HALF) | ((lane == HALF) & (block % 2 == 0))
    pick = (used & (source == jnp.where(plus, HALF + freq, HALF - freq))).astype(F32).astype(BF)
    source = lax.broadcasted_iota(jnp.int32, (FA, 2 * rows), 1) % rows
    target = lax.broadcasted_iota(jnp.int32, (FA, 2 * rows), 0)
    turn = ((source == HALF - target) & (target <= HALF)).astype(F32).astype(BF)
    lane = lax.broadcasted_iota(jnp.int32, (FA, 2 * FB), 1)
    row = lax.broadcasted_iota(jnp.int32, (FA, 2 * FB), 0)
    valid = (row <= HALF) & ((lane <= HALF) | ((row > 0) & (lane >= FB) & (lane < FB + HALF)))
    scale = 1.0 / (FULL * FULL)
    keep_top = jnp.where(valid, scale, 0.0)
    keep_bottom = jnp.where((row == 0) & (lane == HALF), 0.0, keep_top)
    first = lane % FB < HALF
    for copy in copies[:6]:
        copy.wait()
    rim_ref[...] = columns_of(jnp.tanh(mask_steep * theta_ref[...]), waves_ref)
    for cond in range(local_conds):
        for kern in range(KERNELS):
            for piece, ref in enumerate((real_ref, imag_ref)):
                stage[(cond * KERNELS + kern) * 2 + piece, :KSUP, :KSUP] = ref[cond, :, kern, :]
    high, low = split(stage[...].reshape(mats * rows, 2 * FB))
    picked = [dot(piece, pick) for piece in (high, low)]
    extra = jnp.zeros((FA, 2 * FB), F32)
    blocks = []
    for kern in range(local_conds * KERNELS):
        arrays = [[], []]
        for piece in range(2):
            start = (kern * 2 + piece) * rows
            top = picked[0][start + HALF : start + HALF + FA, : 2 * FB] + picked[1][start + HALF : start + HALF + FA, : 2 * FB]
            pieces = jnp.concatenate([half[start : start + rows, 2 * FB :] for half in picked], axis=0)
            bottom = dot(turn, pieces.astype(BF)) * keep_bottom
            top = top * keep_top
            arrays[0].append(top + bottom)
            arrays[1].append(top - bottom)
        for which, (real, imag) in enumerate(arrays):
            blocks.append(jnp.where(first, real, pltpu.roll(imag, HALF, 1)))
            for piece, value in enumerate((real, imag)):
                place = kern * 4 + which * 2 + piece
                extra = jnp.where(lane == place, pltpu.roll(value, (place - HALF) % (2 * FB), 1), extra)
    for i, block in enumerate(blocks):
        if i < SPARE_BLOCKS:
            block = jnp.concatenate([block[: HALF + 1], extra[SPARE * i : SPARE * (i + 1)]], axis=0)
        elif i < SPARE_BLOCKS + local_conds:
            block = jnp.where(row == FA - 1, thresholds_ref[i - SPARE_BLOCKS], block)
        out_ref[i] = block
    weight_sum = weights_ref[0]
    for i in range(1, CONDS):
        weight_sum = weight_sum + weights_ref[i]
    row = lax.broadcasted_iota(jnp.int32, shares_ref.shape, 0)
    shares = jnp.zeros(shares_ref.shape, F32)
    for group, step in enumerate((0, 3, 1, 2)):
        for i in range(local_conds):
            weight = weights_ref[lax.bitwise_xor(part, step) * local_conds + i]
            shares = jnp.where(row == group * local_conds + i, weight.astype(F32), shares)
    shares_ref[...] = shares / weight_sum.astype(F32)
    for copy in copies[6:]:
        copy.wait()


def spectrum_kernel(part_ref, theta_ref, column_ref, rows_ref, out_ref):
    across = columns_of(jnp.tanh(mask_steep * theta_ref[...]), column_ref)
    even, odd = spectrum_of(across, rows_ref[part_of(part_ref)])
    out_ref[0] = even
    out_ref[1] = odd


def rim_kernel(part_ref, spectrum_ref, rim_ref, rows_ref, out_ref):
    rim = jnp.where(has_mask_halo(part_ref), rim_ref[...], 0.0)
    turned = pltpu.roll(rim, FB, 1)
    first = lax.broadcasted_iota(jnp.int32, rim.shape, 1) < FB
    across = jnp.concatenate([jnp.where(first, rim, turned), jnp.where(first, turned, -rim)], axis=1)
    even, odd = spectrum_of(across, rows_ref[part_of(part_ref)])
    out_ref[0] = pack(even + spectrum_ref[0], odd + spectrum_ref[1])


def unpack_group(ref, put):
    lane, row = lanes_and_rows()
    zero_lane = (lane == HALF) & (row <= HALF)
    extra = [ref[i][HALF + 1 :] for i in range(SPARE_BLOCKS)]
    extra = jnp.concatenate(extra + [jnp.zeros((FA - SPARE * SPARE_BLOCKS, 2 * FB), F32)], axis=0)
    for kern in range(ref.shape[0] // 2):
        values = []
        for which in range(2):
            packed = ref[2 * kern + which]
            for part, value in enumerate((packed, pltpu.roll(packed, 2 * FB - HALF, 1))):
                place = kern * 4 + which * 2 + part
                zeroth = pltpu.roll(extra, (HALF - place) % (2 * FB), 1)
                values.append(jnp.where(zero_lane, zeroth, value))
        put(kern, values)


def near_kernels_kernel(part_ref, mixed_ref, target_ref, near_ref, signs_ref):
    local = near_ref.shape[0] // 2
    for group in range(2):
        def put(kern, values, group=group):
            for i, value in enumerate(values):
                near_ref[group * local + kern, i] = value

        unpack_group(mixed_ref.at[pl.ds(group * 2 * local, 2 * local)], put)
    own = pl.ds(pl.multiple_of(part_of(part_ref) * ROWS, ROWS), ROWS)
    signs_ref[...] = 1.0 - 2.0 * target_ref[:, own].astype(F32)


def fields_kernel(
    part_ref, mixed_ref, other_ref, near_ref, signs, shares_ref, forward_ref, backward_ref, row_ref,
    row_turned_ref, out_ref, far_ref, levels_ref, lines, folded, amps, tanhs, total, turned, backs,
):
    count = 2 * far_ref.shape[0]
    local = count // PARTS
    tall = 4 * FA
    each = 2 * local
    even, odd = unpack(mixed_ref[2 * each] + other_ref[2 * each])

    def put_line(kern, values):
        he_real, he_imag, ho_real, ho_imag = values
        start = kern * tall
        for i, value in enumerate(
            (
                even * he_real + odd * ho_imag,
                odd * he_real - even * ho_imag,
                even * he_imag - odd * ho_real,
                odd * he_imag + even * ho_real,
            )
        ):
            lines[start + i * FA : start + (i + 1) * FA] = value

    def arrays_of(kern):
        ref = near_ref if kern < count // 2 else far_ref
        return [ref[kern % (count // 2), i] for i in range(4)]

    for group in range(PARTS):
        ref = (mixed_ref, other_ref)[group // 2].at[pl.ds(group % 2 * each, each)]
        for i in range(CONDS // PARTS):
            place = group * (CONDS // PARTS) + i
            levels_ref[place : place + 1] = ref[SPARE_BLOCKS + i][FA - 1 :]
        if group < 2:
            for kern in range(group * local, (group + 1) * local):
                put_line(kern, arrays_of(kern))
        else:
            def put(kern, values, group=group):
                for i, value in enumerate(values):
                    far_ref[(group - 2) * local + kern, i] = value
                put_line(group * local + kern, values)

            unpack_group(ref, put)

    deep = count // 2 * tall
    line_products = []
    for half in range(2):
        high, low = split(lines[half * deep : (half + 1) * deep])
        line_products.append(
            dot(jnp.concatenate([high, low], axis=1), forward_ref[: 4 * FB]) + dot(high, forward_ref[4 * FB :])
        )
    for kern in range(count):
        lines_folded = line_products[kern // (count // 2)]
        parts = []
        base = tall * (kern % (count // 2))
        for i in range(2):
            x_part = lines_folded[base + 2 * FA * i : base + 2 * FA * i + FA]
            y_part = lines_folded[base + 2 * FA * i + FA : base + 2 * FA * (i + 1)]
            parts.append(
                jnp.concatenate(
                    [x_part[:, :ROWS] + y_part[:, ROWS:], y_part[:, :ROWS] - x_part[:, ROWS:]], axis=0
                )
            )
        high, low = split(jnp.concatenate(parts, axis=1))
        folded[kern] = jnp.concatenate([high, high, low], axis=0)
    total[...] = jnp.zeros_like(total)

    def expose(cond, carry):
        intensity = None
        for kern in range(KERNELS):
            index = cond * KERNELS + kern
            amp = dot(row_ref[...], folded[index])
            amps[index] = amp
            power = amp[:, :ROWS] * amp[:, :ROWS] + amp[:, ROWS:] * amp[:, ROWS:]
            intensity = power if intensity is None else intensity + power
        level = levels_ref[pl.ds(cond, 1), :]
        value = jnp.tanh((0.5 * resist_steep) * (intensity - level))
        tanhs[cond] = value
        total[...] += value
        return carry

    lax.fori_loop(0, CONDS, expose, 0, unroll=4)
    total[...] = total[...] * (band_weight / (CONDS * CONDS))

    def drive(cond, carry):
        weight = shares_ref[pl.ds(cond, 1), :]
        value = tanhs[cond]
        slope = (weight + band_weight / CONDS) * value + weight * signs[...] - total[...]
        field = (0.5 * resist_steep) * (1.0 - value * value) * slope
        field = jnp.concatenate([field, field], axis=1)
        for kern in range(KERNELS):
            index = cond * KERNELS + kern
            high, low = split(field * amps[index])
            long = dot(row_turned_ref[...], high)
            back = long[: 2 * FA] + long[2 * FA :] + dot(row_turned_ref[: 2 * FA], low)
            turned[pl.ds(index * 2, 2)] = jnp.stack([back[:, :ROWS], back[:, ROWS:]])
        return carry

    for half in range(2):
        for cond in range(half * CONDS // 2, (half + 1) * CONDS // 2):
            drive(cond, 0)
        high, low = split(turned[half * count : (half + 1) * count].reshape(count // 2 * tall, ROWS))
        backs[half * count // 2 * tall : (half + 1) * count // 2 * tall] = dot(
            jnp.concatenate([high, low], axis=1), backward_ref[: 2 * ROWS]
        ) + dot(high, backward_ref[2 * ROWS :])

    sum_even = jnp.zeros((FA, 2 * FB), F32)
    sum_odd = jnp.zeros((FA, 2 * FB), F32)
    for kern in range(count):
        grads = []
        for i in range(2):
            c_part = backs[tall * kern + 2 * FA * i : tall * kern + 2 * FA * i + FA]
            s_part = backs[tall * kern + 2 * FA * i + FA : tall * kern + 2 * FA * (i + 1)]
            grads.append(
                (
                    c_part[:, : 2 * FB] - s_part[:, 2 * FB :],
                    s_part[:, : 2 * FB] + c_part[:, 2 * FB :],
                )
            )
        (x_real, y_real), (x_imag, y_imag) = grads
        he_real, he_imag, ho_real, ho_imag = arrays_of(kern)
        sum_even = sum_even + x_real * he_real + x_imag * he_imag - y_real * ho_imag + y_imag * ho_real
        sum_odd = sum_odd + x_real * ho_imag - x_imag * ho_real + y_real * he_real + y_imag * he_imag
    out_ref[...] = pack(sum_even, sum_odd)


def image_rows(packed, rows, turned_ref):
    high, low = split(jnp.concatenate(unpack(packed), axis=0))
    pair = dot(rows, jnp.concatenate([high, high, low], axis=0))
    count = pair.shape[0] // 2
    high, low = split(jnp.concatenate([pair[:count], pair[count:]], axis=1))
    return dot(high, turned_ref[0]) + dot(low, turned_ref[0]) + dot(high, turned_ref[1])


def edge_start(part_ref):
    return pl.multiple_of(jnp.where(part_of(part_ref) == PARTS - 1, ROWS - HALO, 0), HALO)


def gradient_kernel(part_ref, theta_ref, sum_ref, turned_ref, rows_ref, out_ref, edge_ref, scale_ref):
    part = part_of(part_ref)
    mask = jnp.tanh(mask_steep * theta_ref[...])
    scale = mask_steep * (1.0 - mask * mask)
    gradient = image_rows(sum_ref[...], rows_ref[part], turned_ref) * scale
    out_ref[...] = gradient
    last = part == PARTS - 1
    edge_ref[...] = jnp.where(last, gradient[ROWS - HALO :], gradient[:HALO])
    scale_ref[...] = jnp.where(last, scale[ROWS - HALO :], scale[:HALO])


def edge_kernel(part_ref, gradient_hbm, edge_ref, scale_ref, near_ref, turned_ref, rows_ref, out_hbm, stage, sem):
    @pl.when(has_adjoint_halo(part_ref))
    def _():
        rim = image_rows(near_ref[...], rows_ref[part_of(part_ref)], turned_ref)
        stage[...] = edge_ref[...] + rim * scale_ref[...]
        copy = pltpu.make_async_copy(stage, out_hbm.at[pl.ds(edge_start(part_ref), HALO)], sem)
        copy.start()
        copy.wait()


def whole_spec(array):
    del array
    return pl.BlockSpec(memory_space=pltpu.VMEM)


def call(kernel, scalars, operands, specs, out_shapes, scratch=(), name=None, flops=1 << 28, out_specs=None, aliases=None):
    many = isinstance(out_shapes, list)
    if out_specs is None:
        out_specs = [whole_spec(shape) for shape in out_shapes] if many else whole_spec(out_shapes)
    return pl.pallas_call(
        kernel,
        grid_spec=pltpu.PrefetchScalarGridSpec(
            num_scalar_prefetch=len(scalars),
            grid=(1,),
            in_specs=specs,
            out_specs=out_specs,
            scratch_shapes=list(scratch),
        ),
        out_shape=out_shapes,
        input_output_aliases=aliases or {},
        compiler_params=pltpu.CompilerParams(vmem_limit_bytes=48 * 1024 * 1024),
        cost_estimate=pl.CostEstimate(flops=flops, bytes_accessed=1 << 20, transcendentals=0),
        name=name,
    )(*scalars, *operands)


def floats(*shape):
    return jax.ShapeDtypeStruct(shape, F32)


def shards(theta, target, kernel_real, kernel_imag, weights, thresholds):
    table = {name: jnp.asarray(value) for name, value in tables().items()}
    tiles = lax.axis_size("tile")
    part = lax.axis_index("cond")
    tile = lax.axis_index("tile")
    last = PARTS - 1
    above = ((part == 0) & (tile > 0)) | ((part == last) & (tile < tiles - 1))
    below = ((part == 0) & (tile < tiles - 1)) | ((part == last) & (tile > 0))
    parts = (part + PARTS * above.astype(jnp.int32) + 2 * PARTS * below.astype(jnp.int32)).reshape(1).astype(jnp.int32)
    local_conds = kernel_real.shape[0]
    local = local_conds * KERNELS
    count = CONDS * KERNELS
    hbm = pl.BlockSpec(memory_space=pltpu.HBM)

    def across(value, down, up, within):
        pairs = [(PARTS * i + a, PARTS * i + b) for i in range(tiles) for a, b in within]
        pairs += [(PARTS * (i + 1) + down[0], PARTS * i + down[1]) for i in range(tiles - 1)]
        pairs += [(PARTS * i + up[0], PARTS * (i + 1) + up[1]) for i in range(tiles - 1)]
        pairs += [(down[0], up[1]), (PARTS * (tiles - 1) + up[0], PARTS * (tiles - 1) + down[1])]
        return lax.ppermute(value, ("tile", "cond"), pairs)

    def partner(value, step):
        return lax.ppermute(value, "cond", [(i, i ^ step) for i in range(PARTS)])

    kernel_shape = (local_conds, KSUP, KERNELS, KSUP)
    own, rim, shares, forward, backward = call(
        open_kernel,
        (parts,),
        tuple(
            pltpu.with_memory_space_constraint(value, pltpu.HBM)
            for value in (
                theta, table["waves"], kernel_real.transpose(0, 2, 1, 3), kernel_imag.transpose(0, 2, 1, 3), thresholds, weights,
                table["forward"], table["backward"],
            )
        ),
        [hbm] * 8,
        [
            floats(2 * local, FA, 2 * FB),
            floats(HALO, 2 * FB),
            floats(CONDS, ROWS),
            jax.ShapeDtypeStruct(table["forward"].shape[1:], BF),
            jax.ShapeDtypeStruct(table["backward"].shape[1:], BF),
        ],
        scratch=(
            pltpu.VMEM((HALO, TP), F32),
            pltpu.VMEM(table["waves"].shape, BF),
            pltpu.VMEM(kernel_shape, F32),
            pltpu.VMEM(kernel_shape, F32),
            pltpu.SMEM(thresholds.shape, F32),
            pltpu.SMEM(weights.shape, jnp.int32),
            pltpu.VMEM((2 * local, 72, 2 * FB), F32),
            pltpu.SemaphoreType.DMA((8,)),
        ),
        name="open_parts",
    )
    rim = across(rim, (0, 0), (last, last), [(1, 2), (2, 1)])
    spectrum = call(
        spectrum_kernel,
        (parts,),
        (theta, table["column"], table["spectrum_rows"]),
        [whole_spec(theta), whole_spec(table["column"]), whole_spec(table["spectrum_rows"])],
        floats(2, FA, 2 * FB),
        name="own_spectrum",
        flops=1 << 31,
    )
    side = partner(own, 3)
    spectrum = call(
        rim_kernel,
        (parts,),
        (spectrum, rim, table["rim_rows"]),
        [whole_spec(spectrum), whole_spec(rim), whole_spec(table["rim_rows"])],
        floats(1, FA, 2 * FB),
        name="add_rim",
    )
    mixed = jnp.concatenate([own, side, spectrum + partner(spectrum, 3)], axis=0)
    near_kernels, signs = call(
        near_kernels_kernel,
        (parts,),
        (mixed, target),
        [whole_spec(mixed), whole_spec(target)],
        [floats(count // 2, 4, FA, 2 * FB), floats(TP, ROWS)],
        name="near_kernels",
        flops=1 << 30,
    )
    adjoint = call(
        fields_kernel,
        (parts,),
        (
            mixed, partner(mixed, 1), near_kernels, signs, shares, forward, backward, table["row"], table["row_turned"],
        ),
        [
            whole_spec(mixed),
            whole_spec(mixed),
            whole_spec(near_kernels),
            whole_spec(signs),
            whole_spec(shares),
            whole_spec(forward),
            whole_spec(backward),
            whole_spec(table["row"]),
            whole_spec(table["row_turned"]),
        ],
        floats(FA, 2 * FB),
        scratch=(
            pltpu.VMEM((count // 2, 4, FA, 2 * FB), F32),
            pltpu.VMEM((CONDS, ROWS), F32),
            pltpu.VMEM((count * 4 * FA, 2 * FB), F32),
            pltpu.VMEM((count, 6 * FA, 2 * ROWS), BF),
            pltpu.VMEM((count, TP, 2 * ROWS), F32),
            pltpu.VMEM((CONDS, TP, ROWS), F32),
            pltpu.VMEM((TP, ROWS), F32),
            pltpu.VMEM((count * 2, 2 * FA, ROWS), F32),
            pltpu.VMEM((count * 4 * FA, 4 * FB), F32),
        ),
        name="coherent_fields",
        flops=1 << 33,
    )
    adjoint = adjoint + partner(adjoint, 1)
    adjoint = adjoint + partner(adjoint, 3)
    near = across(adjoint, (2, last), (1, 0), [(0, 1), (last, 2)])
    gradient, edge, scale = call(
        gradient_kernel,
        (parts,),
        (theta, adjoint, table["turned"], table["own_rows"]),
        [
            whole_spec(theta),
            whole_spec(adjoint),
            whole_spec(table["turned"]),
            whole_spec(table["own_rows"]),
        ],
        [floats(ROWS, TP), floats(HALO, TP), floats(HALO, TP)],
        out_specs=[
            pl.BlockSpec((ROWS, TP), lambda i, *refs: (0, 0)),
            whole_spec(adjoint),
            whole_spec(adjoint),
        ],
        name="own_gradient",
        flops=1 << 31,
    )
    return call(
        edge_kernel,
        (parts,),
        (gradient, edge, scale, near, table["turned"], table["halo_rows"]),
        [
            hbm,
            whole_spec(edge),
            whole_spec(scale),
            whole_spec(near),
            whole_spec(table["turned"]),
            whole_spec(table["halo_rows"]),
        ],
        floats(ROWS, TP),
        scratch=(pltpu.VMEM((HALO, TP), F32), pltpu.SemaphoreType.DMA),
        name="edge_gradient",
        out_specs=hbm,
        aliases={1: 0},
    )


def solution(mesh):
    in_specs = (
        P(("tile", "cond"), None),
        P("tile", None),
        P("cond", None, None, None),
        P("cond", None, None, None),
        P(),
        P("cond"),
    )
    out_specs = P(("tile", "cond"), None)
    return jax.shard_map(shards, mesh=mesh, in_specs=in_specs, out_specs=out_specs, check_vma=False)
```
